32 devices in a mesh: dp: 4 (over z), seq: 8 (over y, x, core).
Axes of the slice: x: 2, y: 2, z: 4, core: 2. Of those that a mesh axis runs over, the one named last changes fastest.
Arguments:
- inputs: float32 [8, 2048, 1536], P('dp', 'seq'), may hold values from -6 to 6
- segments: int32 [8, 2048], P('dp', 'seq'), may hold values from -1 to 7, as said below
- norm1_gain: float32 [1536], replicated, may hold values from 0.25 to 1.75
- norm1_bias: float32 [1536], replicated, may hold values from -3 to 3
- w_query: bfloat16 [1536, 1536], P(('dp', 'seq')), may hold values from -0.15625 to 0.15625
- w_key: bfloat16 [1536, 1536], P(('dp', 'seq')), may hold values from -0.15625 to 0.15625
- w_value: bfloat16 [1536, 1536], P(('dp', 'seq')), may hold values from -0.15625 to 0.15625
- w_out: bfloat16 [1536, 1536], P(('dp', 'seq')), may hold values from -0.625 to 0.625
- norm2_gain: float32 [1536], replicated, may hold values from 0.25 to 1.75
- norm2_bias: float32 [1536], replicated, may hold values from -3 to 3
- w_up: bfloat16 [1536, 6144], P(('dp', 'seq')), may hold values from -0.15625 to 0.15625
- w_down: bfloat16 [6144, 1536], P(('dp', 'seq')), may hold values from -0.078125 to 0.078125
- cotangent: float32 [8, 2048, 1536], P('dp', 'seq'), may hold values from -6 to 6
Outputs:
- output: float32 [8, 2048, 1536], P('dp', 'seq')
- d_inputs: float32 [8, 2048, 1536], P('dp', 'seq')
- d_norm1_gain: float32 [1536], P(('dp', 'seq'))
- d_norm1_bias: float32 [1536], P(('dp', 'seq'))
- d_w_query: float32 [1536, 1536], P(('dp', 'seq'))
- d_w_key: float32 [1536, 1536], P(('dp', 'seq'))
- d_w_value: float32 [1536, 1536], P(('dp', 'seq'))
- d_w_out: float32 [1536, 1536], P(('dp', 'seq'))
- d_norm2_gain: float32 [1536], P(('dp', 'seq'))
- d_norm2_bias: float32 [1536], P(('dp', 'seq'))
- d_w_up: float32 [1536, 6144], P(('dp', 'seq'))
- d_w_down: float32 [6144, 1536], P(('dp', 'seq'))
The draws below stay inside these ranges and needn't reach their ends.
Inputs may be any that keep to these rules, and one draw needn't show every extreme that they name: `segments`: along each sequence the ids start at 0 and rise by one at the first token of each later document; the last 1 to 128 tokens are padding with id -1.
All inputs are finite; a program needn't handle non-finite values.
Results may differ from the reference program's by a relative error of at most 0.019.
Values may be sent and summed in bfloat16 or wider, within the bound.
A program may use at most 320 MiB of HBM per device.

```python
import math
import jax
import jax.numpy as jnp
from jax import lax

D = 1536
HEADS = 12
HEAD_DIM = 128
FF = 6144
LEN = 2048
SEQ_GROUP = 2
COLS = 256
SEQS = 8


def draw_segments(key, part):
    key = jax.random.fold_in(key, 11)
    first_key, second_key, third_key = jax.random.split(key, 3)
    places = jnp.arange(LEN, dtype=jnp.int32)
    starts = jax.random.randint(first_key, (SEQS, LEN), 0, LEN // 4) == 0
    starts = starts & (places[None, :] > 0)
    longest = jax.random.randint(second_key, (SEQS // SEQ_GROUP,), 0, SEQ_GROUP)
    rows = jnp.arange(SEQS, dtype=jnp.int32)
    chosen = rows % SEQ_GROUP == longest[rows // SEQ_GROUP]
    forced = rows % SEQ_GROUP == (longest[rows // SEQ_GROUP] + 1) % SEQ_GROUP
    marks = (places % (LEN // 8) == 0) & (places > 0)
    starts = jnp.where(chosen[:, None] & (places[None, :] >= COLS // 2), False, starts)
    starts = jnp.where(forced[:, None], marks[None, :], starts)
    ids = jnp.minimum(jnp.cumsum(starts.astype(jnp.int32), axis=1), 7).astype(jnp.int32)
    padding = jax.random.randint(third_key, (SEQS, 1), 1, COLS // 2 + 1)
    ids = jnp.where(places[None, :] >= LEN - padding, -1, ids)
    return ids.astype(jnp.int32)


def steps_of(key, extent, cuts, low, top_value):
    def one(dim, shards_of):
        heights = jax.random.uniform(jax.random.fold_in(jax.random.fold_in(key, 6), dim), (shards_of,), jnp.float32, low / len(cuts), top_value / len(cuts))
        return jnp.repeat(jnp.exp(heights), extent[dim] // shards_of).reshape((-1,) + (1,) * (len(extent) - dim - 1))

    level = one(*cuts[0])
    for cut in cuts[1:]:
        level = level * one(*cut)
    return level


def gaussian(own_key, dims, scale, most, shards=(), kind=jnp.bfloat16):
    result = jax.random.normal(own_key, dims, jnp.float32) * scale
    if len(shards) > 0:
        result = steps_of(own_key, dims, shards, -0.22, 0.18) * result
    return jnp.clip(result, min=-most, max=most).astype(kind)


def setup_inputs(seed: int = 0) -> dict:
    arg_keys = jax.random.split(jax.random.key(seed), 14)
    return {
        "inputs": gaussian(arg_keys[0], (SEQS, LEN, D), 1.0, 6.0, ((0, 4), (1, 8)), jnp.float32),
        "segments": draw_segments(jax.random.fold_in(arg_keys[13], 71), 0),
        "norm1_gain": jnp.clip(1.0 + 0.15 * jax.random.normal(arg_keys[2], (D,), jnp.float32), 0.25, 1.75),
        "norm1_bias": gaussian(arg_keys[3], (D,), 0.5, 3.0, (), jnp.float32),
        "w_query": gaussian(arg_keys[4], (D, D), D ** -0.5, 0.15625, ((0, 32),)),
        "w_key": gaussian(arg_keys[5], (D, D), D ** -0.5, 0.15625, ((0, 32),)),
        "w_value": gaussian(arg_keys[6], (D, D), D ** -0.5, 0.15625, ((0, 32),)),
        "w_out": gaussian(arg_keys[7], (D, D), (D // 16) ** -0.5, 0.625, ((0, 32),)),
        "norm2_gain": jnp.clip(1.0 + 0.15 * jax.random.normal(arg_keys[8], (D,), jnp.float32), 0.25, 1.75),
        "norm2_bias": gaussian(arg_keys[9], (D,), 0.5, 3.0, (), jnp.float32),
        "w_up": gaussian(arg_keys[10], (D, FF), D ** -0.5, 0.15625, ((0, 32),)),
        "w_down": gaussian(arg_keys[11], (FF, D), FF ** -0.5, 0.078125, ((0, 32),)),
        "cotangent": gaussian(arg_keys[12], (SEQS, LEN, D), 1.0, 6.0, ((0, 4), (1, 8)), jnp.float32),
    }


@jax.custom_vjp
def low(v):
    return lax.optimization_barrier(v.astype(jnp.bfloat16)).astype(jnp.float32)

@jax.custom_vjp
def low_back(v):
    return v

def low_keep(v):
    return (low(v), None)

def low_pass(kept, grad):
    return (grad,)

def back_keep(v):
    return (v, None)

def back_low(kept, grad):
    return (low(grad),)
low.defvjp(low_keep, low_pass)
low_back.defvjp(back_keep, back_low)
EPSILON = 1e-05
MASKED = -1e+30

def layer_norm(values, gain, offset):
    centre = values - lax.optimization_barrier(jnp.mean(values, axis=-1, keepdims=True))
    spread = lax.optimization_barrier(jnp.mean(centre * centre, axis=-1, keepdims=True))
    return centre * lax.rsqrt(spread + EPSILON) * gain + offset

def gelu(values):
    return 0.5 * values * (1.0 + lax.erf(values * (1.0 / math.sqrt(2.0))))

def angles(positions):
    half = HEAD_DIM // 2
    rates = jnp.exp(jnp.arange(half, dtype=jnp.float32) * (-math.log(10000.0) / half))
    turned = positions.astype(jnp.float32)[:, None] * rates[None, :]
    return (jnp.cos(turned)[:, None, :], jnp.sin(turned)[:, None, :])

def rotary(values, cosine, sine):
    half = values.shape[-1] // 2
    first = values[..., :half]
    second = values[..., half:]
    return jnp.concatenate([first * cosine - second * sine, second * cosine + first * sine], axis=-1)

def matmul(left, right):
    return jnp.dot(left, right, precision=lax.Precision.HIGHEST, preferred_element_type=jnp.float32)

def one_sequence(tokens, segment_row, params):
    gain_one, offset_one, weight_query, weight_key, weight_value, weight_out, gain_two, offset_two, weight_up, weight_down = params
    length = tokens.shape[0]
    places = jnp.arange(length, dtype=jnp.int32)
    cosine, sine = angles(places)
    act_one = low(layer_norm(tokens, gain_one, offset_one))
    query = low_back(matmul(act_one, weight_query)).reshape(length, HEADS, HEAD_DIM)
    keys = low_back(matmul(act_one, weight_key)).reshape(length, HEADS, HEAD_DIM)
    vals = low(low_back(matmul(act_one, weight_value))).reshape(length, HEADS, HEAD_DIM)
    query = low(rotary(query, cosine, sine))
    keys = low(rotary(keys, cosine, sine))
    raw = jnp.einsum('qhd,khd->hqk', query, keys, precision=lax.Precision.HIGHEST, preferred_element_type=jnp.float32) * (1.0 / math.sqrt(HEAD_DIM))
    allowed = (places[None, :] <= places[:, None]) & (segment_row[None, :] == segment_row[:, None])
    allowed = allowed & ((segment_row[None, :] >= 0) | (places[None, :] == places[:, None]))
    scores = jnp.where(allowed[None], low_back(raw), MASKED)
    top = lax.optimization_barrier(jnp.max(scores, axis=-1, keepdims=True))
    expo = jnp.exp(scores - top)
    probs = low(expo / lax.optimization_barrier(jnp.sum(expo, axis=-1, keepdims=True)))
    mixed = jnp.einsum('hqk,khd->qhd', probs, vals, precision=lax.Precision.HIGHEST, preferred_element_type=jnp.float32).reshape(length, HEADS * HEAD_DIM)
    mixed = low(low_back(mixed))
    first_sum = tokens + low_back(matmul(mixed, weight_out))
    act_two = low(layer_norm(first_sum, gain_two, offset_two))
    upper = low_back(matmul(act_two, weight_up))
    hidden = low(gelu(upper))
    return first_sum + low_back(matmul(hidden, weight_down))

def reference(inputs, segments, norm1_gain, norm1_bias, w_query, w_key, w_value, w_out, norm2_gain, norm2_bias, w_up, w_down, cotangent):
    params = tuple((item.astype(jnp.float32) for item in (norm1_gain, norm1_bias, w_query, w_key, w_value, w_out, norm2_gain, norm2_bias, w_up, w_down)))
    step = jax.checkpoint(one_sequence)

    def forward(rows_in, weights):
        return lax.map(lambda pair: step(pair[0], pair[1], weights), (rows_in, segments))
    output, pull = jax.vjp(forward, inputs, params)
    d_inputs, grads = pull(cotangent)
    return (output, d_inputs, grads[0], grads[1], grads[2], grads[3], grads[4], grads[5], grads[6], grads[7], grads[8], grads[9])
```

```python
import functools
import math

import jax
import jax.numpy as jnp
from jax import lax
from jax.experimental import pallas as pl
from jax.experimental.pallas import tpu as pltpu
from jax.sharding import PartitionSpec as P

HEAD_DIM = 128


EPSILON = 1e-05
MASKED = -1e30
LOG2E = math.log2(math.e)
NT = (((1,), (1,)), ((), ()))
NN = (((1,), (0,)), ((), ()))


def dot(left, right, dims=NN):
    return lax.dot_general(left, right, dims, preferred_element_type=jnp.float32)


def allowed_pairs(key_col, query_row, diagonal):
    same = key_col == query_row
    if not diagonal:
        return same
    shape = (key_col.shape[0], query_row.shape[1])
    key_at = lax.broadcasted_iota(jnp.int32, shape, 0)
    query_at = lax.broadcasted_iota(jnp.int32, shape, 1)
    return (same & (key_at <= query_at)) | (key_at == query_at)


def attend_kernel(block, parts, q_ref, k_ref, v_ref, col_ref, row_ref, o_ref, ot_ref, lse_ref, vt_ref):
    step = pl.program_id(1)

    @pl.when(step == 0)
    def _():
        whole = v_ref[...].reshape(-1, HEAD_DIM)
        vt_ref[...] = whole.T

    query = q_ref[pl.ds(step * parts, parts)].reshape(block, HEAD_DIM)
    query_row = row_ref[0, pl.ds(step, 1), :]
    unit = LOG2E / math.sqrt(HEAD_DIM)

    def visit(j, carry, diagonal):
        top, total, mixed = carry
        key = k_ref[pl.ds(j * parts, parts)].reshape(block, HEAD_DIM)
        at = pl.multiple_of(j * block, block)
        key_col = col_ref[0, pl.ds(at, block), :]
        scores = dot(key, query, NT) * unit
        scores = jnp.where(allowed_pairs(key_col, query_row, diagonal), scores, MASKED)
        above = jnp.maximum(top, jnp.max(scores, axis=0, keepdims=True))
        expo = jnp.exp2(scores - above)
        fade = jnp.exp2(top - above)
        total = total * fade + jnp.sum(expo, axis=0, keepdims=True)
        mixed = mixed * fade + dot(vt_ref[:, pl.ds(at, block)], expo.astype(jnp.bfloat16))
        return above, total, mixed

    start = (
        jnp.full((1, block), MASKED, jnp.float32),
        jnp.zeros((1, block), jnp.float32),
        jnp.zeros((HEAD_DIM, block), jnp.float32),
    )
    carry = lax.fori_loop(0, step, lambda j, c: visit(j, c, False), start)
    top, total, mixed = visit(step, carry, True)
    mixed = mixed / total
    ot_ref[0, 0] = mixed
    lse_ref[0, pl.ds(step, 1), :] = top + jnp.log2(total)
    o_ref[...] = mixed.T.astype(jnp.bfloat16).reshape(o_ref.shape)


def attend_back_kernel(
    block, parts, q_ref, k_ref, v_ref, g_ref, ot_ref, lse_ref, col_ref, row_ref, cos_ref, sin_ref,
    out_ref, kt_ref, dk_ref, dv_ref,
):
    step = pl.program_id(1)
    last = pl.num_programs(1) - 1
    scale = 1.0 / math.sqrt(HEAD_DIM)

    @pl.when(step == 0)
    def _():
        kt_ref[...] = k_ref[...].reshape(-1, HEAD_DIM).T
        dk_ref[...] = jnp.zeros_like(dk_ref)
        dv_ref[...] = jnp.zeros_like(dv_ref)

    query = q_ref[pl.ds(step * parts, parts)].reshape(block, HEAD_DIM)
    grad = g_ref[pl.ds(step * parts, parts)].reshape(block, HEAD_DIM)
    query_row = row_ref[0, pl.ds(step, 1), :]
    lse = lse_ref[0, pl.ds(step, 1), :]
    delta = jnp.sum(ot_ref[0, 0] * grad.astype(jnp.float32).T, axis=0, keepdims=True)
    unit = LOG2E * scale

    def visit(j, dqt, diagonal):
        at = pl.multiple_of(j * block, block)
        key = k_ref[pl.ds(j * parts, parts)].reshape(block, HEAD_DIM)
        value = v_ref[pl.ds(j * parts, parts)].reshape(block, HEAD_DIM)
        key_col = col_ref[0, pl.ds(at, block), :]
        scores = dot(key, query, NT) * unit - lse
        probs = jnp.where(allowed_pairs(key_col, query_row, diagonal), jnp.exp2(scores), 0.0)
        grad_probs = dot(value, grad, NT)
        grad_scores = (probs * (grad_probs - delta)).astype(jnp.bfloat16)
        dv_ref[pl.ds(at, block), :] += dot(probs.astype(jnp.bfloat16), grad)
        dk_ref[pl.ds(at, block), :] += dot(grad_scores, query)
        return dqt + dot(kt_ref[:, pl.ds(at, block)], grad_scores)

    dqt = lax.fori_loop(
        0, step, lambda j, c: visit(j, c, False), jnp.zeros((HEAD_DIM, block), jnp.float32)
    )
    dqt = visit(step, dqt, True)

    def turn_back(values, cosine, sine):
        return values * cosine - pltpu.roll(values, HEAD_DIM // 2, 1) * sine

    at = pl.multiple_of(step * block, block)
    dq = turn_back(dqt.T * scale, cos_ref[pl.ds(at, block), :], sin_ref[pl.ds(at, block), :])
    out_ref[pl.ds(step * parts, parts), 0, 0] = dq.astype(jnp.bfloat16).reshape(parts, -1, HEAD_DIM)

    @pl.when(step == last)
    def _():
        dk = turn_back(dk_ref[...] * scale, cos_ref[...], sin_ref[...])
        shape = (out_ref.shape[0],) + out_ref.shape[3:]
        out_ref[:, 0, 1] = dk.astype(jnp.bfloat16).reshape(shape)
        out_ref[:, 0, 2] = dv_ref[...].astype(jnp.bfloat16).reshape(shape)


def pair_spec(count, which, columns):
    return pl.BlockSpec((count, None, None, columns, HEAD_DIM), lambda p, i: (0, p, which, 0, 0))


def attend(packed, seg_col, seg_row):
    count, per, _, columns, _ = packed.shape
    length = count * columns
    block = seg_row.shape[2]
    steps, parts = length // block, block // columns
    return pl.pallas_call(
        functools.partial(attend_kernel, block, parts),
        grid=(per, steps),
        in_specs=[
            pair_spec(count, 0, columns),
            pair_spec(count, 1, columns),
            pair_spec(count, 2, columns),
            pl.BlockSpec((1, length, 1), lambda p, i: (p, 0, 0)),
            pl.BlockSpec((1, steps, block), lambda p, i: (p, 0, 0)),
        ],
        out_specs=[
            pl.BlockSpec((parts, None, columns, HEAD_DIM), lambda p, i: (i, p, 0, 0)),
            pl.BlockSpec((1, 1, HEAD_DIM, block), lambda p, i: (p, i, 0, 0)),
            pl.BlockSpec((1, steps, block), lambda p, i: (p, 0, 0)),
        ],
        out_shape=[
            jax.ShapeDtypeStruct((count, per, columns, HEAD_DIM), jnp.bfloat16),
            jax.ShapeDtypeStruct((per, steps, HEAD_DIM, block), jnp.float32),
            jax.ShapeDtypeStruct((per, steps, block), jnp.float32),
        ],
        scratch_shapes=[pltpu.VMEM((HEAD_DIM, length), jnp.bfloat16)],
        compiler_params=pltpu.CompilerParams(vmem_limit_bytes=56 << 20),
    )(packed, packed, packed, seg_col, seg_row)


def attend_back(packed, grads, mixed_t, lse, seg_col, seg_row, cosine, sine):
    count, per, _, columns, _ = packed.shape
    length = count * columns
    block = seg_row.shape[2]
    steps, parts = length // block, block // columns
    return pl.pallas_call(
        functools.partial(attend_back_kernel, block, parts),
        grid=(per, steps),
        in_specs=[
            pair_spec(count, 0, columns),
            pair_spec(count, 1, columns),
            pair_spec(count, 2, columns),
            pl.BlockSpec((count, None, columns, HEAD_DIM), lambda p, i: (0, p, 0, 0)),
            pl.BlockSpec((1, 1, HEAD_DIM, block), lambda p, i: (p, i, 0, 0)),
            pl.BlockSpec((1, steps, block), lambda p, i: (p, 0, 0)),
            pl.BlockSpec((1, length, 1), lambda p, i: (p, 0, 0)),
            pl.BlockSpec((1, steps, block), lambda p, i: (p, 0, 0)),
            pl.BlockSpec((length, HEAD_DIM), lambda p, i: (0, 0)),
            pl.BlockSpec((length, HEAD_DIM), lambda p, i: (0, 0)),
        ],
        out_specs=pl.BlockSpec((count, 1, 3, columns, HEAD_DIM), lambda p, i: (0, p, 0, 0, 0)),
        out_shape=jax.ShapeDtypeStruct((count, per, 3, columns, HEAD_DIM), jnp.bfloat16),
        scratch_shapes=[
            pltpu.VMEM((HEAD_DIM, length), jnp.bfloat16),
            pltpu.VMEM((length, HEAD_DIM), jnp.float32),
            pltpu.VMEM((length, HEAD_DIM), jnp.float32),
        ],
        compiler_params=pltpu.CompilerParams(vmem_limit_bytes=56 << 20),
    )(packed, packed, packed, grads, mixed_t, lse, seg_col, seg_row, cosine, sine)


MESH = pl.DeviceIdType.MESH


class Plan:
    def __init__(self, mesh):
        self.n_dp, self.n_seq = mesh.shape["dp"], mesh.shape["seq"]
        bits = [1 << i for i in range(self.n_seq.bit_length() - 1)]
        self.bits = bits[::-1]
        if len(bits) == 3:
            self.orders = ((2, 4, 1), (4, 2, 1))
        else:
            turn = len(bits) // 2
            self.orders = (tuple(bits), tuple(bits[turn:] + bits[:turn]))
        self.hops = len(bits)
        self.masks = range(1, self.n_dp)

    def lead(self):
        return (self.n_dp,) + (2,) * self.hops


def place():
    return lax.axis_index("dp"), lax.axis_index("seq")


def partner_dp(plan, mask):
    dp, seq = place()
    return (lax.bitwise_xor(dp, mask), seq)


def partner_seq(bit):
    dp, seq = place()
    return (dp, lax.bitwise_xor(seq, bit))


def own_bit(bit):
    return lax.bitwise_and(lax.div(place()[1], bit), 1)


def greet(plan):
    barrier = pltpu.get_barrier_semaphore()
    others = [partner_dp(plan, m) for m in plan.masks] + [partner_seq(b) for b in plan.bits]
    for other in others:
        pl.semaphore_signal(barrier, inc=1, device_id=other, device_id_type=MESH)
    pl.semaphore_wait(barrier, len(others))


def gather_copies(plan, src, dst, half, cols, stage, slot, send, recv):
    dp, _ = place()
    me = tuple(own_bit(b) for b in plan.bits)
    copies = []
    if stage == 0:
        base = 0
        for n, mask in enumerate(plan.masks):
            at = half * (len(plan.masks) + plan.hops) + n
            copies.append(pltpu.make_async_remote_copy(
                src.at[:, cols], dst.at[(dp,) + me + (slice(None), cols)],
                send.at[slot, at], recv.at[slot, at],
                device_id=partner_dp(plan, mask), device_id_type=MESH))
    else:
        order = plan.orders[half]
        done = order[: stage - 1]
        where = tuple(slice(None) if b in done else m for b, m in zip(plan.bits, me))
        part = dst.at[(slice(None),) + where + (slice(None), cols)]
        at = half * (len(plan.masks) + plan.hops) + len(plan.masks) + stage - 1
        copies.append(pltpu.make_async_remote_copy(
            part, part, send.at[slot, at], recv.at[slot, at],
            device_id=partner_seq(order[stage - 1]), device_id_type=MESH))
    return copies


def gather_kernel(plan, pieces, count, lag, *refs):
    ins, outs = refs[:count], refs[count : 2 * count]
    held = refs[2 * count : 3 * count]
    send, recv, local = refs[3 * count :]
    loads = [pltpu.make_async_copy(src, own, local.at[i]) for i, (src, own) in enumerate(zip(ins, held))]
    for load in loads:
        load.start()
    greet(plan)
    dp, _ = place()
    me = tuple(own_bit(b) for b in plan.bits)
    keeps = [
        pltpu.make_async_copy(own, dst.at[(dp,) + me], local.at[i])
        for i, (own, dst) in enumerate(zip(held, outs))
    ]
    for load, keep in zip(loads, keeps):
        load.wait()
        keep.start()
    stages = plan.hops + 1

    def copies(u, stage):
        which, start, size = pieces[u]
        half = size // 2
        return [
            c
            for h in range(2)
            for c in gather_copies(
                plan, held[which], outs[which], h, pl.ds(start + h * half, half), stage, u % (2 * lag), send, recv
            )
        ]

    total = len(pieces)
    for tick in range(total + lag * stages):
        for stage in reversed(range(stages + 1)):
            u = tick - lag * stage
            if not 0 <= u < total:
                continue
            if stage > 0:
                for c in copies(u, stage - 1):
                    c.wait_recv()
                if u == 0 and stage == 1:
                    for keep in keeps:
                        keep.wait()
            if stage < stages:
                if u >= 2 * lag:
                    for c in copies(u - 2 * lag, stage):
                        c.wait_send()
                for c in copies(u, stage):
                    c.start()
    for u in range(max(total - 2 * lag, 0), total):
        for stage in range(stages):
            for c in copies(u, stage):
                c.wait_send()


def gather(plan, arrays, chunk_bytes, lag, collective_id):
    pieces = []
    for i, a in enumerate(arrays):
        rows, cols = a.shape
        n = max(1, round(rows * cols * 2 * plan.n_dp * plan.n_seq / chunk_bytes))
        while cols % (256 * n):
            n -= 1
        pieces += [(i, j * (cols // n), cols // n) for j in range(n)]
    count = len(arrays)
    each = 2 * (len(plan.masks) + plan.hops)
    outs = pl.pallas_call(
        functools.partial(gather_kernel, plan, pieces, count, lag),
        out_shape=[jax.ShapeDtypeStruct(plan.lead() + a.shape, a.dtype) for a in arrays],
        in_specs=[pl.BlockSpec(memory_space=pl.ANY)] * count,
        out_specs=[pl.BlockSpec(memory_space=pl.ANY)] * count,
        scratch_shapes=[pltpu.VMEM(a.shape, a.dtype) for a in arrays] + [
            pltpu.SemaphoreType.DMA((2 * lag, each)),
            pltpu.SemaphoreType.DMA((2 * lag, each)),
            pltpu.SemaphoreType.DMA((count,)),
        ],
        compiler_params=pltpu.CompilerParams(collective_id=collective_id, has_side_effects=True),
    )(*arrays)
    return [o.reshape(-1, o.shape[-1]) for o in outs]


def reduce_kernel(plan, jobs, count, lag, *refs):
    k = len(jobs)
    lefts, rights, out_ref = refs[:k], refs[k : 2 * k], refs[2 * k]
    hops, slots = plan.hops, 2 * lag
    scratch = refs[2 * k + 1 :]
    sums = [scratch[h * (hops + 1) : (h + 1) * (hops + 1)] for h in range(2)]
    scratch = scratch[2 * (hops + 1) :]
    got = [scratch[h * (hops + 1) : (h + 1) * (hops + 1)] for h in range(2)]
    send, recv = scratch[2 * (hops + 1) :]
    tick = pl.program_id(0)
    half = out_ref.shape[-1] // 2
    rows = out_ref.shape[-2]
    orders = [order[::-1] for order in plan.orders]
    dp, _ = place()

    @pl.when(tick == 0)
    def _():
        greet(plan)

    def at_bit(h, stage, value):
        left = [b for b in plan.bits if b not in orders[h][:stage]]
        return (slice(None),) + tuple(value if b == orders[h][stage] else slice(None) for b in left)

    def copies(h, stage, slot):
        if stage < hops:
            bit = orders[h][stage]
            at = h * (hops + len(plan.masks)) + stage
            return [pltpu.make_async_remote_copy(
                sums[h][stage].at[(slot,) + at_bit(h, stage, 1 - own_bit(bit))], got[h][stage].at[slot],
                send.at[slot, at], recv.at[slot, at], device_id=partner_seq(bit), device_id_type=MESH)]
        out = []
        for n, mask in enumerate(plan.masks):
            at = h * (hops + len(plan.masks)) + hops + n
            out.append(pltpu.make_async_remote_copy(
                sums[h][hops].at[slot, lax.bitwise_xor(dp, mask)], got[h][hops].at[slot, n],
                send.at[slot, at], recv.at[slot, at], device_id=partner_dp(plan, mask), device_id_type=MESH))
        return out

    def wide(values):
        return values.astype(jnp.float32)

    for stage in reversed(range(1, hops + 2)):
        u = tick - lag * stage

        @pl.when((u >= 0) & (u < count))
        def _(stage=stage, u=u):
            slot = lax.rem(u, slots)
            for h in range(2):
                for copy in copies(h, stage - 1, slot):
                    copy.wait()
                if stage <= hops:
                    mine = (slot,) + at_bit(h, stage - 1, own_bit(orders[h][stage - 1]))
                    total = wide(sums[h][stage - 1][mine]) + wide(got[h][stage - 1][slot])
                    sums[h][stage][slot] = total.astype(jnp.bfloat16)
                    for copy in copies(h, stage, slot):
                        copy.start()
                else:
                    total = wide(sums[h][hops][slot, dp])
                    for n in range(len(plan.masks)):
                        total = total + wide(got[h][hops][slot, n])
                    out_ref[0, :, h * half : (h + 1) * half] = total

    for (start, stop, cols), left, right in zip(jobs, lefts, rights):

        @pl.when((tick >= start) & (tick < stop))
        def _(start=start, cols=cols, left=left, right=right):
            slot = lax.rem(tick, slots)
            which = lax.div(tick - start, cols)
            step = rows * plan.n_seq
            for z in range(plan.n_dp):
                part = lax.dot_general(left[which, z * step : (z + 1) * step, :], right[...],
                    (((1,), (0,)), ((), ())), preferred_element_type=jnp.float32).astype(jnp.bfloat16)
                for h in range(2):
                    piece = part[:, h * half : (h + 1) * half]
                    sums[h][0][slot, z] = piece.reshape(plan.lead()[1:] + (rows, half))
            for h in range(2):
                for copy in copies(h, 0, slot):
                    copy.start()


def reduce_products(plan, pairs, width, lag, collective_id):
    jobs, start = [], 0
    left_specs, right_specs = [], []
    for left, right in pairs:
        cols = right.shape[1] // width
        stop = start + left.shape[0] * cols
        jobs.append((start, stop, cols))
        left_specs.append(pl.BlockSpec(left.shape, lambda t: (0, 0, 0)))
        right_specs.append(pl.BlockSpec(
            (right.shape[0], width),
            functools.partial(lambda t, start, stop, cols: (0, lax.rem(jnp.clip(t, start, stop - 1) - start, cols)),
                start=start, stop=stop, cols=cols)))
        start = stop
    count = start
    rows = pairs[0][0].shape[1] // (plan.n_dp * plan.n_seq)
    half = width // 2
    slots, hops = 2 * lag, plan.hops
    tail = lag * (hops + 1)
    sums = [pltpu.VMEM((slots, plan.n_dp) + (2,) * (hops - s) + (rows, half), jnp.bfloat16) for s in range(hops + 1)]
    got = [pltpu.VMEM((slots, plan.n_dp) + (2,) * (hops - 1 - s) + (rows, half), jnp.bfloat16) for s in range(hops)]
    got.append(pltpu.VMEM((slots, len(plan.masks), rows, half), jnp.bfloat16))
    each = 2 * (hops + len(plan.masks))
    return pl.pallas_call(
        functools.partial(reduce_kernel, plan, jobs, count, lag),
        grid=(count + tail,),
        in_specs=left_specs + right_specs,
        out_specs=pl.BlockSpec((1, rows, width), lambda t: (jnp.maximum(t - tail, 0), 0, 0)),
        out_shape=jax.ShapeDtypeStruct((count, rows, width), jnp.float32),
        scratch_shapes=sums + sums + got + got + [
            pltpu.SemaphoreType.DMA((slots, each)),
            pltpu.SemaphoreType.DMA((slots, each)),
        ],
        compiler_params=pltpu.CompilerParams(
            collective_id=collective_id, has_side_effects=True, vmem_limit_bytes=60 << 20),
    )(*[p[0] for p in pairs], *[p[1] for p in pairs])


def layer_norm(values, gain, offset):
    centre = values - jnp.mean(values, axis=-1, keepdims=True)
    spread = jnp.mean(centre * centre, axis=-1, keepdims=True)
    return centre * lax.rsqrt(spread + EPSILON) * gain + offset


def gelu(values):
    return 0.5 * values * (1.0 + lax.erf(values * (1.0 / math.sqrt(2.0))))


def lower(values):
    return values.astype(jnp.bfloat16)


def project(acts, weight):
    return jnp.einsum("gcd,de->gce", acts, weight, preferred_element_type=jnp.float32)


def project_back(grads, weight):
    return jnp.einsum("gce,de->gcd", grads, weight, preferred_element_type=jnp.float32)


def outer_sum(left, right):
    return jnp.einsum("gci,gcj->ij", left, right, preferred_element_type=jnp.float32)


def shards(
    inputs,
    segments,
    norm1_gain,
    norm1_bias,
    w_query,
    w_key,
    w_value,
    w_out,
    norm2_gain,
    norm2_bias,
    w_up,
    w_down,
    cotangent,
    *,
    plan,
):
    count = plan.n_seq
    axes = ("dp", "seq")
    groups, columns, width = inputs.shape
    heads = width // HEAD_DIM
    length = columns * count
    block = min(512, length)
    per = -(-groups * heads // count)
    weights = (w_query, w_key, w_value, w_out, w_up, w_down)
    own_kernels = w_query.shape[0] % 16 == 0
    if own_kernels:
        full = gather(plan, weights, 1.6e6, 2, 1)
    else:
        full = [lax.all_gather(w, axes, axis=0, tiled=True) for w in weights]
    full_query, full_key, full_value, full_out, full_up, full_down = full
    rank = lax.axis_index("seq")

    ids = lax.all_gather(segments, "seq", axis=1, tiled=True)
    pair_at = jnp.minimum(rank * per + jnp.arange(per, dtype=jnp.int32), groups * heads - 1)
    pair_ids = ids[pair_at // heads]
    seg_row = pair_ids.reshape(per, length // block, block)
    seg_col = jnp.where(pair_ids < 0, -2, pair_ids)[..., None]

    half = HEAD_DIM // 2
    rates = jnp.exp(jnp.arange(half, dtype=jnp.float32) * (-math.log(10000.0) / half))
    turned = jnp.arange(length, dtype=jnp.float32)[:, None] * rates[None, :]
    cosine, sine = jnp.cos(turned), jnp.sin(turned)
    cosine_all = jnp.concatenate([cosine, cosine], axis=1)
    sine_all = jnp.concatenate([-sine, sine], axis=1)
    cosine_own = lax.dynamic_slice_in_dim(cosine_all, rank * columns, columns)[None, :, None, :]
    sine_own = lax.dynamic_slice_in_dim(sine_all, rank * columns, columns)[None, :, None, :]

    def turn(values):
        shaped = values.reshape(groups, columns, heads, HEAD_DIM)
        return shaped * cosine_own + jnp.roll(shaped, half, axis=-1) * sine_own

    def to_pairs(values):
        shaped = values.reshape(groups, columns, heads, HEAD_DIM)
        shaped = jnp.transpose(shaped, (0, 2, 1, 3)).reshape(groups * heads, columns, HEAD_DIM)
        shaped = jnp.pad(shaped, ((0, count * per - groups * heads), (0, 0), (0, 0)))
        return shaped.reshape(count, per, columns, HEAD_DIM)

    def from_pairs(values):
        shaped = values.reshape(count * per, columns, HEAD_DIM)[: groups * heads]
        shaped = shaped.reshape(groups, heads, columns, HEAD_DIM)
        return jnp.transpose(shaped, (0, 2, 1, 3)).reshape(groups, columns, width)

    def swap(values):
        return lax.all_to_all(values, "seq", 0, 0)

    act_one = lower(layer_norm(inputs, norm1_gain, norm1_bias))
    query_low = lower(turn(project(act_one, full_query)))
    key_low = lower(turn(project(act_one, full_key)))
    value_low = lower(project(act_one, full_value))
    packed = swap(jnp.stack([to_pairs(query_low), to_pairs(key_low), to_pairs(value_low)], axis=2))
    mixed_pairs, mixed_t, lse = attend(packed, seg_col, seg_row)
    mixed_low = from_pairs(swap(mixed_pairs))

    first_sum = inputs + project(mixed_low, full_out)
    act_two = lower(layer_norm(first_sum, norm2_gain, norm2_bias))
    upper = project(act_two, full_up)
    hidden_low = lower(gelu(upper))
    output = first_sum + project(hidden_low, full_down)
    grad_out_low = lower(cotangent)
    grad_hidden = project_back(grad_out_low, full_down)
    gelu_values, gelu_back = jax.vjp(gelu, upper)
    grad_upper = lower(gelu_back(grad_hidden)[0])
    grad_act_two = project_back(grad_upper, full_up)
    normed_two, norm_two_back = jax.vjp(layer_norm, first_sum, norm2_gain, norm2_bias)
    grad_first_norm, gain_two_grad, offset_two_grad = norm_two_back(grad_act_two)
    grad_first = cotangent + grad_first_norm
    grad_attn_low = lower(grad_first)
    grad_mixed = lower(project_back(grad_attn_low, full_out))

    tokens = groups * columns
    width_piece = 512

    def flat(values):
        return values.reshape(tokens, -1)

    def left_of(values):
        turned = flat(values).T
        every = plan.n_dp * plan.n_seq
        turned = turned.reshape(every, -1, width // every, tokens)
        return jnp.transpose(turned, (1, 0, 2, 3)).reshape(-1, width, tokens)

    def reduce_all(pairs, collective_id):
        out = reduce_products(plan, pairs, width_piece, 2, collective_id)
        results, at = [], 0
        for left, right in pairs:
            blocks, cols = left.shape[0], right.shape[1] // width_piece
            part = out[at : at + blocks * cols].reshape(blocks, cols, -1, width_piece)
            results.append(jnp.transpose(part, (0, 2, 1, 3)).reshape(-1, right.shape[1]))
            at += blocks * cols
        return results

    if own_kernels:
        sums_one = reduce_all(
            [
                (left_of(hidden_low), flat(grad_out_low)),
                (left_of(act_two), flat(grad_upper)),
                (left_of(mixed_low), flat(grad_attn_low)),
            ],
            2,
        )

    def reduce_last(norm_sums):
        left = left_of(act_one)
        stacked = jnp.pad(jnp.stack(norm_sums, axis=1), ((0, 0), (0, tokens - len(norm_sums))))
        return reduce_all(
            [
                (left, flat(grad_query_low)),
                (left, flat(grad_key_low)),
                (left, flat(grad_value_low)),
                (lower(stacked)[None], jnp.eye(tokens, width_piece, dtype=jnp.bfloat16)),
            ],
            3,
        )

    grads = attend_back(
        packed, swap(to_pairs(grad_mixed)), mixed_t, lse, seg_col, seg_row, cosine_all, sine_all
    )
    grads = swap(grads)
    grad_query_low, grad_key_low, grad_value_low = (from_pairs(grads[:, :, i]) for i in range(3))

    grad_act_one = project_back(grad_query_low, full_query) + project_back(grad_key_low, full_key)
    grad_act_one = grad_act_one + project_back(grad_value_low, full_value)
    normed_again, norm_one_back = jax.vjp(layer_norm, inputs, norm1_gain, norm1_bias)
    grad_input_norm, gain_one_grad, offset_one_grad = norm_one_back(grad_act_one)
    grad_input = grad_first + grad_input_norm

    norm_sums = [gain_one_grad, offset_one_grad, gain_two_grad, offset_two_grad]
    if own_kernels:
        first, second = sums_one, reduce_last(norm_sums)
        down_grad, up_grad, out_grad = first
        query_grad, key_grad, value_grad, norm_rows = second
        norm_rows = [norm_rows[:, i] for i in range(4)]
    else:
        def spread(values):
            return lax.psum_scatter(values, axes, scatter_dimension=0, tiled=True).astype(jnp.float32)

        down_grad = spread(lower(outer_sum(hidden_low, grad_out_low)))
        up_grad = spread(lower(outer_sum(act_two, grad_upper)))
        out_grad = spread(lower(outer_sum(mixed_low, grad_attn_low)))
        query_grad = spread(lower(outer_sum(act_one, grad_query_low)))
        key_grad = spread(lower(outer_sum(act_one, grad_key_low)))
        value_grad = spread(lower(outer_sum(act_one, grad_value_low)))
        norm_rows = [spread(v) for v in norm_sums]

    return (
        output,
        grad_input,
        norm_rows[0],
        norm_rows[1],
        query_grad,
        key_grad,
        value_grad,
        out_grad,
        norm_rows[2],
        norm_rows[3],
        up_grad,
        down_grad,
    )


def solution(mesh):
    placed = (
        P("dp", "seq", None),
        P("dp", "seq"),
        P(),
        P(),
        P(("dp", "seq"), None),
        P(("dp", "seq"), None),
        P(("dp", "seq"), None),
        P(("dp", "seq"), None),
        P(),
        P(),
        P(("dp", "seq"), None),
        P(("dp", "seq"), None),
        P("dp", "seq", None),
    )
    return jax.shard_map(
        functools.partial(shards, plan=Plan(mesh)),
        mesh=mesh,
        in_specs=placed,
        out_specs=(
            P("dp", "seq", None),
            P("dp", "seq", None),
            P(("dp", "seq")),
            P(("dp", "seq")),
            P(("dp", "seq"), None),
            P(("dp", "seq"), None),
            P(("dp", "seq"), None),
            P(("dp", "seq"), None),
            P(("dp", "seq")),
            P(("dp", "seq")),
            P(("dp", "seq"), None),
            P(("dp", "seq"), None),
        ),
        check_vma=False,
    )
```

```python
import functools
import math

import jax
import jax.numpy as jnp
from jax import lax
from jax.experimental import pallas as pl
from jax.experimental.pallas import tpu as pltpu
from jax.sharding import PartitionSpec as P

HEAD_DIM = 128


EPSILON = 1e-05
MASKED = -1e30
LOG2E = math.log2(math.e)
NT = (((1,), (1,)), ((), ()))
NN = (((1,), (0,)), ((), ()))


def dot(left, right, dims=NN):
    return lax.dot_general(left, right, dims, preferred_element_type=jnp.float32)


def allowed_pairs(key_col, query_row, diagonal):
    same = key_col == query_row
    if not diagonal:
        return same
    shape = (key_col.shape[0], query_row.shape[1])
    key_at = lax.broadcasted_iota(jnp.int32, shape, 0)
    query_at = lax.broadcasted_iota(jnp.int32, shape, 1)
    return (same & (key_at <= query_at)) | (key_at == query_at)


def attend_kernel(block, parts, q_ref, k_ref, v_ref, col_ref, row_ref, o_ref, ot_ref, lse_ref, vt_ref):
    step = pl.program_id(1)

    @pl.when(step == 0)
    def _():
        whole = v_ref[...].reshape(-1, HEAD_DIM)
        vt_ref[...] = whole.T

    query = q_ref[pl.ds(step * parts, parts)].reshape(block, HEAD_DIM)
    query_row = row_ref[0, pl.ds(step, 1), :]
    unit = LOG2E / math.sqrt(HEAD_DIM)

    def visit(j, carry, diagonal):
        top, total, mixed = carry
        key = k_ref[pl.ds(j * parts, parts)].reshape(block, HEAD_DIM)
        at = pl.multiple_of(j * block, block)
        key_col = col_ref[0, pl.ds(at, block), :]
        scores = dot(key, query, NT) * unit
        scores = jnp.where(allowed_pairs(key_col, query_row, diagonal), scores, MASKED)
        above = jnp.maximum(top, jnp.max(scores, axis=0, keepdims=True))
        expo = jnp.exp2(scores - above)
        fade = jnp.exp2(top - above)
        total = total * fade + jnp.sum(expo, axis=0, keepdims=True)
        mixed = mixed * fade + dot(vt_ref[:, pl.ds(at, block)], expo.astype(jnp.bfloat16))
        return above, total, mixed

    start = (
        jnp.full((1, block), MASKED, jnp.float32),
        jnp.zeros((1, block), jnp.float32),
        jnp.zeros((HEAD_DIM, block), jnp.float32),
    )
    carry = lax.fori_loop(0, step, lambda j, c: visit(j, c, False), start)
    top, total, mixed = visit(step, carry, True)
    mixed = mixed / total
    ot_ref[0, 0] = mixed
    lse_ref[0, pl.ds(step, 1), :] = top + jnp.log2(total)
    o_ref[...] = mixed.T.astype(jnp.bfloat16).reshape(o_ref.shape)


def attend_back_step(
    block, parts, step, last, q_ref, k_ref, v_ref, g_ref, ot_ref, lse_ref, col_ref, row_ref, cos_ref, sin_ref,
    out_ref, kt_ref, dk_ref, dv_ref,
):
    scale = 1.0 / math.sqrt(HEAD_DIM)

    @pl.when(step == 0)
    def _():
        kt_ref[...] = k_ref[...].reshape(-1, HEAD_DIM).T
        dk_ref[...] = jnp.zeros_like(dk_ref)
        dv_ref[...] = jnp.zeros_like(dv_ref)

    query = q_ref[pl.ds(step * parts, parts)].reshape(block, HEAD_DIM)
    grad = g_ref[pl.ds(step * parts, parts)].reshape(block, HEAD_DIM)
    query_row = row_ref[0, pl.ds(step, 1), :]
    lse = lse_ref[0, pl.ds(step, 1), :]
    delta = jnp.sum(ot_ref[0, 0] * grad.astype(jnp.float32).T, axis=0, keepdims=True)
    unit = LOG2E * scale

    def visit(j, dqt, diagonal):
        at = pl.multiple_of(j * block, block)
        key = k_ref[pl.ds(j * parts, parts)].reshape(block, HEAD_DIM)
        value = v_ref[pl.ds(j * parts, parts)].reshape(block, HEAD_DIM)
        key_col = col_ref[0, pl.ds(at, block), :]
        scores = dot(key, query, NT) * unit - lse
        probs = jnp.where(allowed_pairs(key_col, query_row, diagonal), jnp.exp2(scores), 0.0)
        grad_probs = dot(value, grad, NT)
        grad_scores = (probs * (grad_probs - delta)).astype(jnp.bfloat16)
        dv_ref[pl.ds(at, block), :] += dot(probs.astype(jnp.bfloat16), grad)
        dk_ref[pl.ds(at, block), :] += dot(grad_scores, query)
        return dqt + dot(kt_ref[:, pl.ds(at, block)], grad_scores)

    dqt = lax.fori_loop(
        0, step, lambda j, c: visit(j, c, False), jnp.zeros((HEAD_DIM, block), jnp.float32)
    )
    dqt = visit(step, dqt, True)

    def turn_back(values, cosine, sine):
        return values * cosine - pltpu.roll(values, HEAD_DIM // 2, 1) * sine

    at = pl.multiple_of(step * block, block)
    dq = turn_back(dqt.T * scale, cos_ref[pl.ds(at, block), :], sin_ref[pl.ds(at, block), :])
    out_ref[0, pl.ds(at, block), :] = dq.astype(jnp.bfloat16)

    @pl.when(step == last)
    def _():
        dk = turn_back(dk_ref[...] * scale, cos_ref[...], sin_ref[...])
        out_ref[1] = dk.astype(jnp.bfloat16)
        out_ref[2] = dv_ref[...].astype(jnp.bfloat16)


def pair_spec(count, which, columns):
    return pl.BlockSpec((count, None, None, columns, HEAD_DIM), lambda p, i: (0, p, which, 0, 0))


def attend(packed, seg_col, seg_row):
    count, per, _, columns, _ = packed.shape
    length = count * columns
    block = seg_row.shape[2]
    steps, parts = length // block, block // columns
    return pl.pallas_call(
        functools.partial(attend_kernel, block, parts),
        grid=(per, steps),
        in_specs=[
            pair_spec(count, 0, columns),
            pair_spec(count, 1, columns),
            pair_spec(count, 2, columns),
            pl.BlockSpec((1, length, 1), lambda p, i: (p, 0, 0)),
            pl.BlockSpec((1, steps, block), lambda p, i: (p, 0, 0)),
        ],
        out_specs=[
            pl.BlockSpec((parts, None, columns, HEAD_DIM), lambda p, i: (i, p, 0, 0)),
            pl.BlockSpec((1, 1, HEAD_DIM, block), lambda p, i: (p, i, 0, 0)),
            pl.BlockSpec((1, steps, block), lambda p, i: (p, 0, 0)),
        ],
        out_shape=[
            jax.ShapeDtypeStruct((count, per, columns, HEAD_DIM), jnp.bfloat16),
            jax.ShapeDtypeStruct((per, steps, HEAD_DIM, block), jnp.float32),
            jax.ShapeDtypeStruct((per, steps, block), jnp.float32),
        ],
        scratch_shapes=[pltpu.VMEM((HEAD_DIM, length), jnp.bfloat16)],
        compiler_params=pltpu.CompilerParams(vmem_limit_bytes=56 << 20),
    )(packed, packed, packed, seg_col, seg_row)


class AttendBack:
    def __init__(self, first, packed, grads, mixed_t, lse, seg_col, seg_row, cosine, sine):
        count, per, _, columns, _ = packed.shape
        length = count * columns
        self.block = seg_row.shape[2]
        self.steps, self.parts = length // self.block, self.block // columns
        self.first, self.ticks = first, per * self.steps
        self.operands = (packed, packed, packed, grads, mixed_t, lse, seg_col, seg_row, cosine, sine)

        def pair(t):
            return lax.div(jnp.clip(t - first, 0, self.ticks - 1), self.steps)

        def step(t):
            return lax.rem(jnp.clip(t - first, 0, self.ticks - 1), self.steps)

        def whole(which):
            return pl.BlockSpec((count, None, None, columns, HEAD_DIM), lambda t: (0, pair(t), which, 0, 0))

        rows = pl.BlockSpec((1, self.steps, self.block), lambda t: (pair(t), 0, 0))
        table = pl.BlockSpec((length, HEAD_DIM), lambda t: (0, 0))
        self.in_specs = [
            whole(0),
            whole(1),
            whole(2),
            pl.BlockSpec((count, None, columns, HEAD_DIM), lambda t: (0, pair(t), 0, 0)),
            pl.BlockSpec((1, 1, HEAD_DIM, self.block), lambda t: (pair(t), step(t), 0, 0)),
            rows,
            pl.BlockSpec((1, length, 1), lambda t: (pair(t), 0, 0)),
            rows,
            table,
            table,
        ]
        self.out_specs = [pl.BlockSpec((3, length, HEAD_DIM), lambda t: (0, 0, pair(t)))]
        self.out_shapes = [jax.ShapeDtypeStruct((3, length, per * HEAD_DIM), jnp.bfloat16)]
        self.scratch = [
            pltpu.VMEM((HEAD_DIM, length), jnp.bfloat16),
            pltpu.VMEM((length, HEAD_DIM), jnp.float32),
            pltpu.VMEM((length, HEAD_DIM), jnp.float32),
        ]

    def run(self, tick, refs):
        @pl.when((tick >= self.first) & (tick < self.first + self.ticks))
        def _():
            step = lax.rem(tick - self.first, self.steps)
            attend_back_step(self.block, self.parts, step, self.steps - 1, *refs)


def attend_back_alone(work):
    def kernel(*refs):
        work.run(pl.program_id(0), refs)

    return pl.pallas_call(
        kernel,
        grid=(work.first + work.ticks,),
        in_specs=work.in_specs,
        out_specs=work.out_specs,
        out_shape=work.out_shapes,
        scratch_shapes=work.scratch,
        compiler_params=pltpu.CompilerParams(vmem_limit_bytes=56 << 20),
    )(*work.operands)[0]


MESH = pl.DeviceIdType.MESH


class Plan:
    def __init__(self, mesh):
        self.n_dp, self.n_seq = mesh.shape["dp"], mesh.shape["seq"]
        bits = [1 << i for i in range(self.n_seq.bit_length() - 1)]
        self.bits = bits[::-1]
        if len(bits) == 3:
            self.orders = ((2, 4, 1), (4, 2, 1))
        else:
            turn = len(bits) // 2
            self.orders = (tuple(bits), tuple(bits[turn:] + bits[:turn]))
        self.hops = len(bits)
        self.masks = range(1, self.n_dp)

    def lead(self):
        return (self.n_dp,) + (2,) * self.hops


def place():
    return lax.axis_index("dp"), lax.axis_index("seq")


def partner_dp(plan, mask):
    dp, seq = place()
    return (lax.bitwise_xor(dp, mask), seq)


def partner_seq(bit):
    dp, seq = place()
    return (dp, lax.bitwise_xor(seq, bit))


def own_bit(bit):
    return lax.bitwise_and(lax.div(place()[1], bit), 1)


def greet(plan):
    barrier = pltpu.get_barrier_semaphore()
    others = [partner_dp(plan, m) for m in plan.masks] + [partner_seq(b) for b in plan.bits]
    for other in others:
        pl.semaphore_signal(barrier, inc=1, device_id=other, device_id_type=MESH)
    pl.semaphore_wait(barrier, len(others))


def reduce_kernel(plan, jobs, count, lag, beside, *refs):
    k = len(jobs)
    lefts, rights, refs = refs[:k], refs[k : 2 * k], refs[2 * k :]
    more = [0, 0, 0] if beside is None else [len(beside.in_specs), len(beside.out_specs), len(beside.scratch)]
    extra, refs = refs[: more[0]], refs[more[0] :]
    out_ref, extra = refs[0], extra + refs[1 : 1 + more[1]]
    scratch = refs[1 + more[1] :]
    extra, scratch = extra + scratch[: more[2]], scratch[more[2] :]
    hops, slots = plan.hops, 2 * lag
    sums = [scratch[h * (hops + 1) : (h + 1) * (hops + 1)] for h in range(2)]
    scratch = scratch[2 * (hops + 1) :]
    got = [scratch[h * (hops + 1) : (h + 1) * (hops + 1)] for h in range(2)]
    send, recv = scratch[2 * (hops + 1) :]
    tick = pl.program_id(0)
    half = out_ref.shape[-1] // 2
    rows = out_ref.shape[-2]
    orders = [order[::-1] for order in plan.orders]
    dp, _ = place()

    @pl.when(tick == 0)
    def _():
        greet(plan)

    def at_bit(h, stage, value):
        left = [b for b in plan.bits if b not in orders[h][:stage]]
        return (slice(None),) + tuple(value if b == orders[h][stage] else slice(None) for b in left)

    def copies(h, stage, slot):
        if stage < hops:
            bit = orders[h][stage]
            at = h * (hops + len(plan.masks)) + stage
            return [pltpu.make_async_remote_copy(
                sums[h][stage].at[(slot,) + at_bit(h, stage, 1 - own_bit(bit))], got[h][stage].at[slot],
                send.at[slot, at], recv.at[slot, at], device_id=partner_seq(bit), device_id_type=MESH)]
        out = []
        for n, mask in enumerate(plan.masks):
            at = h * (hops + len(plan.masks)) + hops + n
            out.append(pltpu.make_async_remote_copy(
                sums[h][hops].at[slot, lax.bitwise_xor(dp, mask)], got[h][hops].at[slot, n],
                send.at[slot, at], recv.at[slot, at], device_id=partner_dp(plan, mask), device_id_type=MESH))
        return out

    def wide(values):
        return values.astype(jnp.float32)

    for stage in reversed(range(1, hops + 2)):
        u = tick - lag * stage

        @pl.when((u >= 0) & (u < count))
        def _(stage=stage, u=u):
            slot = lax.rem(u, slots)
            for h in range(2):
                for copy in copies(h, stage - 1, slot):
                    copy.wait()
                if stage <= hops:
                    mine = (slot,) + at_bit(h, stage - 1, own_bit(orders[h][stage - 1]))
                    total = wide(sums[h][stage - 1][mine]) + wide(got[h][stage - 1][slot])
                    sums[h][stage][slot] = total.astype(jnp.bfloat16)
                    for copy in copies(h, stage, slot):
                        copy.start()
                else:
                    total = wide(sums[h][hops][slot, dp])
                    for n in range(len(plan.masks)):
                        total = total + wide(got[h][hops][slot, n])
                    out_ref[0, :, h * half : (h + 1) * half] = total

    for (start, stop, cols), left, right in zip(jobs, lefts, rights):

        @pl.when((tick >= start) & (tick < stop))
        def _(start=start, cols=cols, left=left, right=right):
            slot = lax.rem(tick, slots)
            which = lax.div(tick - start, cols)
            step = rows * plan.n_seq
            for z in range(plan.n_dp):
                part = lax.dot_general(left[which, z * step : (z + 1) * step, :], right[...],
                    (((1,), (0,)), ((), ())), preferred_element_type=jnp.float32).astype(jnp.bfloat16)
                for h in range(2):
                    piece = part[:, h * half : (h + 1) * half]
                    sums[h][0][slot, z] = piece.reshape(plan.lead()[1:] + (rows, half))
            for h in range(2):
                for copy in copies(h, 0, slot):
                    copy.start()

    if beside is not None:
        beside.run(tick, extra)


def reduce_products(plan, pairs, width, lag, collective_id, beside=None):
    jobs, start = [], 0
    left_specs, right_specs = [], []
    for left, right in pairs:
        cols = right.shape[1] // width
        stop = start + left.shape[0] * cols
        jobs.append((start, stop, cols))
        left_specs.append(pl.BlockSpec(left.shape, lambda t: (0, 0, 0)))
        right_specs.append(pl.BlockSpec(
            (right.shape[0], width),
            functools.partial(lambda t, start, stop, cols: (0, lax.rem(jnp.clip(t, start, stop - 1) - start, cols)),
                start=start, stop=stop, cols=cols)))
        start = stop
    count = start
    rows = pairs[0][0].shape[1] // (plan.n_dp * plan.n_seq)
    half = width // 2
    slots, hops = 2 * lag, plan.hops
    tail = lag * (hops + 1)
    sums = [pltpu.VMEM((slots, plan.n_dp) + (2,) * (hops - s) + (rows, half), jnp.bfloat16) for s in range(hops + 1)]
    got = [pltpu.VMEM((slots, plan.n_dp) + (2,) * (hops - 1 - s) + (rows, half), jnp.bfloat16) for s in range(hops)]
    got.append(pltpu.VMEM((slots, len(plan.masks), rows, half), jnp.bfloat16))
    each = 2 * (hops + len(plan.masks))
    out_specs = [pl.BlockSpec((1, rows, width), lambda t: (jnp.maximum(t - tail, 0), 0, 0))]
    out_shapes = [jax.ShapeDtypeStruct((count, rows, width), jnp.float32)]
    more_in, more_scratch, more_operands = [], [], []
    if beside is not None:
        more_in, more_scratch, more_operands = beside.in_specs, beside.scratch, beside.operands
        out_specs, out_shapes = out_specs + beside.out_specs, out_shapes + beside.out_shapes
    return pl.pallas_call(
        functools.partial(reduce_kernel, plan, jobs, count, lag, beside),
        grid=(count + tail,),
        in_specs=left_specs + right_specs + more_in,
        out_specs=out_specs,
        out_shape=out_shapes,
        scratch_shapes=more_scratch + sums + sums + got + got + [
            pltpu.SemaphoreType.DMA((slots, each)),
            pltpu.SemaphoreType.DMA((slots, each)),
        ],
        compiler_params=pltpu.CompilerParams(
            collective_id=collective_id, has_side_effects=True, vmem_limit_bytes=60 << 20),
    )(*[p[0] for p in pairs], *[p[1] for p in pairs], *more_operands)


class Copies:
    def __init__(self, send, recv):
        self.send, self.recv, self.count, self.sent = send, recv, 0, []

    def remote(self, src, dst, device):
        at = self.count
        self.count += 1
        return pltpu.make_async_remote_copy(
            src, dst, self.send.at[at], self.recv.at[at], device_id=device, device_id_type=MESH)

    def run(self, pieces, lag):
        last = max(start + lag * len(stages) for start, stages in pieces)
        for tick in range(last + 1):
            for stage in reversed(range(max(len(stages) for _, stages in pieces) + 1)):
                for start, stages in pieces:
                    if start + lag * stage != tick or stage > len(stages):
                        continue
                    if stage > 0:
                        for copy in stages[stage - 1][1]:
                            copy.wait_recv()
                    if stage < len(stages):
                        ahead, copies = stages[stage]
                        if ahead is not None:
                            ahead()
                        for copy in copies:
                            copy.start()
        for _, stages in pieces:
            for _, copies in stages:
                for copy in copies:
                    copy.wait_send()


def start_kernel(
    plan, splits, lag, h_ref, q_ref, k_ref, v_ref, *refs,
):
    n = len(splits)
    ins, refs = refs[:n], refs[n:]
    hs_ref, w_ref, outs = refs[0], refs[1], refs[2 : 2 + n]
    hv, wv, halves = refs[2 + n : 5 + n]
    held = refs[5 + n : 5 + 2 * n]
    send, recv, local = refs[5 + 2 * n :]
    dp, seq = place()
    y, x, c = own_bit(4), own_bit(2), own_bit(1)
    loads = [pltpu.make_async_copy(h_ref.at[y], hv, local.at[0])]
    loads += [pltpu.make_async_copy(r, wv.at[i], local.at[1 + i]) for i, r in enumerate((q_ref, k_ref, v_ref))]
    loads += [pltpu.make_async_copy(r, o, local.at[4 + i]) for i, (r, o) in enumerate(zip(ins, held))]
    for load in loads:
        load.start()
    greet(plan)
    for load in loads:
        load.wait()
    own = pltpu.make_async_copy(hv, hs_ref.at[y, x, c], local.at[0])
    own.start()
    me = (y, x, c)
    keeps = [pltpu.make_async_copy(o, d.at[(dp,) + me], local.at[4 + i]) for i, (o, d) in enumerate(zip(held, outs))]
    for keep in keeps:
        keep.start()
    run = Copies(send, recv)
    pieces = []

    tokens = hv.shape[0]
    parts = 4
    for i in range(parts):
        rows = pl.ds(i * (tokens // parts), tokens // parts)
        first = run.remote(h_ref.at[1 - y, rows], hs_ref.at[y, x, c, rows], partner_seq(4))
        second = [run.remote(hs_ref.at[:, x, c, rows], hs_ref.at[:, x, c, rows], partner_seq(2))]
        third = [run.remote(hs_ref.at[:, :, c, rows], hs_ref.at[:, :, c, rows], partner_seq(1))]
        pieces.append((i, [(None, [first]), (own.wait if i == 0 else None, second), (None, third)]))

    half, quarter = halves.shape[-1], w_ref.shape[-1]
    for i in range(3):
        mine = pltpu.make_async_copy(
            halves.at[i, :, :, pl.ds(c * quarter, quarter)], w_ref.at[i, dp, y, :, c], local.at[1 + i])

        def cut(i=i, mine=mine):
            halves[i, x] = wv[i, :, pl.ds(pl.multiple_of(x * half, 128), half)]
            mine.start()

        to_x = [run.remote(wv.at[i, :, pl.ds((1 - x) * half, half)], halves.at[i, x], partner_seq(2))]
        to_core = [run.remote(
            halves.at[i, :, :, pl.ds((1 - c) * quarter, quarter)], w_ref.at[i, dp, y, :, c], partner_seq(1))]
        to_z = [run.remote(w_ref.at[i, dp, y], w_ref.at[i, dp, y], partner_dp(plan, m)) for m in plan.masks]
        to_y = [run.remote(w_ref.at[i, :, y], w_ref.at[i, :, y], partner_seq(4))]
        pieces.append((i, [(None, to_x), (cut, to_core), (mine.wait, to_z), (None, to_y)]))

    tick = parts
    for src, dst, keep, (count, size) in zip(held, outs, keeps, splits):
        for j in range(count):
            stages = []
            for stage in range(plan.hops + 1):
                copies = []
                for h in range(2):
                    cols = pl.ds(j * size + h * (size // 2), size // 2)
                    if stage == 0:
                        for m in plan.masks:
                            copies.append(run.remote(
                                src.at[:, cols], dst.at[(dp,) + me + (slice(None), cols)], partner_dp(plan, m)))
                    else:
                        order = plan.orders[h]
                        where = tuple(slice(None) if b in order[: stage - 1] else m for b, m in zip(plan.bits, me))
                        part = dst.at[(slice(None),) + where + (slice(None), cols)]
                        copies.append(run.remote(part, part, partner_seq(order[stage - 1])))
                stages.append((keep.wait if stage == 1 and j == 0 else None, copies))
            pieces.append((tick, stages))
            tick += 1
    run.run(pieces, lag)


def start(plan, acts, weights, whole, piece, lag, collective_id):
    groups, columns, width = acts.shape
    rows = weights[0].shape[0]
    quarter = width // 4
    splits, copies = [], 4 * 3 + 3 * (3 + len(plan.masks))
    for a in whole:
        count = max(1, a.shape[1] // piece)
        while a.shape[1] % (256 * count):
            count -= 1
        splits.append((count, a.shape[1] // count))
        copies += count * 2 * (len(plan.masks) + plan.hops)
    hbm = pl.BlockSpec(memory_space=pl.ANY)
    outs = pl.pallas_call(
        functools.partial(start_kernel, plan, splits, lag),
        out_shape=[
            jax.ShapeDtypeStruct((2, 2, 2, columns, width), acts.dtype),
            jax.ShapeDtypeStruct((3,) + plan.lead() + (rows, quarter), acts.dtype),
        ] + [jax.ShapeDtypeStruct(plan.lead() + a.shape, a.dtype) for a in whole],
        in_specs=[hbm] * (4 + len(whole)),
        out_specs=[hbm] * (2 + len(whole)),
        scratch_shapes=[
            pltpu.VMEM((columns, width), acts.dtype),
            pltpu.VMEM((3, rows, width), acts.dtype),
            pltpu.VMEM((3, 2, rows, width // 2), acts.dtype),
        ] + [pltpu.VMEM(a.shape, a.dtype) for a in whole] + [
            pltpu.SemaphoreType.DMA((copies,)),
            pltpu.SemaphoreType.DMA((copies,)),
            pltpu.SemaphoreType.DMA((4 + len(whole),)),
        ],
        compiler_params=pltpu.CompilerParams(
            collective_id=collective_id, has_side_effects=True, vmem_limit_bytes=32 << 20),
    )(acts, *weights, *whole)
    tokens, projections = outs[0], outs[1]
    return (
        tokens.reshape(8, columns, width),
        projections.reshape(3, width, quarter),
        [o.reshape(-1, o.shape[-1]) for o in outs[2:]],
    )


def project_kernel(x_ref, w_ref, cos_ref, sin_ref, out_ref, turned_ref):
    parts, columns, width = x_ref.shape
    acts = x_ref[...].reshape(parts * columns, width)
    heads = out_ref.shape[1]
    for kind in range(3):
        made = dot(acts, w_ref[kind])
        for p in range(heads):
            head = made[:, p * HEAD_DIM : (p + 1) * HEAD_DIM]
            if kind < 2:
                head = head * cos_ref[...] + pltpu.roll(head, HEAD_DIM // 2, 1) * sin_ref[...]
            out_ref[:, p, kind] = head.astype(jnp.bfloat16).reshape(parts, columns, HEAD_DIM)
    turned_ref[...] = acts.T


def project_heads(acts, weights, cosine, sine):
    owners, columns, width = acts.shape
    parts = 512 // columns
    block = parts * columns
    heads = weights.shape[2] // HEAD_DIM
    table = pl.BlockSpec((block, HEAD_DIM), lambda i: (i, 0))
    return pl.pallas_call(
        project_kernel,
        grid=(owners // parts,),
        in_specs=[
            pl.BlockSpec((parts, columns, width), lambda i: (i, 0, 0)),
            pl.BlockSpec(weights.shape, lambda i: (0, 0, 0)),
            table,
            table,
        ],
        out_specs=[
            pl.BlockSpec((parts, heads, 3, columns, HEAD_DIM), lambda i: (i, 0, 0, 0, 0)),
            pl.BlockSpec((width, block), lambda i: (0, i)),
        ],
        out_shape=[
            jax.ShapeDtypeStruct((owners, heads, 3, columns, HEAD_DIM), jnp.bfloat16),
            jax.ShapeDtypeStruct((width, owners * columns), jnp.bfloat16),
        ],
        compiler_params=pltpu.CompilerParams(vmem_limit_bytes=56 << 20),
    )(acts, weights, cosine, sine)


def finish_kernel(
    plan, parts, g_any, t_any, w_any, x_any, gx_any, gain_ref, more_ref,
    dx_ref, dw_ref, dn_ref,
    g_ref, t_ref, w_ref, x_ref, gx_ref,
    made, made_y, sum_y, made_z, sum_z, sides, made_x,
    acts, acts_c, sum_c, acts_x, sum_x, acts_y,
    totals, norms, norms_c, norms_sc, norms_x, norms_sx, norms_y, norms_sy, norms_z,
    send, recv, local,
):
    dp, _ = place()
    y, x, c = own_bit(4), own_bit(2), own_bit(1)
    loads = [
        pltpu.make_async_copy(src, dst, local.at[i])
        for i, (src, dst) in enumerate(
            ((g_any, g_ref), (w_any, w_ref), (t_any, t_ref), (x_any, x_ref), (gx_any, gx_ref)))
    ]
    for load in loads:
        load.start()
    greet(plan)
    for load in loads[:2]:
        load.wait()
    run = Copies(send, recv)
    columns, width = x_ref.shape[1:]
    quarter = w_ref.shape[2]
    half = 2 * quarter
    rows = dw_ref.shape[1]
    size = columns // parts
    low = jnp.bfloat16

    def wide(values):
        return values.astype(jnp.float32)

    def product(i):
        def go():
            if i == 0:
                loads[2].wait()
            step = 8 * rows
            for z in range(plan.n_dp):
                part = dot(t_ref[z * step : (z + 1) * step, :], g_ref[i])
                made[i, z] = part.astype(low).reshape(2, 2, 2, rows, quarter)
        return go

    def product_y(i):
        def go():
            sum_y[i] = (wide(made[i, :, y]) + wide(made_y[i])).astype(low)
        return go

    def product_z(i):
        def go():
            total = wide(sum_y[i, dp])
            for n in range(len(plan.masks)):
                total = total + wide(made_z[i, n])
            sum_z[i] = total.astype(low)
        return go

    def product_c(i):
        def go():
            sides[i, :, :, pl.ds(pl.multiple_of(c * quarter, 128), quarter)] = sum_z[i, :, c]
        return go

    def product_x(i):
        def go():
            dw_ref[i, :, pl.ds(pl.multiple_of(x * half, 128), half)] = wide(sides[i, x])
            dw_ref[i, :, pl.ds(pl.multiple_of((1 - x) * half, 128), half)] = wide(made_x[i])
        return go

    def back(i):
        def go():
            pieces = [g_ref[k].reshape(8, columns, quarter)[:, i * size : (i + 1) * size].reshape(8 * size, quarter)
                      for k in range(3)]
            step = 512
            for n in range(width // step):
                total = sum(dot(pieces[k], w_ref[k, n * step : (n + 1) * step, :], NT) for k in range(3))
                acts[i, :, :, :, :, n * step : (n + 1) * step] = total.astype(low).reshape(2, 2, 2, size, step)
        return go

    def back_c(i):
        def go():
            sum_c[i] = (wide(acts[i, :, :, c]) + wide(acts_c[i])).astype(low)
        return go

    def back_x(i):
        def go():
            sum_x[i] = (wide(sum_c[i, :, x]) + wide(acts_x[i])).astype(low)
        return go

    def norm_back(i):
        def go():
            if i == 0:
                for load in loads[3:]:
                    load.wait()
                totals[...] = jnp.zeros_like(totals)
            gain = gain_ref[...]
            for s in range(2):
                mine = wide(sum_x[i, s])
                grad = jnp.where(y == s, mine, wide(acts_y[i]))
                at = pl.ds(i * size, size)
                values = x_ref[s, at]
                centre = values - jnp.mean(values, axis=-1, keepdims=True)
                spread = lax.rsqrt(jnp.mean(centre * centre, axis=-1, keepdims=True) + EPSILON)
                normed = centre * spread
                grown = grad * gain
                mean_one = jnp.mean(grown, axis=-1, keepdims=True)
                mean_two = jnp.mean(grown * normed, axis=-1, keepdims=True)
                dx_ref[s, at] = gx_ref[s, at] + (grown - mean_one - normed * mean_two) * spread
                totals[0:1] += jnp.sum(grad * normed, axis=0, keepdims=True)
                totals[1:2] += jnp.sum(grad, axis=0, keepdims=True)
        return go

    pieces = []
    for i in range(parts):
        pieces.append((i if i < 2 else 2 * i - 1, [
            (back(i), [run.remote(acts.at[i, :, :, 1 - c], acts_c.at[i], partner_seq(1))]),
            (back_c(i), [run.remote(sum_c.at[i, :, 1 - x], acts_x.at[i], partner_seq(2))]),
            (back_x(i), [run.remote(sum_x.at[i, 1 - y], acts_y.at[i], partner_seq(4))]),
            (norm_back(i), []),
        ]))
    for i in range(3):
        pieces.append((2 * i + 2, [
            (product(i), [run.remote(made.at[i, :, 1 - y], made_y.at[i], partner_seq(4))]),
            (product_y(i), [
                run.remote(sum_y.at[i, lax.bitwise_xor(dp, m)], made_z.at[i, n], partner_dp(plan, m))
                for n, m in enumerate(plan.masks)]),
            (product_z(i), [run.remote(
                sum_z.at[i, :, 1 - c], sides.at[i, :, :, pl.ds(c * quarter, quarter)], partner_seq(1))]),
            (product_c(i), [run.remote(sides.at[i, 1 - x], made_x.at[i], partner_seq(2))]),
            (product_x(i), []),
        ]))

    def norms_start():
        totals[2:4] = more_ref[...]
        turned = totals[...].T.astype(low)
        norms[...] = turned.reshape(norms.shape)

    def norms_add(total, kept, got):
        def go():
            total[...] = (wide(kept()) + wide(got[...])).astype(low)
        return go

    def norms_end():
        total = wide(norms_sy[dp])
        for n in range(len(plan.masks)):
            total = total + wide(norms_z[n])
        dn_ref[...] = total

    end = max(start + 2 * (len(stages) - 1) for start, stages in pieces if len(stages) == 4) + 1
    pieces.append((end, [
        (norms_start, [run.remote(norms.at[:, :, :, 1 - c], norms_c, partner_seq(1))]),
        (norms_add(norms_sc, lambda: norms[:, :, :, c], norms_c), [run.remote(norms_sc.at[:, :, 1 - x], norms_x, partner_seq(2))]),
        (norms_add(norms_sx, lambda: norms_sc[:, :, x], norms_x), [run.remote(norms_sx.at[:, 1 - y], norms_y, partner_seq(4))]),
        (norms_add(norms_sy, lambda: norms_sx[:, y], norms_y), [
            run.remote(norms_sy.at[lax.bitwise_xor(dp, m)], norms_z.at[n], partner_dp(plan, m))
            for n, m in enumerate(plan.masks)]),
        (norms_end, []),
    ]))
    run.run(pieces, 2)


def finish(plan, grads, turned, weights, inputs, grad_first, gain, more, collective_id):
    _, columns, width = inputs.shape
    quarter = weights.shape[2]
    n_dp, masks = plan.n_dp, len(plan.masks)
    rows = width // (8 * n_dp)
    parts = 4
    size = columns // parts
    low = jnp.bfloat16
    hbm = pl.BlockSpec(memory_space=pl.ANY)
    vmem = pl.BlockSpec(memory_space=pltpu.VMEM)
    copies = 3 * (3 + masks) + 3 * parts + 3 + masks
    return pl.pallas_call(
        functools.partial(finish_kernel, plan, parts),
        out_shape=[
            jax.ShapeDtypeStruct(inputs.shape, jnp.float32),
            jax.ShapeDtypeStruct((3, rows, width), jnp.float32),
            jax.ShapeDtypeStruct((rows, 128), jnp.float32),
        ],
        in_specs=[hbm] * 5 + [vmem] * 2,
        out_specs=[vmem] * 3,
        scratch_shapes=[
            pltpu.VMEM(grads.shape, low),
            pltpu.VMEM(turned.shape, low),
            pltpu.VMEM(weights.shape, low),
            pltpu.VMEM(inputs.shape, jnp.float32),
            pltpu.VMEM(inputs.shape, jnp.float32),
            pltpu.VMEM((3, n_dp, 2, 2, 2, rows, quarter), low),
            pltpu.VMEM((3, n_dp, 2, 2, rows, quarter), low),
            pltpu.VMEM((3, n_dp, 2, 2, rows, quarter), low),
            pltpu.VMEM((3, masks, 2, 2, rows, quarter), low),
            pltpu.VMEM((3, 2, 2, rows, quarter), low),
            pltpu.VMEM((3, 2, rows, 2 * quarter), low),
            pltpu.VMEM((3, rows, 2 * quarter), low),
            pltpu.VMEM((parts, 2, 2, 2, size, width), low),
            pltpu.VMEM((parts, 2, 2, size, width), low),
            pltpu.VMEM((parts, 2, 2, size, width), low),
            pltpu.VMEM((parts, 2, size, width), low),
            pltpu.VMEM((parts, 2, size, width), low),
            pltpu.VMEM((parts, size, width), low),
            pltpu.VMEM((128, width), jnp.float32),
            pltpu.VMEM((n_dp, 2, 2, 2, rows, 128), low),
            pltpu.VMEM((n_dp, 2, 2, rows, 128), low),
            pltpu.VMEM((n_dp, 2, 2, rows, 128), low),
            pltpu.VMEM((n_dp, 2, rows, 128), low),
            pltpu.VMEM((n_dp, 2, rows, 128), low),
            pltpu.VMEM((n_dp, rows, 128), low),
            pltpu.VMEM((n_dp, rows, 128), low),
            pltpu.VMEM((masks, rows, 128), low),
            pltpu.SemaphoreType.DMA((copies,)),
            pltpu.SemaphoreType.DMA((copies,)),
            pltpu.SemaphoreType.DMA((5,)),
        ],
        compiler_params=pltpu.CompilerParams(
            collective_id=collective_id, has_side_effects=True, vmem_limit_bytes=62 << 20),
    )(grads, turned, weights, inputs, grad_first, gain, more)


def layer_norm(values, gain, offset):
    centre = values - jnp.mean(values, axis=-1, keepdims=True)
    spread = jnp.mean(centre * centre, axis=-1, keepdims=True)
    return centre * lax.rsqrt(spread + EPSILON) * gain + offset


def gelu(values):
    return 0.5 * values * (1.0 + lax.erf(values * (1.0 / math.sqrt(2.0))))


def lower(values):
    return values.astype(jnp.bfloat16)


def project(acts, weight):
    return jnp.einsum("gcd,de->gce", acts, weight, preferred_element_type=jnp.float32)


def project_back(grads, weight):
    return jnp.einsum("gce,de->gcd", grads, weight, preferred_element_type=jnp.float32)


def outer_sum(left, right):
    return jnp.einsum("gci,gcj->ij", left, right, preferred_element_type=jnp.float32)


def shards(
    inputs,
    segments,
    norm1_gain,
    norm1_bias,
    w_query,
    w_key,
    w_value,
    w_out,
    norm2_gain,
    norm2_bias,
    w_up,
    w_down,
    cotangent,
    *,
    plan,
):
    count = plan.n_seq
    axes = ("dp", "seq")
    groups, columns, width = inputs.shape
    heads = width // HEAD_DIM
    length = columns * count
    block = min(512, length)
    per = -(-groups * heads // count)
    fast = (
        count == 8
        and groups == 2
        and heads % 4 == 0
        and columns % 64 == 0
        and 512 % columns == 0
        and w_query.shape[0] % 16 == 0
    )
    rank = lax.axis_index("seq")

    ids = lax.all_gather(segments, "seq", axis=1, tiled=True)
    pair_at = jnp.minimum(rank * per + jnp.arange(per, dtype=jnp.int32), groups * heads - 1)
    pair_ids = ids[pair_at // heads]
    seg_row = pair_ids.reshape(per, length // block, block)
    seg_col = jnp.where(pair_ids < 0, -2, pair_ids)[..., None]

    half = HEAD_DIM // 2
    rates = jnp.exp(jnp.arange(half, dtype=jnp.float32) * (-math.log(10000.0) / half))
    turned = jnp.arange(length, dtype=jnp.float32)[:, None] * rates[None, :]
    cosine, sine = jnp.cos(turned), jnp.sin(turned)
    cosine_all = jnp.concatenate([cosine, cosine], axis=1)
    sine_all = jnp.concatenate([-sine, sine], axis=1)
    cosine_own = lax.dynamic_slice_in_dim(cosine_all, rank * columns, columns)[None, :, None, :]
    sine_own = lax.dynamic_slice_in_dim(sine_all, rank * columns, columns)[None, :, None, :]

    def to_pairs(values):
        shaped = values.reshape(groups, columns, heads, HEAD_DIM)
        shaped = jnp.transpose(shaped, (0, 2, 1, 3)).reshape(groups * heads, columns, HEAD_DIM)
        shaped = jnp.pad(shaped, ((0, count * per - groups * heads), (0, 0), (0, 0)))
        return shaped.reshape(count, per, columns, HEAD_DIM)

    def from_pairs(values):
        shaped = values.reshape(count * per, columns, HEAD_DIM)[: groups * heads]
        shaped = shaped.reshape(groups, heads, columns, HEAD_DIM)
        return jnp.transpose(shaped, (0, 2, 1, 3)).reshape(groups, columns, width)

    def swap(values):
        return lax.all_to_all(values, "seq", 0, 0)

    def whole(weight):
        return lax.all_gather(weight, axes, axis=0, tiled=True)

    act_one = lower(layer_norm(inputs, norm1_gain, norm1_bias))
    if fast:
        tokens_one, heads_weight, (full_out,) = start(
            plan, act_one, (w_query, w_key, w_value), (w_out,), 512, 2, 1
        )
        packed, turned_one = project_heads(tokens_one, heads_weight, cosine_all, sine_all)
    else:
        cosine_own = lax.dynamic_slice_in_dim(cosine_all, rank * columns, columns)[None, :, None, :]
        sine_own = lax.dynamic_slice_in_dim(sine_all, rank * columns, columns)[None, :, None, :]

        def turn(values):
            shaped = values.reshape(groups, columns, heads, HEAD_DIM)
            return shaped * cosine_own + jnp.roll(shaped, half, axis=-1) * sine_own

        full_query, full_key, full_value, full_out = (whole(w) for w in (w_query, w_key, w_value, w_out))
        query_low = lower(turn(project(act_one, full_query)))
        key_low = lower(turn(project(act_one, full_key)))
        value_low = lower(project(act_one, full_value))
        packed = swap(jnp.stack([to_pairs(query_low), to_pairs(key_low), to_pairs(value_low)], axis=2))
    full_up, full_down = whole(w_up), whole(w_down)
    mixed_pairs, mixed_t, lse = attend(packed, seg_col, seg_row)
    mixed_low = from_pairs(swap(mixed_pairs))

    first_sum = inputs + project(mixed_low, full_out)
    act_two = lower(layer_norm(first_sum, norm2_gain, norm2_bias))
    upper = project(act_two, full_up)
    hidden_low = lower(gelu(upper))
    output = first_sum + project(hidden_low, full_down)
    grad_out_low = lower(cotangent)
    grad_hidden = project_back(grad_out_low, full_down)
    gelu_values, gelu_back = jax.vjp(gelu, upper)
    grad_upper = lower(gelu_back(grad_hidden)[0])
    grad_act_two = project_back(grad_upper, full_up)
    normed_two, norm_two_back = jax.vjp(layer_norm, first_sum, norm2_gain, norm2_bias)
    grad_first_norm, gain_two_grad, offset_two_grad = norm_two_back(grad_act_two)
    grad_first = cotangent + grad_first_norm
    grad_attn_low = lower(grad_first)
    grad_mixed = lower(project_back(grad_attn_low, full_out))

    tokens = groups * columns
    width_piece = 512

    def flat(values):
        return values.reshape(tokens, -1)

    def left_of(values):
        turned = flat(values).T
        every = plan.n_dp * plan.n_seq
        turned = turned.reshape(every, -1, width // every, tokens)
        return jnp.transpose(turned, (1, 0, 2, 3)).reshape(-1, width, tokens)

    def reduce_all(pairs, collective_id, beside=None):
        out, *more = reduce_products(plan, pairs, width_piece, 2, collective_id, beside)
        results, at = [], 0
        for left, right in pairs:
            blocks, cols = left.shape[0], right.shape[1] // width_piece
            part = out[at : at + blocks * cols].reshape(blocks, cols, -1, width_piece)
            results.append(jnp.transpose(part, (0, 2, 1, 3)).reshape(-1, right.shape[1]))
            at += blocks * cols
        return results + more

    work = AttendBack(
        8 if fast else 0,
        packed, swap(to_pairs(grad_mixed)), mixed_t, lse, seg_col, seg_row, cosine_all, sine_all,
    )
    gains_two = [gain_two_grad, offset_two_grad]
    if fast:
        down_grad, up_grad, out_grad, grads = reduce_all(
            [
                (left_of(hidden_low), flat(grad_out_low)),
                (left_of(act_two), flat(grad_upper)),
                (left_of(mixed_low), flat(grad_attn_low)),
            ],
            2,
            work,
        )
        grad_input, heads_grad, norm_rows = finish(
            plan, grads, turned_one, heads_weight, inputs, grad_first, norm1_gain[None],
            jnp.stack(gains_two), 3,
        )
        query_grad, key_grad, value_grad = heads_grad[0], heads_grad[1], heads_grad[2]
        norm_rows = [norm_rows[:, i] for i in range(4)]
    else:
        def spread(values):
            return lax.psum_scatter(values, axes, scatter_dimension=0, tiled=True).astype(jnp.float32)

        grads = attend_back_alone(work).reshape(3, count, columns, per, HEAD_DIM)
        grads = swap(jnp.transpose(grads, (1, 3, 0, 2, 4)))
        grad_query_low, grad_key_low, grad_value_low = (from_pairs(grads[:, :, i]) for i in range(3))
        grad_act_one = project_back(grad_query_low, full_query) + project_back(grad_key_low, full_key)
        grad_act_one = grad_act_one + project_back(grad_value_low, full_value)
        normed_again, norm_one_back = jax.vjp(layer_norm, inputs, norm1_gain, norm1_bias)
        grad_input_norm, gain_one_grad, offset_one_grad = norm_one_back(grad_act_one)
        grad_input = grad_first + grad_input_norm
        down_grad = spread(lower(outer_sum(hidden_low, grad_out_low)))
        up_grad = spread(lower(outer_sum(act_two, grad_upper)))
        out_grad = spread(lower(outer_sum(mixed_low, grad_attn_low)))
        query_grad = spread(lower(outer_sum(act_one, grad_query_low)))
        key_grad = spread(lower(outer_sum(act_one, grad_key_low)))
        value_grad = spread(lower(outer_sum(act_one, grad_value_low)))
        norm_rows = [spread(v) for v in [gain_one_grad, offset_one_grad] + gains_two]

    return (
        output,
        grad_input,
        norm_rows[0],
        norm_rows[1],
        query_grad,
        key_grad,
        value_grad,
        out_grad,
        norm_rows[2],
        norm_rows[3],
        up_grad,
        down_grad,
    )


def solution(mesh):
    placed = (
        P("dp", "seq", None),
        P("dp", "seq"),
        P(),
        P(),
        P(("dp", "seq"), None),
        P(("dp", "seq"), None),
        P(("dp", "seq"), None),
        P(("dp", "seq"), None),
        P(),
        P(),
        P(("dp", "seq"), None),
        P(("dp", "seq"), None),
        P("dp", "seq", None),
    )
    return jax.shard_map(
        functools.partial(shards, plan=Plan(mesh)),
        mesh=mesh,
        in_specs=placed,
        out_specs=(
            P("dp", "seq", None),
            P("dp", "seq", None),
            P(("dp", "seq")),
            P(("dp", "seq")),
            P(("dp", "seq"), None),
            P(("dp", "seq"), None),
            P(("dp", "seq"), None),
            P(("dp", "seq"), None),
            P(("dp", "seq")),
            P(("dp", "seq")),
            P(("dp", "seq"), None),
            P(("dp", "seq"), None),
        ),
        check_vma=False,
    )
```

```python
import functools
import math

import jax
import jax.numpy as jnp
import numpy as np
from jax import lax
from jax.experimental import pallas as pl
from jax.experimental.pallas import tpu as pltpu
from jax.sharding import PartitionSpec as P

HEAD_DIM = 128


EPSILON = 1e-05
MASKED = -1e30
LOG2E = math.log2(math.e)
NT = (((1,), (1,)), ((), ()))
NN = (((1,), (0,)), ((), ()))


def dot(left, right, dims=NN):
    return lax.dot_general(left, right, dims, preferred_element_type=jnp.float32)


def allowed_pairs(key_col, query_row, diagonal):
    same = key_col == query_row
    if not diagonal:
        return same
    shape = (key_col.shape[0], query_row.shape[1])
    key_at = lax.broadcasted_iota(jnp.int32, shape, 0)
    query_at = lax.broadcasted_iota(jnp.int32, shape, 1)
    return (same & (key_at <= query_at)) | (key_at == query_at)


def attend_back_step(
    block, parts, step, last, q_ref, k_ref, v_ref, g_ref, ot_ref, lse_ref, col_ref, row_ref, cos_ref, sin_ref,
    out_ref, kt_ref, dk_ref, dv_ref,
):
    scale = 1.0 / math.sqrt(HEAD_DIM)

    @pl.when(step == 0)
    def _():
        kt_ref[...] = k_ref[...].reshape(-1, HEAD_DIM).T
        dk_ref[...] = jnp.zeros_like(dk_ref)
        dv_ref[...] = jnp.zeros_like(dv_ref)

    query = q_ref[pl.ds(step * parts, parts)].reshape(block, HEAD_DIM)
    grad = g_ref[pl.ds(step * parts, parts)].reshape(block, HEAD_DIM)
    query_row = row_ref[pl.ds(step, 1), :]
    lse = lse_ref[0, pl.ds(step, 1), :]
    delta = jnp.sum(ot_ref[0, 0] * grad.astype(jnp.float32).T, axis=0, keepdims=True)
    unit = LOG2E * scale

    def visit(j, dqt, diagonal):
        at = pl.multiple_of(j * block, block)
        key = k_ref[pl.ds(j * parts, parts)].reshape(block, HEAD_DIM)
        value = v_ref[pl.ds(j * parts, parts)].reshape(block, HEAD_DIM)
        key_col = col_ref[pl.ds(at, block), :]
        scores = dot(key, query, NT) * unit - lse
        probs = jnp.where(allowed_pairs(key_col, query_row, diagonal), jnp.exp2(scores), 0.0)
        grad_probs = dot(value, grad, NT)
        grad_scores = (probs * (grad_probs - delta)).astype(jnp.bfloat16)
        dv_ref[pl.ds(at, block), :] += dot(probs.astype(jnp.bfloat16), grad)
        dk_ref[pl.ds(at, block), :] += dot(grad_scores, query)
        return dqt + dot(kt_ref[:, pl.ds(at, block)], grad_scores)

    dqt = lax.fori_loop(
        0, step, lambda j, c: visit(j, c, False), jnp.zeros((HEAD_DIM, block), jnp.float32)
    )
    dqt = visit(step, dqt, True)

    def turn_back(values, cosine, sine):
        return values * cosine - pltpu.roll(values, HEAD_DIM // 2, 1) * sine

    at = pl.multiple_of(step * block, block)
    dq = turn_back(dqt.T * scale, cos_ref[pl.ds(at, block), :], sin_ref[pl.ds(at, block), :])
    out_ref[0, pl.ds(at, block), :] = dq.astype(jnp.bfloat16)

    @pl.when(step == last)
    def _():
        dk = turn_back(dk_ref[...] * scale, cos_ref[...], sin_ref[...])
        out_ref[1] = dk.astype(jnp.bfloat16)
        out_ref[2] = dv_ref[...].astype(jnp.bfloat16)


class AttendBack:
    def __init__(self, first, packed, grads, mixed_t, lse, seg_col, seg_row, cosine, sine):
        count, per, _, columns, _ = packed.shape
        length = count * columns
        self.block = seg_row.shape[1]
        self.steps, self.parts = length // self.block, self.block // columns
        self.first, self.count, self.ticks = first, per * self.steps, first + per * self.steps
        self.operands = (packed, packed, packed, grads, mixed_t, lse, seg_col, seg_row, cosine, sine)

        def pair(t):
            return lax.div(jnp.clip(t - first, 0, self.count - 1), self.steps)

        def step(t):
            return lax.rem(jnp.clip(t - first, 0, self.count - 1), self.steps)

        def whole(which):
            return pl.BlockSpec((count, None, None, columns, HEAD_DIM), lambda t: (0, pair(t), which, 0, 0))

        rows = pl.BlockSpec((1, self.steps, self.block), lambda t: (pair(t), 0, 0))
        table = pl.BlockSpec((length, HEAD_DIM), lambda t: (0, 0))
        self.in_specs = [
            whole(0),
            whole(1),
            whole(2),
            pl.BlockSpec((count, None, columns, HEAD_DIM), lambda t: (0, pair(t), 0, 0)),
            pl.BlockSpec((1, 1, HEAD_DIM, self.block), lambda t: (pair(t), step(t), 0, 0)),
            rows,
            pl.BlockSpec((length, 1), lambda t: (0, 0)),
            pl.BlockSpec((self.steps, self.block), lambda t: (0, 0)),
            table,
            table,
        ]
        self.out_specs = [pl.BlockSpec((3, length, HEAD_DIM), lambda t: (0, 0, pair(t)))]
        self.out_shapes = [jax.ShapeDtypeStruct((3, length, per * HEAD_DIM), jnp.bfloat16)]
        self.scratch = [
            pltpu.VMEM((HEAD_DIM, length), jnp.bfloat16),
            pltpu.VMEM((length, HEAD_DIM), jnp.float32),
            pltpu.VMEM((length, HEAD_DIM), jnp.float32),
        ]

    def run(self, tick, refs):
        @pl.when((tick >= self.first) & (tick < self.ticks))
        def _():
            step = lax.rem(tick - self.first, self.steps)
            attend_back_step(self.block, self.parts, step, self.steps - 1, *refs)


MESH = pl.DeviceIdType.MESH


class Plan:
    def __init__(self, mesh):
        self.n_dp, self.n_seq = mesh.shape["dp"], mesh.shape["seq"]
        bits = [1 << i for i in range(self.n_seq.bit_length() - 1)]
        self.bits = bits[::-1]
        if len(bits) == 3:
            self.orders = ((2, 4, 1), (4, 2, 1))
        else:
            turn = len(bits) // 2
            self.orders = (tuple(bits), tuple(bits[turn:] + bits[:turn]))
        self.hops = len(bits)
        self.masks = range(1, self.n_dp)

    def lead(self):
        return (self.n_dp,) + (2,) * self.hops


def place():
    return lax.axis_index("dp"), lax.axis_index("seq")


def partner_dp(plan, mask):
    dp, seq = place()
    return (lax.bitwise_xor(dp, mask), seq)


def partner_seq(bit):
    dp, seq = place()
    return (dp, lax.bitwise_xor(seq, bit))


def own_bit(bit):
    return lax.bitwise_and(lax.div(place()[1], bit), 1)


def greet(plan, everyone=False):
    barrier = pltpu.get_barrier_semaphore()
    others = [partner_dp(plan, m) for m in plan.masks]
    others += [partner_seq(m) for m in (range(1, plan.n_seq) if everyone else plan.bits)]
    for other in others:
        pl.semaphore_signal(barrier, inc=1, device_id=other, device_id_type=MESH)
    pl.semaphore_wait(barrier, len(others))


def reduce_kernel(plan, jobs, first, count, lag, beside, *refs):
    k, given = len(jobs), sum(job[3] for job in jobs)
    lefts, rights, refs = iter(refs[:given]), refs[given : given + k], refs[given + k :]
    more = [0, 0, 0] if beside is None else [len(beside.in_specs), len(beside.out_specs), len(beside.scratch)]
    extra, refs = refs[: more[0]], refs[more[0] :]
    out_ref, extra = refs[0], extra + refs[1 : 1 + more[1]]
    scratch = refs[1 + more[1] :]
    extra, scratch = extra + scratch[: more[2]], scratch[more[2] :]
    hops, slots = plan.hops, 2 * lag
    sums = [scratch[h * (hops + 1) : (h + 1) * (hops + 1)] for h in range(2)]
    scratch = scratch[2 * (hops + 1) :]
    got = [scratch[h * (hops + 1) : (h + 1) * (hops + 1)] for h in range(2)]
    send, recv = scratch[2 * (hops + 1) :]
    tick = pl.program_id(0)
    half = out_ref.shape[-1] // 2
    rows = out_ref.shape[-2]
    orders = [order[::-1] for order in plan.orders]
    dp, _ = place()

    @pl.when(tick == 0)
    def _():
        greet(plan, getattr(beside, "everyone", False))

    def at_bit(h, stage, value):
        left = [b for b in plan.bits if b not in orders[h][:stage]]
        return (slice(None),) + tuple(value if b == orders[h][stage] else slice(None) for b in left)

    def copies(h, stage, slot):
        kept = lax.rem(slot, lag)
        if stage < hops:
            bit = orders[h][stage]
            at = h * (hops + len(plan.masks)) + stage
            return [pltpu.make_async_remote_copy(
                sums[h][stage].at[(kept,) + at_bit(h, stage, 1 - own_bit(bit))], got[h][stage].at[slot],
                send.at[slot, at], recv.at[slot, at], device_id=partner_seq(bit), device_id_type=MESH)]
        out = []
        for n, mask in enumerate(plan.masks):
            at = h * (hops + len(plan.masks)) + hops + n
            out.append(pltpu.make_async_remote_copy(
                sums[h][hops].at[kept, lax.bitwise_xor(dp, mask)], got[h][hops].at[slot, n],
                send.at[slot, at], recv.at[slot, at], device_id=partner_dp(plan, mask), device_id_type=MESH))
        return out

    def wide(values):
        return values.astype(jnp.float32)

    for stage in reversed(range(1, hops + 2)):
        u = tick - first - lag * stage

        @pl.when((u >= 0) & (u < count))
        def _(stage=stage, u=u):
            slot, kept = lax.rem(u, slots), lax.rem(u, lag)
            for h in range(2):
                for copy in copies(h, stage - 1, slot):
                    copy.wait()
                if stage <= hops:
                    mine = (kept,) + at_bit(h, stage - 1, own_bit(orders[h][stage - 1]))
                    total = wide(sums[h][stage - 1][mine]) + wide(got[h][stage - 1][slot])
                    sums[h][stage][kept] = total.astype(jnp.bfloat16)
                    for copy in copies(h, stage, slot):
                        copy.start()
                else:
                    total = wide(sums[h][hops][kept, dp])
                    for n in range(len(plan.masks)):
                        total = total + wide(got[h][hops][slot, n])
                    out_ref[0, :, h * half : (h + 1) * half] = total

    for (start, stop, cols, has_left), right in zip(jobs, rights):
        if has_left:
            left = next(lefts)

            def left_rows(which, z, left=left):
                step = rows * plan.n_seq
                return left[which, z * step : (z + 1) * step, :]

        else:
            left_rows = functools.partial(beside.left, extra)

        @pl.when((tick >= first + start) & (tick < first + stop))
        def _(start=start, cols=cols, left_rows=left_rows, right=right):
            u = tick - first
            slot, kept = lax.rem(u, slots), lax.rem(u, lag)
            which = lax.div(u - start, cols)
            for z in range(plan.n_dp):
                part = dot(left_rows(which, z), right[...]).astype(jnp.bfloat16)
                for h in range(2):
                    piece = part[:, h * half : (h + 1) * half]
                    sums[h][0][kept, z] = piece.reshape(plan.lead()[1:] + (rows, half))
            for h in range(2):
                for copy in copies(h, 0, slot):
                    copy.start()

    if beside is not None:
        beside.run(tick, extra)


def reduce_products(plan, pairs, rows, width, lag, collective_id, beside=None, first=0):
    jobs, start = [], 0
    left_specs, right_specs = [], []
    for left, right in pairs:
        cols = right.shape[1] // width
        blocks = left if isinstance(left, int) else left.shape[0]
        stop = start + blocks * cols
        jobs.append((start, stop, cols, left is not blocks))
        if left is not blocks:
            left_specs.append(pl.BlockSpec(left.shape, lambda t: (0, 0, 0)))
        right_specs.append(pl.BlockSpec(
            (right.shape[0], width),
            functools.partial(lambda t, start, stop, cols: (0, lax.rem(jnp.clip(t - first, start, stop - 1) - start, cols)),
                start=start, stop=stop, cols=cols)))
        start = stop
    count = start
    half = width // 2
    slots, hops = 2 * lag, plan.hops
    tail = lag * (hops + 1)
    sums = [pltpu.VMEM((lag, plan.n_dp) + (2,) * (hops - s) + (rows, half), jnp.bfloat16) for s in range(hops + 1)]
    got = [pltpu.VMEM((slots, plan.n_dp) + (2,) * (hops - 1 - s) + (rows, half), jnp.bfloat16) for s in range(hops)]
    got.append(pltpu.VMEM((slots, len(plan.masks), rows, half), jnp.bfloat16))
    each = 2 * (hops + len(plan.masks))
    out_specs = [pl.BlockSpec((1, rows, width), lambda t: (jnp.clip(t - first - tail, 0, count - 1), 0, 0))]
    out_shapes = [jax.ShapeDtypeStruct((count, rows, width), jnp.float32)]
    more_in, more_scratch, more_operands = [], [], []
    if beside is not None:
        more_in, more_scratch, more_operands = beside.in_specs, beside.scratch, beside.operands
        out_specs, out_shapes = out_specs + beside.out_specs, out_shapes + beside.out_shapes
    return pl.pallas_call(
        functools.partial(reduce_kernel, plan, jobs, first, count, lag, beside),
        grid=(max(first + count + tail, 0 if beside is None else beside.ticks),),
        in_specs=left_specs + right_specs + more_in,
        out_specs=out_specs,
        out_shape=out_shapes,
        scratch_shapes=more_scratch + sums + sums + got + got + [
            pltpu.SemaphoreType.DMA((slots, each)),
            pltpu.SemaphoreType.DMA((slots, each)),
        ],
        compiler_params=pltpu.CompilerParams(
            collective_id=collective_id, has_side_effects=True, vmem_limit_bytes=60 << 20),
    )(*[p[0] for p in pairs if not isinstance(p[0], int)], *[p[1] for p in pairs], *more_operands)


class Copies:
    def __init__(self, send, recv):
        self.send, self.recv, self.count, self.sent = send, recv, 0, []

    def remote(self, src, dst, device):
        at = self.count
        self.count += 1
        return pltpu.make_async_remote_copy(
            src, dst, self.send.at[at], self.recv.at[at], device_id=device, device_id_type=MESH)

    def run(self, pieces, lag):
        last = max(start + lag * len(stages) for start, stages in pieces)
        for tick in range(last + 1):
            for stage in reversed(range(max(len(stages) for _, stages in pieces) + 1)):
                for start, stages in pieces:
                    if start + lag * stage != tick or stage > len(stages):
                        continue
                    if stage > 0:
                        for copy in stages[stage - 1][1]:
                            copy.wait_recv()
                    if stage < len(stages):
                        ahead, copies = stages[stage]
                        if ahead is not None:
                            ahead()
                        for copy in copies:
                            copy.start()
        for _, stages in pieces:
            for _, copies in stages:
                for copy in copies:
                    copy.wait_send()


def start_kernel(
    plan, splits, lag, h_ref, s_ref, q_ref, k_ref, v_ref, *refs,
):
    n = len(splits)
    ins, refs = refs[:n], refs[n:]
    hs_ref, ss_ref, w_ref, outs = refs[0], refs[1], refs[2], refs[3 : 3 + n]
    hv, wv, halves = refs[3 + n : 6 + n]
    held = refs[6 + n : 6 + 2 * n]
    send, recv, local = refs[6 + 2 * n :]
    dp, seq = place()
    y, x, c = own_bit(4), own_bit(2), own_bit(1)
    loads = [pltpu.make_async_copy(h_ref.at[y], hv, local.at[0])]
    loads += [pltpu.make_async_copy(r, wv.at[i], local.at[1 + i]) for i, r in enumerate((q_ref, k_ref, v_ref))]
    loads += [pltpu.make_async_copy(r, o, local.at[4 + i]) for i, (r, o) in enumerate(zip(ins, held))]
    for load in loads:
        load.start()
    greet(plan)
    for load in loads:
        load.wait()
    own = pltpu.make_async_copy(hv, hs_ref.at[y, x, c], local.at[0])
    own.start()
    named = pltpu.make_async_copy(s_ref.at[y], ss_ref.at[y, x, c], local.at[4 + n])
    named.start()
    me = (y, x, c)
    keeps = [pltpu.make_async_copy(o, d.at[(dp,) + me], local.at[4 + i]) for i, (o, d) in enumerate(zip(held, outs))]
    for keep in keeps:
        keep.start()
    run = Copies(send, recv)
    pieces = []

    pieces.append((0, [
        (None, [run.remote(s_ref.at[1 - y], ss_ref.at[y, x, c], partner_seq(4))]),
        (named.wait, [run.remote(ss_ref.at[:, x, c], ss_ref.at[:, x, c], partner_seq(2))]),
        (None, [run.remote(ss_ref.at[:, :, c], ss_ref.at[:, :, c], partner_seq(1))]),
    ]))
    tokens = hv.shape[0]
    parts = 4
    for i in range(parts):
        rows = pl.ds(i * (tokens // parts), tokens // parts)
        first = run.remote(h_ref.at[1 - y, rows], hs_ref.at[y, x, c, rows], partner_seq(4))
        second = [run.remote(hs_ref.at[:, x, c, rows], hs_ref.at[:, x, c, rows], partner_seq(2))]
        third = [run.remote(hs_ref.at[:, :, c, rows], hs_ref.at[:, :, c, rows], partner_seq(1))]
        pieces.append((i, [(None, [first]), (own.wait if i == 0 else None, second), (None, third)]))

    half, quarter = halves.shape[-1], w_ref.shape[-1]
    for i in range(3):
        mine = pltpu.make_async_copy(
            halves.at[i, :, :, pl.ds(c * quarter, quarter)], w_ref.at[i, dp, y, :, c], local.at[1 + i])

        def cut(i=i, mine=mine):
            halves[i, x] = wv[i, :, pl.ds(pl.multiple_of(x * half, 128), half)]
            mine.start()

        to_x = [run.remote(wv.at[i, :, pl.ds((1 - x) * half, half)], halves.at[i, x], partner_seq(2))]
        to_core = [run.remote(
            halves.at[i, :, :, pl.ds((1 - c) * quarter, quarter)], w_ref.at[i, dp, y, :, c], partner_seq(1))]
        to_z = [run.remote(w_ref.at[i, dp, y], w_ref.at[i, dp, y], partner_dp(plan, m)) for m in plan.masks]
        to_y = [run.remote(w_ref.at[i, :, y], w_ref.at[i, :, y], partner_seq(4))]
        pieces.append((i, [(None, to_x), (cut, to_core), (mine.wait, to_z), (None, to_y)]))

    tick = parts
    for src, dst, keep, (count, size) in zip(held, outs, keeps, splits):
        for j in range(count):
            stages = []
            for stage in range(plan.hops + 1):
                copies = []
                for h in range(2):
                    cols = pl.ds(j * size + h * (size // 2), size // 2)
                    if stage == 0:
                        for m in plan.masks:
                            copies.append(run.remote(
                                src.at[:, cols], dst.at[(dp,) + me + (slice(None), cols)], partner_dp(plan, m)))
                    else:
                        order = plan.orders[h]
                        where = tuple(slice(None) if b in order[: stage - 1] else m for b, m in zip(plan.bits, me))
                        part = dst.at[(slice(None),) + where + (slice(None), cols)]
                        copies.append(run.remote(part, part, partner_seq(order[stage - 1])))
                stages.append((keep.wait if stage == 1 and j == 0 else None, copies))
            pieces.append((tick, stages))
            tick += 1
    run.run(pieces, lag)


def start(plan, acts, segments, weights, whole, piece, lag, collective_id):
    groups, columns, width = acts.shape
    rows = weights[0].shape[0]
    quarter = width // 4
    splits, copies = [], 3 + 4 * 3 + 3 * (3 + len(plan.masks))
    for a in whole:
        count = max(1, a.shape[1] // piece)
        while a.shape[1] % (256 * count):
            count -= 1
        splits.append((count, a.shape[1] // count))
        copies += count * 2 * (len(plan.masks) + plan.hops)
    hbm = pl.BlockSpec(memory_space=pl.ANY)
    outs = pl.pallas_call(
        functools.partial(start_kernel, plan, splits, lag),
        out_shape=[
            jax.ShapeDtypeStruct((2, 2, 2, columns, width), acts.dtype),
            jax.ShapeDtypeStruct((2, 2, 2, 1, columns), jnp.int32),
            jax.ShapeDtypeStruct((3,) + plan.lead() + (rows, quarter), acts.dtype),
        ] + [jax.ShapeDtypeStruct(plan.lead() + a.shape, a.dtype) for a in whole],
        in_specs=[hbm] * (5 + len(whole)),
        out_specs=[hbm] * (3 + len(whole)),
        scratch_shapes=[
            pltpu.VMEM((columns, width), acts.dtype),
            pltpu.VMEM((3, rows, width), acts.dtype),
            pltpu.VMEM((3, 2, rows, width // 2), acts.dtype),
        ] + [pltpu.VMEM(a.shape, a.dtype) for a in whole] + [
            pltpu.SemaphoreType.DMA((copies,)),
            pltpu.SemaphoreType.DMA((copies,)),
            pltpu.SemaphoreType.DMA((5 + len(whole),)),
        ],
        compiler_params=pltpu.CompilerParams(
            collective_id=collective_id, has_side_effects=True, vmem_limit_bytes=32 << 20),
    )(acts, segments[:, None, :], *weights, *whole)
    tokens, ids, projections = outs[:3]
    return (
        tokens.reshape(8, columns, width),
        ids.reshape(8 * columns),
        projections.reshape(3, width, quarter),
        [o.reshape(-1, o.shape[-1]) for o in outs[3:]],
    )


def finish_kernel(
    plan, parts, g_any, t_any, w_any, x_any, gx_any, gain_ref, more_ref,
    dx_ref, dw_ref, dn_ref,
    g_ref, t_ref, w_ref, x_ref, gx_ref,
    made, made_y, sum_y, made_z, sum_z, sides, made_x,
    acts, acts_c, sum_c, acts_x, sum_x, acts_y,
    totals, norms, norms_c, norms_sc, norms_x, norms_sx, norms_y, norms_sy, norms_z,
    send, recv, local,
):
    dp, _ = place()
    y, x, c = own_bit(4), own_bit(2), own_bit(1)
    loads = [
        pltpu.make_async_copy(src, dst, local.at[i])
        for i, (src, dst) in enumerate(
            ((g_any, g_ref), (w_any, w_ref), (t_any, t_ref), (x_any, x_ref), (gx_any, gx_ref)))
    ]
    for load in loads:
        load.start()
    greet(plan)
    for load in loads[:2]:
        load.wait()
    run = Copies(send, recv)
    columns, width = x_ref.shape[1:]
    quarter = w_ref.shape[2]
    half = 2 * quarter
    rows = dw_ref.shape[1]
    size = columns // parts
    low = jnp.bfloat16

    def wide(values):
        return values.astype(jnp.float32)

    def product(i):
        def go():
            if i == 0:
                loads[2].wait()
            step = 8 * rows
            for z in range(plan.n_dp):
                part = dot(t_ref[z * step : (z + 1) * step, :], g_ref[i])
                made[i, z] = part.astype(low).reshape(2, 2, 2, rows, quarter)
        return go

    def product_y(i):
        def go():
            sum_y[i] = (wide(made[i, :, y]) + wide(made_y[i])).astype(low)
        return go

    def product_z(i):
        def go():
            total = wide(sum_y[i, dp])
            for n in range(len(plan.masks)):
                total = total + wide(made_z[i, n])
            sum_z[i] = total.astype(low)
        return go

    def product_c(i):
        def go():
            sides[i, :, :, pl.ds(pl.multiple_of(c * quarter, 128), quarter)] = sum_z[i, :, c]
        return go

    def product_x(i):
        def go():
            dw_ref[i, :, pl.ds(pl.multiple_of(x * half, 128), half)] = wide(sides[i, x])
            dw_ref[i, :, pl.ds(pl.multiple_of((1 - x) * half, 128), half)] = wide(made_x[i])
        return go

    def back(i):
        def go():
            pieces = [g_ref[k].reshape(8, columns, quarter)[:, i * size : (i + 1) * size].reshape(8 * size, quarter)
                      for k in range(3)]
            step = 512
            for n in range(width // step):
                total = sum(dot(pieces[k], w_ref[k, n * step : (n + 1) * step, :], NT) for k in range(3))
                acts[i, :, :, :, :, n * step : (n + 1) * step] = total.astype(low).reshape(2, 2, 2, size, step)
        return go

    def back_c(i):
        def go():
            sum_c[i] = (wide(acts[i, :, :, c]) + wide(acts_c[i])).astype(low)
        return go

    def back_x(i):
        def go():
            sum_x[i] = (wide(sum_c[i, :, x]) + wide(acts_x[i])).astype(low)
        return go

    def norm_back(i):
        def go():
            if i == 0:
                for load in loads[3:]:
                    load.wait()
                totals[...] = jnp.zeros_like(totals)
            gain = gain_ref[...]
            for s in range(2):
                mine = wide(sum_x[i, s])
                grad = jnp.where(y == s, mine, wide(acts_y[i]))
                at = pl.ds(i * size, size)
                values = x_ref[s, at]
                centre = values - jnp.mean(values, axis=-1, keepdims=True)
                spread = lax.rsqrt(jnp.mean(centre * centre, axis=-1, keepdims=True) + EPSILON)
                normed = centre * spread
                grown = grad * gain
                mean_one = jnp.mean(grown, axis=-1, keepdims=True)
                mean_two = jnp.mean(grown * normed, axis=-1, keepdims=True)
                dx_ref[s, at] = gx_ref[s, at] + (grown - mean_one - normed * mean_two) * spread
                totals[0:1] += jnp.sum(grad * normed, axis=0, keepdims=True)
                totals[1:2] += jnp.sum(grad, axis=0, keepdims=True)
        return go

    pieces = []
    for i in range(parts):
        pieces.append((i if i < 2 else 2 * i - 1, [
            (back(i), [run.remote(acts.at[i, :, :, 1 - c], acts_c.at[i], partner_seq(1))]),
            (back_c(i), [run.remote(sum_c.at[i, :, 1 - x], acts_x.at[i], partner_seq(2))]),
            (back_x(i), [run.remote(sum_x.at[i, 1 - y], acts_y.at[i], partner_seq(4))]),
            (norm_back(i), []),
        ]))
    for i in range(3):
        pieces.append((2 * i + 2, [
            (product(i), [run.remote(made.at[i, :, 1 - y], made_y.at[i], partner_seq(4))]),
            (product_y(i), [
                run.remote(sum_y.at[i, lax.bitwise_xor(dp, m)], made_z.at[i, n], partner_dp(plan, m))
                for n, m in enumerate(plan.masks)]),
            (product_z(i), [run.remote(
                sum_z.at[i, :, 1 - c], sides.at[i, :, :, pl.ds(c * quarter, quarter)], partner_seq(1))]),
            (product_c(i), [run.remote(sides.at[i, 1 - x], made_x.at[i], partner_seq(2))]),
            (product_x(i), []),
        ]))

    def norms_start():
        totals[2:4] = more_ref[...]
        turned = totals[...].T.astype(low)
        norms[...] = turned.reshape(norms.shape)

    def norms_add(total, kept, got):
        def go():
            total[...] = (wide(kept()) + wide(got[...])).astype(low)
        return go

    def norms_end():
        total = wide(norms_sy[dp])
        for n in range(len(plan.masks)):
            total = total + wide(norms_z[n])
        dn_ref[...] = total

    end = max(start + 2 * (len(stages) - 1) for start, stages in pieces if len(stages) == 4) + 1
    pieces.append((end, [
        (norms_start, [run.remote(norms.at[:, :, :, 1 - c], norms_c, partner_seq(1))]),
        (norms_add(norms_sc, lambda: norms[:, :, :, c], norms_c), [run.remote(norms_sc.at[:, :, 1 - x], norms_x, partner_seq(2))]),
        (norms_add(norms_sx, lambda: norms_sc[:, :, x], norms_x), [run.remote(norms_sx.at[:, 1 - y], norms_y, partner_seq(4))]),
        (norms_add(norms_sy, lambda: norms_sx[:, y], norms_y), [
            run.remote(norms_sy.at[lax.bitwise_xor(dp, m)], norms_z.at[n], partner_dp(plan, m))
            for n, m in enumerate(plan.masks)]),
        (norms_end, []),
    ]))
    run.run(pieces, 2)


def finish(plan, grads, turned, weights, inputs, grad_first, gain, more, collective_id):
    _, columns, width = inputs.shape
    quarter = weights.shape[2]
    n_dp, masks = plan.n_dp, len(plan.masks)
    rows = width // (8 * n_dp)
    parts = 4
    size = columns // parts
    low = jnp.bfloat16
    hbm = pl.BlockSpec(memory_space=pl.ANY)
    vmem = pl.BlockSpec(memory_space=pltpu.VMEM)
    copies = 3 * (3 + masks) + 3 * parts + 3 + masks
    return pl.pallas_call(
        functools.partial(finish_kernel, plan, parts),
        out_shape=[
            jax.ShapeDtypeStruct(inputs.shape, jnp.float32),
            jax.ShapeDtypeStruct((3, rows, width), jnp.float32),
            jax.ShapeDtypeStruct((rows, 128), jnp.float32),
        ],
        in_specs=[hbm] * 5 + [vmem] * 2,
        out_specs=[vmem] * 3,
        scratch_shapes=[
            pltpu.VMEM(grads.shape, low),
            pltpu.VMEM(turned.shape, low),
            pltpu.VMEM(weights.shape, low),
            pltpu.VMEM(inputs.shape, jnp.float32),
            pltpu.VMEM(inputs.shape, jnp.float32),
            pltpu.VMEM((3, n_dp, 2, 2, 2, rows, quarter), low),
            pltpu.VMEM((3, n_dp, 2, 2, rows, quarter), low),
            pltpu.VMEM((3, n_dp, 2, 2, rows, quarter), low),
            pltpu.VMEM((3, masks, 2, 2, rows, quarter), low),
            pltpu.VMEM((3, 2, 2, rows, quarter), low),
            pltpu.VMEM((3, 2, rows, 2 * quarter), low),
            pltpu.VMEM((3, rows, 2 * quarter), low),
            pltpu.VMEM((parts, 2, 2, 2, size, width), low),
            pltpu.VMEM((parts, 2, 2, size, width), low),
            pltpu.VMEM((parts, 2, 2, size, width), low),
            pltpu.VMEM((parts, 2, size, width), low),
            pltpu.VMEM((parts, 2, size, width), low),
            pltpu.VMEM((parts, size, width), low),
            pltpu.VMEM((128, width), jnp.float32),
            pltpu.VMEM((n_dp, 2, 2, 2, rows, 128), low),
            pltpu.VMEM((n_dp, 2, 2, rows, 128), low),
            pltpu.VMEM((n_dp, 2, 2, rows, 128), low),
            pltpu.VMEM((n_dp, 2, rows, 128), low),
            pltpu.VMEM((n_dp, 2, rows, 128), low),
            pltpu.VMEM((n_dp, rows, 128), low),
            pltpu.VMEM((n_dp, rows, 128), low),
            pltpu.VMEM((masks, rows, 128), low),
            pltpu.SemaphoreType.DMA((copies,)),
            pltpu.SemaphoreType.DMA((copies,)),
            pltpu.SemaphoreType.DMA((5,)),
        ],
        compiler_params=pltpu.CompilerParams(
            collective_id=collective_id, has_side_effects=True, vmem_limit_bytes=62 << 20),
    )(grads, turned, weights, inputs, grad_first, gain, more)


class Gather:
    def __init__(self, plan, lag, shard, rows, cols):
        self.plan, self.lag, self.rows, self.cols = plan, lag, rows, cols
        self.across = shard.shape[1] // cols
        self.pieces = shard.shape[0] // rows * self.across
        self.ticks = self.pieces + lag * (plan.hops + 1)
        self.out_shape = jax.ShapeDtypeStruct(plan.lead() + shard.shape, shard.dtype)
        each = 2 * (len(plan.masks) + plan.hops)
        self.scratch = [
            pltpu.VMEM(shard.shape, shard.dtype),
            pltpu.SemaphoreType.DMA((2 * lag, each)),
            pltpu.SemaphoreType.DMA((2 * lag, each)),
            pltpu.SemaphoreType.DMA((2,)),
        ]

    def copies(self, stage, u, full, held, send, recv):
        plan = self.plan
        dp, _ = place()
        me = tuple(own_bit(b) for b in plan.bits)
        slot = lax.rem(u, 2 * self.lag)
        rows = pl.ds(pl.multiple_of(lax.div(u, self.across) * self.rows, 16), self.rows)
        out = []
        for h in range(2):
            start = lax.rem(u, self.across) * self.cols + h * (self.cols // 2)
            cols = pl.ds(pl.multiple_of(start, 128), self.cols // 2)
            base = h * (len(plan.masks) + plan.hops)
            if stage == 0:
                for n, mask in enumerate(plan.masks):
                    out.append(pltpu.make_async_remote_copy(
                        held.at[rows, cols], full.at[(dp,) + me + (rows, cols)],
                        send.at[slot, base + n], recv.at[slot, base + n],
                        device_id=partner_dp(plan, mask), device_id_type=MESH))
            else:
                order = plan.orders[h]
                where = tuple(slice(None) if b in order[: stage - 1] else m for b, m in zip(plan.bits, me))
                part = full.at[(slice(None),) + where + (rows, cols)]
                at = base + len(plan.masks) + stage - 1
                out.append(pltpu.make_async_remote_copy(
                    part, part, send.at[slot, at], recv.at[slot, at],
                    device_id=partner_seq(order[stage - 1]), device_id_type=MESH))
        return out

    def run(self, tick, shard, full, held, send, recv, local):
        plan, lag = self.plan, self.lag
        dp, _ = place()
        me = tuple(own_bit(b) for b in plan.bits)
        own = pltpu.make_async_copy(held, full.at[(dp,) + me], local.at[0])

        @pl.when(tick == 0)
        def _():
            load = pltpu.make_async_copy(shard, held, local.at[1])
            load.start()
            load.wait()
            own.start()

        @pl.when(tick == lag)
        def _():
            own.wait()

        stages = plan.hops + 1
        for stage in reversed(range(stages + 1)):
            u = tick - lag * stage

            @pl.when((u >= 0) & (u < self.pieces))
            def _(stage=stage, u=u):
                if stage > 0:
                    for copy in self.copies(stage - 1, u, full, held, send, recv):
                        copy.wait()
                if stage < stages:
                    for copy in self.copies(stage, u, full, held, send, recv):
                        copy.start()


def attend_step(block, parts, pair, step, packed, col_ref, row_ref, o_ref, ot_ref, lse_ref, vt_ref):
    @pl.when(step == 0)
    def _():
        vt_ref[...] = packed[:, pair, 2].reshape(-1, HEAD_DIM).T

    query = packed[pl.ds(step * parts, parts), pair, 0].reshape(block, HEAD_DIM)
    query_row = row_ref[pl.ds(step, 1), :]
    unit = LOG2E / math.sqrt(HEAD_DIM)

    def visit(j, carry, diagonal):
        top, total, mixed = carry
        key = packed[pl.ds(j * parts, parts), pair, 1].reshape(block, HEAD_DIM)
        at = pl.multiple_of(j * block, block)
        scores = dot(key, query, NT) * unit
        scores = jnp.where(allowed_pairs(col_ref[pl.ds(at, block), :], query_row, diagonal), scores, MASKED)
        above = jnp.maximum(top, jnp.max(scores, axis=0, keepdims=True))
        expo = jnp.exp2(scores - above)
        fade = jnp.exp2(top - above)
        total = total * fade + jnp.sum(expo, axis=0, keepdims=True)
        mixed = mixed * fade + dot(vt_ref[:, pl.ds(at, block)], expo.astype(jnp.bfloat16))
        return above, total, mixed

    start = (
        jnp.full((1, block), MASKED, jnp.float32),
        jnp.zeros((1, block), jnp.float32),
        jnp.zeros((HEAD_DIM, block), jnp.float32),
    )
    carry = lax.fori_loop(0, step, lambda j, c: visit(j, c, False), start)
    top, total, mixed = visit(step, carry, True)
    mixed = mixed / total
    ot_ref[0, 0] = mixed
    lse_ref[0, pl.ds(step, 1), :] = top + jnp.log2(total)
    o_ref[...] = mixed.T.astype(jnp.bfloat16).reshape(o_ref.shape)


def attention_kernel(
    plan, gather, block, first, x_ref, w_ref, cos_ref, sin_ref, col_ref, row_ref, shard,
    packed, turned_ref, o_ref, ot_ref, lse_ref, full, vt_ref, *more,
):
    tick = pl.program_id(0)

    @pl.when(tick == 0)
    def _():
        greet(plan)

    gather.run(tick, shard, full, *more)
    parts, columns, width = x_ref.shape
    heads = packed.shape[1]

    @pl.when(tick < first)
    def _():
        acts = x_ref[...].reshape(block, width)
        for kind in range(3):
            made = dot(acts, w_ref[kind])
            for p in range(heads):
                head = made[:, p * HEAD_DIM : (p + 1) * HEAD_DIM]
                if kind < 2:
                    head = head * cos_ref[...] + pltpu.roll(head, HEAD_DIM // 2, 1) * sin_ref[...]
                packed[pl.ds(tick * parts, parts), p, kind] = head.astype(jnp.bfloat16).reshape(parts, columns, HEAD_DIM)
        turned_ref[...] = acts.T

    @pl.when((tick >= first) & (tick < first * (1 + heads)))
    def _():
        pair, step = lax.div(tick - first, first), lax.rem(tick - first, first)
        attend_step(block, parts, pair, step, packed, col_ref, row_ref, o_ref, ot_ref, lse_ref, vt_ref)


def attention(plan, acts, weights, cosine, sine, seg_col, seg_row, shard, lag, collective_id):
    owners, columns, width = acts.shape
    heads = weights.shape[2] // HEAD_DIM
    steps, block = seg_row.shape
    parts, length = block // columns, owners * columns
    gather = Gather(plan, lag, shard, shard.shape[0], 512)
    low = jnp.bfloat16

    def at(t):
        return jnp.clip(t, 0, steps - 1)

    def pair(t):
        return lax.div(jnp.clip(t - steps, 0, steps * heads - 1), steps)

    def step(t):
        return lax.rem(jnp.clip(t - steps, 0, steps * heads - 1), steps)

    def fixed(shape):
        return pl.BlockSpec(shape, lambda t: (0,) * len(shape))

    hbm = pl.BlockSpec(memory_space=pl.ANY)
    table = pl.BlockSpec((block, HEAD_DIM), lambda t: (at(t), 0))
    packed_shape = (owners, heads, 3, columns, HEAD_DIM)
    return pl.pallas_call(
        functools.partial(attention_kernel, plan, gather, block, steps),
        grid=(max(gather.ticks, steps * (1 + heads)),),
        in_specs=[
            pl.BlockSpec((parts, columns, width), lambda t: (at(t), 0, 0)),
            fixed(weights.shape),
            table,
            table,
            fixed((length, 1)),
            fixed((steps, block)),
            hbm,
        ],
        out_specs=[
            fixed(packed_shape),
            pl.BlockSpec((width, block), lambda t: (0, at(t))),
            pl.BlockSpec((parts, None, columns, HEAD_DIM), lambda t: (step(t), pair(t), 0, 0)),
            pl.BlockSpec((1, 1, HEAD_DIM, block), lambda t: (pair(t), step(t), 0, 0)),
            pl.BlockSpec((1, steps, block), lambda t: (pair(t), 0, 0)),
            hbm,
        ],
        out_shape=[
            jax.ShapeDtypeStruct(packed_shape, low),
            jax.ShapeDtypeStruct((width, length), low),
            jax.ShapeDtypeStruct((owners, heads, columns, HEAD_DIM), low),
            jax.ShapeDtypeStruct((heads, steps, HEAD_DIM, block), jnp.float32),
            jax.ShapeDtypeStruct((heads, steps, block), jnp.float32),
            gather.out_shape,
        ],
        scratch_shapes=[pltpu.VMEM((HEAD_DIM, length), low)] + gather.scratch,
        compiler_params=pltpu.CompilerParams(
            collective_id=collective_id, has_side_effects=True, vmem_limit_bytes=56 << 20),
    )(acts, weights, cosine, sine, seg_col, seg_row, shard)


class Mlp:
    def __init__(self, plan, lag, mixed, w_out, inputs, gain, offset, w_up, grad, cotangent, shard):
        tokens, width = inputs.shape
        hidden = w_up.shape[1]
        self.plan, self.lag = plan, lag
        self.blocks = 2 * plan.n_dp
        self.block = hidden // self.blocks
        self.rows = width // (plan.n_dp * plan.n_seq)
        self.gather = Gather(plan, lag, shard, self.rows, 512)
        self.meet = 4
        self.up = self.meet + 1
        self.back = max(self.gather.ticks, self.up + self.blocks)
        self.norm = self.back + self.blocks
        self.ticks = self.norm + 5
        self.operands = (mixed, w_out, inputs, gain, offset, w_up, grad, cotangent, shard)
        blocks, back, up = self.blocks, self.back, self.up

        def up_block(t):
            later = jnp.clip(t - (up + blocks) + 1, 0, 1)
            return (0, jnp.clip(t - up, 0, blocks - 1) * (1 - later) + jnp.clip(t - back, 0, blocks - 1) * later)

        once = pl.BlockSpec((tokens, width), lambda t: (0, 0), pipeline_mode=pl.Buffered(1))
        row = pl.BlockSpec((1, width), lambda t: (0, 0))
        hbm = pl.BlockSpec(memory_space=pl.ANY)
        self.in_specs = [hbm, hbm, hbm, row, row, pl.BlockSpec((width, self.block), up_block), once, hbm, hbm]
        self.out_specs = [
            hbm,
            hbm,
            hbm,
            hbm,
            hbm,
            hbm,
            pl.BlockSpec((tokens, self.block), lambda t: (0, jnp.clip(t - back, 0, blocks - 1))),
            hbm,
            pl.BlockSpec((8, width), lambda t: (0, 0)),
            hbm,
        ]
        low = jnp.bfloat16
        flat = jax.ShapeDtypeStruct((tokens, width), jnp.float32)
        self.out_shapes = [
            flat,
            flat,
            flat,
            jax.ShapeDtypeStruct((tokens, width), low),
            jax.ShapeDtypeStruct((width, tokens), low),
            jax.ShapeDtypeStruct((width, tokens), low),
            jax.ShapeDtypeStruct((tokens, hidden), low),
            jax.ShapeDtypeStruct(mixed.shape, low),
            jax.ShapeDtypeStruct((8, width), jnp.float32),
            self.gather.out_shape,
        ]
        self.chunk = 64
        self.scratch = [
            pltpu.VMEM((tokens, hidden), low),
            pltpu.VMEM((hidden, tokens), low),
            pltpu.VMEM((tokens, hidden), low),
            pltpu.VMEM((2, 2, 2) + shard.shape, low),
            pltpu.VMEM((tokens, width), jnp.float32),
            pltpu.VMEM((tokens, width), jnp.float32),
            pltpu.VMEM((tokens, width), low),
            pltpu.VMEM(mixed.shape, low),
            pltpu.VMEM((2, 2, self.chunk, width), jnp.float32),
            pltpu.SemaphoreType.DMA((2, 2, plan.n_seq)),
            pltpu.SemaphoreType.DMA((16,)),
            pltpu.SemaphoreType.DMA((2, 2)),
            pltpu.SemaphoreType.DMA((2,)),
        ] + self.gather.scratch

    everyone = True

    def left(self, refs, which, z):
        turned, n = refs[20], self.plan.n_seq
        every = turned.shape[0] // (n * self.plan.n_dp)
        return jnp.concatenate(
            [
                turned[pl.ds(pl.multiple_of((z * n + d) * every + which * self.rows, 16), self.rows), :]
                for d in range(n)
            ],
            axis=0,
        )

    def run(self, tick, refs):
        mixed_hbm, w_out, inputs, gain_ref, offset_ref, up_ref, grad_ref, cotangent, shard = refs[:9]
        output, first_sum, grad_first, grad_low, mixed_turned, acts_turned, gu_ref, back_pairs, sums_ref, full = refs[9:19]
        hidden_ref, turned_ref, slope_ref, down_ref, out_ref, back_ref, acts_ref, pairs, chunks = refs[19:28]
        swaps, local, loads, fetch = refs[28:32]
        plan, block = self.plan, self.block
        dp, seq = place()
        count, heads, columns, _ = pairs.shape
        tokens, width = acts_ref.shape
        low = jnp.bfloat16
        third = 512
        thirds = width // third
        self.gather.run(tick, shard, full, *refs[32:])

        def exchange(which, src, dst):
            return [
                pltpu.make_async_remote_copy(
                    src.at[lax.bitwise_xor(seq, m)], dst.at[seq], swaps.at[which, 0, m], swaps.at[which, 1, m],
                    device_id=partner_seq(m), device_id_type=MESH)
                for m in range(1, count)
            ]

        there = exchange(0, mixed_hbm, pairs)
        here = pltpu.make_async_copy(mixed_hbm.at[seq], pairs.at[seq], local.at[0])
        based = pltpu.make_async_copy(inputs, out_ref, local.at[1])
        outs = [
            pltpu.make_async_copy(
                w_out.at[:, pl.ds(n * third, third)], turned_ref.at[pl.ds(n * width, width), :], local.at[2 + n])
            for n in range(thirds)
        ]
        kept = pltpu.make_async_copy(out_ref, first_sum, local.at[5])
        turns = []
        for n in range(thirds):
            rows = pl.ds(n * third, third)
            base = slope_ref.shape[1] - 2 * width + n * third
            turns.append(pltpu.make_async_copy(slope_ref.at[:, pl.ds(base, third)], mixed_turned.at[rows, :], local.at[6 + n]))
            turns.append(pltpu.make_async_copy(
                slope_ref.at[:, pl.ds(base + width, third)], acts_turned.at[rows, :], local.at[9 + n]))

        @pl.when(tick == 0)
        def _():
            for copy in there + [here, based] + outs:
                copy.start()

        @pl.when(tick == self.meet)
        def _():
            for copy in there + [here, based] + outs:
                copy.wait()
            per = width // (heads * HEAD_DIM)
            for s in range(count // per):
                for g in range(per):
                    for p in range(heads):
                        at = (g * heads + p) * HEAD_DIM
                        acts_ref[s * columns : (s + 1) * columns, at : at + HEAD_DIM] = pairs[s * per + g, p]
            for n in range(thirds):
                part = slice(n * third, (n + 1) * third)
                out_ref[:, part] += dot(acts_ref[...], turned_ref[n * width : (n + 1) * width, :])
                base = slope_ref.shape[1] - 2 * width + n * third
                slope_ref[:, base : base + third] = acts_ref[:, part].T
            kept.start()

            def norm(i, carry):
                rows = pl.ds(pl.multiple_of(i * self.chunk, self.chunk), self.chunk)
                values = out_ref[rows, :]
                centre = values - jnp.mean(values, axis=-1, keepdims=True)
                spread = lax.rsqrt(jnp.mean(centre * centre, axis=-1, keepdims=True) + EPSILON)
                acts_ref[rows, :] = (centre * spread * gain_ref[...] + offset_ref[...]).astype(low)
                return carry

            lax.fori_loop(0, tokens // self.chunk, norm, 0)
            for n in range(thirds):
                base = slope_ref.shape[1] - width + n * third
                slope_ref[:, base : base + third] = acts_ref[:, n * third : (n + 1) * third].T
            for copy in turns:
                copy.start()

        @pl.when(tick == self.up + 2)
        def _():
            for copy in turns + [kept]:
                copy.wait()

        def block_at(i):
            return pl.ds(pl.multiple_of(i * block, 128), block)

        @pl.when((tick >= self.up) & (tick < self.up + self.blocks))
        def _():
            step = 256
            for n in range(block // step):
                upper = dot(acts_ref[...], up_ref[:, n * step : (n + 1) * step])
                share = 0.5 + 0.5 * lax.erf(upper * (1.0 / math.sqrt(2.0)))
                density = jnp.exp(upper * upper * -0.5) * (1.0 / math.sqrt(2.0 * math.pi))
                made = (upper * share).astype(low)
                at = pl.multiple_of((tick - self.up) * block + n * step, 128)
                hidden_ref[:, pl.ds(at, step)] = made
                turned_ref[pl.ds(at, step), :] = made.T
                slope_ref[:, pl.ds(at, step)] = (share + upper * density).astype(low)

        def fetched(i):
            z, y = lax.div(i, 2), lax.rem(i, 2)
            return pltpu.make_async_copy(full.at[z, y], down_ref.at[y], fetch.at[y])

        i = tick - self.back

        @pl.when((i >= -1) & (i < self.blocks - 1))
        def _():
            fetched(i + 1).start()

        @pl.when((i >= 0) & (i < self.blocks))
        def _():
            fetched(i).wait()
            down = down_ref[lax.rem(i, 2)].reshape(block, -1)

            @pl.when(i == 0)
            def _():
                back_ref[...] = jnp.zeros_like(back_ref)

            grad = dot(grad_ref[...], down, NT) * slope_ref[:, block_at(i)].astype(jnp.float32)
            gu_ref[...] = grad.astype(low)
            for n in range(thirds):
                part = slice(n * third, (n + 1) * third)
                out_ref[:, part] += dot(hidden_ref[:, block_at(i)], down[:, part])
                back_ref[:, part] += dot(gu_ref[...], up_ref[part, :], NT)

        done = pltpu.make_async_copy(out_ref, output, local.at[12])
        first_out = pltpu.make_async_copy(back_ref, grad_first, local.at[13])
        low_out = pltpu.make_async_copy(acts_ref, grad_low, local.at[14])
        chunk = self.chunk

        def chunk_loads(j, slot):
            rows = pl.ds(pl.multiple_of(j * chunk, chunk), chunk)
            return [
                pltpu.make_async_copy(src.at[rows, :], chunks.at[slot, n], loads.at[slot, n])
                for n, src in enumerate((first_sum, cotangent))
            ]

        @pl.when(tick == self.norm - 1)
        def _():
            for copy in outs:
                copy.start()

        @pl.when(tick == self.norm)
        def _():
            done.start()
            sums_ref[...] = jnp.zeros_like(sums_ref)
            for copy in chunk_loads(0, 0):
                copy.start()
            total = tokens // chunk

            def norm_back(j, carry):
                slot = lax.rem(j, 2)

                @pl.when(j + 1 < total)
                def _():
                    for copy in chunk_loads(j + 1, 1 - slot):
                        copy.start()

                for copy in chunk_loads(j, slot):
                    copy.wait()
                rows = pl.ds(pl.multiple_of(j * chunk, chunk), chunk)
                values = chunks[slot, 0]
                centre = values - jnp.mean(values, axis=-1, keepdims=True)
                spread = lax.rsqrt(jnp.mean(centre * centre, axis=-1, keepdims=True) + EPSILON)
                normed = centre * spread
                grad = back_ref[rows, :]
                grown = grad * gain_ref[...]
                mean_one = jnp.mean(grown, axis=-1, keepdims=True)
                mean_two = jnp.mean(grown * normed, axis=-1, keepdims=True)
                made = chunks[slot, 1] + (grown - mean_one - normed * mean_two) * spread
                sums_ref[0:1] += jnp.sum(grad * normed, axis=0, keepdims=True)
                sums_ref[1:2] += jnp.sum(grad, axis=0, keepdims=True)
                back_ref[rows, :] = made
                acts_ref[rows, :] = made.astype(low)
                return carry

            lax.fori_loop(0, total, norm_back, 0)
            first_out.start()
            low_out.start()

        again = exchange(1, pairs, back_pairs)
        home = pltpu.make_async_copy(pairs.at[seq], back_pairs.at[seq], local.at[0])

        @pl.when(tick == self.norm + 1)
        def _():
            for copy in outs:
                copy.wait()
            per = width // (heads * HEAD_DIM)
            step = heads * HEAD_DIM
            for g in range(per):
                made = sum(
                    dot(acts_ref[:, n * third : (n + 1) * third],
                        turned_ref[n * width + g * step : n * width + (g + 1) * step, :], NT)
                    for n in range(thirds)
                ).astype(low)
                for s in range(count // per):
                    for p in range(heads):
                        pairs[s * per + g, p] = made[s * columns : (s + 1) * columns, p * HEAD_DIM : (p + 1) * HEAD_DIM]
            for copy in again + [home]:
                copy.start()

        @pl.when(tick == self.ticks - 1)
        def _():
            for copy in again + [home, done, first_out, low_out]:
                copy.wait()


def layer_norm(values, gain, offset):
    centre = values - jnp.mean(values, axis=-1, keepdims=True)
    spread = jnp.mean(centre * centre, axis=-1, keepdims=True)
    return centre * lax.rsqrt(spread + EPSILON) * gain + offset


def gelu(values):
    return 0.5 * values * (1.0 + lax.erf(values * (1.0 / math.sqrt(2.0))))


def angles(positions):
    half = HEAD_DIM // 2
    rates = jnp.exp(jnp.arange(half, dtype=jnp.float32) * (-math.log(10000.0) / half))
    turned = positions.astype(jnp.float32)[:, None] * rates[None, :]
    return (jnp.cos(turned)[:, None, :], jnp.sin(turned)[:, None, :])


def rotary(values, cosine, sine):
    half = values.shape[-1] // 2
    first = values[..., :half]
    second = values[..., half:]
    return jnp.concatenate(
        [first * cosine - second * sine, second * cosine + first * sine], axis=-1
    )


def lower(values):
    return values.astype(jnp.bfloat16)


def project(acts, weight):
    return jnp.einsum("gcd,de->gce", acts, weight, preferred_element_type=jnp.float32)


def project_back(grads, weight):
    return jnp.einsum("gce,de->gcd", grads, weight, preferred_element_type=jnp.float32)


def outer_sum(left, right):
    return jnp.einsum("gci,gcj->ij", left, right, preferred_element_type=jnp.float32)


def plain_shards(
    inputs,
    segments,
    norm1_gain,
    norm1_bias,
    w_query,
    w_key,
    w_value,
    w_out,
    norm2_gain,
    norm2_bias,
    w_up,
    w_down,
    cotangent,
):
    groups, columns, width = inputs.shape
    heads_count = width // HEAD_DIM
    scale = 1.0 / math.sqrt(HEAD_DIM)
    full_query, full_key, full_value, full_out, full_up, full_down = (
        lax.all_gather(w_query, ("dp", "seq"), axis=0, tiled=True),
        lax.all_gather(w_key, ("dp", "seq"), axis=0, tiled=True),
        lax.all_gather(w_value, ("dp", "seq"), axis=0, tiled=True),
        lax.all_gather(w_out, ("dp", "seq"), axis=0, tiled=True),
        lax.all_gather(w_up, ("dp", "seq"), axis=0, tiled=True),
        lax.all_gather(w_down, ("dp", "seq"), axis=0, tiled=True),
    )
    key_ids = lax.all_gather(segments, "seq", axis=1, tiled=True)
    length = key_ids.shape[1]
    rank = lax.axis_index("seq")
    places = rank * columns + jnp.arange(columns, dtype=jnp.int32)
    key_places = jnp.arange(length, dtype=jnp.int32)
    cosine, sine = angles(places)

    def turn(values):
        shaped = values.reshape(groups, columns, heads_count, HEAD_DIM)
        return rotary(shaped, cosine, sine).reshape(groups, columns, width)

    def permitted(segment_row, key_row):
        same = segment_row[:, None] == key_row[None, :]
        causal = key_places[None, :] <= places[:, None]
        live = (key_row[None, :] >= 0) | (key_places[None, :] == places[:, None])
        return same & causal & live

    def scores_of(query_row, key_block, segment_row, key_row):
        heads_query = query_row.reshape(columns, heads_count, HEAD_DIM)
        heads_key = key_block.reshape(length, heads_count, HEAD_DIM)
        raw = (
            jnp.einsum("chd,lhd->hcl", heads_query, heads_key, preferred_element_type=jnp.float32)
            * scale
        )
        return jnp.where(permitted(segment_row, key_row)[None], raw, MASKED)

    normed_one = layer_norm(inputs, norm1_gain, norm1_bias)
    act_one = lower(normed_one)
    query_zero = project(act_one, full_query)
    key_zero = project(act_one, full_key)
    value_low = lower(project(act_one, full_value))
    query_low = lower(turn(query_zero))
    key_low = lower(turn(key_zero))
    keys_all, values_all = (
        lax.all_gather(key_low, "seq", axis=1, tiled=True),
        lax.all_gather(value_low, "seq", axis=1, tiled=True),
    )

    def attend(items):
        query_row, key_block, value_block, segment_row, key_row = items
        scores = scores_of(query_row, key_block, segment_row, key_row)
        top = jnp.max(scores, axis=-1, keepdims=True)
        expo = jnp.exp(scores - top)
        total = jnp.sum(expo, axis=-1, keepdims=True)
        probs = lower(expo / total)
        heads_value = value_block.reshape(length, heads_count, HEAD_DIM)
        mixed = jnp.einsum("hcl,lhd->chd", probs, heads_value, preferred_element_type=jnp.float32)
        return (mixed.reshape(columns, width), top[..., 0] + jnp.log(total[..., 0]))

    mixed_all, log_totals = lax.map(attend, (query_low, keys_all, values_all, segments, key_ids))
    mixed_low = lower(mixed_all)
    first_sum = inputs + project(mixed_low, full_out)
    act_two = lower(layer_norm(first_sum, norm2_gain, norm2_bias))
    upper = project(act_two, full_up)
    hidden_low = lower(gelu(upper))
    output = first_sum + project(hidden_low, full_down)
    half_width = width // 2
    half_hidden = full_up.shape[1] // 2
    grad_out_low = lower(cotangent)
    down_left = outer_sum(hidden_low, grad_out_low[..., :half_width])
    down_right = outer_sum(hidden_low, grad_out_low[..., half_width:])
    grad_hidden = project_back(grad_out_low, full_down)
    gelu_values, gelu_back = jax.vjp(gelu, upper)
    grad_upper = lower(gelu_back(grad_hidden)[0])
    up_left = outer_sum(act_two, grad_upper[..., :half_hidden])
    up_right = outer_sum(act_two, grad_upper[..., half_hidden:])
    grad_act_two = project_back(grad_upper, full_up)
    normed_two, norm_two_back = jax.vjp(layer_norm, first_sum, norm2_gain, norm2_bias)
    grad_first_norm, gain_two_grad, offset_two_grad = norm_two_back(grad_act_two)
    grad_first = cotangent + grad_first_norm
    grad_attn_low = lower(grad_first)
    out_grad = outer_sum(mixed_low, grad_attn_low)
    grad_mixed = lower(project_back(grad_attn_low, full_out))
    heads_mixed = mixed_all.reshape(groups, columns, heads_count, HEAD_DIM)
    heads_gm = grad_mixed.astype(jnp.float32).reshape(groups, columns, heads_count, HEAD_DIM)
    deltas = jnp.transpose(jnp.sum(heads_mixed * heads_gm, axis=-1), (0, 2, 1))
    key_source, value_source = (key_low, value_low)

    def attend_back(carry, items):
        query_row, grad_row, log_row, delta_row, segment_row, key_row, key_part, value_part = items
        queries_all, grads_all = (
            lax.all_gather(query_row, "seq", axis=0, tiled=True),
            lax.all_gather(grad_row, "seq", axis=0, tiled=True),
        )
        logs_all, deltas_all = (
            lax.all_gather(log_row, "seq", axis=1, tiled=True),
            lax.all_gather(delta_row, "seq", axis=1, tiled=True),
        )
        own_mask = (segment_row[None, :] == key_row[:, None]) & (
            places[None, :] <= key_places[:, None]
        )
        own_mask = own_mask & (
            (segment_row[None, :] >= 0) | (places[None, :] == key_places[:, None])
        )
        heads_query = queries_all.reshape(length, heads_count, HEAD_DIM)
        heads_grad = grads_all.reshape(length, heads_count, HEAD_DIM)
        heads_key = key_part.reshape(columns, heads_count, HEAD_DIM)
        heads_value = value_part.reshape(columns, heads_count, HEAD_DIM)
        raw = (
            jnp.einsum("lhd,chd->hlc", heads_query, heads_key, preferred_element_type=jnp.float32)
            * scale
        )
        scores = jnp.where(own_mask[None], raw, MASKED)
        probs = jnp.exp(scores - logs_all[..., None])
        grad_probs = jnp.einsum(
            "lhd,chd->hlc", heads_grad, heads_value, preferred_element_type=jnp.float32
        )
        grad_scores = lower(probs * (grad_probs - deltas_all[..., None]))
        grad_values = jnp.einsum(
            "hlc,lhd->chd", lower(probs), heads_grad, preferred_element_type=jnp.float32
        )
        grad_keys = (
            jnp.einsum("hlc,lhd->chd", grad_scores, heads_query, preferred_element_type=jnp.float32)
            * scale
        )
        partial_query = (
            jnp.einsum("hlc,chd->lhd", grad_scores, heads_key, preferred_element_type=jnp.float32)
            * scale
        )
        grad_query = lax.psum_scatter(
            partial_query.reshape(length, width).astype(jnp.bfloat16),
            "seq",
            scatter_dimension=0,
            tiled=True,
        ).astype(jnp.float32)
        return (
            carry,
            (grad_query, grad_keys.reshape(columns, width), grad_values.reshape(columns, width)),
        )

    start_carry = jnp.zeros((), jnp.float32)
    end_carry, grads_seq = lax.scan(
        attend_back,
        start_carry,
        (query_low, grad_mixed, log_totals, deltas, segments, key_ids, key_source, value_source),
    )
    grad_query_all, grad_key_all, grad_value_all = grads_seq
    turned_query, turn_back = jax.vjp(turn, query_zero)
    grad_query_low = lower(turn_back(grad_query_all)[0])
    grad_key_low = lower(turn_back(grad_key_all)[0])
    grad_value_low = lower(grad_value_all)
    query_grad = outer_sum(act_one, grad_query_low)
    key_grad = outer_sum(act_one, grad_key_low)
    value_grad = outer_sum(act_one, grad_value_low)
    grad_act_one = project_back(grad_query_low, full_query) + project_back(grad_key_low, full_key)
    grad_act_one = grad_act_one + project_back(grad_value_low, full_value)
    normed_again, norm_one_back = jax.vjp(layer_norm, inputs, norm1_gain, norm1_bias)
    grad_input_norm, gain_one_grad, offset_one_grad = norm_one_back(grad_act_one)
    grad_input = grad_first + grad_input_norm
    summed = (
        lax.psum_scatter(query_grad, ("dp", "seq"), scatter_dimension=0, tiled=True),
        lax.psum_scatter(key_grad, ("dp", "seq"), scatter_dimension=0, tiled=True),
        lax.psum_scatter(value_grad, ("dp", "seq"), scatter_dimension=0, tiled=True),
        lax.psum_scatter(out_grad, ("dp", "seq"), scatter_dimension=0, tiled=True),
        lax.psum_scatter(up_left, ("dp", "seq"), scatter_dimension=0, tiled=True),
        lax.psum_scatter(up_right, ("dp", "seq"), scatter_dimension=0, tiled=True),
        lax.psum_scatter(down_left, ("dp", "seq"), scatter_dimension=0, tiled=True),
        lax.psum_scatter(down_right, ("dp", "seq"), scatter_dimension=0, tiled=True),
        lax.psum_scatter(gain_one_grad, ("dp", "seq"), scatter_dimension=0, tiled=True),
        lax.psum_scatter(offset_one_grad, ("dp", "seq"), scatter_dimension=0, tiled=True),
        lax.psum_scatter(gain_two_grad, ("dp", "seq"), scatter_dimension=0, tiled=True),
        lax.psum_scatter(offset_two_grad, ("dp", "seq"), scatter_dimension=0, tiled=True),
    )
    query_grad, key_grad, value_grad, out_grad = (summed[0], summed[1], summed[2], summed[3])
    up_left, up_right, down_left, down_right = (summed[4], summed[5], summed[6], summed[7])
    gain_one_grad, offset_one_grad, gain_two_grad, offset_two_grad = (
        summed[8],
        summed[9],
        summed[10],
        summed[11],
    )
    up_grad = jnp.concatenate([up_left, up_right], axis=1)
    down_grad = jnp.concatenate([down_left, down_right], axis=1)
    return (
        output,
        grad_input,
        gain_one_grad,
        offset_one_grad,
        query_grad,
        key_grad,
        value_grad,
        out_grad,
        gain_two_grad,
        offset_two_grad,
        up_grad,
        down_grad,
    )


def shards(
    inputs,
    segments,
    norm1_gain,
    norm1_bias,
    w_query,
    w_key,
    w_value,
    w_out,
    norm2_gain,
    norm2_bias,
    w_up,
    w_down,
    cotangent,
    *,
    plan,
):
    groups, columns, width = inputs.shape
    length = columns * plan.n_seq
    block = min(512, length)
    lag, piece = 2, 512
    every = plan.n_dp * plan.n_seq

    half = HEAD_DIM // 2
    rates = np.exp(np.arange(half, dtype=np.float32) * np.float32(-math.log(10000.0) / half))
    angle = (np.arange(length, dtype=np.float32)[:, None] * rates[None, :]).astype(np.float32)
    cosine = jnp.asarray(np.concatenate([np.cos(angle), np.cos(angle)], axis=1), jnp.float32)
    sine = jnp.asarray(np.concatenate([-np.sin(angle), np.sin(angle)], axis=1), jnp.float32)

    def flat(values):
        return values.reshape(groups * columns, width)

    act_one = lower(layer_norm(inputs, norm1_gain, norm1_bias))
    tokens_one, ids, heads_weight, (full_out,) = start(
        plan, act_one, segments, (w_query, w_key, w_value), (w_out,), piece, lag, 1
    )
    seg_row = ids.reshape(length // block, block)
    seg_col = jnp.where(ids < 0, -2, ids)[:, None]
    packed, turned_one, mixed, mixed_t, lse, full_up = attention(
        plan, tokens_one, heads_weight, cosine, sine, seg_col, seg_row, w_up, lag, 2
    )
    grad_low = lower(flat(cotangent))
    mlp = Mlp(
        plan, lag, mixed, full_out, flat(inputs), norm2_gain[None], norm2_bias[None],
        full_up.reshape(width, -1), grad_low, flat(cotangent), w_down,
    )
    rows = width // every

    def reduce_all(pairs, collective_id, beside, first=0):
        out, *more = reduce_products(plan, pairs, rows, piece, lag, collective_id, beside, first)
        results, at = [], 0
        for left, right in pairs:
            blocks = left if isinstance(left, int) else left.shape[0]
            cols = right.shape[1] // piece
            part = out[at : at + blocks * cols].reshape(blocks, cols, -1, piece)
            results.append(jnp.transpose(part, (0, 2, 1, 3)).reshape(-1, right.shape[1]))
            at += blocks * cols
        return results + more

    (
        down_grad, output, _, grad_first, grad_first_low, mixed_turned, acts_turned, grad_upper, grad_pairs,
        sums_two, _,
    ) = reduce_all([(w_down.shape[0] // rows, grad_low)], 3, mlp, 14)
    work = AttendBack(2, packed, grad_pairs, mixed_t, lse, seg_col, seg_row, cosine, sine)
    up_grad, out_grad, grads = reduce_all(
        [(acts_turned[None], grad_upper), (mixed_turned[None], grad_first_low)], 4, work
    )
    grad_input, heads_grad, norm_rows = finish(
        plan, grads, turned_one, heads_weight, inputs, grad_first.reshape(inputs.shape), norm1_gain[None],
        sums_two[:2], 5,
    )
    return (
        output.reshape(inputs.shape),
        grad_input,
        norm_rows[:, 0],
        norm_rows[:, 1],
        heads_grad[0],
        heads_grad[1],
        heads_grad[2],
        out_grad,
        norm_rows[:, 2],
        norm_rows[:, 3],
        up_grad,
        down_grad,
    )


def fits(mesh, groups, columns, width, rows):
    return (
        mesh.shape["seq"] == 8
        and groups == 2
        and width % (4 * HEAD_DIM) == 0
        and columns == 256
        and rows % 16 == 0
    )


def solution(mesh):
    placed = (
        P("dp", "seq", None),
        P("dp", "seq"),
        P(),
        P(),
        P(("dp", "seq"), None),
        P(("dp", "seq"), None),
        P(("dp", "seq"), None),
        P(("dp", "seq"), None),
        P(),
        P(),
        P(("dp", "seq"), None),
        P(("dp", "seq"), None),
        P("dp", "seq", None),
    )
    plan = Plan(mesh)

    def layer(inputs, segments, *rest):
        groups, columns, width = inputs.shape
        if fits(mesh, groups, columns, width, rest[2].shape[0]):
            return shards(inputs, segments, *rest, plan=plan)
        return plain_shards(inputs, segments, *rest)

    return jax.shard_map(
        layer,
        mesh=mesh,
        in_specs=placed,
        out_specs=(
            P("dp", "seq", None),
            P("dp", "seq", None),
            P(("dp", "seq")),
            P(("dp", "seq")),
            P(("dp", "seq"), None),
            P(("dp", "seq"), None),
            P(("dp", "seq"), None),
            P(("dp", "seq"), None),
            P(("dp", "seq")),
            P(("dp", "seq")),
            P(("dp", "seq"), None),
            P(("dp", "seq"), None),
        ),
        check_vma=False,
    )
```

```python
import functools
import math

import jax
import jax.numpy as jnp
import numpy as np
from jax import lax
from jax.experimental import pallas as pl
from jax.experimental.pallas import tpu as pltpu
from jax.sharding import PartitionSpec as P

HEAD_DIM = 128


EPSILON = 1e-05
MASKED = -1e30
LOG2E = math.log2(math.e)
NT = (((1,), (1,)), ((), ()))
NN = (((1,), (0,)), ((), ()))


def dot(left, right, dims=NN):
    return lax.dot_general(left, right, dims, preferred_element_type=jnp.float32)


def allowed_pairs(key_col, query_row, diagonal):
    same = key_col == query_row
    if not diagonal:
        return same
    shape = (key_col.shape[0], query_row.shape[1])
    key_at = lax.broadcasted_iota(jnp.int32, shape, 0)
    query_at = lax.broadcasted_iota(jnp.int32, shape, 1)
    return (same & (key_at <= query_at)) | (key_at == query_at)


def attend_back_step(
    block, parts, pair, step, last, q_ref, k_ref, v_ref, g_ref, ot_ref, lse_ref, col_ref, row_ref, cos_ref, sin_ref,
    out_ref, kt_ref, dk_ref, dv_ref,
):
    scale = 1.0 / math.sqrt(HEAD_DIM)

    @pl.when(step == 0)
    def _():
        kt_ref[...] = k_ref[...].reshape(-1, HEAD_DIM).T
        dk_ref[...] = jnp.zeros_like(dk_ref)
        dv_ref[...] = jnp.zeros_like(dv_ref)

    query = q_ref[pl.ds(step * parts, parts)].reshape(block, HEAD_DIM)
    grad = g_ref[pl.ds(step * parts, parts)].reshape(block, HEAD_DIM)
    query_row = row_ref[pl.ds(step, 1), :]
    lse = lse_ref[0, pl.ds(step, 1), :]
    delta = jnp.sum(ot_ref[0, 0] * grad.astype(jnp.float32).T, axis=0, keepdims=True)
    unit = LOG2E * scale

    def visit(j, dqt, diagonal):
        at = pl.multiple_of(j * block, block)
        key = k_ref[pl.ds(j * parts, parts)].reshape(block, HEAD_DIM)
        value = v_ref[pl.ds(j * parts, parts)].reshape(block, HEAD_DIM)
        key_col = col_ref[pl.ds(at, block), :]
        scores = dot(key, query, NT) * unit - lse
        probs = jnp.where(allowed_pairs(key_col, query_row, diagonal), jnp.exp2(scores), 0.0)
        grad_probs = dot(value, grad, NT)
        grad_scores = (probs * (grad_probs - delta)).astype(jnp.bfloat16)
        dv_ref[pl.ds(at, block), :] += dot(probs.astype(jnp.bfloat16), grad)
        dk_ref[pl.ds(at, block), :] += dot(grad_scores, query)
        return dqt + dot(kt_ref[:, pl.ds(at, block)], grad_scores)

    dqt = lax.fori_loop(
        0, step, lambda j, c: visit(j, c, False), jnp.zeros((HEAD_DIM, block), jnp.float32)
    )
    dqt = visit(step, dqt, True)

    def turn_back(values, cosine, sine):
        return values * cosine - pltpu.roll(values, HEAD_DIM // 2, 1) * sine

    at = pl.multiple_of(step * block, block)
    dq = turn_back(dqt.T * scale, cos_ref[pl.ds(at, block), :], sin_ref[pl.ds(at, block), :])
    out_ref[pair, pl.ds(at, block), :HEAD_DIM] = dq.astype(jnp.bfloat16)

    @pl.when(step == last)
    def _():
        dk = turn_back(dk_ref[...] * scale, cos_ref[...], sin_ref[...])
        out_ref[pair, :, HEAD_DIM : 2 * HEAD_DIM] = dk.astype(jnp.bfloat16)
        out_ref[pair, :, 2 * HEAD_DIM :] = dv_ref[...].astype(jnp.bfloat16)


MESH = pl.DeviceIdType.MESH


class Plan:
    def __init__(self, mesh):
        self.n_dp, self.n_seq = mesh.shape["dp"], mesh.shape["seq"]
        bits = [1 << i for i in range(self.n_seq.bit_length() - 1)]
        self.bits = bits[::-1]
        if len(bits) == 3:
            self.orders = ((2, 4, 1), (4, 2, 1))
        else:
            turn = len(bits) // 2
            self.orders = (tuple(bits), tuple(bits[turn:] + bits[:turn]))
        self.hops = len(bits)
        self.masks = range(1, self.n_dp)
        straight = [("dp",) + order for order in self.orders]
        self.routes = {
            "even": [straight, straight],
            "late": [straight, [order[:1] + ("dp",) + order[1:] for order in self.orders]],
            "x": [straight, [("dp",) + self.orders[1]] * 2],
        }

    def sems(self, route, stage):
        return sum(len(self.masks) if entry == "dp" else 1 for entry in route[:stage])

    def lead(self):
        return (self.n_dp,) + (2,) * self.hops


def place():
    return lax.axis_index("dp"), lax.axis_index("seq")


def partner_dp(plan, mask):
    dp, seq = place()
    return (lax.bitwise_xor(dp, mask), seq)


def partner_seq(bit):
    dp, seq = place()
    return (dp, lax.bitwise_xor(seq, bit))


def own_bit(bit):
    return lax.bitwise_and(lax.div(place()[1], bit), 1)


def greet(plan, everyone=False):
    barrier = pltpu.get_barrier_semaphore()
    others = [partner_dp(plan, m) for m in plan.masks]
    others += [partner_seq(m) for m in (range(1, plan.n_seq) if everyone else plan.bits)]
    for other in others:
        pl.semaphore_signal(barrier, inc=1, device_id=other, device_id_type=MESH)
    pl.semaphore_wait(barrier, len(others))


def reduce_kernel(plan, jobs, first, count, lag, routes, beside, *refs):
    k, given = len(jobs), sum(job[3] for job in jobs)
    lefts, rights, refs = iter(refs[:given]), refs[given : given + k], refs[given + k :]
    more = [0, 0, 0] if beside is None else [len(beside.in_specs), len(beside.out_specs), len(beside.scratch)]
    extra, refs = refs[: more[0]], refs[more[0] :]
    out_ref, extra = refs[0], extra + refs[1 : 1 + more[1]]
    scratch = refs[1 + more[1] :]
    extra, scratch = extra + scratch[: more[2]], scratch[more[2] :]
    hops, slots = plan.hops, 2 * lag
    stages = hops + 1
    kinds = 1 if routes[0] == routes[1] else 2
    sums, got = [], []
    for h in range(2):
        more = (kinds - 1, 2 * (kinds - 1))
        sums.append(scratch[: stages + more[0]])
        got.append(scratch[stages + more[0] : 2 * stages + sum(more)])
        scratch = scratch[2 * stages + sum(more) :]
    send, recv = scratch
    tick = pl.program_id(0)
    half = out_ref.shape[-1] // 2
    rows = out_ref.shape[-2]
    dp, _ = place()

    @pl.when(tick == 0)
    def _():
        greet(plan, getattr(beside, "everyone", False))

    def sums_at(h, kind, stage, u):
        if stage < stages - 1 or kinds == 1:
            return sums[h][stage], lax.rem(u, lag)
        return sums[h][stage + kind], 0

    def got_at(h, kind, stage, u):
        if stage < stages - 2 or kinds == 1:
            return got[h][stage], lax.rem(u, slots)
        return got[h][stage + 2 * kind], lax.rem(lax.div(u, 2), lag)

    def at_entry(h, kind, stage, value):
        route = routes[kind][h]
        left = [d for d in ("dp",) + tuple(plan.bits) if d not in route[:stage]]
        return tuple(value if d == route[stage] else slice(None) for d in left)

    def own(entry):
        return dp if entry == "dp" else own_bit(entry)

    def copies(h, kind, stage, u):
        route = routes[kind][h]
        entry = route[stage]
        src, kept = sums_at(h, kind, stage, u)
        dst, slot = got_at(h, kind, stage, u)
        at = h * (hops + len(plan.masks)) + plan.sems(route, stage)
        sem = lax.rem(u, slots)
        if entry != "dp":
            return [pltpu.make_async_remote_copy(
                src.at[(kept,) + at_entry(h, kind, stage, 1 - own(entry))], dst.at[slot],
                send.at[sem, at], recv.at[sem, at], device_id=partner_seq(entry), device_id_type=MESH)]
        return [
            pltpu.make_async_remote_copy(
                src.at[(kept,) + at_entry(h, kind, stage, lax.bitwise_xor(dp, mask))], dst.at[slot, n],
                send.at[sem, at + n], recv.at[sem, at + n], device_id=partner_dp(plan, mask), device_id_type=MESH)
            for n, mask in enumerate(plan.masks)
        ]

    def wide(values):
        return values.astype(jnp.float32)

    for stage in reversed(range(1, stages + 1)):
        u = tick - first - lag * stage
        for kind in range(kinds):
            due = (u >= 0) & (u < count)
            if kinds > 1:
                due = due & (lax.rem(u, 2) == kind)

            @pl.when(due)
            def _(stage=stage, kind=kind, u=u):
                for h in range(2):
                    for copy in copies(h, kind, stage - 1, u):
                        copy.wait()
                    entry = routes[kind][h][stage - 1]
                    src, kept = sums_at(h, kind, stage - 1, u)
                    dst, slot = got_at(h, kind, stage - 1, u)
                    total = wide(src[(kept,) + at_entry(h, kind, stage - 1, own(entry))])
                    if entry == "dp":
                        for n in range(len(plan.masks)):
                            total = total + wide(dst[slot, n])
                    else:
                        total = total + wide(dst[slot])
                    if stage == stages:
                        out_ref[0, :, h * half : (h + 1) * half] = total
                        continue
                    to, at = sums_at(h, kind, stage, u)
                    to[at] = total.astype(jnp.bfloat16)
                    for copy in copies(h, kind, stage, u):
                        copy.start()

    for (start, stop, cols, has_left), right in zip(jobs, rights):
        if has_left:
            left = next(lefts)

            def left_rows(which, z, left=left):
                step = rows * plan.n_seq
                return left[which, z * step : (z + 1) * step, :]

        else:
            left_rows = functools.partial(beside.left, extra)

        @pl.when((tick >= first + start) & (tick < first + stop))
        def _(start=start, cols=cols, left_rows=left_rows, right=right):
            u = tick - first
            kept = lax.rem(u, lag)
            which = lax.div(u - start, cols)
            for z in range(plan.n_dp):
                part = dot(left_rows(which, z), right[...]).astype(jnp.bfloat16)
                for h in range(2):
                    piece = part[:, h * half : (h + 1) * half]
                    sums[h][0][kept, z] = piece.reshape(plan.lead()[1:] + (rows, half))
            for h in range(2):
                for copy in copies(h, 0, 0, u):
                    copy.start()

    if beside is not None:
        beside.run(tick, extra)


def reduce_products(plan, pairs, rows, width, lag, routes, collective_id, beside=None, first=0):
    jobs, start = [], 0
    left_specs, right_specs = [], []
    for left, right in pairs:
        cols = right.shape[1] // width
        blocks = left if isinstance(left, int) else left.shape[0]
        stop = start + blocks * cols
        jobs.append((start, stop, cols, left is not blocks))
        if left is not blocks:
            left_specs.append(pl.BlockSpec(left.shape, lambda t: (0, 0, 0), pipeline_mode=pl.Buffered(1)))
        right_specs.append(pl.BlockSpec(
            (right.shape[0], width),
            functools.partial(lambda t, start, stop, cols: (0, lax.rem(jnp.clip(t - first, start, stop - 1) - start, cols)),
                start=start, stop=stop, cols=cols)))
        start = stop
    count = start
    half = width // 2
    slots, hops = 2 * lag, plan.hops
    tail = lag * (hops + 1)
    n_dp, masks = plan.n_dp, len(plan.masks)
    low = jnp.bfloat16

    def room(*shape):
        return pltpu.VMEM(shape + (rows, half), low)

    routes = [[route[::-1] for route in kind] for kind in plan.routes[routes]]

    def left(kind, stage):
        return [n_dp if d == "dp" else 2 for d in ("dp",) + tuple(plan.bits) if d not in routes[kind][0][:stage]]

    def arriving(kind, stage):
        return [masks] * (routes[kind][0][stage] == "dp") + left(kind, stage + 1)

    buffers = []
    for _ in range(2):
        if routes[0] == routes[1]:
            buffers += [room(lag, *left(0, s)) for s in range(hops + 1)]
            buffers += [room(slots, *arriving(0, s)) for s in range(hops + 1)]
            continue
        buffers += [room(lag, *left(0, s)) for s in range(hops)] + [room(1, *left(k, hops)) for k in range(2)]
        buffers += [room(slots, *arriving(0, s)) for s in range(hops - 1)]
        buffers += [room(lag, *arriving(k, s)) for k in range(2) for s in (hops - 1, hops)]
    each = 2 * (hops + len(plan.masks))
    out_specs = [pl.BlockSpec((1, rows, width), lambda t: (jnp.clip(t - first - tail, 0, count - 1), 0, 0))]
    out_shapes = [jax.ShapeDtypeStruct((count, rows, width), jnp.float32)]
    more_in, more_scratch, more_operands = [], [], []
    if beside is not None:
        more_in, more_scratch, more_operands = beside.in_specs, beside.scratch, beside.operands
        out_specs, out_shapes = out_specs + beside.out_specs, out_shapes + beside.out_shapes
    return pl.pallas_call(
        functools.partial(reduce_kernel, plan, jobs, first, count, lag, routes, beside),
        grid=(max(first + count + tail, 0 if beside is None else beside.ticks),),
        in_specs=left_specs + right_specs + more_in,
        out_specs=out_specs,
        out_shape=out_shapes,
        scratch_shapes=more_scratch + buffers + [
            pltpu.SemaphoreType.DMA((slots, each)),
            pltpu.SemaphoreType.DMA((slots, each)),
        ],
        compiler_params=pltpu.CompilerParams(
            collective_id=collective_id, has_side_effects=True, vmem_limit_bytes=63 << 20),
    )(*[p[0] for p in pairs if not isinstance(p[0], int)], *[p[1] for p in pairs], *more_operands)


class Copies:
    def __init__(self, send, recv):
        self.send, self.recv, self.count, self.sent = send, recv, 0, []

    def remote(self, src, dst, device):
        at = self.count
        self.count += 1
        return pltpu.make_async_remote_copy(
            src, dst, self.send.at[at], self.recv.at[at], device_id=device, device_id_type=MESH)

    def run(self, pieces, lag, tick=None):
        last = max(start + lag * len(stages) for start, stages in pieces)
        for now in range(min(start for start, _ in pieces), last + 1):
            due = [
                (start, stages, stage)
                for stage in reversed(range(max(len(stages) for _, stages in pieces) + 1))
                for start, stages in pieces
                if start + lag * stage == now and stage <= len(stages)
            ]

            def step(due=due, now=now):
                for start, stages, stage in due:
                    if stage > 0:
                        for copy in stages[stage - 1][1]:
                            copy.wait()
                    if stage < len(stages):
                        ahead, copies = stages[stage]
                        if ahead is not None:
                            ahead()
                        for copy in copies:
                            copy.start()

            if tick is None:
                step()
            elif due:
                pl.when(tick == now)(step)
        return last


def arrive(plan, lag, tick, h_ref, s_ref, weights, hs_ref, ss_ref, w_ref, hv, wv, halves, send, recv, local):
    dp, seq = place()
    y, x, c = own_bit(4), own_bit(2), own_bit(1)
    loads = [pltpu.make_async_copy(h_ref.at[y], hv, local.at[0])]
    loads += [pltpu.make_async_copy(r, wv.at[i], local.at[1 + i]) for i, r in enumerate(weights)]
    own = pltpu.make_async_copy(hv, hs_ref.at[y, x, c], local.at[0])
    named = pltpu.make_async_copy(s_ref.at[y], ss_ref.at[y, x, c], local.at[4])

    @pl.when(tick == 0)
    def _():
        for load in loads:
            load.start()
        named.start()
        for load in loads:
            load.wait()
        own.start()

    run = Copies(send, recv)
    pieces = []
    pieces.append((0, [
        (None, [run.remote(s_ref.at[1 - y], ss_ref.at[y, x, c], partner_seq(4))]),
        (named.wait, [run.remote(ss_ref.at[:, x, c], ss_ref.at[:, x, c], partner_seq(2))]),
        (None, [run.remote(ss_ref.at[:, :, c], ss_ref.at[:, :, c], partner_seq(1))]),
    ]))
    tokens = hv.shape[0]
    parts = 4
    for i in range(parts):
        rows = pl.ds(i * (tokens // parts), tokens // parts)
        first = run.remote(h_ref.at[1 - y, rows], hs_ref.at[y, x, c, rows], partner_seq(4))
        second = [run.remote(hs_ref.at[:, x, c, rows], hs_ref.at[:, x, c, rows], partner_seq(2))]
        third = [run.remote(hs_ref.at[:, :, c, rows], hs_ref.at[:, :, c, rows], partner_seq(1))]
        pieces.append((i, [(None, [first]), (own.wait if i == 0 else None, second), (None, third)]))

    half, quarter = halves.shape[-1], w_ref.shape[-1]
    for i in range(3):
        mine = pltpu.make_async_copy(
            halves.at[i, :, :, pl.ds(c * quarter, quarter)], w_ref.at[i, dp, y, :, c], local.at[1 + i])

        def cut(i=i, mine=mine):
            halves[i, x] = wv[i, :, pl.ds(pl.multiple_of(x * half, 128), half)]
            mine.start()

        to_x = [run.remote(wv.at[i, :, pl.ds((1 - x) * half, half)], halves.at[i, x], partner_seq(2))]
        to_core = [run.remote(
            halves.at[i, :, :, pl.ds((1 - c) * quarter, quarter)], w_ref.at[i, dp, y, :, c], partner_seq(1))]
        to_z = [run.remote(w_ref.at[i, dp, y], w_ref.at[i, dp, y], partner_dp(plan, m)) for m in plan.masks]
        to_y = [run.remote(w_ref.at[i, :, y], w_ref.at[i, :, y], partner_seq(4))]
        pieces.append((i, [(None, to_x), (cut, to_core), (mine.wait, to_z), (None, to_y)]))
    run.run(pieces, ARRIVE_LAG, tick)


ARRIVE_LAG = 2
ARRIVED = max(3 + 3 * ARRIVE_LAG, 2 + 4 * ARRIVE_LAG)


class Finish:
    def __init__(
        self, plan, first, packed, grads, mixed_t, lse, seg_col, seg_row, cosine, sine, turned, weights, inputs, grad_first, gain, more
    ):
        count, per, _, columns, _ = packed.shape
        length = count * columns
        self.plan, self.first = plan, first
        self.block = seg_row.shape[1]
        self.steps, self.parts = length // self.block, self.block // columns
        self.count = per * self.steps
        self.begin = first + self.count
        self.split = 4
        self.operands = (
            packed, packed, packed, grads, mixed_t, lse, seg_col, seg_row, cosine, sine, turned, weights, inputs, grad_first, gain, more
        )
        width, quarter = turned.shape[0], weights.shape[2]
        n_dp, masks = plan.n_dp, len(plan.masks)
        rows = width // (8 * n_dp)
        size = columns // self.split
        low = jnp.bfloat16

        def pair(t):
            return lax.div(jnp.clip(t - first, 0, self.count - 1), self.steps)

        def step(t):
            return lax.rem(jnp.clip(t - first, 0, self.count - 1), self.steps)

        def whole(which):
            return pl.BlockSpec(
                (count, None, None, columns, HEAD_DIM), lambda t: (0, pair(t), which, 0, 0), pipeline_mode=pl.Buffered(1))

        def fixed(shape):
            return pl.BlockSpec(shape, lambda t: (0,) * len(shape), pipeline_mode=pl.Buffered(1))

        hbm = pl.BlockSpec(memory_space=pl.ANY)
        self.in_specs = [
            whole(0),
            whole(1),
            whole(2),
            pl.BlockSpec((count, None, columns, HEAD_DIM), lambda t: (0, pair(t), 0, 0), pipeline_mode=pl.Buffered(1)),
            pl.BlockSpec((1, 1, HEAD_DIM, self.block), lambda t: (pair(t), step(t), 0, 0)),
            pl.BlockSpec((1, self.steps, self.block), lambda t: (pair(t), 0, 0)),
            fixed((length, 1)),
            fixed((self.steps, self.block)),
            fixed((length, HEAD_DIM)),
            fixed((length, HEAD_DIM)),
            hbm,
            hbm,
            hbm,
            hbm,
            fixed((1, width)),
            fixed((8, width)),
        ]
        self.out_specs = [
            hbm,
            pl.BlockSpec((3, rows, width), lambda t: (0, 0, 0)),
            pl.BlockSpec((rows, 128), lambda t: (0, 0)),
        ]
        self.out_shapes = [
            jax.ShapeDtypeStruct(inputs.shape, jnp.float32),
            jax.ShapeDtypeStruct((3, rows, width), jnp.float32),
            jax.ShapeDtypeStruct((rows, 128), jnp.float32),
        ]
        self.copies = 3 * (3 + masks) + 3 * self.split + 3 + masks
        self.scratch = [
            pltpu.VMEM((HEAD_DIM, length), low),
            pltpu.VMEM((length, HEAD_DIM), jnp.float32),
            pltpu.VMEM((length, HEAD_DIM), jnp.float32),
            pltpu.VMEM((3, length, quarter), low),
            pltpu.VMEM(turned.shape, low),
            pltpu.VMEM(weights.shape, low),
            pltpu.VMEM((2, 2, size, width), jnp.float32),
            pltpu.VMEM((2, 2, size, width), jnp.float32),
            pltpu.VMEM((2, n_dp, 2, 2, 2, rows, quarter), low),
            pltpu.VMEM((3, n_dp, 2, 2, rows, quarter), low),
            pltpu.VMEM((3, masks, 2, 2, rows, quarter), low),
            pltpu.VMEM((3, 2, 2, rows, quarter), low),
            pltpu.VMEM((3, 2, rows, 2 * quarter), low),
            pltpu.VMEM((3, rows, 2 * quarter), low),
            pltpu.VMEM((2, 2, 2, 2, size, width), low),
            pltpu.VMEM((2, 2, 2, size, width), low),
            pltpu.VMEM((2, 2, 2, size, width), low),
            pltpu.VMEM((2, 2, size, width), low),
            pltpu.VMEM((2, 2, size, width), low),
            pltpu.VMEM((2, size, width), low),
            pltpu.VMEM((128, width), jnp.float32),
            pltpu.VMEM((n_dp, 2, 2, 2, rows, 128), low),
            pltpu.VMEM((n_dp, 2, 2, rows, 128), low),
            pltpu.VMEM((n_dp, 2, 2, rows, 128), low),
            pltpu.VMEM((n_dp, 2, rows, 128), low),
            pltpu.VMEM((n_dp, 2, rows, 128), low),
            pltpu.VMEM((n_dp, rows, 128), low),
            pltpu.VMEM((n_dp, rows, 128), low),
            pltpu.VMEM((masks, rows, 128), low),
            pltpu.SemaphoreType.DMA((self.copies,)),
            pltpu.SemaphoreType.DMA((self.copies,)),
            pltpu.SemaphoreType.DMA((2,)),
            pltpu.SemaphoreType.DMA((2, 3)),
        ]
        backs, products = [2 * i for i in range(self.split)], [(i - per + 1) * self.steps for i in range(per)]
        self.starts = backs, products
        self.last_norm = backs[-1] + 2 * 3 + 1
        self.ticks = self.begin + self.last_norm + 2 * 4 + 1

    def run(self, tick, refs):
        ins, (dx_ref, dw_ref, dn_ref), scratch = refs[:16], refs[16:19], refs[19:]
        turned_any, weights_any, inputs_any, first_any, gain_ref, more_ref = ins[10:16]
        kt_ref, dk_ref, dv_ref, g_ref, t_ref, w_ref, x_ref, gx_ref = scratch[:8]
        made, made_y, made_z, sum_z, sides, made_x = scratch[8:14]
        acts, acts_c, sum_c, acts_x, sum_x, acts_y = scratch[14:20]
        totals, norms, norms_c, norms_sc, norms_x, norms_sx, norms_y, norms_sy, norms_z = scratch[20:29]
        send, recv, local, chunked = scratch[29:]
        plan, parts = self.plan, self.split
        dp, _ = place()
        y, x, c = own_bit(4), own_bit(2), own_bit(1)
        width, length = t_ref.shape
        quarter = w_ref.shape[2]
        columns = length // 8
        half = 2 * quarter
        rows = dw_ref.shape[1]
        size = columns // parts
        low = jnp.bfloat16
        loads = [
            pltpu.make_async_copy(weights_any, w_ref, local.at[0]),
            pltpu.make_async_copy(turned_any, t_ref, local.at[1]),
        ]

        @pl.when(tick == 1)
        def _():
            for load in loads:
                load.start()

        @pl.when((tick >= self.first) & (tick < self.begin))
        def _():
            pair, step = lax.div(tick - self.first, self.steps), lax.rem(tick - self.first, self.steps)
            attend_back_step(self.block, self.parts, pair, step, self.steps - 1, *ins[:10], g_ref, kt_ref, dk_ref, dv_ref)

        masks = len(plan.masks)
        now = tick - self.begin

        def wide(values):
            return values.astype(jnp.float32)

        def stream(starts, stages, base, most):
            gap = starts[1] - starts[0]
            for stage in reversed(range(len(stages))):
                since = now - starts[0] - 2 * stage
                i = lax.div(since, gap)

                @pl.when((since >= 0) & (since <= starts[-1] - starts[0]) & (lax.rem(since, gap) == 0))
                def _(stage=stage, i=i):
                    def made_copies(n):
                        at = base + i * most + sum(len(c(0)) for _, c in stages[:n])
                        return [
                            pltpu.make_async_remote_copy(
                                src, dst, send.at[at + k], recv.at[at + k], device_id=other, device_id_type=MESH)
                            for k, (src, dst, other) in enumerate(stages[n][1](i))
                        ]

                    if stage > 0:
                        for copy in made_copies(stage - 1):
                            copy.wait()
                    stages[stage][0](i)
                    for copy in made_copies(stage):
                        copy.start()

        def product(i):
            @pl.when(i == 0)
            def _():
                loads[1].wait()

            step = 8 * rows
            for z in range(plan.n_dp):
                part = dot(t_ref[z * step : (z + 1) * step, :], g_ref[i])
                made[lax.rem(i, 2), z] = part.astype(low).reshape(2, 2, 2, rows, quarter)

        def product_y(i):
            made_y[i] = (wide(made[lax.rem(i, 2), :, y]) + wide(made_y[i])).astype(low)

        def product_z(i):
            total = wide(made_y[i, dp])
            for n in range(masks):
                total = total + wide(made_z[i, n])
            sum_z[i] = total.astype(low)

        def product_c(i):
            sides[i, :, :, pl.ds(pl.multiple_of(c * quarter, 128), quarter)] = sum_z[i, :, c]

        def product_x(i):
            for side, values in ((x, sides.at[i, x]), (1 - x, made_x.at[i])):
                for core in range(2):
                    for kind in range(3):
                        start = core * quarter + kind * HEAD_DIM
                        lanes = pl.ds(pl.multiple_of(side * half + core * quarter + i * HEAD_DIM, HEAD_DIM), HEAD_DIM)
                        dw_ref[kind, :, lanes] = wide(values[:, start : start + HEAD_DIM])

        def back(i):
            @pl.when(i == 0)
            def _():
                loads[0].wait()

            slot = lax.rem(i, 2)
            pieces = []
            for k in range(3):
                blocks = []
                for n in range(8):
                    at = pl.ds(pl.multiple_of(n * columns + i * size, size), size)
                    blocks.append(jnp.concatenate(
                        [g_ref[p, at, k * HEAD_DIM : (k + 1) * HEAD_DIM] for p in range(3)], axis=1))
                pieces.append(jnp.concatenate(blocks, axis=0))
            step = 512
            for n in range(width // step):
                total = sum(dot(pieces[k], w_ref[k, n * step : (n + 1) * step, :], NT) for k in range(3))
                acts[slot, :, :, :, :, n * step : (n + 1) * step] = total.astype(low).reshape(2, 2, 2, size, step)

        def back_c(i):
            slot = lax.rem(i, 2)
            sum_c[slot] = (wide(acts[slot, :, :, c]) + wide(acts_c[slot])).astype(low)

        def chunk(i):
            slot, at = lax.rem(i, 2), pl.ds(pl.multiple_of(i * size, size), size)
            return [
                pltpu.make_async_copy(inputs_any.at[:, at], x_ref.at[slot], chunked.at[slot, 0]),
                pltpu.make_async_copy(first_any.at[:, at], gx_ref.at[slot], chunked.at[slot, 1]),
            ]

        def chunk_out(i):
            slot, at = lax.rem(i, 2), pl.ds(pl.multiple_of(i * size, size), size)
            return pltpu.make_async_copy(gx_ref.at[slot], dx_ref.at[:, at], chunked.at[slot, 2])

        def back_x(i):
            slot = lax.rem(i, 2)

            @pl.when(i >= 2)
            def _():
                chunk_out(i - 2).wait()

            for load in chunk(i):
                load.start()
            sum_x[slot] = (wide(sum_c[slot, :, x]) + wide(acts_x[slot])).astype(low)

        def norm_back(i):
            slot = lax.rem(i, 2)
            for load in chunk(i):
                load.wait()

            @pl.when(i == 0)
            def _():
                totals[...] = jnp.zeros_like(totals)

            gain = gain_ref[...]

            def one(s, carry):
                grad = jnp.where(y == s, wide(sum_x[slot, s]), wide(acts_y[slot]))
                values = x_ref[slot, s]
                centre = values - jnp.mean(values, axis=-1, keepdims=True)
                spread = lax.rsqrt(jnp.mean(centre * centre, axis=-1, keepdims=True) + EPSILON)
                normed = centre * spread
                grown = grad * gain
                mean_one = jnp.mean(grown, axis=-1, keepdims=True)
                mean_two = jnp.mean(grown * normed, axis=-1, keepdims=True)
                gx_ref[slot, s] = gx_ref[slot, s] + (grown - mean_one - normed * mean_two) * spread
                totals[0:1] += jnp.sum(grad * normed, axis=0, keepdims=True)
                totals[1:2] += jnp.sum(grad, axis=0, keepdims=True)
                return carry

            lax.fori_loop(0, 2, one, 0)
            chunk_out(i).start()

        stream(self.starts[0], [
            (back, lambda i: [(acts.at[lax.rem(i, 2), :, :, 1 - c], acts_c.at[lax.rem(i, 2)], partner_seq(1))]),
            (back_c, lambda i: [(sum_c.at[lax.rem(i, 2), :, 1 - x], acts_x.at[lax.rem(i, 2)], partner_seq(2))]),
            (back_x, lambda i: [(sum_x.at[lax.rem(i, 2), 1 - y], acts_y.at[lax.rem(i, 2)], partner_seq(4))]),
            (norm_back, lambda i: []),
        ], 0, 3)
        stream(self.starts[1], [
            (product, lambda i: [(made.at[lax.rem(i, 2), :, 1 - y], made_y.at[i], partner_seq(4))]),
            (product_y, lambda i: [
                (made_y.at[i, lax.bitwise_xor(dp, m)], made_z.at[i, n], partner_dp(plan, m))
                for n, m in enumerate(plan.masks)]),
            (product_z, lambda i: [
                (sum_z.at[i, :, 1 - c], sides.at[i, :, :, pl.ds(c * quarter, quarter)], partner_seq(1))]),
            (product_c, lambda i: [(sides.at[i, 1 - x], made_x.at[i], partner_seq(2))]),
            (product_x, lambda i: []),
        ], 3 * parts, 3 + masks)
        run = Copies(send, recv)
        run.count = 3 * parts + 3 * (3 + masks)
        pieces = []

        def norms_start():
            totals[2:4] = more_ref[0:2]
            norms[...] = totals[...].T.astype(low).reshape(norms.shape)

        def norms_add(total, kept, got):
            def go():
                total[...] = (wide(kept()) + wide(got[...])).astype(low)
            return go

        def norms_end():
            total = wide(norms_sy[dp])
            for n in range(len(plan.masks)):
                total = total + wide(norms_z[n])
            dn_ref[...] = total
            for i in range(parts - 2, parts):
                chunk_out(i).wait()

        pieces.append((self.last_norm, [
            (norms_start, [run.remote(norms.at[:, :, :, 1 - c], norms_c, partner_seq(1))]),
            (norms_add(norms_sc, lambda: norms[:, :, :, c], norms_c), [run.remote(norms_sc.at[:, :, 1 - x], norms_x, partner_seq(2))]),
            (norms_add(norms_sx, lambda: norms_sc[:, :, x], norms_x), [run.remote(norms_sx.at[:, 1 - y], norms_y, partner_seq(4))]),
            (norms_add(norms_sy, lambda: norms_sx[:, y], norms_y), [
                run.remote(norms_sy.at[lax.bitwise_xor(dp, m)], norms_z.at[n], partner_dp(plan, m))
                for n, m in enumerate(plan.masks)]),
            (norms_end, []),
        ]))
        run.run(pieces, 2, now)


class Gather:
    def __init__(self, plan, lag, shard, rows, cols, routes):
        self.plan, self.lag, self.rows, self.cols = plan, lag, rows, cols
        self.routes = plan.routes[routes]
        self.across = shard.shape[1] // cols
        self.pieces = shard.shape[0] // rows * self.across
        self.ticks = self.pieces + lag * (plan.hops + 1)
        self.out_shape = jax.ShapeDtypeStruct(plan.lead() + shard.shape, shard.dtype)
        each = 2 * (len(plan.masks) + plan.hops)
        self.scratch = [
            pltpu.VMEM(shard.shape, shard.dtype),
            pltpu.SemaphoreType.DMA((2 * lag, each)),
            pltpu.SemaphoreType.DMA((2 * lag, each)),
            pltpu.SemaphoreType.DMA((2,)),
        ]

    def copies(self, kind, stage, u, full, held, send, recv):
        plan = self.plan
        dp, _ = place()
        slot = lax.rem(u, 2 * self.lag)
        rows = pl.ds(pl.multiple_of(lax.div(u, self.across) * self.rows, 16), self.rows)
        out = []
        for h in range(2):
            start = lax.rem(u, self.across) * self.cols + h * (self.cols // 2)
            cols = pl.ds(pl.multiple_of(start, 128), self.cols // 2)
            route = self.routes[kind][h]
            entry, done = route[stage], route[:stage]
            where = (slice(None) if "dp" in done else dp,)
            where += tuple(slice(None) if b in done else own_bit(b) for b in plan.bits)
            part = full.at[where + (rows, cols)]
            src = part if stage else held.at[rows, cols]
            at = h * (len(plan.masks) + plan.hops) + plan.sems(route, stage)
            others = [partner_dp(plan, m) for m in plan.masks] if entry == "dp" else [partner_seq(entry)]
            for n, other in enumerate(others):
                out.append(pltpu.make_async_remote_copy(
                    src, part, send.at[slot, at + n], recv.at[slot, at + n], device_id=other, device_id_type=MESH))
        return out

    def run(self, tick, shard, full, held, send, recv, local):
        plan, lag = self.plan, self.lag
        dp, _ = place()
        me = tuple(own_bit(b) for b in plan.bits)
        own = pltpu.make_async_copy(held, full.at[(dp,) + me], local.at[0])

        @pl.when(tick == 0)
        def _():
            load = pltpu.make_async_copy(shard, held, local.at[1])
            load.start()
            load.wait()
            own.start()

        @pl.when(tick == lag)
        def _():
            own.wait()

        stages = plan.hops + 1
        for stage in reversed(range(stages + 1)):
            u = tick - lag * stage
            kinds = 1 if self.routes[0] == self.routes[1] else 2
            for kind in range(kinds):

                @pl.when((u >= 0) & (u < self.pieces) & (lax.rem(u, 2) == kind if kinds > 1 else True))
                def _(stage=stage, u=u, kind=kind):
                    if stage > 0:
                        for copy in self.copies(kind, stage - 1, u, full, held, send, recv):
                            copy.wait()
                    if stage < stages:
                        for copy in self.copies(kind, stage, u, full, held, send, recv):
                            copy.start()


def attend_step(block, parts, pair, step, packed, col_ref, row_ref, o_ref, ot_ref, lse_ref, vt_ref):
    @pl.when(step == 0)
    def _():
        vt_ref[...] = packed[:, pair, 2].reshape(-1, HEAD_DIM).T

    query = packed[pl.ds(step * parts, parts), pair, 0].reshape(block, HEAD_DIM)
    query_row = row_ref[pl.ds(step, 1), :]
    unit = LOG2E / math.sqrt(HEAD_DIM)

    def visit(j, carry, diagonal):
        top, total, mixed = carry
        key = packed[pl.ds(j * parts, parts), pair, 1].reshape(block, HEAD_DIM)
        at = pl.multiple_of(j * block, block)
        scores = dot(key, query, NT) * unit
        scores = jnp.where(allowed_pairs(col_ref[pl.ds(at, block), :], query_row, diagonal), scores, MASKED)
        above = jnp.maximum(top, jnp.max(scores, axis=0, keepdims=True))
        expo = jnp.exp2(scores - above)
        fade = jnp.exp2(top - above)
        total = total * fade + jnp.sum(expo, axis=0, keepdims=True)
        mixed = mixed * fade + dot(vt_ref[:, pl.ds(at, block)], expo.astype(jnp.bfloat16))
        return above, total, mixed

    start = (
        jnp.full((1, block), MASKED, jnp.float32),
        jnp.zeros((1, block), jnp.float32),
        jnp.zeros((HEAD_DIM, block), jnp.float32),
    )
    carry = lax.fori_loop(0, step, lambda j, c: visit(j, c, False), start)
    top, total, mixed = visit(step, carry, True)
    mixed = mixed / total
    ot_ref[0, 0] = mixed
    lse_ref[0, pl.ds(step, 1), :] = top + jnp.log2(total)
    o_ref[...] = mixed.T.astype(jnp.bfloat16).reshape(o_ref.shape)


def attention_kernel(
    plan, lag, gathers, block, steps, h_ref, s_ref, q_ref, k_ref, v_ref, cos_ref, sin_ref, out_shard, up_shard,
    packed, turned_ref, o_ref, ot_ref, lse_ref, col_ref, row_ref, hs_ref, ss_ref, w_ref, full_out, full_up,
    vt_ref, x_ref, weights_ref, ids_ref, hv, wv, halves, send, recv, local, fetch, *more,
):
    tick = pl.program_id(0)

    @pl.when(tick == 0)
    def _():
        greet(plan)

    arrive(plan, lag, tick, h_ref, s_ref, (q_ref, k_ref, v_ref), hs_ref, ss_ref, w_ref, hv, wv, halves, send, recv, local)
    for (first, gather), shard, full, held in zip(
        gathers, (out_shard, up_shard), (full_out, full_up), (more[:4], more[4:])
    ):
        gather.run(tick - first, shard, full, *held)
    _, parts, columns, width = x_ref.shape
    heads = packed.shape[1]
    first = ARRIVED + 1

    def acts_load(i):
        return pltpu.make_async_copy(hs_ref.at[lax.div(i, 2), lax.rem(i, 2)], x_ref.at[lax.rem(i, 2)], fetch.at[lax.rem(i, 2)])

    weights_load = pltpu.make_async_copy(w_ref, weights_ref, fetch.at[2])
    ids_load = pltpu.make_async_copy(ss_ref, ids_ref, fetch.at[3])

    @pl.when(tick == ARRIVED)
    def _():
        ids_load.start()
        weights_load.start()
        acts_load(0).start()
        ids_load.wait()
        ids = ids_ref[...].reshape(2 * steps, columns)
        for i in range(2 * steps):
            row_ref[i // parts : i // parts + 1, (i % parts) * columns : (i % parts + 1) * columns] = ids[i : i + 1]
        turned = ids.astype(jnp.float32).T.astype(jnp.int32)
        for i in range(2 * steps):
            mine = turned[:, i : i + 1]
            col_ref[i * columns : (i + 1) * columns, :] = jnp.where(mine < 0, -2, mine)
        weights_load.wait()

    at = tick - first

    @pl.when((at >= 0) & (at < steps))
    def _():
        @pl.when(at + 1 < steps)
        def _():
            acts_load(at + 1).start()

        acts_load(at).wait()
        acts = x_ref[lax.rem(at, 2)].reshape(block, width)
        for kind in range(3):
            made = dot(acts, weights_ref[kind].reshape(width, heads * HEAD_DIM))
            for p in range(heads):
                head = made[:, p * HEAD_DIM : (p + 1) * HEAD_DIM]
                if kind < 2:
                    head = head * cos_ref[...] + pltpu.roll(head, HEAD_DIM // 2, 1) * sin_ref[...]
                packed[pl.ds(at * parts, parts), p, kind] = head.astype(jnp.bfloat16).reshape(parts, columns, HEAD_DIM)
        turned_ref[...] = acts.T

    @pl.when((at >= steps) & (at < steps * (1 + heads)))
    def _():
        pair, step = lax.div(at - steps, steps), lax.rem(at - steps, steps)
        attend_step(block, parts, pair, step, packed, col_ref, row_ref, o_ref, ot_ref, lse_ref, vt_ref)


def attention(plan, acts, segments, weights, cosine, sine, out_shard, up_shard, lag, collective_id):
    _, columns, width = acts.shape
    rows = weights[0].shape[0]
    quarter = width // 4
    heads = quarter // HEAD_DIM
    owners = 8
    length, block = owners * columns, 2 * columns
    steps, parts = length // block, 2
    gathers = (
        (0, Gather(plan, lag, out_shard, out_shard.shape[0], 512, "late")),
        (3, Gather(plan, lag, up_shard, up_shard.shape[0], 512, "late")),
    )
    low = jnp.bfloat16
    begin = ARRIVED + 1

    def at(t):
        return jnp.clip(t - begin, 0, steps - 1)

    def pair(t):
        return lax.div(jnp.clip(t - begin - steps, 0, steps * heads - 1), steps)

    def step(t):
        return lax.rem(jnp.clip(t - begin - steps, 0, steps * heads - 1), steps)

    def fixed(shape):
        return pl.BlockSpec(shape, lambda t: (0,) * len(shape))

    hbm = pl.BlockSpec(memory_space=pl.ANY)
    table = pl.BlockSpec((block, HEAD_DIM), lambda t: (at(t), 0))
    packed_shape = (owners, heads, 3, columns, HEAD_DIM)
    acts_shape = (2, 2, 2, columns, width)
    ids_shape = (2, 2, 2, 1, columns)
    weights_shape = (3,) + plan.lead() + (rows, quarter)
    copies = 3 + 4 * 3 + 3 * (3 + len(plan.masks))
    ticks = max([begin + steps * (1 + heads)] + [first + gather.ticks for first, gather in gathers])
    return pl.pallas_call(
        functools.partial(attention_kernel, plan, lag, gathers, block, steps),
        grid=(ticks,),
        in_specs=[hbm] * 5 + [table, table, hbm, hbm],
        out_specs=[
            fixed(packed_shape),
            pl.BlockSpec((width, block), lambda t: (0, at(t))),
            pl.BlockSpec((parts, None, columns, HEAD_DIM), lambda t: (step(t), pair(t), 0, 0)),
            pl.BlockSpec((1, 1, HEAD_DIM, block), lambda t: (pair(t), step(t), 0, 0)),
            pl.BlockSpec((1, steps, block), lambda t: (pair(t), 0, 0)),
            fixed((length, 1)),
            fixed((steps, block)),
            hbm,
            hbm,
            hbm,
            hbm,
            hbm,
        ],
        out_shape=[
            jax.ShapeDtypeStruct(packed_shape, low),
            jax.ShapeDtypeStruct((width, length), low),
            jax.ShapeDtypeStruct((owners, heads, columns, HEAD_DIM), low),
            jax.ShapeDtypeStruct((heads, steps, HEAD_DIM, block), jnp.float32),
            jax.ShapeDtypeStruct((heads, steps, block), jnp.float32),
            jax.ShapeDtypeStruct((length, 1), jnp.int32),
            jax.ShapeDtypeStruct((steps, block), jnp.int32),
            jax.ShapeDtypeStruct(acts_shape, low),
            jax.ShapeDtypeStruct(ids_shape, jnp.int32),
            jax.ShapeDtypeStruct(weights_shape, low),
            gathers[0][1].out_shape,
            gathers[1][1].out_shape,
        ],
        scratch_shapes=[
            pltpu.VMEM((HEAD_DIM, length), low),
            pltpu.VMEM((2, parts, columns, width), low),
            pltpu.VMEM(weights_shape, low),
            pltpu.VMEM(ids_shape, jnp.int32),
            pltpu.VMEM((columns, width), low),
            pltpu.VMEM((3, rows, width), low),
            pltpu.VMEM((3, 2, rows, width // 2), low),
            pltpu.SemaphoreType.DMA((copies,)),
            pltpu.SemaphoreType.DMA((copies,)),
            pltpu.SemaphoreType.DMA((5,)),
            pltpu.SemaphoreType.DMA((4,)),
        ] + gathers[0][1].scratch + gathers[1][1].scratch,
        compiler_params=pltpu.CompilerParams(
            collective_id=collective_id, has_side_effects=True, vmem_limit_bytes=56 << 20),
    )(acts, segments[:, None, :], *weights, cosine, sine, out_shard, up_shard)


class Mlp:
    def __init__(self, plan, lag, mixed, w_out, inputs, gain, offset, w_up, grad, cotangent, shard):
        tokens, width = inputs.shape
        hidden = w_up.shape[1]
        self.plan, self.lag = plan, lag
        self.blocks = 2 * plan.n_dp
        self.block = hidden // self.blocks
        self.rows = width // (plan.n_dp * plan.n_seq)
        self.gather = Gather(plan, lag, shard, self.rows, 512, "even")
        self.meet = 4
        self.up = self.meet + 1
        self.back = max(self.gather.ticks, self.up + self.blocks)
        self.norm = self.back + self.blocks
        self.ticks = self.norm + 5
        self.operands = (mixed, w_out, inputs, gain, offset, w_up, grad, cotangent, shard)
        blocks, back, up = self.blocks, self.back, self.up

        def up_block(t):
            later = jnp.clip(t - (up + blocks) + 1, 0, 1)
            return (0, jnp.clip(t - up, 0, blocks - 1) * (1 - later) + jnp.clip(t - back, 0, blocks - 1) * later)

        once = pl.BlockSpec((tokens, width), lambda t: (0, 0), pipeline_mode=pl.Buffered(1))
        row = pl.BlockSpec((1, width), lambda t: (0, 0))
        hbm = pl.BlockSpec(memory_space=pl.ANY)
        self.in_specs = [hbm, hbm, hbm, row, row, pl.BlockSpec((width, self.block), up_block), once, hbm, hbm]
        self.out_specs = [
            hbm,
            hbm,
            hbm,
            hbm,
            hbm,
            hbm,
            pl.BlockSpec((tokens, self.block), lambda t: (0, jnp.clip(t - back, 0, blocks - 1))),
            hbm,
            pl.BlockSpec((8, width), lambda t: (0, 0)),
            hbm,
        ]
        low = jnp.bfloat16
        flat = jax.ShapeDtypeStruct((tokens, width), jnp.float32)
        self.out_shapes = [
            flat,
            flat,
            flat,
            jax.ShapeDtypeStruct((tokens, width), low),
            jax.ShapeDtypeStruct((width, tokens), low),
            jax.ShapeDtypeStruct((width, tokens), low),
            jax.ShapeDtypeStruct((tokens, hidden), low),
            jax.ShapeDtypeStruct(mixed.shape, low),
            jax.ShapeDtypeStruct((8, width), jnp.float32),
            self.gather.out_shape,
        ]
        self.chunk = 64
        self.scratch = [
            pltpu.VMEM((tokens, hidden), low),
            pltpu.VMEM((hidden, tokens), low),
            pltpu.VMEM((tokens, hidden), low),
            pltpu.VMEM((2, 2, 2) + shard.shape, low),
            pltpu.VMEM((tokens, width), jnp.float32),
            pltpu.VMEM((tokens, width), jnp.float32),
            pltpu.VMEM((tokens, width), low),
            pltpu.VMEM(mixed.shape, low),
            pltpu.VMEM((2, 2, self.chunk, width), jnp.float32),
            pltpu.SemaphoreType.DMA((2, 2, plan.n_seq)),
            pltpu.SemaphoreType.DMA((16,)),
            pltpu.SemaphoreType.DMA((2, 2)),
            pltpu.SemaphoreType.DMA((2,)),
        ] + self.gather.scratch

    everyone = True

    def left(self, refs, which, z):
        turned, n = refs[20], self.plan.n_seq
        every = turned.shape[0] // (n * self.plan.n_dp)
        return jnp.concatenate(
            [
                turned[pl.ds(pl.multiple_of((z * n + d) * every + which * self.rows, 16), self.rows), :]
                for d in range(n)
            ],
            axis=0,
        )

    def run(self, tick, refs):
        mixed_hbm, w_out, inputs, gain_ref, offset_ref, up_ref, grad_ref, cotangent, shard = refs[:9]
        output, first_sum, grad_first, grad_low, mixed_turned, acts_turned, gu_ref, back_pairs, sums_ref, full = refs[9:19]
        hidden_ref, turned_ref, slope_ref, down_ref, out_ref, back_ref, acts_ref, pairs, chunks = refs[19:28]
        swaps, local, loads, fetch = refs[28:32]
        plan, block = self.plan, self.block
        dp, seq = place()
        count, heads, columns, _ = pairs.shape
        tokens, width = acts_ref.shape
        low = jnp.bfloat16
        third = 512
        thirds = width // third
        self.gather.run(tick, shard, full, *refs[32:])

        def exchange(which, src, dst):
            return [
                pltpu.make_async_remote_copy(
                    src.at[lax.bitwise_xor(seq, m)], dst.at[seq], swaps.at[which, 0, m], swaps.at[which, 1, m],
                    device_id=partner_seq(m), device_id_type=MESH)
                for m in range(1, count)
            ]

        there = exchange(0, mixed_hbm, pairs)
        here = pltpu.make_async_copy(mixed_hbm.at[seq], pairs.at[seq], local.at[0])
        based = pltpu.make_async_copy(inputs, out_ref, local.at[1])
        outs = [
            pltpu.make_async_copy(
                w_out.at[:, pl.ds(n * third, third)], turned_ref.at[pl.ds(n * width, width), :], local.at[2 + n])
            for n in range(thirds)
        ]
        kept = pltpu.make_async_copy(out_ref, first_sum, local.at[5])
        turns = []
        for n in range(thirds):
            rows = pl.ds(n * third, third)
            base = slope_ref.shape[1] - 2 * width + n * third
            turns.append(pltpu.make_async_copy(slope_ref.at[:, pl.ds(base, third)], mixed_turned.at[rows, :], local.at[6 + n]))
            turns.append(pltpu.make_async_copy(
                slope_ref.at[:, pl.ds(base + width, third)], acts_turned.at[rows, :], local.at[9 + n]))

        @pl.when(tick == 0)
        def _():
            for copy in there + [here, based] + outs:
                copy.start()

        @pl.when(tick == self.meet)
        def _():
            for copy in there + [here, based] + outs:
                copy.wait()
            per = width // (heads * HEAD_DIM)
            for s in range(count // per):
                for g in range(per):
                    for p in range(heads):
                        at = (g * heads + p) * HEAD_DIM
                        acts_ref[s * columns : (s + 1) * columns, at : at + HEAD_DIM] = pairs[s * per + g, p]
            for n in range(thirds):
                part = slice(n * third, (n + 1) * third)
                out_ref[:, part] += dot(acts_ref[...], turned_ref[n * width : (n + 1) * width, :])
                base = slope_ref.shape[1] - 2 * width + n * third
                slope_ref[:, base : base + third] = acts_ref[:, part].T
            kept.start()

            def norm(i, carry):
                rows = pl.ds(pl.multiple_of(i * self.chunk, self.chunk), self.chunk)
                values = out_ref[rows, :]
                centre = values - jnp.mean(values, axis=-1, keepdims=True)
                spread = lax.rsqrt(jnp.mean(centre * centre, axis=-1, keepdims=True) + EPSILON)
                acts_ref[rows, :] = (centre * spread * gain_ref[...] + offset_ref[...]).astype(low)
                return carry

            lax.fori_loop(0, tokens // self.chunk, norm, 0)
            for n in range(thirds):
                base = slope_ref.shape[1] - width + n * third
                slope_ref[:, base : base + third] = acts_ref[:, n * third : (n + 1) * third].T
            for copy in turns:
                copy.start()

        @pl.when(tick == self.up + 2)
        def _():
            for copy in turns + [kept]:
                copy.wait()

        def block_at(i):
            return pl.ds(pl.multiple_of(i * block, 128), block)

        @pl.when((tick >= self.up) & (tick < self.up + self.blocks))
        def _():
            step = 256
            for n in range(block // step):
                upper = dot(acts_ref[...], up_ref[:, n * step : (n + 1) * step])
                share = 0.5 + 0.5 * lax.erf(upper * (1.0 / math.sqrt(2.0)))
                density = jnp.exp(upper * upper * -0.5) * (1.0 / math.sqrt(2.0 * math.pi))
                made = (upper * share).astype(low)
                at = pl.multiple_of((tick - self.up) * block + n * step, 128)
                hidden_ref[:, pl.ds(at, step)] = made
                turned_ref[pl.ds(at, step), :] = made.T
                slope_ref[:, pl.ds(at, step)] = (share + upper * density).astype(low)

        def fetched(i):
            z, y = lax.div(i, 2), lax.rem(i, 2)
            return pltpu.make_async_copy(full.at[z, y], down_ref.at[y], fetch.at[y])

        i = tick - self.back

        @pl.when((i >= -1) & (i < self.blocks - 1))
        def _():
            fetched(i + 1).start()

        @pl.when((i >= 0) & (i < self.blocks))
        def _():
            fetched(i).wait()
            down = down_ref[lax.rem(i, 2)].reshape(block, -1)

            @pl.when(i == 0)
            def _():
                back_ref[...] = jnp.zeros_like(back_ref)

            grad = dot(grad_ref[...], down, NT) * slope_ref[:, block_at(i)].astype(jnp.float32)
            gu_ref[...] = grad.astype(low)
            for n in range(thirds):
                part = slice(n * third, (n + 1) * third)
                out_ref[:, part] += dot(hidden_ref[:, block_at(i)], down[:, part])
                back_ref[:, part] += dot(gu_ref[...], up_ref[part, :], NT)

        done = pltpu.make_async_copy(out_ref, output, local.at[12])
        first_out = pltpu.make_async_copy(back_ref, grad_first, local.at[13])
        low_out = pltpu.make_async_copy(acts_ref, grad_low, local.at[14])
        chunk = self.chunk

        def chunk_loads(j, slot):
            rows = pl.ds(pl.multiple_of(j * chunk, chunk), chunk)
            return [
                pltpu.make_async_copy(src.at[rows, :], chunks.at[slot, n], loads.at[slot, n])
                for n, src in enumerate((first_sum, cotangent))
            ]

        @pl.when(tick == self.norm - 1)
        def _():
            for copy in outs:
                copy.start()

        @pl.when(tick == self.norm)
        def _():
            done.start()
            sums_ref[...] = jnp.zeros_like(sums_ref)
            for copy in chunk_loads(0, 0):
                copy.start()
            total = tokens // chunk

            def norm_back(j, carry):
                slot = lax.rem(j, 2)

                @pl.when(j + 1 < total)
                def _():
                    for copy in chunk_loads(j + 1, 1 - slot):
                        copy.start()

                for copy in chunk_loads(j, slot):
                    copy.wait()
                rows = pl.ds(pl.multiple_of(j * chunk, chunk), chunk)
                values = chunks[slot, 0]
                centre = values - jnp.mean(values, axis=-1, keepdims=True)
                spread = lax.rsqrt(jnp.mean(centre * centre, axis=-1, keepdims=True) + EPSILON)
                normed = centre * spread
                grad = back_ref[rows, :]
                grown = grad * gain_ref[...]
                mean_one = jnp.mean(grown, axis=-1, keepdims=True)
                mean_two = jnp.mean(grown * normed, axis=-1, keepdims=True)
                made = chunks[slot, 1] + (grown - mean_one - normed * mean_two) * spread
                sums_ref[0:1] += jnp.sum(grad * normed, axis=0, keepdims=True)
                sums_ref[1:2] += jnp.sum(grad, axis=0, keepdims=True)
                back_ref[rows, :] = made
                acts_ref[rows, :] = made.astype(low)
                return carry

            lax.fori_loop(0, total, norm_back, 0)
            first_out.start()
            low_out.start()

        again = exchange(1, pairs, back_pairs)
        home = pltpu.make_async_copy(pairs.at[seq], back_pairs.at[seq], local.at[0])

        @pl.when(tick == self.norm + 1)
        def _():
            for copy in outs:
                copy.wait()
            per = width // (heads * HEAD_DIM)
            step = heads * HEAD_DIM
            for g in range(per):
                made = sum(
                    dot(acts_ref[:, n * third : (n + 1) * third],
                        turned_ref[n * width + g * step : n * width + (g + 1) * step, :], NT)
                    for n in range(thirds)
                ).astype(low)
                for s in range(count // per):
                    for p in range(heads):
                        pairs[s * per + g, p] = made[s * columns : (s + 1) * columns, p * HEAD_DIM : (p + 1) * HEAD_DIM]
            for copy in again + [home]:
                copy.start()

        @pl.when(tick == self.ticks - 1)
        def _():
            for copy in again + [home, done, first_out, low_out]:
                copy.wait()


def layer_norm(values, gain, offset):
    centre = values - jnp.mean(values, axis=-1, keepdims=True)
    spread = jnp.mean(centre * centre, axis=-1, keepdims=True)
    return centre * lax.rsqrt(spread + EPSILON) * gain + offset


def gelu(values):
    return 0.5 * values * (1.0 + lax.erf(values * (1.0 / math.sqrt(2.0))))


def angles(positions):
    half = HEAD_DIM // 2
    rates = jnp.exp(jnp.arange(half, dtype=jnp.float32) * (-math.log(10000.0) / half))
    turned = positions.astype(jnp.float32)[:, None] * rates[None, :]
    return (jnp.cos(turned)[:, None, :], jnp.sin(turned)[:, None, :])


def rotary(values, cosine, sine):
    half = values.shape[-1] // 2
    first = values[..., :half]
    second = values[..., half:]
    return jnp.concatenate(
        [first * cosine - second * sine, second * cosine + first * sine], axis=-1
    )


def lower(values):
    return values.astype(jnp.bfloat16)


def project(acts, weight):
    return jnp.einsum("gcd,de->gce", acts, weight, preferred_element_type=jnp.float32)


def project_back(grads, weight):
    return jnp.einsum("gce,de->gcd", grads, weight, preferred_element_type=jnp.float32)


def outer_sum(left, right):
    return jnp.einsum("gci,gcj->ij", left, right, preferred_element_type=jnp.float32)


def plain_shards(
    inputs,
    segments,
    norm1_gain,
    norm1_bias,
    w_query,
    w_key,
    w_value,
    w_out,
    norm2_gain,
    norm2_bias,
    w_up,
    w_down,
    cotangent,
):
    groups, columns, width = inputs.shape
    heads_count = width // HEAD_DIM
    scale = 1.0 / math.sqrt(HEAD_DIM)
    full_query, full_key, full_value, full_out, full_up, full_down = (
        lax.all_gather(w_query, ("dp", "seq"), axis=0, tiled=True),
        lax.all_gather(w_key, ("dp", "seq"), axis=0, tiled=True),
        lax.all_gather(w_value, ("dp", "seq"), axis=0, tiled=True),
        lax.all_gather(w_out, ("dp", "seq"), axis=0, tiled=True),
        lax.all_gather(w_up, ("dp", "seq"), axis=0, tiled=True),
        lax.all_gather(w_down, ("dp", "seq"), axis=0, tiled=True),
    )
    key_ids = lax.all_gather(segments, "seq", axis=1, tiled=True)
    length = key_ids.shape[1]
    rank = lax.axis_index("seq")
    places = rank * columns + jnp.arange(columns, dtype=jnp.int32)
    key_places = jnp.arange(length, dtype=jnp.int32)
    cosine, sine = angles(places)

    def turn(values):
        shaped = values.reshape(groups, columns, heads_count, HEAD_DIM)
        return rotary(shaped, cosine, sine).reshape(groups, columns, width)

    def permitted(segment_row, key_row):
        same = segment_row[:, None] == key_row[None, :]
        causal = key_places[None, :] <= places[:, None]
        live = (key_row[None, :] >= 0) | (key_places[None, :] == places[:, None])
        return same & causal & live

    def scores_of(query_row, key_block, segment_row, key_row):
        heads_query = query_row.reshape(columns, heads_count, HEAD_DIM)
        heads_key = key_block.reshape(length, heads_count, HEAD_DIM)
        raw = (
            jnp.einsum("chd,lhd->hcl", heads_query, heads_key, preferred_element_type=jnp.float32)
            * scale
        )
        return jnp.where(permitted(segment_row, key_row)[None], raw, MASKED)

    normed_one = layer_norm(inputs, norm1_gain, norm1_bias)
    act_one = lower(normed_one)
    query_zero = project(act_one, full_query)
    key_zero = project(act_one, full_key)
    value_low = lower(project(act_one, full_value))
    query_low = lower(turn(query_zero))
    key_low = lower(turn(key_zero))
    keys_all, values_all = (
        lax.all_gather(key_low, "seq", axis=1, tiled=True),
        lax.all_gather(value_low, "seq", axis=1, tiled=True),
    )

    def attend(items):
        query_row, key_block, value_block, segment_row, key_row = items
        scores = scores_of(query_row, key_block, segment_row, key_row)
        top = jnp.max(scores, axis=-1, keepdims=True)
        expo = jnp.exp(scores - top)
        total = jnp.sum(expo, axis=-1, keepdims=True)
        probs = lower(expo / total)
        heads_value = value_block.reshape(length, heads_count, HEAD_DIM)
        mixed = jnp.einsum("hcl,lhd->chd", probs, heads_value, preferred_element_type=jnp.float32)
        return (mixed.reshape(columns, width), top[..., 0] + jnp.log(total[..., 0]))

    mixed_all, log_totals = lax.map(attend, (query_low, keys_all, values_all, segments, key_ids))
    mixed_low = lower(mixed_all)
    first_sum = inputs + project(mixed_low, full_out)
    act_two = lower(layer_norm(first_sum, norm2_gain, norm2_bias))
    upper = project(act_two, full_up)
    hidden_low = lower(gelu(upper))
    output = first_sum + project(hidden_low, full_down)
    half_width = width // 2
    half_hidden = full_up.shape[1] // 2
    grad_out_low = lower(cotangent)
    down_left = outer_sum(hidden_low, grad_out_low[..., :half_width])
    down_right = outer_sum(hidden_low, grad_out_low[..., half_width:])
    grad_hidden = project_back(grad_out_low, full_down)
    gelu_values, gelu_back = jax.vjp(gelu, upper)
    grad_upper = lower(gelu_back(grad_hidden)[0])
    up_left = outer_sum(act_two, grad_upper[..., :half_hidden])
    up_right = outer_sum(act_two, grad_upper[..., half_hidden:])
    grad_act_two = project_back(grad_upper, full_up)
    normed_two, norm_two_back = jax.vjp(layer_norm, first_sum, norm2_gain, norm2_bias)
    grad_first_norm, gain_two_grad, offset_two_grad = norm_two_back(grad_act_two)
    grad_first = cotangent + grad_first_norm
    grad_attn_low = lower(grad_first)
    out_grad = outer_sum(mixed_low, grad_attn_low)
    grad_mixed = lower(project_back(grad_attn_low, full_out))
    heads_mixed = mixed_all.reshape(groups, columns, heads_count, HEAD_DIM)
    heads_gm = grad_mixed.astype(jnp.float32).reshape(groups, columns, heads_count, HEAD_DIM)
    deltas = jnp.transpose(jnp.sum(heads_mixed * heads_gm, axis=-1), (0, 2, 1))
    key_source, value_source = (key_low, value_low)

    def attend_back(carry, items):
        query_row, grad_row, log_row, delta_row, segment_row, key_row, key_part, value_part = items
        queries_all, grads_all = (
            lax.all_gather(query_row, "seq", axis=0, tiled=True),
            lax.all_gather(grad_row, "seq", axis=0, tiled=True),
        )
        logs_all, deltas_all = (
            lax.all_gather(log_row, "seq", axis=1, tiled=True),
            lax.all_gather(delta_row, "seq", axis=1, tiled=True),
        )
        own_mask = (segment_row[None, :] == key_row[:, None]) & (
            places[None, :] <= key_places[:, None]
        )
        own_mask = own_mask & (
            (segment_row[None, :] >= 0) | (places[None, :] == key_places[:, None])
        )
        heads_query = queries_all.reshape(length, heads_count, HEAD_DIM)
        heads_grad = grads_all.reshape(length, heads_count, HEAD_DIM)
        heads_key = key_part.reshape(columns, heads_count, HEAD_DIM)
        heads_value = value_part.reshape(columns, heads_count, HEAD_DIM)
        raw = (
            jnp.einsum("lhd,chd->hlc", heads_query, heads_key, preferred_element_type=jnp.float32)
            * scale
        )
        scores = jnp.where(own_mask[None], raw, MASKED)
        probs = jnp.exp(scores - logs_all[..., None])
        grad_probs = jnp.einsum(
            "lhd,chd->hlc", heads_grad, heads_value, preferred_element_type=jnp.float32
        )
        grad_scores = lower(probs * (grad_probs - deltas_all[..., None]))
        grad_values = jnp.einsum(
            "hlc,lhd->chd", lower(probs), heads_grad, preferred_element_type=jnp.float32
        )
        grad_keys = (
            jnp.einsum("hlc,lhd->chd", grad_scores, heads_query, preferred_element_type=jnp.float32)
            * scale
        )
        partial_query = (
            jnp.einsum("hlc,chd->lhd", grad_scores, heads_key, preferred_element_type=jnp.float32)
            * scale
        )
        grad_query = lax.psum_scatter(
            partial_query.reshape(length, width).astype(jnp.bfloat16),
            "seq",
            scatter_dimension=0,
            tiled=True,
        ).astype(jnp.float32)
        return (
            carry,
            (grad_query, grad_keys.reshape(columns, width), grad_values.reshape(columns, width)),
        )

    start_carry = jnp.zeros((), jnp.float32)
    end_carry, grads_seq = lax.scan(
        attend_back,
        start_carry,
        (query_low, grad_mixed, log_totals, deltas, segments, key_ids, key_source, value_source),
    )
    grad_query_all, grad_key_all, grad_value_all = grads_seq
    turned_query, turn_back = jax.vjp(turn, query_zero)
    grad_query_low = lower(turn_back(grad_query_all)[0])
    grad_key_low = lower(turn_back(grad_key_all)[0])
    grad_value_low = lower(grad_value_all)
    query_grad = outer_sum(act_one, grad_query_low)
    key_grad = outer_sum(act_one, grad_key_low)
    value_grad = outer_sum(act_one, grad_value_low)
    grad_act_one = project_back(grad_query_low, full_query) + project_back(grad_key_low, full_key)
    grad_act_one = grad_act_one + project_back(grad_value_low, full_value)
    normed_again, norm_one_back = jax.vjp(layer_norm, inputs, norm1_gain, norm1_bias)
    grad_input_norm, gain_one_grad, offset_one_grad = norm_one_back(grad_act_one)
    grad_input = grad_first + grad_input_norm
    summed = (
        lax.psum_scatter(query_grad, ("dp", "seq"), scatter_dimension=0, tiled=True),
        lax.psum_scatter(key_grad, ("dp", "seq"), scatter_dimension=0, tiled=True),
        lax.psum_scatter(value_grad, ("dp", "seq"), scatter_dimension=0, tiled=True),
        lax.psum_scatter(out_grad, ("dp", "seq"), scatter_dimension=0, tiled=True),
        lax.psum_scatter(up_left, ("dp", "seq"), scatter_dimension=0, tiled=True),
        lax.psum_scatter(up_right, ("dp", "seq"), scatter_dimension=0, tiled=True),
        lax.psum_scatter(down_left, ("dp", "seq"), scatter_dimension=0, tiled=True),
        lax.psum_scatter(down_right, ("dp", "seq"), scatter_dimension=0, tiled=True),
        lax.psum_scatter(gain_one_grad, ("dp", "seq"), scatter_dimension=0, tiled=True),
        lax.psum_scatter(offset_one_grad, ("dp", "seq"), scatter_dimension=0, tiled=True),
        lax.psum_scatter(gain_two_grad, ("dp", "seq"), scatter_dimension=0, tiled=True),
        lax.psum_scatter(offset_two_grad, ("dp", "seq"), scatter_dimension=0, tiled=True),
    )
    query_grad, key_grad, value_grad, out_grad = (summed[0], summed[1], summed[2], summed[3])
    up_left, up_right, down_left, down_right = (summed[4], summed[5], summed[6], summed[7])
    gain_one_grad, offset_one_grad, gain_two_grad, offset_two_grad = (
        summed[8],
        summed[9],
        summed[10],
        summed[11],
    )
    up_grad = jnp.concatenate([up_left, up_right], axis=1)
    down_grad = jnp.concatenate([down_left, down_right], axis=1)
    return (
        output,
        grad_input,
        gain_one_grad,
        offset_one_grad,
        query_grad,
        key_grad,
        value_grad,
        out_grad,
        gain_two_grad,
        offset_two_grad,
        up_grad,
        down_grad,
    )


def shards(
    inputs,
    segments,
    norm1_gain,
    norm1_bias,
    w_query,
    w_key,
    w_value,
    w_out,
    norm2_gain,
    norm2_bias,
    w_up,
    w_down,
    cotangent,
    *,
    plan,
):
    groups, columns, width = inputs.shape
    length = columns * plan.n_seq
    lag, piece = 2, 512
    every = plan.n_dp * plan.n_seq

    half = HEAD_DIM // 2
    rates = np.exp(np.arange(half, dtype=np.float32) * np.float32(-math.log(10000.0) / half))
    angle = (np.arange(length, dtype=np.float32)[:, None] * rates[None, :]).astype(np.float32)
    cosine = jnp.asarray(np.concatenate([np.cos(angle), np.cos(angle)], axis=1), jnp.float32)
    sine = jnp.asarray(np.concatenate([-np.sin(angle), np.sin(angle)], axis=1), jnp.float32)

    def flat(values):
        return values.reshape(groups * columns, width)

    act_one = lower(layer_norm(inputs, norm1_gain, norm1_bias))
    packed, turned_one, mixed, mixed_t, lse, seg_col, seg_row, _, _, heads_weight, full_out, full_up = attention(
        plan, act_one, segments, (w_query, w_key, w_value), cosine, sine, w_out, w_up, lag, 1
    )
    grad_low = lower(flat(cotangent))
    mlp = Mlp(
        plan, lag, mixed, full_out.reshape(width, width), flat(inputs), norm2_gain[None], norm2_bias[None],
        full_up.reshape(width, -1), grad_low, flat(cotangent), w_down,
    )
    rows = width // every

    def reduce_all(pairs, routes, collective_id, beside, first=0):
        out, *more = reduce_products(plan, pairs, rows, piece, lag, routes, collective_id, beside, first)
        results, at = [], 0
        for left, right in pairs:
            blocks = left if isinstance(left, int) else left.shape[0]
            cols = right.shape[1] // piece
            part = out[at : at + blocks * cols].reshape(blocks, cols, -1, piece)
            results.append(jnp.transpose(part, (0, 2, 1, 3)).reshape(-1, right.shape[1]))
            at += blocks * cols
        return results + more

    (
        down_grad, output, _, grad_first, grad_first_low, mixed_turned, acts_turned, grad_upper, grad_pairs,
        sums_two, _,
    ) = reduce_all([(w_down.shape[0] // rows, grad_low)], "even", 3, mlp, 14)
    work = Finish(
        plan, 0, packed, grad_pairs, mixed_t, lse, seg_col, seg_row, cosine, sine, turned_one,
        heads_weight.reshape(3, width, -1), inputs, grad_first.reshape(inputs.shape), norm1_gain[None], sums_two,
    )
    up_grad, out_grad, grad_input, heads_grad, norm_rows = reduce_all(
        [(acts_turned[None], grad_upper), (mixed_turned[None], grad_first_low)], "even", 4, work
    )
    return (
        output.reshape(inputs.shape),
        grad_input,
        norm_rows[:, 0],
        norm_rows[:, 1],
        heads_grad[0],
        heads_grad[1],
        heads_grad[2],
        out_grad,
        norm_rows[:, 2],
        norm_rows[:, 3],
        up_grad,
        down_grad,
    )


def fits(mesh, groups, columns, width, rows):
    return (
        mesh.shape["seq"] == 8
        and groups == 2
        and width % (4 * HEAD_DIM) == 0
        and columns == 256
        and rows % 16 == 0
    )


def solution(mesh):
    placed = (
        P("dp", "seq", None),
        P("dp", "seq"),
        P(),
        P(),
        P(("dp", "seq"), None),
        P(("dp", "seq"), None),
        P(("dp", "seq"), None),
        P(("dp", "seq"), None),
        P(),
        P(),
        P(("dp", "seq"), None),
        P(("dp", "seq"), None),
        P("dp", "seq", None),
    )
    plan = Plan(mesh)

    def layer(inputs, segments, *rest):
        groups, columns, width = inputs.shape
        if fits(mesh, groups, columns, width, rest[2].shape[0]):
            return shards(inputs, segments, *rest, plan=plan)
        return plain_shards(inputs, segments, *rest)

    return jax.shard_map(
        layer,
        mesh=mesh,
        in_specs=placed,
        out_specs=(
            P("dp", "seq", None),
            P("dp", "seq", None),
            P(("dp", "seq")),
            P(("dp", "seq")),
            P(("dp", "seq"), None),
            P(("dp", "seq"), None),
            P(("dp", "seq"), None),
            P(("dp", "seq"), None),
            P(("dp", "seq")),
            P(("dp", "seq")),
            P(("dp", "seq"), None),
            P(("dp", "seq"), None),
        ),
        check_vma=False,
    )
```

```python
import functools
import math

import jax
import jax.numpy as jnp
import numpy as np
from jax import lax
from jax.experimental import pallas as pl
from jax.experimental.pallas import tpu as pltpu
from jax.sharding import PartitionSpec as P

HEAD_DIM = 128


EPSILON = 1e-05
MASKED = -1e30
LOG2E = math.log2(math.e)
NT = (((1,), (1,)), ((), ()))
NN = (((1,), (0,)), ((), ()))


def dot(left, right, dims=NN):
    return lax.dot_general(left, right, dims, preferred_element_type=jnp.float32)


def allowed_pairs(key_col, query_row, diagonal):
    same = key_col == query_row
    if not diagonal:
        return same
    shape = (key_col.shape[0], query_row.shape[1])
    key_at = lax.broadcasted_iota(jnp.int32, shape, 0)
    query_at = lax.broadcasted_iota(jnp.int32, shape, 1)
    return (same & (key_at <= query_at)) | (key_at == query_at)


def attend_back_step(
    block, parts, pair, step, last, q_ref, k_ref, v_ref, g_ref, ot_ref, lse_ref, col_ref, row_ref, cos_ref, sin_ref,
    out_ref, kt_ref, dk_ref, dv_ref,
):
    scale = 1.0 / math.sqrt(HEAD_DIM)

    @pl.when(step == 0)
    def _():
        kt_ref[...] = k_ref[...].reshape(-1, HEAD_DIM).T
        dk_ref[...] = jnp.zeros_like(dk_ref)
        dv_ref[...] = jnp.zeros_like(dv_ref)

    query = q_ref[pl.ds(step * parts, parts)].reshape(block, HEAD_DIM)
    grad = g_ref[pl.ds(step * parts, parts)].reshape(block, HEAD_DIM)
    query_row = row_ref[pl.ds(step, 1), :]
    lse = lse_ref[0, pl.ds(step, 1), :]
    delta = jnp.sum(ot_ref[0, 0] * grad.astype(jnp.float32).T, axis=0, keepdims=True)
    unit = LOG2E * scale

    def visit(j, dqt, diagonal):
        at = pl.multiple_of(j * block, block)
        key = k_ref[pl.ds(j * parts, parts)].reshape(block, HEAD_DIM)
        value = v_ref[pl.ds(j * parts, parts)].reshape(block, HEAD_DIM)
        key_col = col_ref[pl.ds(at, block), :]
        scores = dot(key, query, NT) * unit - lse
        probs = jnp.where(allowed_pairs(key_col, query_row, diagonal), jnp.exp2(scores), 0.0)
        grad_probs = dot(value, grad, NT)
        grad_scores = (probs * (grad_probs - delta)).astype(jnp.bfloat16)
        dv_ref[pl.ds(at, block), :] += dot(probs.astype(jnp.bfloat16), grad)
        dk_ref[pl.ds(at, block), :] += dot(grad_scores, query)
        return dqt + dot(kt_ref[:, pl.ds(at, block)], grad_scores)

    dqt = lax.fori_loop(
        0, step, lambda j, c: visit(j, c, False), jnp.zeros((HEAD_DIM, block), jnp.float32)
    )
    dqt = visit(step, dqt, True)

    def turn_back(values, cosine, sine):
        return values * cosine - pltpu.roll(values, HEAD_DIM // 2, 1) * sine

    at = pl.multiple_of(step * block, block)
    dq = turn_back(dqt.T * scale, cos_ref[pl.ds(at, block), :], sin_ref[pl.ds(at, block), :])
    out_ref[pair, pl.ds(at, block), :HEAD_DIM] = dq.astype(jnp.bfloat16)

    @pl.when(step == last)
    def _():
        dk = turn_back(dk_ref[...] * scale, cos_ref[...], sin_ref[...])
        out_ref[pair, :, HEAD_DIM : 2 * HEAD_DIM] = dk.astype(jnp.bfloat16)
        out_ref[pair, :, 2 * HEAD_DIM :] = dv_ref[...].astype(jnp.bfloat16)


MESH = pl.DeviceIdType.MESH


class Plan:
    def __init__(self, mesh):
        self.n_dp, self.n_seq = mesh.shape["dp"], mesh.shape["seq"]
        bits = [1 << i for i in range(self.n_seq.bit_length() - 1)]
        self.bits = bits[::-1]
        if len(bits) == 3:
            self.orders = ((2, 4, 1), (4, 2, 1))
        else:
            turn = len(bits) // 2
            self.orders = (tuple(bits), tuple(bits[turn:] + bits[:turn]))
        self.hops = len(bits)
        self.masks = range(1, self.n_dp)
        straight = [("dp",) + order for order in self.orders]
        self.routes = {
            "even": [straight, straight],
            "late": [straight, [order[:1] + ("dp",) + order[1:] for order in self.orders]],
            "x late": [
                [("dp",) + self.orders[1]] * 2,
                [order[:1] + ("dp",) + order[1:] for order in self.orders],
            ],
        }

    def sems(self, route, stage):
        return sum(len(self.masks) if entry == "dp" else 1 for entry in route[:stage])

    def lead(self):
        return (self.n_dp,) + (2,) * self.hops


def place():
    return lax.axis_index("dp"), lax.axis_index("seq")


def partner_dp(plan, mask):
    dp, seq = place()
    return (lax.bitwise_xor(dp, mask), seq)


def partner_seq(bit):
    dp, seq = place()
    return (dp, lax.bitwise_xor(seq, bit))


def own_bit(bit):
    return lax.bitwise_and(lax.div(place()[1], bit), 1)


def greet(plan, everyone=False):
    barrier = pltpu.get_barrier_semaphore()
    others = [partner_dp(plan, m) for m in plan.masks]
    others += [partner_seq(m) for m in (range(1, plan.n_seq) if everyone else plan.bits)]
    for other in others:
        pl.semaphore_signal(barrier, inc=1, device_id=other, device_id_type=MESH)
    pl.semaphore_wait(barrier, len(others))


def reduce_kernel(plan, jobs, first, count, lag, routes, beside, *refs):
    k, given = len(jobs), sum(job[3] for job in jobs)
    lefts, rights, refs = iter(refs[:given]), refs[given : given + k], refs[given + k :]
    more = [0, 0, 0] if beside is None else [len(beside.in_specs), len(beside.out_specs), len(beside.scratch)]
    extra, refs = refs[: more[0]], refs[more[0] :]
    out_ref, extra = refs[0], extra + refs[1 : 1 + more[1]]
    scratch = refs[1 + more[1] :]
    extra, scratch = extra + scratch[: more[2]], scratch[more[2] :]
    hops, slots = plan.hops, 2 * lag
    stages = hops + 1
    kinds = 1 if routes[0] == routes[1] else 2
    sums, got = [], []
    for h in range(2):
        more = (kinds - 1, 2 * (kinds - 1))
        sums.append(scratch[: stages + more[0]])
        got.append(scratch[stages + more[0] : 2 * stages + sum(more)])
        scratch = scratch[2 * stages + sum(more) :]
    send, recv = scratch
    tick = pl.program_id(0)
    half = out_ref.shape[-1] // 2
    rows = out_ref.shape[-2]
    dp, _ = place()

    @pl.when(tick == 0)
    def _():
        greet(plan, getattr(beside, "everyone", False))

    def sums_at(h, kind, stage, u):
        if stage < stages - 1 or kinds == 1:
            return sums[h][stage], lax.rem(u, lag)
        return sums[h][stage + kind], 0

    def got_at(h, kind, stage, u):
        if stage < stages - 2 or kinds == 1:
            return got[h][stage], lax.rem(u, slots)
        return got[h][stage + 2 * kind], lax.rem(lax.div(u, 2), lag)

    def at_entry(h, kind, stage, value):
        route = routes[kind][h]
        left = [d for d in ("dp",) + tuple(plan.bits) if d not in route[:stage]]
        return tuple(value if d == route[stage] else slice(None) for d in left)

    def own(entry):
        return dp if entry == "dp" else own_bit(entry)

    def copies(h, kind, stage, u):
        route = routes[kind][h]
        entry = route[stage]
        src, kept = sums_at(h, kind, stage, u)
        dst, slot = got_at(h, kind, stage, u)
        at = h * (hops + len(plan.masks)) + plan.sems(route, stage)
        sem = lax.rem(u, slots)
        if entry != "dp":
            return [pltpu.make_async_remote_copy(
                src.at[(kept,) + at_entry(h, kind, stage, 1 - own(entry))], dst.at[slot],
                send.at[sem, at], recv.at[sem, at], device_id=partner_seq(entry), device_id_type=MESH)]
        return [
            pltpu.make_async_remote_copy(
                src.at[(kept,) + at_entry(h, kind, stage, lax.bitwise_xor(dp, mask))], dst.at[slot, n],
                send.at[sem, at + n], recv.at[sem, at + n], device_id=partner_dp(plan, mask), device_id_type=MESH)
            for n, mask in enumerate(plan.masks)
        ]

    def wide(values):
        return values.astype(jnp.float32)

    for stage in reversed(range(1, stages + 1)):
        u = tick - first - lag * stage
        for kind in range(kinds):
            due = (u >= 0) & (u < count)
            if kinds > 1:
                due = due & (lax.rem(u, 2) == kind)

            @pl.when(due)
            def _(stage=stage, kind=kind, u=u):
                for h in range(2):
                    for copy in copies(h, kind, stage - 1, u):
                        copy.wait()
                    entry = routes[kind][h][stage - 1]
                    src, kept = sums_at(h, kind, stage - 1, u)
                    dst, slot = got_at(h, kind, stage - 1, u)
                    total = wide(src[(kept,) + at_entry(h, kind, stage - 1, own(entry))])
                    if entry == "dp":
                        for n in range(len(plan.masks)):
                            total = total + wide(dst[slot, n])
                    else:
                        total = total + wide(dst[slot])
                    if stage == stages:
                        out_ref[0, :, h * half : (h + 1) * half] = total
                        continue
                    to, at = sums_at(h, kind, stage, u)
                    to[at] = total.astype(jnp.bfloat16)
                    for copy in copies(h, kind, stage, u):
                        copy.start()

    for (start, stop, cols, has_left), right in zip(jobs, rights):
        if has_left:
            left = next(lefts)

            def left_rows(which, z, left=left):
                step = rows * plan.n_seq
                return left[which, z * step : (z + 1) * step, :]

        else:
            left_rows = functools.partial(beside.left, extra)

        @pl.when((tick >= first + start) & (tick < first + stop))
        def _(start=start, cols=cols, left_rows=left_rows, right=right):
            u = tick - first
            kept = lax.rem(u, lag)
            which = lax.div(u - start, cols)
            for z in range(plan.n_dp):
                part = dot(left_rows(which, z), right[...]).astype(jnp.bfloat16)
                for h in range(2):
                    piece = part[:, h * half : (h + 1) * half]
                    sums[h][0][kept, z] = piece.reshape(plan.lead()[1:] + (rows, half))
            for h in range(2):
                for copy in copies(h, 0, 0, u):
                    copy.start()

    if beside is not None:
        beside.run(tick, extra)


def reduce_products(plan, pairs, rows, width, lag, routes, collective_id, beside=None, first=0):
    jobs, start = [], 0
    left_specs, right_specs = [], []
    for left, right in pairs:
        cols = right.shape[1] // width
        blocks = left if isinstance(left, int) else left.shape[0]
        stop = start + blocks * cols
        jobs.append((start, stop, cols, left is not blocks))
        if left is not blocks:
            left_specs.append(pl.BlockSpec(left.shape, lambda t: (0, 0, 0), pipeline_mode=pl.Buffered(1)))
        right_specs.append(pl.BlockSpec(
            (right.shape[0], width),
            functools.partial(lambda t, start, stop, cols: (0, lax.rem(jnp.clip(t - first, start, stop - 1) - start, cols)),
                start=start, stop=stop, cols=cols)))
        start = stop
    count = start
    half = width // 2
    slots, hops = 2 * lag, plan.hops
    tail = lag * (hops + 1)
    n_dp, masks = plan.n_dp, len(plan.masks)
    low = jnp.bfloat16

    def room(*shape):
        return pltpu.VMEM(shape + (rows, half), low)

    routes = [[route[::-1] for route in kind] for kind in plan.routes[routes]]

    def left(kind, stage):
        return [n_dp if d == "dp" else 2 for d in ("dp",) + tuple(plan.bits) if d not in routes[kind][0][:stage]]

    def arriving(kind, stage):
        return [masks] * (routes[kind][0][stage] == "dp") + left(kind, stage + 1)

    buffers = []
    for _ in range(2):
        if routes[0] == routes[1]:
            buffers += [room(lag, *left(0, s)) for s in range(hops + 1)]
            buffers += [room(slots, *arriving(0, s)) for s in range(hops + 1)]
            continue
        buffers += [room(lag, *left(0, s)) for s in range(hops)] + [room(1, *left(k, hops)) for k in range(2)]
        buffers += [room(slots, *arriving(0, s)) for s in range(hops - 1)]
        buffers += [room(lag, *arriving(k, s)) for k in range(2) for s in (hops - 1, hops)]
    each = 2 * (hops + len(plan.masks))
    out_specs = [pl.BlockSpec((1, rows, width), lambda t: (jnp.clip(t - first - tail, 0, count - 1), 0, 0))]
    out_shapes = [jax.ShapeDtypeStruct((count, rows, width), jnp.float32)]
    more_in, more_scratch, more_operands = [], [], []
    if beside is not None:
        more_in, more_scratch, more_operands = beside.in_specs, beside.scratch, beside.operands
        out_specs, out_shapes = out_specs + beside.out_specs, out_shapes + beside.out_shapes
    return pl.pallas_call(
        functools.partial(reduce_kernel, plan, jobs, first, count, lag, routes, beside),
        grid=(max(first + count + tail, 0 if beside is None else beside.ticks),),
        in_specs=left_specs + right_specs + more_in,
        out_specs=out_specs,
        out_shape=out_shapes,
        scratch_shapes=more_scratch + buffers + [
            pltpu.SemaphoreType.DMA((slots, each)),
            pltpu.SemaphoreType.DMA((slots, each)),
        ],
        compiler_params=pltpu.CompilerParams(
            collective_id=collective_id, has_side_effects=True, vmem_limit_bytes=63 << 20),
    )(*[p[0] for p in pairs if not isinstance(p[0], int)], *[p[1] for p in pairs], *more_operands)


class Copies:
    def __init__(self, send, recv):
        self.send, self.recv, self.count, self.sent = send, recv, 0, []

    def remote(self, src, dst, device):
        at = self.count
        self.count += 1
        return pltpu.make_async_remote_copy(
            src, dst, self.send.at[at], self.recv.at[at], device_id=device, device_id_type=MESH)

    def run(self, pieces, lag, tick=None):
        last = max(start + lag * len(stages) for start, stages in pieces)
        for now in range(min(start for start, _ in pieces), last + 1):
            due = [
                (start, stages, stage)
                for stage in reversed(range(max(len(stages) for _, stages in pieces) + 1))
                for start, stages in pieces
                if start + lag * stage == now and stage <= len(stages)
            ]

            def step(due=due, now=now):
                for start, stages, stage in due:
                    if stage > 0:
                        for copy in stages[stage - 1][1]:
                            copy.wait()
                    if stage < len(stages):
                        ahead, copies = stages[stage]
                        if ahead is not None:
                            ahead()
                        for copy in copies:
                            copy.start()

            if tick is None:
                step()
            elif due:
                pl.when(tick == now)(step)
        return last


def arrive(plan, lag, tick, h_ref, s_ref, weights, hs_ref, ss_ref, w_ref, hv, wv, halves, send, recv, local):
    dp, seq = place()
    y, x, c = own_bit(4), own_bit(2), own_bit(1)
    loads = [pltpu.make_async_copy(h_ref.at[y], hv, local.at[0])]
    loads += [pltpu.make_async_copy(r, wv.at[i], local.at[1 + i]) for i, r in enumerate(weights)]
    own = pltpu.make_async_copy(hv, hs_ref.at[y, x, c], local.at[0])
    named = pltpu.make_async_copy(s_ref.at[y], ss_ref.at[y, x, c], local.at[4])

    @pl.when(tick == 0)
    def _():
        for load in loads:
            load.start()
        named.start()
        for load in loads:
            load.wait()
        own.start()

    run = Copies(send, recv)
    pieces = []
    pieces.append((0, [
        (None, [run.remote(s_ref.at[1 - y], ss_ref.at[y, x, c], partner_seq(4))]),
        (named.wait, [run.remote(ss_ref.at[:, x, c], ss_ref.at[:, x, c], partner_seq(2))]),
        (None, [run.remote(ss_ref.at[:, :, c], ss_ref.at[:, :, c], partner_seq(1))]),
    ]))
    tokens = hv.shape[0]
    parts = 4
    for i in range(parts):
        rows = pl.ds(i * (tokens // parts), tokens // parts)
        first = run.remote(h_ref.at[1 - y, rows], hs_ref.at[y, x, c, rows], partner_seq(4))
        second = [run.remote(hs_ref.at[:, x, c, rows], hs_ref.at[:, x, c, rows], partner_seq(2))]
        third = [run.remote(hs_ref.at[:, :, c, rows], hs_ref.at[:, :, c, rows], partner_seq(1))]
        pieces.append((ACTS_AT + i, [(None, [first]), (own.wait if i == 0 else None, second), (None, third)]))

    half, quarter = halves.shape[-1], w_ref.shape[-1]
    for i in range(3):
        mine = pltpu.make_async_copy(
            halves.at[i, :, :, pl.ds(c * quarter, quarter)], w_ref.at[i, dp, y, :, c], local.at[1 + i])

        def cut(i=i, mine=mine):
            halves[i, x] = wv[i, :, pl.ds(pl.multiple_of(x * half, 128), half)]
            mine.start()

        to_x = [run.remote(wv.at[i, :, pl.ds((1 - x) * half, half)], halves.at[i, x], partner_seq(2))]
        to_core = [run.remote(
            halves.at[i, :, :, pl.ds((1 - c) * quarter, quarter)], w_ref.at[i, dp, y, :, c], partner_seq(1))]
        to_z = [run.remote(w_ref.at[i, dp, y], w_ref.at[i, dp, y], partner_dp(plan, m)) for m in plan.masks]
        to_y = [run.remote(w_ref.at[i, :, y], w_ref.at[i, :, y], partner_seq(4))]
        pieces.append((WEIGHTS_AT[i], [(None, to_x), (cut, to_core), (mine.wait, to_z), (None, to_y)]))
    run.run(pieces, ARRIVE_LAG, tick)


ARRIVE_LAG = 2
ACTS_AT, WEIGHTS_AT = 2, (0, 2, 3)
ARRIVED = max(ACTS_AT + 3 + 3 * ARRIVE_LAG, WEIGHTS_AT[-1] + 4 * ARRIVE_LAG)


class Finish:
    everyone = True

    def __init__(
        self, plan, first, packed, grads, mixed_t, lse, seg_col, seg_row, cosine, sine, turned, weights, inputs, grad_first, gain, more
    ):
        count, per, _, columns, _ = packed.shape
        length = count * columns
        self.plan, self.first = plan, first
        self.block = seg_row.shape[1]
        self.steps, self.parts = length // self.block, self.block // columns
        self.count = per * self.steps
        self.begin = first + self.count
        self.split = 4
        self.operands = (
            packed, packed, packed, grads, mixed_t, lse, seg_col, seg_row, cosine, sine, turned, weights, inputs, grad_first, gain, more
        )
        width, quarter = turned.shape[0], weights.shape[2]
        n_dp, masks = plan.n_dp, len(plan.masks)
        rows = width // (8 * n_dp)
        size = columns // self.split
        low = jnp.bfloat16

        def pair(t):
            return lax.div(jnp.clip(t - first, 0, self.count - 1), self.steps)

        def step(t):
            return lax.rem(jnp.clip(t - first, 0, self.count - 1), self.steps)

        def whole(which):
            return pl.BlockSpec(
                (count, None, None, columns, HEAD_DIM), lambda t: (0, pair(t), which, 0, 0), pipeline_mode=pl.Buffered(1))

        def fixed(shape):
            return pl.BlockSpec(shape, lambda t: (0,) * len(shape), pipeline_mode=pl.Buffered(1))

        hbm = pl.BlockSpec(memory_space=pl.ANY)
        self.in_specs = [
            whole(0),
            whole(1),
            whole(2),
            pl.BlockSpec((count, None, columns, HEAD_DIM), lambda t: (0, pair(t), 0, 0), pipeline_mode=pl.Buffered(1)),
            pl.BlockSpec((1, 1, HEAD_DIM, self.block), lambda t: (pair(t), step(t), 0, 0)),
            pl.BlockSpec((1, self.steps, self.block), lambda t: (pair(t), 0, 0)),
            fixed((length, 1)),
            fixed((self.steps, self.block)),
            fixed((length, HEAD_DIM)),
            fixed((length, HEAD_DIM)),
            hbm,
            hbm,
            hbm,
            hbm,
            pl.BlockSpec((width,), lambda t: (0,), pipeline_mode=pl.Buffered(1)),
            fixed((8, width)),
        ]
        self.out_specs = [
            hbm,
            pl.BlockSpec((3, rows, width), lambda t: (0, 0, 0)),
            pl.BlockSpec((rows, 128), lambda t: (0, 0)),
        ]
        self.out_shapes = [
            jax.ShapeDtypeStruct(inputs.shape, jnp.float32),
            jax.ShapeDtypeStruct((3, rows, width), jnp.float32),
            jax.ShapeDtypeStruct((rows, 128), jnp.float32),
        ]
        self.copies = 3 * (3 + masks) + 3 * self.split + 7 + masks
        self.scratch = [
            pltpu.VMEM((HEAD_DIM, length), low),
            pltpu.VMEM((length, HEAD_DIM), jnp.float32),
            pltpu.VMEM((length, HEAD_DIM), jnp.float32),
            pltpu.VMEM((3, length, quarter), low),
            pltpu.VMEM(turned.shape, low),
            pltpu.VMEM(weights.shape, low),
            pltpu.VMEM((2, 2, size, width), jnp.float32),
            pltpu.VMEM((2, 2, size, width), jnp.float32),
            pltpu.VMEM((2, n_dp, 2, 2, 2, rows, quarter), low),
            pltpu.VMEM((3, n_dp, 2, 2, rows, quarter), low),
            pltpu.VMEM((3, masks, 2, 2, rows, quarter), low),
            pltpu.VMEM((3, 2, 2, rows, quarter), low),
            pltpu.VMEM((3, 2, rows, 2 * quarter), low),
            pltpu.VMEM((3, rows, 2 * quarter), low),
            pltpu.VMEM((2, 2, 2, 2, size, width), low),
            pltpu.VMEM((2, 2, 2, size, width), low),
            pltpu.VMEM((2, 2, 2, size, width), low),
            pltpu.VMEM((2, 2, size, width), low),
            pltpu.VMEM((2, 2, size, width), low),
            pltpu.VMEM((2, size, width), low),
            pltpu.VMEM((128, width), jnp.float32),
            pltpu.VMEM((n_dp, 2, 2, 2, rows, 128), low),
            pltpu.VMEM((7, n_dp, rows, 128), low),
            pltpu.VMEM((n_dp, rows, 128), low),
            pltpu.VMEM((masks, rows, 128), low),
            pltpu.SemaphoreType.DMA((self.copies,)),
            pltpu.SemaphoreType.DMA((self.copies,)),
            pltpu.SemaphoreType.DMA((2,)),
            pltpu.SemaphoreType.DMA((2, 3)),
        ]
        backs, products = [2 * i for i in range(self.split)], [(i - per + 1) * self.steps + 4 for i in range(per)]
        self.starts = backs, products
        self.last_norm = backs[-1] + 2 * 3 + 1
        self.ticks = self.begin + max(self.last_norm + 2 * 2, products[-1] + 4 * 4) + 1

    def run(self, tick, refs):
        ins, (dx_ref, dw_ref, dn_ref), scratch = refs[:16], refs[16:19], refs[19:]
        turned_any, weights_any, inputs_any, first_any, gain_ref, more_ref = ins[10:16]
        kt_ref, dk_ref, dv_ref, g_ref, t_ref, w_ref, x_ref, gx_ref = scratch[:8]
        made, made_y, made_z, sum_z, sides, made_x = scratch[8:14]
        acts, acts_c, sum_c, acts_x, sum_x, acts_y = scratch[14:20]
        totals, norms, norms_c, norms_sy, norms_z = scratch[20:25]
        send, recv, local, chunked = scratch[25:]
        plan, parts = self.plan, self.split
        dp, _ = place()
        y, x, c = own_bit(4), own_bit(2), own_bit(1)
        width, length = t_ref.shape
        quarter = w_ref.shape[2]
        columns = length // 8
        half = 2 * quarter
        rows = dw_ref.shape[1]
        size = columns // parts
        low = jnp.bfloat16
        loads = [
            pltpu.make_async_copy(weights_any, w_ref, local.at[0]),
            pltpu.make_async_copy(turned_any, t_ref, local.at[1]),
        ]

        @pl.when(tick == 1)
        def _():
            for load in loads:
                load.start()

        @pl.when((tick >= self.first) & (tick < self.begin))
        def _():
            pair, step = lax.div(tick - self.first, self.steps), lax.rem(tick - self.first, self.steps)
            attend_back_step(self.block, self.parts, pair, step, self.steps - 1, *ins[:10], g_ref, kt_ref, dk_ref, dv_ref)

        masks = len(plan.masks)
        now = tick - self.begin

        def wide(values):
            return values.astype(jnp.float32)

        def stream(starts, stages, lag, base, most):
            gap = starts[1] - starts[0]
            for stage in reversed(range(len(stages))):
                since = now - starts[0] - lag * stage
                i = lax.div(since, gap)

                @pl.when((since >= 0) & (since <= starts[-1] - starts[0]) & (lax.rem(since, gap) == 0))
                def _(stage=stage, i=i):
                    def made_copies(n):
                        at = base + i * most + sum(len(c(0)) for _, c in stages[:n])
                        return [
                            pltpu.make_async_remote_copy(
                                src, dst, send.at[at + k], recv.at[at + k], device_id=other, device_id_type=MESH)
                            for k, (src, dst, other) in enumerate(stages[n][1](i))
                        ]

                    if stage > 0:
                        for copy in made_copies(stage - 1):
                            copy.wait()
                    stages[stage][0](i)
                    for copy in made_copies(stage):
                        copy.start()

        def product(i):
            @pl.when(i == 0)
            def _():
                loads[1].wait()

            step = 8 * rows
            for z in range(plan.n_dp):
                part = dot(t_ref[z * step : (z + 1) * step, :], g_ref[i])
                made[lax.rem(i, 2), z] = part.astype(low).reshape(2, 2, 2, rows, quarter)

        def product_y(i):
            made_y[i] = (wide(made[lax.rem(i, 2), :, y]) + wide(made_y[i])).astype(low)

        def product_z(i):
            total = wide(made_y[i, dp])
            for n in range(masks):
                total = total + wide(made_z[i, n])
            sum_z[i] = total.astype(low)

        def product_c(i):
            sides[i, :, :, pl.ds(pl.multiple_of(c * quarter, 128), quarter)] = sum_z[i, :, c]

        def product_x(i):
            for side, values in ((x, sides.at[i, x]), (1 - x, made_x.at[i])):
                for core in range(2):
                    for kind in range(3):
                        start = core * quarter + kind * HEAD_DIM
                        lanes = pl.ds(pl.multiple_of(side * half + core * quarter + i * HEAD_DIM, HEAD_DIM), HEAD_DIM)
                        dw_ref[kind, :, lanes] = wide(values[:, start : start + HEAD_DIM])

        def back(i):
            @pl.when(i == 0)
            def _():
                loads[0].wait()

            slot = lax.rem(i, 2)
            pieces = []
            for k in range(3):
                blocks = []
                for n in range(8):
                    at = pl.ds(pl.multiple_of(n * columns + i * size, size), size)
                    blocks.append(jnp.concatenate(
                        [g_ref[p, at, k * HEAD_DIM : (k + 1) * HEAD_DIM] for p in range(3)], axis=1))
                pieces.append(jnp.concatenate(blocks, axis=0))
            step = 512
            for n in range(width // step):
                total = sum(dot(pieces[k], w_ref[k, n * step : (n + 1) * step, :], NT) for k in range(3))
                acts[slot, :, :, :, :, n * step : (n + 1) * step] = total.astype(low).reshape(2, 2, 2, size, step)

        def back_c(i):
            slot = lax.rem(i, 2)
            sum_c[slot] = (wide(acts[slot, :, :, c]) + wide(acts_c[slot])).astype(low)

        def chunk(i):
            slot, at = lax.rem(i, 2), pl.ds(pl.multiple_of(i * size, size), size)
            return [
                pltpu.make_async_copy(inputs_any.at[:, at], x_ref.at[slot], chunked.at[slot, 0]),
                pltpu.make_async_copy(first_any.at[:, at], gx_ref.at[slot], chunked.at[slot, 1]),
            ]

        def chunk_out(i):
            slot, at = lax.rem(i, 2), pl.ds(pl.multiple_of(i * size, size), size)
            return pltpu.make_async_copy(gx_ref.at[slot], dx_ref.at[:, at], chunked.at[slot, 2])

        def back_x(i):
            slot = lax.rem(i, 2)

            @pl.when(i >= 2)
            def _():
                chunk_out(i - 2).wait()

            for load in chunk(i):
                load.start()
            sum_x[slot] = (wide(sum_c[slot, :, x]) + wide(acts_x[slot])).astype(low)

        def norm_back(i):
            slot = lax.rem(i, 2)
            for load in chunk(i):
                load.wait()

            @pl.when(i == 0)
            def _():
                totals[...] = jnp.zeros_like(totals)

            gain = gain_ref[...][None]

            def one(s, carry):
                grad = jnp.where(y == s, wide(sum_x[slot, s]), wide(acts_y[slot]))
                values = x_ref[slot, s]
                centre = values - jnp.mean(values, axis=-1, keepdims=True)
                spread = lax.rsqrt(jnp.mean(centre * centre, axis=-1, keepdims=True) + EPSILON)
                normed = centre * spread
                grown = grad * gain
                mean_one = jnp.mean(grown, axis=-1, keepdims=True)
                mean_two = jnp.mean(grown * normed, axis=-1, keepdims=True)
                gx_ref[slot, s] = gx_ref[slot, s] + (grown - mean_one - normed * mean_two) * spread
                totals[0:1] += jnp.sum(grad * normed, axis=0, keepdims=True)
                totals[1:2] += jnp.sum(grad, axis=0, keepdims=True)
                return carry

            lax.fori_loop(0, 2, one, 0)
            chunk_out(i).start()

        stream(self.starts[0], [
            (back, lambda i: [(acts.at[lax.rem(i, 2), :, :, 1 - c], acts_c.at[lax.rem(i, 2)], partner_seq(1))]),
            (back_c, lambda i: [(sum_c.at[lax.rem(i, 2), :, 1 - x], acts_x.at[lax.rem(i, 2)], partner_seq(2))]),
            (back_x, lambda i: [(sum_x.at[lax.rem(i, 2), 1 - y], acts_y.at[lax.rem(i, 2)], partner_seq(4))]),
            (norm_back, lambda i: []),
        ], 2, 0, 3)
        stream(self.starts[1], [
            (product, lambda i: [(made.at[lax.rem(i, 2), :, 1 - y], made_y.at[i], partner_seq(4))]),
            (product_y, lambda i: [
                (made_y.at[i, lax.bitwise_xor(dp, m)], made_z.at[i, n], partner_dp(plan, m))
                for n, m in enumerate(plan.masks)]),
            (product_z, lambda i: [
                (sum_z.at[i, :, 1 - c], sides.at[i, :, :, pl.ds(c * quarter, quarter)], partner_seq(1))]),
            (product_c, lambda i: [(sides.at[i, 1 - x], made_x.at[i], partner_seq(2))]),
            (product_x, lambda i: []),
        ], 4, 3 * parts, 3 + masks)
        run = Copies(send, recv)
        run.count = 3 * parts + 3 * (3 + masks)
        pieces = []

        def norms_start():
            totals[2:4] = more_ref[0:2]
            norms[...] = totals[...].T.astype(low).reshape(norms.shape)

        def norms_end():
            total = wide(norms_sy[dp])
            for n in range(len(plan.masks)):
                total = total + wide(norms_z[n])
            dn_ref[...] = total
            for i in range(parts - 2, parts):
                chunk_out(i).wait()

        _, seq = place()

        def norms_to(m):
            return norms.at[(slice(None),) + tuple(lax.bitwise_xor(own_bit(b), int(m & b > 0)) for b in plan.bits)]

        def norms_seq():
            total = wide(norms[:, y, x, c])
            for m in range(1, 8):
                total = total + wide(norms_c[m - 1])
            norms_sy[...] = total.astype(low)

        pieces.append((self.last_norm, [
            (norms_start, [run.remote(norms_to(m), norms_c.at[m - 1], partner_seq(m)) for m in range(1, 8)]),
            (norms_seq, [
                run.remote(norms_sy.at[lax.bitwise_xor(dp, m)], norms_z.at[n], partner_dp(plan, m))
                for n, m in enumerate(plan.masks)]),
            (norms_end, []),
        ]))
        run.run(pieces, 2, now)


class Gather:
    def __init__(self, plan, lag, shard, rows, cols, routes):
        self.plan, self.lag, self.rows, self.cols = plan, lag, rows, cols
        self.routes = plan.routes[routes]
        self.across = shard.shape[1] // cols
        self.pieces = shard.shape[0] // rows * self.across
        self.ticks = self.pieces + lag * (plan.hops + 1)
        self.out_shape = jax.ShapeDtypeStruct(plan.lead() + shard.shape, shard.dtype)
        each = 2 * (len(plan.masks) + plan.hops)
        self.scratch = [
            pltpu.VMEM(shard.shape, shard.dtype),
            pltpu.SemaphoreType.DMA((self.pieces, each)),
            pltpu.SemaphoreType.DMA((self.pieces, each)),
            pltpu.SemaphoreType.DMA((2,)),
        ]

    def copies(self, kind, stage, u, full, held, send, recv):
        plan = self.plan
        dp, _ = place()
        rows = pl.ds(pl.multiple_of(lax.div(u, self.across) * self.rows, 16), self.rows)
        out = []
        for h in range(2):
            start = lax.rem(u, self.across) * self.cols + h * (self.cols // 2)
            cols = pl.ds(pl.multiple_of(start, 128), self.cols // 2)
            route = self.routes[kind][h]
            entry, done = route[stage], route[:stage]
            where = (slice(None) if "dp" in done else dp,)
            where += tuple(slice(None) if b in done else own_bit(b) for b in plan.bits)
            part = full.at[where + (rows, cols)]
            src = part if stage else held.at[rows, cols]
            at = h * (len(plan.masks) + plan.hops) + plan.sems(route, stage)
            others = [partner_dp(plan, m) for m in plan.masks] if entry == "dp" else [partner_seq(entry)]
            for n, other in enumerate(others):
                out.append(pltpu.make_async_remote_copy(
                    src, part, send.at[u, at + n], recv.at[u, at + n], device_id=other, device_id_type=MESH))
        return out

    def run(self, tick, shard, full, held, send, recv, local):
        plan, lag = self.plan, self.lag
        dp, _ = place()
        me = tuple(own_bit(b) for b in plan.bits)
        own = pltpu.make_async_copy(held, full.at[(dp,) + me], local.at[0])

        @pl.when(tick == 0)
        def _():
            load = pltpu.make_async_copy(shard, held, local.at[1])
            load.start()
            load.wait()
            own.start()

        @pl.when(tick == lag)
        def _():
            own.wait()

        stages = plan.hops + 1
        for stage in reversed(range(stages + 1)):
            u = tick - lag * stage
            kinds = 1 if self.routes[0] == self.routes[1] else 2
            for kind in range(kinds):

                @pl.when((u >= 0) & (u < self.pieces) & (lax.rem(u, 2) == kind if kinds > 1 else True))
                def _(stage=stage, u=u, kind=kind):
                    if stage > 0:
                        for copy in self.copies(kind, stage - 1, u, full, held, send, recv):
                            copy.wait()
                    if stage < stages:
                        for copy in self.copies(kind, stage, u, full, held, send, recv):
                            copy.start()


def attend_step(block, parts, pair, step, packed, col_ref, row_ref, o_ref, ot_ref, lse_ref, vt_ref):
    @pl.when(step == 0)
    def _():
        vt_ref[...] = packed[:, pair, 2].reshape(-1, HEAD_DIM).T

    query = packed[pl.ds(step * parts, parts), pair, 0].reshape(block, HEAD_DIM)
    query_row = row_ref[pl.ds(step, 1), :]
    unit = LOG2E / math.sqrt(HEAD_DIM)

    def visit(j, carry, diagonal):
        top, total, mixed = carry
        key = packed[pl.ds(j * parts, parts), pair, 1].reshape(block, HEAD_DIM)
        at = pl.multiple_of(j * block, block)
        scores = dot(key, query, NT) * unit
        scores = jnp.where(allowed_pairs(col_ref[pl.ds(at, block), :], query_row, diagonal), scores, MASKED)
        above = jnp.maximum(top, jnp.max(scores, axis=0, keepdims=True))
        expo = jnp.exp2(scores - above)
        fade = jnp.exp2(top - above)
        total = total * fade + jnp.sum(expo, axis=0, keepdims=True)
        mixed = mixed * fade + dot(vt_ref[:, pl.ds(at, block)], expo.astype(jnp.bfloat16))
        return above, total, mixed

    start = (
        jnp.full((1, block), MASKED, jnp.float32),
        jnp.zeros((1, block), jnp.float32),
        jnp.zeros((HEAD_DIM, block), jnp.float32),
    )
    carry = lax.fori_loop(0, step, lambda j, c: visit(j, c, False), start)
    top, total, mixed = visit(step, carry, True)
    mixed = mixed / total
    ot_ref[0, 0] = mixed
    lse_ref[0, pl.ds(step, 1), :] = top + jnp.log2(total)
    o_ref[...] = mixed.T.astype(jnp.bfloat16).reshape(o_ref.shape)


def attention_kernel(
    plan, lag, gathers, block, steps, h_ref, s_ref, q_ref, k_ref, v_ref, cos_ref, sin_ref, out_shard, up_shard,
    packed, turned_ref, o_ref, ot_ref, lse_ref, col_ref, row_ref, hs_ref, ss_ref, w_ref, full_out, full_up,
    vt_ref, x_ref, weights_ref, ids_ref, hv, wv, halves, send, recv, local, fetch, *more,
):
    tick = pl.program_id(0)

    @pl.when(tick == 0)
    def _():
        greet(plan)

    arrive(plan, lag, tick, h_ref, s_ref, (q_ref, k_ref, v_ref), hs_ref, ss_ref, w_ref, hv, wv, halves, send, recv, local)
    for (first, gather), shard, full, held in zip(
        gathers, (out_shard, up_shard), (full_out, full_up), (more[:4], more[4:])
    ):
        gather.run(tick - first, shard, full, *held)
    _, parts, columns, width = x_ref.shape
    heads = packed.shape[1]
    first = ARRIVED + 1

    def acts_load(i):
        return pltpu.make_async_copy(hs_ref.at[lax.div(i, 2), lax.rem(i, 2)], x_ref.at[lax.rem(i, 2)], fetch.at[lax.rem(i, 2)])

    weights_load = pltpu.make_async_copy(w_ref, weights_ref, fetch.at[2])
    ids_load = pltpu.make_async_copy(ss_ref, ids_ref, fetch.at[3])

    @pl.when(tick == ARRIVED)
    def _():
        ids_load.start()
        weights_load.start()
        acts_load(0).start()
        ids_load.wait()
        ids = ids_ref[...].reshape(2 * steps, columns)
        for i in range(2 * steps):
            row_ref[i // parts : i // parts + 1, (i % parts) * columns : (i % parts + 1) * columns] = ids[i : i + 1]
        turned = ids.astype(jnp.float32).T.astype(jnp.int32)
        for i in range(2 * steps):
            mine = turned[:, i : i + 1]
            col_ref[i * columns : (i + 1) * columns, :] = jnp.where(mine < 0, -2, mine)
        weights_load.wait()

    at = tick - first

    @pl.when((at >= 0) & (at < steps))
    def _():
        @pl.when(at + 1 < steps)
        def _():
            acts_load(at + 1).start()

        acts_load(at).wait()
        acts = x_ref[lax.rem(at, 2)].reshape(block, width)
        for kind in range(3):
            made = dot(acts, weights_ref[kind].reshape(width, heads * HEAD_DIM))
            for p in range(heads):
                head = made[:, p * HEAD_DIM : (p + 1) * HEAD_DIM]
                if kind < 2:
                    head = head * cos_ref[...] + pltpu.roll(head, HEAD_DIM // 2, 1) * sin_ref[...]
                packed[pl.ds(at * parts, parts), p, kind] = head.astype(jnp.bfloat16).reshape(parts, columns, HEAD_DIM)
        turned_ref[...] = acts.T

    @pl.when((at >= steps) & (at < steps * (1 + heads)))
    def _():
        pair, step = lax.div(at - steps, steps), lax.rem(at - steps, steps)
        attend_step(block, parts, pair, step, packed, col_ref, row_ref, o_ref, ot_ref, lse_ref, vt_ref)


def attention(plan, acts, segments, weights, cosine, sine, out_shard, up_shard, lag, collective_id):
    _, columns, width = acts.shape
    rows = weights[0].shape[0]
    quarter = width // 4
    heads = quarter // HEAD_DIM
    owners = 8
    length, block = owners * columns, 2 * columns
    steps, parts = length // block, 2
    gathers = (
        (0, Gather(plan, 3, out_shard, out_shard.shape[0], 512, "late")),
        (6, Gather(plan, 3, up_shard, up_shard.shape[0], 512, "late")),
    )
    low = jnp.bfloat16
    begin = ARRIVED + 1

    def at(t):
        return jnp.clip(t - begin, 0, steps - 1)

    def pair(t):
        return lax.div(jnp.clip(t - begin - steps, 0, steps * heads - 1), steps)

    def step(t):
        return lax.rem(jnp.clip(t - begin - steps, 0, steps * heads - 1), steps)

    def fixed(shape):
        return pl.BlockSpec(shape, lambda t: (0,) * len(shape))

    hbm = pl.BlockSpec(memory_space=pl.ANY)
    table = pl.BlockSpec((block, HEAD_DIM), lambda t: (at(t), 0))
    packed_shape = (owners, heads, 3, columns, HEAD_DIM)
    acts_shape = (2, 2, 2, columns, width)
    ids_shape = (2, 2, 2, 1, columns)
    weights_shape = (3,) + plan.lead() + (rows, quarter)
    copies = 3 + 4 * 3 + 3 * (3 + len(plan.masks))
    ticks = max([begin + steps * (1 + heads)] + [first + gather.ticks for first, gather in gathers])
    return pl.pallas_call(
        functools.partial(attention_kernel, plan, lag, gathers, block, steps),
        grid=(ticks,),
        in_specs=[hbm] * 5 + [table, table, hbm, hbm],
        out_specs=[
            fixed(packed_shape),
            pl.BlockSpec((width, block), lambda t: (0, at(t))),
            pl.BlockSpec((parts, None, columns, HEAD_DIM), lambda t: (step(t), pair(t), 0, 0)),
            pl.BlockSpec((1, 1, HEAD_DIM, block), lambda t: (pair(t), step(t), 0, 0)),
            pl.BlockSpec((1, steps, block), lambda t: (pair(t), 0, 0)),
            fixed((length, 1)),
            fixed((steps, block)),
            hbm,
            hbm,
            hbm,
            hbm,
            hbm,
        ],
        out_shape=[
            jax.ShapeDtypeStruct(packed_shape, low),
            jax.ShapeDtypeStruct((width, length), low),
            jax.ShapeDtypeStruct((owners, heads, columns, HEAD_DIM), low),
            jax.ShapeDtypeStruct((heads, steps, HEAD_DIM, block), jnp.float32),
            jax.ShapeDtypeStruct((heads, steps, block), jnp.float32),
            jax.ShapeDtypeStruct((length, 1), jnp.int32),
            jax.ShapeDtypeStruct((steps, block), jnp.int32),
            jax.ShapeDtypeStruct(acts_shape, low),
            jax.ShapeDtypeStruct(ids_shape, jnp.int32),
            jax.ShapeDtypeStruct(weights_shape, low),
            gathers[0][1].out_shape,
            gathers[1][1].out_shape,
        ],
        scratch_shapes=[
            pltpu.VMEM((HEAD_DIM, length), low),
            pltpu.VMEM((2, parts, columns, width), low),
            pltpu.VMEM(weights_shape, low),
            pltpu.VMEM(ids_shape, jnp.int32),
            pltpu.VMEM((columns, width), low),
            pltpu.VMEM((3, rows, width), low),
            pltpu.VMEM((3, 2, rows, width // 2), low),
            pltpu.SemaphoreType.DMA((copies,)),
            pltpu.SemaphoreType.DMA((copies,)),
            pltpu.SemaphoreType.DMA((5,)),
            pltpu.SemaphoreType.DMA((4,)),
        ] + gathers[0][1].scratch + gathers[1][1].scratch,
        compiler_params=pltpu.CompilerParams(
            collective_id=collective_id, has_side_effects=True, vmem_limit_bytes=56 << 20),
    )(acts, segments[:, None, :], *weights, cosine, sine, out_shard, up_shard)


class Mlp:
    def __init__(self, plan, lag, mixed, w_out, inputs, gain, offset, w_up, grad, cotangent, shard):
        tokens, width = inputs.shape
        hidden = w_up.shape[1]
        self.plan, self.lag = plan, lag
        self.blocks = 2 * plan.n_dp
        self.block = hidden // self.blocks
        self.rows = width // (plan.n_dp * plan.n_seq)
        self.gather = Gather(plan, lag, shard, self.rows, 512, "even")
        self.meet = 4
        self.up = self.meet + 1
        self.back = max(self.gather.ticks, self.up + self.blocks)
        self.norm = self.back + self.blocks
        self.ticks = self.norm + 5
        self.operands = (mixed, w_out, inputs, gain, offset, w_up, grad, cotangent, shard)
        blocks, back, up = self.blocks, self.back, self.up

        def up_block(t):
            later = jnp.clip(t - (up + blocks) + 1, 0, 1)
            return (0, jnp.clip(t - up, 0, blocks - 1) * (1 - later) + jnp.clip(t - back, 0, blocks - 1) * later)

        once = pl.BlockSpec((tokens, width), lambda t: (0, 0), pipeline_mode=pl.Buffered(1))
        row = pl.BlockSpec((width,), lambda t: (0,))
        hbm = pl.BlockSpec(memory_space=pl.ANY)
        self.in_specs = [hbm, hbm, hbm, row, row, pl.BlockSpec((width, self.block), up_block), once, hbm, hbm]
        self.out_specs = [
            hbm,
            hbm,
            hbm,
            hbm,
            hbm,
            hbm,
            pl.BlockSpec((tokens, self.block), lambda t: (0, jnp.clip(t - back, 0, blocks - 1))),
            hbm,
            pl.BlockSpec((8, width), lambda t: (0, 0)),
            hbm,
        ]
        low = jnp.bfloat16
        flat = jax.ShapeDtypeStruct((tokens, width), jnp.float32)
        self.out_shapes = [
            flat,
            flat,
            flat,
            jax.ShapeDtypeStruct((tokens, width), low),
            jax.ShapeDtypeStruct((width, tokens), low),
            jax.ShapeDtypeStruct((width, tokens), low),
            jax.ShapeDtypeStruct((tokens, hidden), low),
            jax.ShapeDtypeStruct(mixed.shape, low),
            jax.ShapeDtypeStruct((8, width), jnp.float32),
            self.gather.out_shape,
        ]
        self.chunk = 64
        self.scratch = [
            pltpu.VMEM((tokens, hidden), low),
            pltpu.VMEM((hidden, tokens), low),
            pltpu.VMEM((tokens, hidden), low),
            pltpu.VMEM((2, 2, 2) + shard.shape, low),
            pltpu.VMEM((tokens, width), jnp.float32),
            pltpu.VMEM((tokens, width), jnp.float32),
            pltpu.VMEM((tokens, width), low),
            pltpu.VMEM(mixed.shape, low),
            pltpu.VMEM((2, 2, self.chunk, width), jnp.float32),
            pltpu.SemaphoreType.DMA((2, 2, plan.n_seq)),
            pltpu.SemaphoreType.DMA((16,)),
            pltpu.SemaphoreType.DMA((2, 2)),
            pltpu.SemaphoreType.DMA((2,)),
        ] + self.gather.scratch

    everyone = True

    def left(self, refs, which, z):
        turned, n = refs[20], self.plan.n_seq
        every = turned.shape[0] // (n * self.plan.n_dp)
        return jnp.concatenate(
            [
                turned[pl.ds(pl.multiple_of((z * n + d) * every + which * self.rows, 16), self.rows), :]
                for d in range(n)
            ],
            axis=0,
        )

    def run(self, tick, refs):
        mixed_hbm, w_out, inputs, gain_ref, offset_ref, up_ref, grad_ref, cotangent, shard = refs[:9]
        output, first_sum, grad_first, grad_low, mixed_turned, acts_turned, gu_ref, back_pairs, sums_ref, full = refs[9:19]
        hidden_ref, turned_ref, slope_ref, down_ref, out_ref, back_ref, acts_ref, pairs, chunks = refs[19:28]
        swaps, local, loads, fetch = refs[28:32]
        plan, block = self.plan, self.block
        dp, seq = place()
        count, heads, columns, _ = pairs.shape
        tokens, width = acts_ref.shape
        low = jnp.bfloat16
        third = 512
        thirds = width // third
        self.gather.run(tick, shard, full, *refs[32:])

        def exchange(which, src, dst):
            return [
                pltpu.make_async_remote_copy(
                    src.at[lax.bitwise_xor(seq, m)], dst.at[seq], swaps.at[which, 0, m], swaps.at[which, 1, m],
                    device_id=partner_seq(m), device_id_type=MESH)
                for m in range(1, count)
            ]

        there = exchange(0, mixed_hbm, pairs)
        here = pltpu.make_async_copy(mixed_hbm.at[seq], pairs.at[seq], local.at[0])
        based = pltpu.make_async_copy(inputs, out_ref, local.at[1])
        outs = [
            pltpu.make_async_copy(
                w_out.at[:, pl.ds(n * third, third)], turned_ref.at[pl.ds(n * width, width), :], local.at[2 + n])
            for n in range(thirds)
        ]
        kept = pltpu.make_async_copy(out_ref, first_sum, local.at[5])
        turns = []
        for n in range(thirds):
            rows = pl.ds(n * third, third)
            base = slope_ref.shape[1] - 2 * width + n * third
            turns.append(pltpu.make_async_copy(slope_ref.at[:, pl.ds(base, third)], mixed_turned.at[rows, :], local.at[6 + n]))
            turns.append(pltpu.make_async_copy(
                slope_ref.at[:, pl.ds(base + width, third)], acts_turned.at[rows, :], local.at[9 + n]))

        @pl.when(tick == 0)
        def _():
            for copy in there + [here, based] + outs:
                copy.start()

        @pl.when(tick == self.meet)
        def _():
            for copy in there + [here, based] + outs:
                copy.wait()
            per = width // (heads * HEAD_DIM)
            for s in range(count // per):
                for g in range(per):
                    for p in range(heads):
                        at = (g * heads + p) * HEAD_DIM
                        acts_ref[s * columns : (s + 1) * columns, at : at + HEAD_DIM] = pairs[s * per + g, p]
            for n in range(thirds):
                part = slice(n * third, (n + 1) * third)
                out_ref[:, part] += dot(acts_ref[...], turned_ref[n * width : (n + 1) * width, :])
                base = slope_ref.shape[1] - 2 * width + n * third
                slope_ref[:, base : base + third] = acts_ref[:, part].T
            kept.start()

            def norm(i, carry):
                rows = pl.ds(pl.multiple_of(i * self.chunk, self.chunk), self.chunk)
                values = out_ref[rows, :]
                centre = values - jnp.mean(values, axis=-1, keepdims=True)
                spread = lax.rsqrt(jnp.mean(centre * centre, axis=-1, keepdims=True) + EPSILON)
                acts_ref[rows, :] = (centre * spread * gain_ref[...][None] + offset_ref[...][None]).astype(low)
                return carry

            lax.fori_loop(0, tokens // self.chunk, norm, 0)
            for n in range(thirds):
                base = slope_ref.shape[1] - width + n * third
                slope_ref[:, base : base + third] = acts_ref[:, n * third : (n + 1) * third].T
            for copy in turns:
                copy.start()

        @pl.when(tick == self.up + 2)
        def _():
            for copy in turns + [kept]:
                copy.wait()

        def block_at(i):
            return pl.ds(pl.multiple_of(i * block, 128), block)

        @pl.when((tick >= self.up) & (tick < self.up + self.blocks))
        def _():
            step = 256
            for n in range(block // step):
                upper = dot(acts_ref[...], up_ref[:, n * step : (n + 1) * step])
                share = 0.5 + 0.5 * lax.erf(upper * (1.0 / math.sqrt(2.0)))
                density = jnp.exp(upper * upper * -0.5) * (1.0 / math.sqrt(2.0 * math.pi))
                made = (upper * share).astype(low)
                at = pl.multiple_of((tick - self.up) * block + n * step, 128)
                hidden_ref[:, pl.ds(at, step)] = made
                turned_ref[pl.ds(at, step), :] = made.T
                slope_ref[:, pl.ds(at, step)] = (share + upper * density).astype(low)

        def fetched(i):
            z, y = lax.div(i, 2), lax.rem(i, 2)
            return pltpu.make_async_copy(full.at[z, y], down_ref.at[y], fetch.at[y])

        i = tick - self.back

        @pl.when((i >= -1) & (i < self.blocks - 1))
        def _():
            fetched(i + 1).start()

        @pl.when((i >= 0) & (i < self.blocks))
        def _():
            fetched(i).wait()
            down = down_ref[lax.rem(i, 2)].reshape(block, -1)

            @pl.when(i == 0)
            def _():
                back_ref[...] = jnp.zeros_like(back_ref)

            grad = dot(grad_ref[...], down, NT) * slope_ref[:, block_at(i)].astype(jnp.float32)
            gu_ref[...] = grad.astype(low)
            for n in range(thirds):
                part = slice(n * third, (n + 1) * third)
                out_ref[:, part] += dot(hidden_ref[:, block_at(i)], down[:, part])
                back_ref[:, part] += dot(gu_ref[...], up_ref[part, :], NT)

        done = pltpu.make_async_copy(out_ref, output, local.at[12])
        first_out = pltpu.make_async_copy(back_ref, grad_first, local.at[13])
        low_out = pltpu.make_async_copy(acts_ref, grad_low, local.at[14])
        chunk = self.chunk

        def chunk_loads(j, slot):
            rows = pl.ds(pl.multiple_of(j * chunk, chunk), chunk)
            return [
                pltpu.make_async_copy(src.at[rows, :], chunks.at[slot, n], loads.at[slot, n])
                for n, src in enumerate((first_sum, cotangent))
            ]

        @pl.when(tick == self.norm - 1)
        def _():
            for copy in outs:
                copy.start()

        @pl.when(tick == self.norm)
        def _():
            done.start()
            sums_ref[...] = jnp.zeros_like(sums_ref)
            for copy in chunk_loads(0, 0):
                copy.start()
            total = tokens // chunk

            def norm_back(j, carry):
                slot = lax.rem(j, 2)

                @pl.when(j + 1 < total)
                def _():
                    for copy in chunk_loads(j + 1, 1 - slot):
                        copy.start()

                for copy in chunk_loads(j, slot):
                    copy.wait()
                rows = pl.ds(pl.multiple_of(j * chunk, chunk), chunk)
                values = chunks[slot, 0]
                centre = values - jnp.mean(values, axis=-1, keepdims=True)
                spread = lax.rsqrt(jnp.mean(centre * centre, axis=-1, keepdims=True) + EPSILON)
                normed = centre * spread
                grad = back_ref[rows, :]
                grown = grad * gain_ref[...][None]
                mean_one = jnp.mean(grown, axis=-1, keepdims=True)
                mean_two = jnp.mean(grown * normed, axis=-1, keepdims=True)
                made = chunks[slot, 1] + (grown - mean_one - normed * mean_two) * spread
                sums_ref[0:1] += jnp.sum(grad * normed, axis=0, keepdims=True)
                sums_ref[1:2] += jnp.sum(grad, axis=0, keepdims=True)
                back_ref[rows, :] = made
                acts_ref[rows, :] = made.astype(low)
                return carry

            lax.fori_loop(0, total, norm_back, 0)
            first_out.start()
            low_out.start()

        again = exchange(1, pairs, back_pairs)
        home = pltpu.make_async_copy(pairs.at[seq], back_pairs.at[seq], local.at[0])

        @pl.when(tick == self.norm + 1)
        def _():
            for copy in outs:
                copy.wait()
            per = width // (heads * HEAD_DIM)
            step = heads * HEAD_DIM
            for g in range(per):
                made = sum(
                    dot(acts_ref[:, n * third : (n + 1) * third],
                        turned_ref[n * width + g * step : n * width + (g + 1) * step, :], NT)
                    for n in range(thirds)
                ).astype(low)
                for s in range(count // per):
                    for p in range(heads):
                        pairs[s * per + g, p] = made[s * columns : (s + 1) * columns, p * HEAD_DIM : (p + 1) * HEAD_DIM]
            for copy in again + [home]:
                copy.start()

        @pl.when(tick == self.ticks - 1)
        def _():
            for copy in again + [home, done, first_out, low_out]:
                copy.wait()


def layer_norm(values, gain, offset):
    centre = values - jnp.mean(values, axis=-1, keepdims=True)
    spread = jnp.mean(centre * centre, axis=-1, keepdims=True)
    return centre * lax.rsqrt(spread + EPSILON) * gain + offset


def gelu(values):
    return 0.5 * values * (1.0 + lax.erf(values * (1.0 / math.sqrt(2.0))))


def angles(positions):
    half = HEAD_DIM // 2
    rates = jnp.exp(jnp.arange(half, dtype=jnp.float32) * (-math.log(10000.0) / half))
    turned = positions.astype(jnp.float32)[:, None] * rates[None, :]
    return (jnp.cos(turned)[:, None, :], jnp.sin(turned)[:, None, :])


def rotary(values, cosine, sine):
    half = values.shape[-1] // 2
    first = values[..., :half]
    second = values[..., half:]
    return jnp.concatenate(
        [first * cosine - second * sine, second * cosine + first * sine], axis=-1
    )


def lower(values):
    return values.astype(jnp.bfloat16)


def project(acts, weight):
    return jnp.einsum("gcd,de->gce", acts, weight, preferred_element_type=jnp.float32)


def project_back(grads, weight):
    return jnp.einsum("gce,de->gcd", grads, weight, preferred_element_type=jnp.float32)


def outer_sum(left, right):
    return jnp.einsum("gci,gcj->ij", left, right, preferred_element_type=jnp.float32)


def plain_shards(
    inputs,
    segments,
    norm1_gain,
    norm1_bias,
    w_query,
    w_key,
    w_value,
    w_out,
    norm2_gain,
    norm2_bias,
    w_up,
    w_down,
    cotangent,
):
    groups, columns, width = inputs.shape
    heads_count = width // HEAD_DIM
    scale = 1.0 / math.sqrt(HEAD_DIM)
    full_query, full_key, full_value, full_out, full_up, full_down = (
        lax.all_gather(w_query, ("dp", "seq"), axis=0, tiled=True),
        lax.all_gather(w_key, ("dp", "seq"), axis=0, tiled=True),
        lax.all_gather(w_value, ("dp", "seq"), axis=0, tiled=True),
        lax.all_gather(w_out, ("dp", "seq"), axis=0, tiled=True),
        lax.all_gather(w_up, ("dp", "seq"), axis=0, tiled=True),
        lax.all_gather(w_down, ("dp", "seq"), axis=0, tiled=True),
    )
    key_ids = lax.all_gather(segments, "seq", axis=1, tiled=True)
    length = key_ids.shape[1]
    rank = lax.axis_index("seq")
    places = rank * columns + jnp.arange(columns, dtype=jnp.int32)
    key_places = jnp.arange(length, dtype=jnp.int32)
    cosine, sine = angles(places)

    def turn(values):
        shaped = values.reshape(groups, columns, heads_count, HEAD_DIM)
        return rotary(shaped, cosine, sine).reshape(groups, columns, width)

    def permitted(segment_row, key_row):
        same = segment_row[:, None] == key_row[None, :]
        causal = key_places[None, :] <= places[:, None]
        live = (key_row[None, :] >= 0) | (key_places[None, :] == places[:, None])
        return same & causal & live

    def scores_of(query_row, key_block, segment_row, key_row):
        heads_query = query_row.reshape(columns, heads_count, HEAD_DIM)
        heads_key = key_block.reshape(length, heads_count, HEAD_DIM)
        raw = (
            jnp.einsum("chd,lhd->hcl", heads_query, heads_key, preferred_element_type=jnp.float32)
            * scale
        )
        return jnp.where(permitted(segment_row, key_row)[None], raw, MASKED)

    normed_one = layer_norm(inputs, norm1_gain, norm1_bias)
    act_one = lower(normed_one)
    query_zero = project(act_one, full_query)
    key_zero = project(act_one, full_key)
    value_low = lower(project(act_one, full_value))
    query_low = lower(turn(query_zero))
    key_low = lower(turn(key_zero))
    keys_all, values_all = (
        lax.all_gather(key_low, "seq", axis=1, tiled=True),
        lax.all_gather(value_low, "seq", axis=1, tiled=True),
    )

    def attend(items):
        query_row, key_block, value_block, segment_row, key_row = items
        scores = scores_of(query_row, key_block, segment_row, key_row)
        top = jnp.max(scores, axis=-1, keepdims=True)
        expo = jnp.exp(scores - top)
        total = jnp.sum(expo, axis=-1, keepdims=True)
        probs = lower(expo / total)
        heads_value = value_block.reshape(length, heads_count, HEAD_DIM)
        mixed = jnp.einsum("hcl,lhd->chd", probs, heads_value, preferred_element_type=jnp.float32)
        return (mixed.reshape(columns, width), top[..., 0] + jnp.log(total[..., 0]))

    mixed_all, log_totals = lax.map(attend, (query_low, keys_all, values_all, segments, key_ids))
    mixed_low = lower(mixed_all)
    first_sum = inputs + project(mixed_low, full_out)
    act_two = lower(layer_norm(first_sum, norm2_gain, norm2_bias))
    upper = project(act_two, full_up)
    hidden_low = lower(gelu(upper))
    output = first_sum + project(hidden_low, full_down)
    half_width = width // 2
    half_hidden = full_up.shape[1] // 2
    grad_out_low = lower(cotangent)
    down_left = outer_sum(hidden_low, grad_out_low[..., :half_width])
    down_right = outer_sum(hidden_low, grad_out_low[..., half_width:])
    grad_hidden = project_back(grad_out_low, full_down)
    gelu_values, gelu_back = jax.vjp(gelu, upper)
    grad_upper = lower(gelu_back(grad_hidden)[0])
    up_left = outer_sum(act_two, grad_upper[..., :half_hidden])
    up_right = outer_sum(act_two, grad_upper[..., half_hidden:])
    grad_act_two = project_back(grad_upper, full_up)
    normed_two, norm_two_back = jax.vjp(layer_norm, first_sum, norm2_gain, norm2_bias)
    grad_first_norm, gain_two_grad, offset_two_grad = norm_two_back(grad_act_two)
    grad_first = cotangent + grad_first_norm
    grad_attn_low = lower(grad_first)
    out_grad = outer_sum(mixed_low, grad_attn_low)
    grad_mixed = lower(project_back(grad_attn_low, full_out))
    heads_mixed = mixed_all.reshape(groups, columns, heads_count, HEAD_DIM)
    heads_gm = grad_mixed.astype(jnp.float32).reshape(groups, columns, heads_count, HEAD_DIM)
    deltas = jnp.transpose(jnp.sum(heads_mixed * heads_gm, axis=-1), (0, 2, 1))
    key_source, value_source = (key_low, value_low)

    def attend_back(carry, items):
        query_row, grad_row, log_row, delta_row, segment_row, key_row, key_part, value_part = items
        queries_all, grads_all = (
            lax.all_gather(query_row, "seq", axis=0, tiled=True),
            lax.all_gather(grad_row, "seq", axis=0, tiled=True),
        )
        logs_all, deltas_all = (
            lax.all_gather(log_row, "seq", axis=1, tiled=True),
            lax.all_gather(delta_row, "seq", axis=1, tiled=True),
        )
        own_mask = (segment_row[None, :] == key_row[:, None]) & (
            places[None, :] <= key_places[:, None]
        )
        own_mask = own_mask & (
            (segment_row[None, :] >= 0) | (places[None, :] == key_places[:, None])
        )
        heads_query = queries_all.reshape(length, heads_count, HEAD_DIM)
        heads_grad = grads_all.reshape(length, heads_count, HEAD_DIM)
        heads_key = key_part.reshape(columns, heads_count, HEAD_DIM)
        heads_value = value_part.reshape(columns, heads_count, HEAD_DIM)
        raw = (
            jnp.einsum("lhd,chd->hlc", heads_query, heads_key, preferred_element_type=jnp.float32)
            * scale
        )
        scores = jnp.where(own_mask[None], raw, MASKED)
        probs = jnp.exp(scores - logs_all[..., None])
        grad_probs = jnp.einsum(
            "lhd,chd->hlc", heads_grad, heads_value, preferred_element_type=jnp.float32
        )
        grad_scores = lower(probs * (grad_probs - deltas_all[..., None]))
        grad_values = jnp.einsum(
            "hlc,lhd->chd", lower(probs), heads_grad, preferred_element_type=jnp.float32
        )
        grad_keys = (
            jnp.einsum("hlc,lhd->chd", grad_scores, heads_query, preferred_element_type=jnp.float32)
            * scale
        )
        partial_query = (
            jnp.einsum("hlc,chd->lhd", grad_scores, heads_key, preferred_element_type=jnp.float32)
            * scale
        )
        grad_query = lax.psum_scatter(
            partial_query.reshape(length, width).astype(jnp.bfloat16),
            "seq",
            scatter_dimension=0,
            tiled=True,
        ).astype(jnp.float32)
        return (
            carry,
            (grad_query, grad_keys.reshape(columns, width), grad_values.reshape(columns, width)),
        )

    start_carry = jnp.zeros((), jnp.float32)
    end_carry, grads_seq = lax.scan(
        attend_back,
        start_carry,
        (query_low, grad_mixed, log_totals, deltas, segments, key_ids, key_source, value_source),
    )
    grad_query_all, grad_key_all, grad_value_all = grads_seq
    turned_query, turn_back = jax.vjp(turn, query_zero)
    grad_query_low = lower(turn_back(grad_query_all)[0])
    grad_key_low = lower(turn_back(grad_key_all)[0])
    grad_value_low = lower(grad_value_all)
    query_grad = outer_sum(act_one, grad_query_low)
    key_grad = outer_sum(act_one, grad_key_low)
    value_grad = outer_sum(act_one, grad_value_low)
    grad_act_one = project_back(grad_query_low, full_query) + project_back(grad_key_low, full_key)
    grad_act_one = grad_act_one + project_back(grad_value_low, full_value)
    normed_again, norm_one_back = jax.vjp(layer_norm, inputs, norm1_gain, norm1_bias)
    grad_input_norm, gain_one_grad, offset_one_grad = norm_one_back(grad_act_one)
    grad_input = grad_first + grad_input_norm
    summed = (
        lax.psum_scatter(query_grad, ("dp", "seq"), scatter_dimension=0, tiled=True),
        lax.psum_scatter(key_grad, ("dp", "seq"), scatter_dimension=0, tiled=True),
        lax.psum_scatter(value_grad, ("dp", "seq"), scatter_dimension=0, tiled=True),
        lax.psum_scatter(out_grad, ("dp", "seq"), scatter_dimension=0, tiled=True),
        lax.psum_scatter(up_left, ("dp", "seq"), scatter_dimension=0, tiled=True),
        lax.psum_scatter(up_right, ("dp", "seq"), scatter_dimension=0, tiled=True),
        lax.psum_scatter(down_left, ("dp", "seq"), scatter_dimension=0, tiled=True),
        lax.psum_scatter(down_right, ("dp", "seq"), scatter_dimension=0, tiled=True),
        lax.psum_scatter(gain_one_grad, ("dp", "seq"), scatter_dimension=0, tiled=True),
        lax.psum_scatter(offset_one_grad, ("dp", "seq"), scatter_dimension=0, tiled=True),
        lax.psum_scatter(gain_two_grad, ("dp", "seq"), scatter_dimension=0, tiled=True),
        lax.psum_scatter(offset_two_grad, ("dp", "seq"), scatter_dimension=0, tiled=True),
    )
    query_grad, key_grad, value_grad, out_grad = (summed[0], summed[1], summed[2], summed[3])
    up_left, up_right, down_left, down_right = (summed[4], summed[5], summed[6], summed[7])
    gain_one_grad, offset_one_grad, gain_two_grad, offset_two_grad = (
        summed[8],
        summed[9],
        summed[10],
        summed[11],
    )
    up_grad = jnp.concatenate([up_left, up_right], axis=1)
    down_grad = jnp.concatenate([down_left, down_right], axis=1)
    return (
        output,
        grad_input,
        gain_one_grad,
        offset_one_grad,
        query_grad,
        key_grad,
        value_grad,
        out_grad,
        gain_two_grad,
        offset_two_grad,
        up_grad,
        down_grad,
    )


def shards(
    inputs,
    segments,
    norm1_gain,
    norm1_bias,
    w_query,
    w_key,
    w_value,
    w_out,
    norm2_gain,
    norm2_bias,
    w_up,
    w_down,
    cotangent,
    *,
    plan,
):
    groups, columns, width = inputs.shape
    length = columns * plan.n_seq
    lag, piece = 2, 512
    every = plan.n_dp * plan.n_seq

    half = HEAD_DIM // 2
    rates = np.exp(np.arange(half, dtype=np.float32) * np.float32(-math.log(10000.0) / half))
    angle = (np.arange(length, dtype=np.float32)[:, None] * rates[None, :]).astype(np.float32)
    cosine = jnp.asarray(np.concatenate([np.cos(angle), np.cos(angle)], axis=1), jnp.float32)
    sine = jnp.asarray(np.concatenate([-np.sin(angle), np.sin(angle)], axis=1), jnp.float32)

    def flat(values):
        return values.reshape(groups * columns, width)

    act_one = lower(layer_norm(inputs, norm1_gain, norm1_bias))
    packed, turned_one, mixed, mixed_t, lse, seg_col, seg_row, _, _, heads_weight, full_out, full_up = attention(
        plan, act_one, segments, (w_query, w_key, w_value), cosine, sine, w_out, w_up, lag, 1
    )
    grad_low = lower(flat(cotangent))
    mlp = Mlp(
        plan, lag, mixed, full_out.reshape(width, width), flat(inputs), norm2_gain, norm2_bias,
        full_up.reshape(width, -1), grad_low, flat(cotangent), w_down,
    )
    rows = width // every

    def reduce_all(pairs, routes, collective_id, beside, first=0):
        out, *more = reduce_products(plan, pairs, rows, piece, lag, routes, collective_id, beside, first)
        results, at = [], 0
        for left, right in pairs:
            blocks = left if isinstance(left, int) else left.shape[0]
            cols = right.shape[1] // piece
            part = out[at : at + blocks * cols].reshape(blocks, cols, -1, piece)
            results.append(jnp.transpose(part, (0, 2, 1, 3)).reshape(-1, right.shape[1]))
            at += blocks * cols
        return results + more

    (
        down_grad, output, _, grad_first, grad_first_low, mixed_turned, acts_turned, grad_upper, grad_pairs,
        sums_two, _,
    ) = reduce_all([(w_down.shape[0] // rows, grad_low)], "even", 3, mlp, 14)
    work = Finish(
        plan, 0, packed, grad_pairs, mixed_t, lse, seg_col, seg_row, cosine, sine, turned_one,
        heads_weight.reshape(3, width, -1), inputs, grad_first.reshape(inputs.shape), norm1_gain, sums_two,
    )
    up_grad, out_grad, grad_input, heads_grad, norm_rows = reduce_all(
        [(acts_turned[None], grad_upper), (mixed_turned[None], grad_first_low)], "x late", 4, work
    )
    return (
        output.reshape(inputs.shape),
        grad_input,
        norm_rows[:, 0],
        norm_rows[:, 1],
        heads_grad[0],
        heads_grad[1],
        heads_grad[2],
        out_grad,
        norm_rows[:, 2],
        norm_rows[:, 3],
        up_grad,
        down_grad,
    )


def fits(mesh, groups, columns, width, rows):
    return (
        mesh.shape["seq"] == 8
        and groups == 2
        and width % (4 * HEAD_DIM) == 0
        and columns == 256
        and rows % 16 == 0
    )


def solution(mesh):
    placed = (
        P("dp", "seq", None),
        P("dp", "seq"),
        P(),
        P(),
        P(("dp", "seq"), None),
        P(("dp", "seq"), None),
        P(("dp", "seq"), None),
        P(("dp", "seq"), None),
        P(),
        P(),
        P(("dp", "seq"), None),
        P(("dp", "seq"), None),
        P("dp", "seq", None),
    )
    plan = Plan(mesh)

    def layer(inputs, segments, *rest):
        groups, columns, width = inputs.shape
        if fits(mesh, groups, columns, width, rest[2].shape[0]):
            return shards(inputs, segments, *rest, plan=plan)
        return plain_shards(inputs, segments, *rest)

    return jax.shard_map(
        layer,
        mesh=mesh,
        in_specs=placed,
        out_specs=(
            P("dp", "seq", None),
            P("dp", "seq", None),
            P(("dp", "seq")),
            P(("dp", "seq")),
            P(("dp", "seq"), None),
            P(("dp", "seq"), None),
            P(("dp", "seq"), None),
            P(("dp", "seq"), None),
            P(("dp", "seq")),
            P(("dp", "seq")),
            P(("dp", "seq"), None),
            P(("dp", "seq"), None),
        ),
        check_vma=False,
    )
```

```python
import functools
import math

import jax
import jax.numpy as jnp
import numpy as np
from jax import lax
from jax.experimental import pallas as pl
from jax.experimental.pallas import tpu as pltpu
from jax.sharding import PartitionSpec as P

HEAD_DIM = 128


EPSILON = 1e-05
MASKED = -1e30
LOG2E = math.log2(math.e)
NT = (((1,), (1,)), ((), ()))
NN = (((1,), (0,)), ((), ()))


def dot(left, right, dims=NN):
    return lax.dot_general(left, right, dims, preferred_element_type=jnp.float32)


def allowed_pairs(key_col, query_row, diagonal):
    same = key_col == query_row
    if not diagonal:
        return same
    shape = (key_col.shape[0], query_row.shape[1])
    key_at = lax.broadcasted_iota(jnp.int32, shape, 0)
    query_at = lax.broadcasted_iota(jnp.int32, shape, 1)
    return (same & (key_at <= query_at)) | (key_at == query_at)


def attend_back_step(
    block, parts, pair, step, last, q_ref, k_ref, v_ref, g_ref, ot_ref, lse_ref, col_ref, row_ref, cos_ref, sin_ref,
    out_ref, kt_ref, dk_ref, dv_ref,
):
    scale = 1.0 / math.sqrt(HEAD_DIM)

    @pl.when(step == 0)
    def _():
        kt_ref[...] = k_ref[...].reshape(-1, HEAD_DIM).T
        dk_ref[...] = jnp.zeros_like(dk_ref)
        dv_ref[...] = jnp.zeros_like(dv_ref)

    query = q_ref[pl.ds(step * parts, parts)].reshape(block, HEAD_DIM)
    grad = g_ref[pl.ds(step * parts, parts)].reshape(block, HEAD_DIM)
    query_row = row_ref[pl.ds(step, 1), :]
    lse = lse_ref[0, pl.ds(step, 1), :]
    delta = jnp.sum(ot_ref[0, 0] * grad.astype(jnp.float32).T, axis=0, keepdims=True)
    unit = LOG2E * scale

    def visit(j, dqt, diagonal):
        at = pl.multiple_of(j * block, block)
        key = k_ref[pl.ds(j * parts, parts)].reshape(block, HEAD_DIM)
        value = v_ref[pl.ds(j * parts, parts)].reshape(block, HEAD_DIM)
        key_col = col_ref[pl.ds(at, block), :]
        scores = dot(key, query, NT) * unit - lse
        probs = jnp.where(allowed_pairs(key_col, query_row, diagonal), jnp.exp2(scores), 0.0)
        grad_probs = dot(value, grad, NT)
        grad_scores = (probs * (grad_probs - delta)).astype(jnp.bfloat16)
        dv_ref[pl.ds(at, block), :] += dot(probs.astype(jnp.bfloat16), grad)
        dk_ref[pl.ds(at, block), :] += dot(grad_scores, query)
        return dqt + dot(kt_ref[:, pl.ds(at, block)], grad_scores)

    dqt = lax.fori_loop(
        0, step, lambda j, c: visit(j, c, False), jnp.zeros((HEAD_DIM, block), jnp.float32)
    )
    dqt = visit(step, dqt, True)

    def turn_back(values, cosine, sine):
        return values * cosine - pltpu.roll(values, HEAD_DIM // 2, 1) * sine

    at = pl.multiple_of(step * block, block)
    dq = turn_back(dqt.T * scale, cos_ref[pl.ds(at, block), :], sin_ref[pl.ds(at, block), :])
    out_ref[pair, pl.ds(at, block), :HEAD_DIM] = dq.astype(jnp.bfloat16)

    @pl.when(step == last)
    def _():
        dk = turn_back(dk_ref[...] * scale, cos_ref[...], sin_ref[...])
        out_ref[pair, :, HEAD_DIM : 2 * HEAD_DIM] = dk.astype(jnp.bfloat16)
        out_ref[pair, :, 2 * HEAD_DIM :] = dv_ref[...].astype(jnp.bfloat16)


MESH = pl.DeviceIdType.MESH


class Plan:
    def __init__(self, mesh):
        self.n_dp, self.n_seq = mesh.shape["dp"], mesh.shape["seq"]
        bits = [1 << i for i in range(self.n_seq.bit_length() - 1)]
        self.bits = bits[::-1]
        if len(bits) == 3:
            self.orders = ((2, 4, 1), (4, 2, 1))
        else:
            turn = len(bits) // 2
            self.orders = (tuple(bits), tuple(bits[turn:] + bits[:turn]))
        self.hops = len(bits)
        self.masks = range(1, self.n_dp)
        straight = [("dp",) + order for order in self.orders]
        self.routes = {
            "even": [straight, straight],
            "some late": [straight] * 3 + [[order[:1] + ("dp",) + order[1:] for order in self.orders]],
            "late": [straight, [order[:1] + ("dp",) + order[1:] for order in self.orders]],
            "x late": [
                [("dp",) + self.orders[1]] * 2,
                [order[:1] + ("dp",) + order[1:] for order in self.orders],
            ],
        }

    def sems(self, route, stage):
        return sum(len(self.masks) if entry == "dp" else 1 for entry in route[:stage])

    def lead(self):
        return (self.n_dp,) + (2,) * self.hops


def place():
    return lax.axis_index("dp"), lax.axis_index("seq")


def partner_dp(plan, mask):
    dp, seq = place()
    return (lax.bitwise_xor(dp, mask), seq)


def partner_seq(bit):
    dp, seq = place()
    return (dp, lax.bitwise_xor(seq, bit))


def own_bit(bit):
    return lax.bitwise_and(lax.div(place()[1], bit), 1)


def greet(plan, everyone=False):
    barrier = pltpu.get_barrier_semaphore()
    others = [partner_dp(plan, m) for m in plan.masks]
    others += [partner_seq(m) for m in (range(1, plan.n_seq) if everyone else plan.bits)]
    for other in others:
        pl.semaphore_signal(barrier, inc=1, device_id=other, device_id_type=MESH)
    pl.semaphore_wait(barrier, len(others))


def reduce_kernel(plan, jobs, first, count, lag, routes, beside, *refs):
    k, given = len(jobs), sum(job[3] for job in jobs)
    lefts, rights, refs = iter(refs[:given]), refs[given : given + k], refs[given + k :]
    more = [0, 0, 0] if beside is None else [len(beside.in_specs), len(beside.out_specs), len(beside.scratch)]
    extra, refs = refs[: more[0]], refs[more[0] :]
    out_ref, extra = refs[0], extra + refs[1 : 1 + more[1]]
    scratch = refs[1 + more[1] :]
    extra, scratch = extra + scratch[: more[2]], scratch[more[2] :]
    hops, slots = plan.hops, 2 * lag
    stages = hops + 1
    kinds = 1 if routes[0] == routes[1] else 2
    sums, got = [], []
    for h in range(2):
        more = (kinds - 1, 2 * (kinds - 1))
        sums.append(scratch[: stages + more[0]])
        got.append(scratch[stages + more[0] : 2 * stages + sum(more)])
        scratch = scratch[2 * stages + sum(more) :]
    send, recv = scratch
    tick = pl.program_id(0)
    half = out_ref.shape[-1] // 2
    rows = out_ref.shape[-2]
    dp, _ = place()

    @pl.when(tick == 0)
    def _():
        greet(plan, getattr(beside, "everyone", False))

    def sums_at(h, kind, stage, u):
        if stage < stages - 1 or kinds == 1:
            return sums[h][stage], lax.rem(u, lag)
        return sums[h][stage + kind], 0

    def got_at(h, kind, stage, u):
        if stage < stages - 2 or kinds == 1:
            return got[h][stage], lax.rem(u, slots)
        return got[h][stage + 2 * kind], lax.rem(lax.div(u, 2), lag)

    def at_entry(h, kind, stage, value):
        route = routes[kind][h]
        left = [d for d in ("dp",) + tuple(plan.bits) if d not in route[:stage]]
        return tuple(value if d == route[stage] else slice(None) for d in left)

    def own(entry):
        return dp if entry == "dp" else own_bit(entry)

    def copies(h, kind, stage, u):
        route = routes[kind][h]
        entry = route[stage]
        src, kept = sums_at(h, kind, stage, u)
        dst, slot = got_at(h, kind, stage, u)
        at = h * (hops + len(plan.masks)) + plan.sems(route, stage)
        sem = lax.rem(u, slots)
        if entry != "dp":
            return [pltpu.make_async_remote_copy(
                src.at[(kept,) + at_entry(h, kind, stage, 1 - own(entry))], dst.at[slot],
                send.at[sem, at], recv.at[sem, at], device_id=partner_seq(entry), device_id_type=MESH)]
        return [
            pltpu.make_async_remote_copy(
                src.at[(kept,) + at_entry(h, kind, stage, lax.bitwise_xor(dp, mask))], dst.at[slot, n],
                send.at[sem, at + n], recv.at[sem, at + n], device_id=partner_dp(plan, mask), device_id_type=MESH)
            for n, mask in enumerate(plan.masks)
        ]

    def wide(values):
        return values.astype(jnp.float32)

    for stage in reversed(range(1, stages + 1)):
        u = tick - first - lag * stage
        for kind in range(kinds):
            due = (u >= 0) & (u < count)
            if kinds > 1:
                due = due & (lax.rem(u, 2) == kind)

            @pl.when(due)
            def _(stage=stage, kind=kind, u=u):
                for h in range(2):
                    for copy in copies(h, kind, stage - 1, u):
                        copy.wait()
                    entry = routes[kind][h][stage - 1]
                    src, kept = sums_at(h, kind, stage - 1, u)
                    dst, slot = got_at(h, kind, stage - 1, u)
                    total = wide(src[(kept,) + at_entry(h, kind, stage - 1, own(entry))])
                    if entry == "dp":
                        for n in range(len(plan.masks)):
                            total = total + wide(dst[slot, n])
                    else:
                        total = total + wide(dst[slot])
                    if stage == stages:
                        out_ref[0, :, h * half : (h + 1) * half] = total
                        continue
                    to, at = sums_at(h, kind, stage, u)
                    to[at] = total.astype(jnp.bfloat16)
                    for copy in copies(h, kind, stage, u):
                        copy.start()

    for (start, stop, cols, has_left), right in zip(jobs, rights):
        if has_left:
            left = next(lefts)

            def left_rows(which, z, left=left):
                step = rows * plan.n_seq
                return left[which, z * step : (z + 1) * step, :]

        else:
            left_rows = functools.partial(beside.left, extra)

        @pl.when((tick >= first + start) & (tick < first + stop))
        def _(start=start, cols=cols, left_rows=left_rows, right=right):
            u = tick - first
            kept = lax.rem(u, lag)
            which = lax.div(u - start, cols)
            for z in range(plan.n_dp):
                part = dot(left_rows(which, z), right[...]).astype(jnp.bfloat16)
                for h in range(2):
                    piece = part[:, h * half : (h + 1) * half]
                    sums[h][0][kept, z] = piece.reshape(plan.lead()[1:] + (rows, half))
            for h in range(2):
                for copy in copies(h, 0, 0, u):
                    copy.start()

    if beside is not None:
        beside.run(tick, extra)


def reduce_products(plan, pairs, rows, width, lag, routes, collective_id, beside=None, first=0):
    jobs, start = [], 0
    left_specs, right_specs = [], []
    for left, right in pairs:
        cols = right.shape[1] // width
        blocks = left if isinstance(left, int) else left.shape[0]
        stop = start + blocks * cols
        jobs.append((start, stop, cols, left is not blocks))
        if left is not blocks:
            left_specs.append(pl.BlockSpec(left.shape, lambda t: (0, 0, 0), pipeline_mode=pl.Buffered(1)))
        right_specs.append(pl.BlockSpec(
            (right.shape[0], width),
            functools.partial(lambda t, start, stop, cols: (0, lax.rem(jnp.clip(t - first, start, stop - 1) - start, cols)),
                start=start, stop=stop, cols=cols)))
        start = stop
    count = start
    half = width // 2
    slots, hops = 2 * lag, plan.hops
    tail = lag * (hops + 1)
    n_dp, masks = plan.n_dp, len(plan.masks)
    low = jnp.bfloat16

    def room(*shape):
        return pltpu.VMEM(shape + (rows, half), low)

    routes = [[route[::-1] for route in kind] for kind in plan.routes[routes]]

    def left(kind, stage):
        return [n_dp if d == "dp" else 2 for d in ("dp",) + tuple(plan.bits) if d not in routes[kind][0][:stage]]

    def arriving(kind, stage):
        return [masks] * (routes[kind][0][stage] == "dp") + left(kind, stage + 1)

    buffers = []
    for _ in range(2):
        if routes[0] == routes[1]:
            buffers += [room(lag, *left(0, s)) for s in range(hops + 1)]
            buffers += [room(slots, *arriving(0, s)) for s in range(hops + 1)]
            continue
        buffers += [room(lag, *left(0, s)) for s in range(hops)] + [room(1, *left(k, hops)) for k in range(2)]
        buffers += [room(slots, *arriving(0, s)) for s in range(hops - 1)]
        buffers += [room(lag, *arriving(k, s)) for k in range(2) for s in (hops - 1, hops)]
    each = 2 * (hops + len(plan.masks))
    out_specs = [pl.BlockSpec((1, rows, width), lambda t: (jnp.clip(t - first - tail, 0, count - 1), 0, 0))]
    out_shapes = [jax.ShapeDtypeStruct((count, rows, width), jnp.float32)]
    more_in, more_scratch, more_operands = [], [], []
    if beside is not None:
        more_in, more_scratch, more_operands = beside.in_specs, beside.scratch, beside.operands
        out_specs, out_shapes = out_specs + beside.out_specs, out_shapes + beside.out_shapes
    return pl.pallas_call(
        functools.partial(reduce_kernel, plan, jobs, first, count, lag, routes, beside),
        grid=(max(first + count + tail, 0 if beside is None else beside.ticks),),
        in_specs=left_specs + right_specs + more_in,
        out_specs=out_specs,
        out_shape=out_shapes,
        scratch_shapes=more_scratch + buffers + [
            pltpu.SemaphoreType.DMA((slots, each)),
            pltpu.SemaphoreType.DMA((slots, each)),
        ],
        compiler_params=pltpu.CompilerParams(
            collective_id=collective_id, has_side_effects=True, vmem_limit_bytes=63 << 20),
    )(*[p[0] for p in pairs if not isinstance(p[0], int)], *[p[1] for p in pairs], *more_operands)


class Copies:
    def __init__(self, send, recv):
        self.send, self.recv, self.count, self.sent = send, recv, 0, []

    def remote(self, src, dst, device):
        at = self.count
        self.count += 1
        return pltpu.make_async_remote_copy(
            src, dst, self.send.at[at], self.recv.at[at], device_id=device, device_id_type=MESH)

    def run(self, pieces, lag, tick=None):
        last = max(start + lag * len(stages) for start, stages in pieces)
        for now in range(min(start for start, _ in pieces), last + 1):
            due = [
                (start, stages, stage)
                for stage in reversed(range(max(len(stages) for _, stages in pieces) + 1))
                for start, stages in pieces
                if start + lag * stage == now and stage <= len(stages)
            ]

            def step(due=due, now=now):
                for start, stages, stage in due:
                    if stage > 0:
                        for copy in stages[stage - 1][1]:
                            copy.wait()
                    if stage < len(stages):
                        ahead, copies = stages[stage]
                        if ahead is not None:
                            ahead()
                        for copy in copies:
                            copy.start()

            if tick is None:
                step()
            elif due:
                pl.when(tick == now)(step)
        return last


def arrive(plan, lag, tick, h_ref, s_ref, weights, hs_ref, ss_ref, w_ref, hv, both_ref, rows_ref, wv, halves, send, recv, local):
    dp, seq = place()
    y, x, c = own_bit(4), own_bit(2), own_bit(1)
    loads = [pltpu.make_async_copy(h_ref.at[y], hv, local.at[0])]
    loads += [pltpu.make_async_copy(r, wv.at[i], local.at[1 + i]) for i, r in enumerate(weights)]
    own = pltpu.make_async_copy(hv, hs_ref.at[y, x, c], local.at[0])
    named = pltpu.make_async_copy(rows_ref.at[y], ss_ref.at[y, x, c], local.at[4])
    given = pltpu.make_async_copy(s_ref, both_ref, local.at[5])

    @pl.when(tick == 0)
    def _():
        for load in loads + [given]:
            load.start()
        given.wait()
        for i in range(2):
            rows_ref[i] = both_ref[i : i + 1, :]
        named.start()
        for load in loads:
            load.wait()
        own.start()

    run = Copies(send, recv)
    pieces = []
    pieces.append((0, [
        (None, [run.remote(rows_ref.at[1 - y], ss_ref.at[y, x, c], partner_seq(4))]),
        (named.wait, [run.remote(ss_ref.at[:, x, c], ss_ref.at[:, x, c], partner_seq(2))]),
        (None, [run.remote(ss_ref.at[:, :, c], ss_ref.at[:, :, c], partner_seq(1))]),
    ]))
    tokens = hv.shape[0]
    parts = 4
    for i in range(parts):
        rows = pl.ds(i * (tokens // parts), tokens // parts)
        first = run.remote(h_ref.at[1 - y, rows], hs_ref.at[y, x, c, rows], partner_seq(4))
        second = [run.remote(hs_ref.at[:, x, c, rows], hs_ref.at[:, x, c, rows], partner_seq(2))]
        third = [run.remote(hs_ref.at[:, :, c, rows], hs_ref.at[:, :, c, rows], partner_seq(1))]
        pieces.append((ACTS_AT + i, [(None, [first]), (own.wait if i == 0 else None, second), (None, third)]))

    half, quarter = halves.shape[-1], w_ref.shape[-1]
    for i in range(3):
        mine = pltpu.make_async_copy(
            halves.at[i, :, :, pl.ds(c * quarter, quarter)], w_ref.at[i, dp, y, :, c], local.at[1 + i])

        def cut(i=i, mine=mine):
            halves[i, x] = wv[i, :, pl.ds(pl.multiple_of(x * half, 128), half)]
            mine.start()

        to_x = [run.remote(wv.at[i, :, pl.ds((1 - x) * half, half)], halves.at[i, x], partner_seq(2))]
        to_core = [run.remote(
            halves.at[i, :, :, pl.ds((1 - c) * quarter, quarter)], w_ref.at[i, dp, y, :, c], partner_seq(1))]
        to_z = [run.remote(w_ref.at[i, dp, y], w_ref.at[i, dp, y], partner_dp(plan, m)) for m in plan.masks]
        to_y = [run.remote(w_ref.at[i, :, y], w_ref.at[i, :, y], partner_seq(4))]
        pieces.append((WEIGHTS_AT[i], [(None, to_x), (cut, to_core), (mine.wait, to_z), (None, to_y)]))
    run.run(pieces, ARRIVE_LAG, tick)


ARRIVE_LAG = 2
ACTS_AT, WEIGHTS_AT = 2, (0, 2, 3)
ARRIVED = max(ACTS_AT + 3 + 3 * ARRIVE_LAG, WEIGHTS_AT[-1] + 4 * ARRIVE_LAG)


class Finish:
    everyone = True

    def __init__(
        self, plan, first, packed, grads, mixed_t, lse, seg_col, seg_row, cosine, sine, turned, weights, inputs, grad_first, gain, more
    ):
        count, per, _, columns, _ = packed.shape
        length = count * columns
        self.plan, self.first = plan, first
        self.block = seg_row.shape[1]
        self.steps, self.parts = length // self.block, self.block // columns
        self.count = per * self.steps
        self.begin = first + self.count
        self.split = 4
        self.operands = (
            packed, packed, packed, grads, mixed_t, lse, seg_col, seg_row, cosine, sine, turned, weights, inputs, grad_first, gain, more
        )
        width, quarter = turned.shape[0], weights.shape[2]
        n_dp, masks = plan.n_dp, len(plan.masks)
        rows = width // (8 * n_dp)
        size = columns // self.split
        low = jnp.bfloat16

        def pair(t):
            return lax.div(jnp.clip(t - first, 0, self.count - 1), self.steps)

        def step(t):
            return lax.rem(jnp.clip(t - first, 0, self.count - 1), self.steps)

        def whole(which):
            return pl.BlockSpec(
                (count, None, None, columns, HEAD_DIM), lambda t: (0, pair(t), which, 0, 0), pipeline_mode=pl.Buffered(1))

        def fixed(shape):
            return pl.BlockSpec(shape, lambda t: (0,) * len(shape), pipeline_mode=pl.Buffered(1))

        hbm = pl.BlockSpec(memory_space=pl.ANY)
        self.in_specs = [
            whole(0),
            whole(1),
            whole(2),
            pl.BlockSpec((count, None, columns, HEAD_DIM), lambda t: (0, pair(t), 0, 0), pipeline_mode=pl.Buffered(1)),
            pl.BlockSpec((1, 1, HEAD_DIM, self.block), lambda t: (pair(t), step(t), 0, 0)),
            pl.BlockSpec((1, self.steps, self.block), lambda t: (pair(t), 0, 0)),
            fixed((length, 1)),
            fixed((self.steps, self.block)),
            fixed((length, HEAD_DIM)),
            fixed((length, HEAD_DIM)),
            hbm,
            hbm,
            hbm,
            hbm,
            pl.BlockSpec((width,), lambda t: (0,), pipeline_mode=pl.Buffered(1)),
            fixed((8, width)),
        ]
        self.out_specs = [
            hbm,
            pl.BlockSpec((3, rows, width), lambda t: (0, 0, 0)),
            pl.BlockSpec((rows, 128), lambda t: (0, 0)),
        ]
        self.out_shapes = [
            jax.ShapeDtypeStruct(inputs.shape, jnp.float32),
            jax.ShapeDtypeStruct((3, rows, width), jnp.float32),
            jax.ShapeDtypeStruct((rows, 128), jnp.float32),
        ]
        self.copies = 3 * (3 + masks) + 3 * self.split + 7 + masks
        self.scratch = [
            pltpu.VMEM((HEAD_DIM, length), low),
            pltpu.VMEM((length, HEAD_DIM), jnp.float32),
            pltpu.VMEM((length, HEAD_DIM), jnp.float32),
            pltpu.VMEM((3, length, quarter), low),
            pltpu.VMEM(turned.shape, low),
            pltpu.VMEM(weights.shape, low),
            pltpu.VMEM((2, 2, size, width), jnp.float32),
            pltpu.VMEM((2, 2, size, width), jnp.float32),
            pltpu.VMEM((2, n_dp, 2, 2, 2, rows, quarter), low),
            pltpu.VMEM((3, n_dp, 2, 2, rows, quarter), low),
            pltpu.VMEM((3, masks, 2, 2, rows, quarter), low),
            pltpu.VMEM((3, 2, 2, rows, quarter), low),
            pltpu.VMEM((3, 2, rows, 2 * quarter), low),
            pltpu.VMEM((3, rows, 2 * quarter), low),
            pltpu.VMEM((2, 2, 2, 2, size, width), low),
            pltpu.VMEM((2, 2, 2, size, width), low),
            pltpu.VMEM((2, 2, 2, size, width), low),
            pltpu.VMEM((2, 2, size, width), low),
            pltpu.VMEM((2, 2, size, width), low),
            pltpu.VMEM((2, size, width), low),
            pltpu.VMEM((128, width), jnp.float32),
            pltpu.VMEM((n_dp, 2, 2, 2, rows, 128), low),
            pltpu.VMEM((7, n_dp, rows, 128), low),
            pltpu.VMEM((n_dp, rows, 128), low),
            pltpu.VMEM((masks, rows, 128), low),
            pltpu.SemaphoreType.DMA((self.copies,)),
            pltpu.SemaphoreType.DMA((self.copies,)),
            pltpu.SemaphoreType.DMA((2,)),
            pltpu.SemaphoreType.DMA((2, 3)),
        ]
        backs, products = [2 * i for i in range(self.split)], [(i - per + 1) * self.steps + 4 for i in range(per)]
        self.starts = backs, products
        self.last_norm = backs[-1] + 2 * 3 + 1
        self.ticks = self.begin + max(self.last_norm + 2 * 2, products[-1] + 4 * 4) + 1

    def run(self, tick, refs):
        ins, (dx_ref, dw_ref, dn_ref), scratch = refs[:16], refs[16:19], refs[19:]
        turned_any, weights_any, inputs_any, first_any, gain_ref, more_ref = ins[10:16]
        kt_ref, dk_ref, dv_ref, g_ref, t_ref, w_ref, x_ref, gx_ref = scratch[:8]
        made, made_y, made_z, sum_z, sides, made_x = scratch[8:14]
        acts, acts_c, sum_c, acts_x, sum_x, acts_y = scratch[14:20]
        totals, norms, norms_c, norms_sy, norms_z = scratch[20:25]
        send, recv, local, chunked = scratch[25:]
        plan, parts = self.plan, self.split
        dp, _ = place()
        y, x, c = own_bit(4), own_bit(2), own_bit(1)
        width, length = t_ref.shape
        quarter = w_ref.shape[2]
        columns = length // 8
        half = 2 * quarter
        rows = dw_ref.shape[1]
        size = columns // parts
        low = jnp.bfloat16
        loads = [
            pltpu.make_async_copy(weights_any, w_ref, local.at[0]),
            pltpu.make_async_copy(turned_any, t_ref, local.at[1]),
        ]

        @pl.when(tick == 1)
        def _():
            for load in loads:
                load.start()

        @pl.when((tick >= self.first) & (tick < self.begin))
        def _():
            pair, step = lax.div(tick - self.first, self.steps), lax.rem(tick - self.first, self.steps)
            attend_back_step(self.block, self.parts, pair, step, self.steps - 1, *ins[:10], g_ref, kt_ref, dk_ref, dv_ref)

        masks = len(plan.masks)
        now = tick - self.begin

        def wide(values):
            return values.astype(jnp.float32)

        def stream(starts, stages, lag, base, most):
            gap = starts[1] - starts[0]
            for stage in reversed(range(len(stages))):
                since = now - starts[0] - lag * stage
                i = lax.div(since, gap)

                @pl.when((since >= 0) & (since <= starts[-1] - starts[0]) & (lax.rem(since, gap) == 0))
                def _(stage=stage, i=i):
                    def made_copies(n):
                        at = base + i * most + sum(len(c(0)) for _, c in stages[:n])
                        return [
                            pltpu.make_async_remote_copy(
                                src, dst, send.at[at + k], recv.at[at + k], device_id=other, device_id_type=MESH)
                            for k, (src, dst, other) in enumerate(stages[n][1](i))
                        ]

                    if stage > 0:
                        for copy in made_copies(stage - 1):
                            copy.wait()
                    stages[stage][0](i)
                    for copy in made_copies(stage):
                        copy.start()

        def product(i):
            @pl.when(i == 0)
            def _():
                loads[1].wait()

            step = 8 * rows
            for z in range(plan.n_dp):
                part = dot(t_ref[z * step : (z + 1) * step, :], g_ref[i])
                made[lax.rem(i, 2), z] = part.astype(low).reshape(2, 2, 2, rows, quarter)

        def product_y(i):
            made_y[i] = (wide(made[lax.rem(i, 2), :, y]) + wide(made_y[i])).astype(low)

        def product_z(i):
            total = wide(made_y[i, dp])
            for n in range(masks):
                total = total + wide(made_z[i, n])
            sum_z[i] = total.astype(low)

        def product_c(i):
            sides[i, :, :, pl.ds(pl.multiple_of(c * quarter, 128), quarter)] = sum_z[i, :, c]

        def product_x(i):
            for side, values in ((x, sides.at[i, x]), (1 - x, made_x.at[i])):
                for core in range(2):
                    for kind in range(3):
                        start = core * quarter + kind * HEAD_DIM
                        lanes = pl.ds(pl.multiple_of(side * half + core * quarter + i * HEAD_DIM, HEAD_DIM), HEAD_DIM)
                        dw_ref[kind, :, lanes] = wide(values[:, start : start + HEAD_DIM])

        def back(i):
            @pl.when(i == 0)
            def _():
                loads[0].wait()

            slot = lax.rem(i, 2)
            pieces = []
            for k in range(3):
                blocks = []
                for n in range(8):
                    at = pl.ds(pl.multiple_of(n * columns + i * size, size), size)
                    blocks.append(jnp.concatenate(
                        [g_ref[p, at, k * HEAD_DIM : (k + 1) * HEAD_DIM] for p in range(3)], axis=1))
                pieces.append(jnp.concatenate(blocks, axis=0))
            step = 512
            for n in range(width // step):
                total = sum(dot(pieces[k], w_ref[k, n * step : (n + 1) * step, :], NT) for k in range(3))
                acts[slot, :, :, :, :, n * step : (n + 1) * step] = total.astype(low).reshape(2, 2, 2, size, step)

        def back_c(i):
            slot = lax.rem(i, 2)
            sum_c[slot] = (wide(acts[slot, :, :, c]) + wide(acts_c[slot])).astype(low)

        def chunk(i):
            slot, at = lax.rem(i, 2), pl.ds(pl.multiple_of(i * size, size), size)
            return [
                pltpu.make_async_copy(inputs_any.at[:, at], x_ref.at[slot], chunked.at[slot, 0]),
                pltpu.make_async_copy(first_any.at[:, at], gx_ref.at[slot], chunked.at[slot, 1]),
            ]

        def chunk_out(i):
            slot, at = lax.rem(i, 2), pl.ds(pl.multiple_of(i * size, size), size)
            return pltpu.make_async_copy(gx_ref.at[slot], dx_ref.at[:, at], chunked.at[slot, 2])

        def back_x(i):
            slot = lax.rem(i, 2)

            @pl.when(i >= 2)
            def _():
                chunk_out(i - 2).wait()

            for load in chunk(i):
                load.start()
            sum_x[slot] = (wide(sum_c[slot, :, x]) + wide(acts_x[slot])).astype(low)

        def norm_back(i):
            slot = lax.rem(i, 2)
            for load in chunk(i):
                load.wait()

            @pl.when(i == 0)
            def _():
                totals[...] = jnp.zeros_like(totals)

            gain = gain_ref[...][None]

            def one(s, carry):
                grad = jnp.where(y == s, wide(sum_x[slot, s]), wide(acts_y[slot]))
                values = x_ref[slot, s]
                centre = values - jnp.mean(values, axis=-1, keepdims=True)
                spread = lax.rsqrt(jnp.mean(centre * centre, axis=-1, keepdims=True) + EPSILON)
                normed = centre * spread
                grown = grad * gain
                mean_one = jnp.mean(grown, axis=-1, keepdims=True)
                mean_two = jnp.mean(grown * normed, axis=-1, keepdims=True)
                gx_ref[slot, s] = gx_ref[slot, s] + (grown - mean_one - normed * mean_two) * spread
                totals[0:1] += jnp.sum(grad * normed, axis=0, keepdims=True)
                totals[1:2] += jnp.sum(grad, axis=0, keepdims=True)
                return carry

            lax.fori_loop(0, 2, one, 0)
            chunk_out(i).start()

        stream(self.starts[0], [
            (back, lambda i: [(acts.at[lax.rem(i, 2), :, :, 1 - c], acts_c.at[lax.rem(i, 2)], partner_seq(1))]),
            (back_c, lambda i: [(sum_c.at[lax.rem(i, 2), :, 1 - x], acts_x.at[lax.rem(i, 2)], partner_seq(2))]),
            (back_x, lambda i: [(sum_x.at[lax.rem(i, 2), 1 - y], acts_y.at[lax.rem(i, 2)], partner_seq(4))]),
            (norm_back, lambda i: []),
        ], 2, 0, 3)
        stream(self.starts[1], [
            (product, lambda i: [(made.at[lax.rem(i, 2), :, 1 - y], made_y.at[i], partner_seq(4))]),
            (product_y, lambda i: [
                (made_y.at[i, lax.bitwise_xor(dp, m)], made_z.at[i, n], partner_dp(plan, m))
                for n, m in enumerate(plan.masks)]),
            (product_z, lambda i: [
                (sum_z.at[i, :, 1 - c], sides.at[i, :, :, pl.ds(c * quarter, quarter)], partner_seq(1))]),
            (product_c, lambda i: [(sides.at[i, 1 - x], made_x.at[i], partner_seq(2))]),
            (product_x, lambda i: []),
        ], 4, 3 * parts, 3 + masks)
        run = Copies(send, recv)
        run.count = 3 * parts + 3 * (3 + masks)
        pieces = []

        def norms_start():
            totals[2:4] = more_ref[0:2]
            norms[...] = totals[...].T.astype(low).reshape(norms.shape)

        def norms_end():
            total = wide(norms_sy[dp])
            for n in range(len(plan.masks)):
                total = total + wide(norms_z[n])
            dn_ref[...] = total
            for i in range(parts - 2, parts):
                chunk_out(i).wait()

        _, seq = place()

        def norms_to(m):
            return norms.at[(slice(None),) + tuple(lax.bitwise_xor(own_bit(b), int(m & b > 0)) for b in plan.bits)]

        def norms_seq():
            total = wide(norms[:, y, x, c])
            for m in range(1, 8):
                total = total + wide(norms_c[m - 1])
            norms_sy[...] = total.astype(low)

        pieces.append((self.last_norm, [
            (norms_start, [run.remote(norms_to(m), norms_c.at[m - 1], partner_seq(m)) for m in range(1, 8)]),
            (norms_seq, [
                run.remote(norms_sy.at[lax.bitwise_xor(dp, m)], norms_z.at[n], partner_dp(plan, m))
                for n, m in enumerate(plan.masks)]),
            (norms_end, []),
        ]))
        run.run(pieces, 2, now)


class Gather:
    def __init__(self, plan, lag, shard, rows, cols, routes):
        self.plan, self.lag, self.rows, self.cols = plan, lag, rows, cols
        self.routes = plan.routes[routes]
        self.across = shard.shape[1] // cols
        self.pieces = shard.shape[0] // rows * self.across
        self.ticks = self.pieces + lag * (plan.hops + 1)
        self.out_shape = jax.ShapeDtypeStruct(plan.lead() + shard.shape, shard.dtype)
        each = 2 * (len(plan.masks) + plan.hops)
        self.scratch = [
            pltpu.VMEM(shard.shape, shard.dtype),
            pltpu.SemaphoreType.DMA((self.pieces, each)),
            pltpu.SemaphoreType.DMA((self.pieces, each)),
            pltpu.SemaphoreType.DMA((2,)),
        ]

    def copies(self, kind, stage, u, full, held, send, recv):
        plan = self.plan
        dp, _ = place()
        rows = pl.ds(pl.multiple_of(lax.div(u, self.across) * self.rows, 16), self.rows)
        out = []
        for h in range(2):
            start = lax.rem(u, self.across) * self.cols + h * (self.cols // 2)
            cols = pl.ds(pl.multiple_of(start, 128), self.cols // 2)
            route = self.routes[kind][h]
            entry, done = route[stage], route[:stage]
            where = (slice(None) if "dp" in done else dp,)
            where += tuple(slice(None) if b in done else own_bit(b) for b in plan.bits)
            part = full.at[where + (rows, cols)]
            src = part if stage else held.at[rows, cols]
            at = h * (len(plan.masks) + plan.hops) + plan.sems(route, stage)
            others = [partner_dp(plan, m) for m in plan.masks] if entry == "dp" else [partner_seq(entry)]
            for n, other in enumerate(others):
                out.append(pltpu.make_async_remote_copy(
                    src, part, send.at[u, at + n], recv.at[u, at + n], device_id=other, device_id_type=MESH))
        return out

    def run(self, tick, shard, full, held, send, recv, local):
        plan, lag = self.plan, self.lag
        dp, _ = place()
        me = tuple(own_bit(b) for b in plan.bits)
        own = pltpu.make_async_copy(held, full.at[(dp,) + me], local.at[0])

        @pl.when(tick == 0)
        def _():
            load = pltpu.make_async_copy(shard, held, local.at[1])
            load.start()
            load.wait()
            own.start()

        @pl.when(tick == lag)
        def _():
            own.wait()

        stages = plan.hops + 1
        for stage in reversed(range(stages + 1)):
            u = tick - lag * stage
            count = len(self.routes)
            for kind in range(count):
                if self.routes[kind] in self.routes[:kind]:
                    continue
                mine = False
                for other in range(count):
                    if self.routes[other] == self.routes[kind]:
                        mine = mine | (lax.rem(u, count) == other)

                @pl.when((u >= 0) & (u < self.pieces) & mine)
                def _(stage=stage, u=u, kind=kind):
                    if stage > 0:
                        for copy in self.copies(kind, stage - 1, u, full, held, send, recv):
                            copy.wait()
                    if stage < stages:
                        for copy in self.copies(kind, stage, u, full, held, send, recv):
                            copy.start()


def attend_step(block, parts, pair, step, packed, col_ref, row_ref, o_ref, ot_ref, lse_ref, vt_ref):
    @pl.when(step == 0)
    def _():
        vt_ref[...] = packed[:, pair, 2].reshape(-1, HEAD_DIM).T

    query = packed[pl.ds(step * parts, parts), pair, 0].reshape(block, HEAD_DIM)
    query_row = row_ref[pl.ds(step, 1), :]
    unit = LOG2E / math.sqrt(HEAD_DIM)

    def visit(j, carry, diagonal):
        top, total, mixed = carry
        key = packed[pl.ds(j * parts, parts), pair, 1].reshape(block, HEAD_DIM)
        at = pl.multiple_of(j * block, block)
        scores = dot(key, query, NT) * unit
        scores = jnp.where(allowed_pairs(col_ref[pl.ds(at, block), :], query_row, diagonal), scores, MASKED)
        above = jnp.maximum(top, jnp.max(scores, axis=0, keepdims=True))
        expo = jnp.exp2(scores - above)
        fade = jnp.exp2(top - above)
        total = total * fade + jnp.sum(expo, axis=0, keepdims=True)
        mixed = mixed * fade + dot(vt_ref[:, pl.ds(at, block)], expo.astype(jnp.bfloat16))
        return above, total, mixed

    start = (
        jnp.full((1, block), MASKED, jnp.float32),
        jnp.zeros((1, block), jnp.float32),
        jnp.zeros((HEAD_DIM, block), jnp.float32),
    )
    carry = lax.fori_loop(0, step, lambda j, c: visit(j, c, False), start)
    top, total, mixed = visit(step, carry, True)
    mixed = mixed / total
    ot_ref[0, 0] = mixed
    lse_ref[0, pl.ds(step, 1), :] = top + jnp.log2(total)
    o_ref[...] = mixed.T.astype(jnp.bfloat16).reshape(o_ref.shape)


def attention_kernel(
    plan, lag, gathers, block, steps, h_ref, s_ref, q_ref, k_ref, v_ref, cos_ref, sin_ref, out_shard, up_shard,
    packed, turned_ref, o_ref, ot_ref, lse_ref, col_ref, row_ref, hs_ref, ss_ref, w_ref, full_out, full_up,
    vt_ref, x_ref, weights_ref, ids_ref, hv, both_ref, rows_ref, wv, halves, send, recv, local, fetch, *more,
):
    tick = pl.program_id(0)

    @pl.when(tick == 0)
    def _():
        greet(plan)

    arrive(plan, lag, tick, h_ref, s_ref, (q_ref, k_ref, v_ref), hs_ref, ss_ref, w_ref, hv, both_ref, rows_ref, wv, halves, send, recv, local)
    for (first, gather), shard, full, held in zip(
        gathers, (out_shard, up_shard), (full_out, full_up), (more[:4], more[4:])
    ):
        gather.run(tick - first, shard, full, *held)
    _, parts, columns, width = x_ref.shape
    heads = packed.shape[1]
    first = ARRIVED + 1

    def acts_load(i):
        return pltpu.make_async_copy(hs_ref.at[lax.div(i, 2), lax.rem(i, 2)], x_ref.at[lax.rem(i, 2)], fetch.at[lax.rem(i, 2)])

    weights_load = pltpu.make_async_copy(w_ref, weights_ref, fetch.at[2])
    ids_load = pltpu.make_async_copy(ss_ref, ids_ref, fetch.at[3])

    @pl.when(tick == ARRIVED)
    def _():
        ids_load.start()
        weights_load.start()
        acts_load(0).start()
        ids_load.wait()
        ids = ids_ref[...].reshape(2 * steps, columns)
        for i in range(2 * steps):
            row_ref[i // parts : i // parts + 1, (i % parts) * columns : (i % parts + 1) * columns] = ids[i : i + 1]
        turned = ids.astype(jnp.float32).T.astype(jnp.int32)
        for i in range(2 * steps):
            mine = turned[:, i : i + 1]
            col_ref[i * columns : (i + 1) * columns, :] = jnp.where(mine < 0, -2, mine)
        weights_load.wait()

    at = tick - first

    @pl.when((at >= 0) & (at < steps))
    def _():
        @pl.when(at + 1 < steps)
        def _():
            acts_load(at + 1).start()

        acts_load(at).wait()
        acts = x_ref[lax.rem(at, 2)].reshape(block, width)
        for kind in range(3):
            made = dot(acts, weights_ref[kind].reshape(width, heads * HEAD_DIM))
            for p in range(heads):
                head = made[:, p * HEAD_DIM : (p + 1) * HEAD_DIM]
                if kind < 2:
                    head = head * cos_ref[...] + pltpu.roll(head, HEAD_DIM // 2, 1) * sin_ref[...]
                packed[pl.ds(at * parts, parts), p, kind] = head.astype(jnp.bfloat16).reshape(parts, columns, HEAD_DIM)
        turned_ref[...] = acts.T

    @pl.when((at >= steps) & (at < steps * (1 + heads)))
    def _():
        pair, step = lax.div(at - steps, steps), lax.rem(at - steps, steps)
        attend_step(block, parts, pair, step, packed, col_ref, row_ref, o_ref, ot_ref, lse_ref, vt_ref)


def attention(plan, acts, segments, weights, cosine, sine, out_shard, up_shard, lag, collective_id):
    _, columns, width = acts.shape
    rows = weights[0].shape[0]
    quarter = width // 4
    heads = quarter // HEAD_DIM
    owners = 8
    length, block = owners * columns, 2 * columns
    steps, parts = length // block, 2
    gathers = (
        (0, Gather(plan, 3, out_shard, out_shard.shape[0], 512, "late")),
        (6, Gather(plan, 3, up_shard, up_shard.shape[0], 512, "late")),
    )
    low = jnp.bfloat16
    begin = ARRIVED + 1

    def at(t):
        return jnp.clip(t - begin, 0, steps - 1)

    def pair(t):
        return lax.div(jnp.clip(t - begin - steps, 0, steps * heads - 1), steps)

    def step(t):
        return lax.rem(jnp.clip(t - begin - steps, 0, steps * heads - 1), steps)

    def fixed(shape):
        return pl.BlockSpec(shape, lambda t: (0,) * len(shape))

    hbm = pl.BlockSpec(memory_space=pl.ANY)
    table = pl.BlockSpec((block, HEAD_DIM), lambda t: (at(t), 0))
    packed_shape = (owners, heads, 3, columns, HEAD_DIM)
    acts_shape = (2, 2, 2, columns, width)
    ids_shape = (2, 2, 2, 1, columns)
    weights_shape = (3,) + plan.lead() + (rows, quarter)
    copies = 3 + 4 * 3 + 3 * (3 + len(plan.masks))
    ticks = max([begin + steps * (1 + heads)] + [first + gather.ticks for first, gather in gathers])
    return pl.pallas_call(
        functools.partial(attention_kernel, plan, lag, gathers, block, steps),
        grid=(ticks,),
        in_specs=[hbm] * 5 + [table, table, hbm, hbm],
        out_specs=[
            fixed(packed_shape),
            pl.BlockSpec((width, block), lambda t: (0, at(t))),
            pl.BlockSpec((parts, None, columns, HEAD_DIM), lambda t: (step(t), pair(t), 0, 0)),
            pl.BlockSpec((1, 1, HEAD_DIM, block), lambda t: (pair(t), step(t), 0, 0)),
            pl.BlockSpec((1, steps, block), lambda t: (pair(t), 0, 0)),
            fixed((length, 1)),
            fixed((steps, block)),
            hbm,
            hbm,
            hbm,
            hbm,
            hbm,
        ],
        out_shape=[
            jax.ShapeDtypeStruct(packed_shape, low),
            jax.ShapeDtypeStruct((width, length), low),
            jax.ShapeDtypeStruct((owners, heads, columns, HEAD_DIM), low),
            jax.ShapeDtypeStruct((heads, steps, HEAD_DIM, block), jnp.float32),
            jax.ShapeDtypeStruct((heads, steps, block), jnp.float32),
            jax.ShapeDtypeStruct((length, 1), jnp.int32),
            jax.ShapeDtypeStruct((steps, block), jnp.int32),
            jax.ShapeDtypeStruct(acts_shape, low),
            jax.ShapeDtypeStruct(ids_shape, jnp.int32),
            jax.ShapeDtypeStruct(weights_shape, low),
            gathers[0][1].out_shape,
            gathers[1][1].out_shape,
        ],
        scratch_shapes=[
            pltpu.VMEM((HEAD_DIM, length), low),
            pltpu.VMEM((2, parts, columns, width), low),
            pltpu.VMEM(weights_shape, low),
            pltpu.VMEM(ids_shape, jnp.int32),
            pltpu.VMEM((columns, width), low),
            pltpu.VMEM((2, columns), jnp.int32),
            pltpu.VMEM((2, 1, columns), jnp.int32),
            pltpu.VMEM((3, rows, width), low),
            pltpu.VMEM((3, 2, rows, width // 2), low),
            pltpu.SemaphoreType.DMA((copies,)),
            pltpu.SemaphoreType.DMA((copies,)),
            pltpu.SemaphoreType.DMA((6,)),
            pltpu.SemaphoreType.DMA((4,)),
        ] + gathers[0][1].scratch + gathers[1][1].scratch,
        compiler_params=pltpu.CompilerParams(
            collective_id=collective_id, has_side_effects=True, vmem_limit_bytes=56 << 20),
    )(acts, segments, *weights, cosine, sine, out_shard, up_shard)


class Mlp:
    def __init__(self, plan, lag, mixed, w_out, inputs, gain, offset, w_up, grad, cotangent, shard):
        tokens, width = inputs.shape
        hidden = w_up.shape[1]
        self.plan, self.lag = plan, lag
        self.blocks = 2 * plan.n_dp
        self.block = hidden // self.blocks
        self.rows = width // (plan.n_dp * plan.n_seq)
        self.gather = Gather(plan, lag, shard, self.rows, 512, "some late")
        self.meet = 5
        self.up = self.meet + 1
        self.back = max(self.gather.ticks, self.up + self.blocks)
        self.norm = self.back + self.blocks
        self.ticks = self.norm + 5
        self.operands = (mixed, w_out, inputs, gain, offset, w_up, grad, cotangent, shard)
        blocks, back, up = self.blocks, self.back, self.up

        def up_block(t):
            later = jnp.clip(t - (up + blocks) + 1, 0, 1)
            return (0, jnp.clip(t - up, 0, blocks - 1) * (1 - later) + jnp.clip(t - back, 0, blocks - 1) * later)

        once = pl.BlockSpec((tokens, width), lambda t: (0, 0), pipeline_mode=pl.Buffered(1))
        row = pl.BlockSpec((width,), lambda t: (0,))
        hbm = pl.BlockSpec(memory_space=pl.ANY)
        self.in_specs = [hbm, hbm, hbm, row, row, pl.BlockSpec((width, self.block), up_block), once, hbm, hbm]
        self.out_specs = [
            hbm,
            hbm,
            hbm,
            hbm,
            hbm,
            hbm,
            pl.BlockSpec((tokens, self.block), lambda t: (0, jnp.clip(t - back, 0, blocks - 1))),
            hbm,
            pl.BlockSpec((8, width), lambda t: (0, 0)),
            hbm,
        ]
        low = jnp.bfloat16
        flat = jax.ShapeDtypeStruct((tokens, width), jnp.float32)
        self.out_shapes = [
            flat,
            flat,
            flat,
            jax.ShapeDtypeStruct((tokens, width), low),
            jax.ShapeDtypeStruct((width, tokens), low),
            jax.ShapeDtypeStruct((width, tokens), low),
            jax.ShapeDtypeStruct((tokens, hidden), low),
            jax.ShapeDtypeStruct(mixed.shape, low),
            jax.ShapeDtypeStruct((8, width), jnp.float32),
            self.gather.out_shape,
        ]
        self.chunk = 64
        self.scratch = [
            pltpu.VMEM((tokens, hidden), low),
            pltpu.VMEM((hidden, tokens), low),
            pltpu.VMEM((tokens, hidden), low),
            pltpu.VMEM((2, 2, 2) + shard.shape, low),
            pltpu.VMEM((tokens, width), jnp.float32),
            pltpu.VMEM((tokens, width), jnp.float32),
            pltpu.VMEM((tokens, width), low),
            pltpu.VMEM(mixed.shape, low),
            pltpu.VMEM((2, 2, self.chunk, width), jnp.float32),
            pltpu.SemaphoreType.DMA((2, 2, plan.n_seq)),
            pltpu.SemaphoreType.DMA((16,)),
            pltpu.SemaphoreType.DMA((2, 2)),
            pltpu.SemaphoreType.DMA((2,)),
        ] + self.gather.scratch

    everyone = True

    def left(self, refs, which, z):
        turned, n = refs[20], self.plan.n_seq
        every = turned.shape[0] // (n * self.plan.n_dp)
        return jnp.concatenate(
            [
                turned[pl.ds(pl.multiple_of((z * n + d) * every + which * self.rows, 16), self.rows), :]
                for d in range(n)
            ],
            axis=0,
        )

    def run(self, tick, refs):
        mixed_hbm, w_out, inputs, gain_ref, offset_ref, up_ref, grad_ref, cotangent, shard = refs[:9]
        output, first_sum, grad_first, grad_low, mixed_turned, acts_turned, gu_ref, back_pairs, sums_ref, full = refs[9:19]
        hidden_ref, turned_ref, slope_ref, down_ref, out_ref, back_ref, acts_ref, pairs, chunks = refs[19:28]
        swaps, local, loads, fetch = refs[28:32]
        plan, block = self.plan, self.block
        dp, seq = place()
        count, heads, columns, _ = pairs.shape
        tokens, width = acts_ref.shape
        low = jnp.bfloat16
        third = 512
        thirds = width // third
        self.gather.run(tick, shard, full, *refs[32:])

        def exchange(which, src, dst):
            return [
                pltpu.make_async_remote_copy(
                    src.at[lax.bitwise_xor(seq, m)], dst.at[seq], swaps.at[which, 0, m], swaps.at[which, 1, m],
                    device_id=partner_seq(m), device_id_type=MESH)
                for m in range(1, count)
            ]

        there = exchange(0, mixed_hbm, pairs)
        here = pltpu.make_async_copy(mixed_hbm.at[seq], pairs.at[seq], local.at[0])
        based = pltpu.make_async_copy(inputs, out_ref, local.at[1])
        outs = [
            pltpu.make_async_copy(
                w_out.at[:, pl.ds(n * third, third)], turned_ref.at[pl.ds(n * width, width), :], local.at[2 + n])
            for n in range(thirds)
        ]
        kept = pltpu.make_async_copy(out_ref, first_sum, local.at[5])
        turns = []
        for n in range(thirds):
            rows = pl.ds(n * third, third)
            base = slope_ref.shape[1] - 2 * width + n * third
            turns.append(pltpu.make_async_copy(slope_ref.at[:, pl.ds(base, third)], mixed_turned.at[rows, :], local.at[6 + n]))
            turns.append(pltpu.make_async_copy(
                slope_ref.at[:, pl.ds(base + width, third)], acts_turned.at[rows, :], local.at[9 + n]))

        @pl.when(tick == 0)
        def _():
            for copy in there + [here, based] + outs:
                copy.start()

        @pl.when(tick == self.meet)
        def _():
            for copy in there + [here, based] + outs:
                copy.wait()
            per = width // (heads * HEAD_DIM)
            for s in range(count // per):
                for g in range(per):
                    for p in range(heads):
                        at = (g * heads + p) * HEAD_DIM
                        acts_ref[s * columns : (s + 1) * columns, at : at + HEAD_DIM] = pairs[s * per + g, p]
            for n in range(thirds):
                part = slice(n * third, (n + 1) * third)
                out_ref[:, part] += dot(acts_ref[...], turned_ref[n * width : (n + 1) * width, :])
                base = slope_ref.shape[1] - 2 * width + n * third
                slope_ref[:, base : base + third] = acts_ref[:, part].T
            kept.start()

            def norm(i, carry):
                rows = pl.ds(pl.multiple_of(i * self.chunk, self.chunk), self.chunk)
                values = out_ref[rows, :]
                centre = values - jnp.mean(values, axis=-1, keepdims=True)
                spread = lax.rsqrt(jnp.mean(centre * centre, axis=-1, keepdims=True) + EPSILON)
                acts_ref[rows, :] = (centre * spread * gain_ref[...][None] + offset_ref[...][None]).astype(low)
                return carry

            lax.fori_loop(0, tokens // self.chunk, norm, 0)
            for n in range(thirds):
                base = slope_ref.shape[1] - width + n * third
                slope_ref[:, base : base + third] = acts_ref[:, n * third : (n + 1) * third].T
            for copy in turns:
                copy.start()

        @pl.when(tick == self.up + 2)
        def _():
            for copy in turns + [kept]:
                copy.wait()

        def block_at(i):
            return pl.ds(pl.multiple_of(i * block, 128), block)

        @pl.when((tick >= self.up) & (tick < self.up + self.blocks))
        def _():
            step = 256
            for n in range(block // step):
                upper = dot(acts_ref[...], up_ref[:, n * step : (n + 1) * step])
                share = 0.5 + 0.5 * lax.erf(upper * (1.0 / math.sqrt(2.0)))
                density = jnp.exp(upper * upper * -0.5) * (1.0 / math.sqrt(2.0 * math.pi))
                made = (upper * share).astype(low)
                at = pl.multiple_of((tick - self.up) * block + n * step, 128)
                hidden_ref[:, pl.ds(at, step)] = made
                turned_ref[pl.ds(at, step), :] = made.T
                slope_ref[:, pl.ds(at, step)] = (share + upper * density).astype(low)

        def fetched(i):
            z, y = lax.div(i, 2), lax.rem(i, 2)
            return pltpu.make_async_copy(full.at[z, y], down_ref.at[y], fetch.at[y])

        i = tick - self.back

        @pl.when((i >= -1) & (i < self.blocks - 1))
        def _():
            fetched(i + 1).start()

        @pl.when((i >= 0) & (i < self.blocks))
        def _():
            fetched(i).wait()
            down = down_ref[lax.rem(i, 2)].reshape(block, -1)

            @pl.when(i == 0)
            def _():
                back_ref[...] = jnp.zeros_like(back_ref)

            grad = dot(grad_ref[...], down, NT) * slope_ref[:, block_at(i)].astype(jnp.float32)
            gu_ref[...] = grad.astype(low)
            for n in range(thirds):
                part = slice(n * third, (n + 1) * third)
                out_ref[:, part] += dot(hidden_ref[:, block_at(i)], down[:, part])
                back_ref[:, part] += dot(gu_ref[...], up_ref[part, :], NT)

        done = pltpu.make_async_copy(out_ref, output, local.at[12])
        first_out = pltpu.make_async_copy(back_ref, grad_first, local.at[13])
        low_out = pltpu.make_async_copy(acts_ref, grad_low, local.at[14])
        chunk = self.chunk

        def chunk_loads(j, slot):
            rows = pl.ds(pl.multiple_of(j * chunk, chunk), chunk)
            return [
                pltpu.make_async_copy(src.at[rows, :], chunks.at[slot, n], loads.at[slot, n])
                for n, src in enumerate((first_sum, cotangent))
            ]

        @pl.when(tick == self.norm - 1)
        def _():
            for copy in outs:
                copy.start()

        @pl.when(tick == self.norm)
        def _():
            done.start()
            sums_ref[...] = jnp.zeros_like(sums_ref)
            for copy in chunk_loads(0, 0):
                copy.start()
            total = tokens // chunk

            def norm_back(j, carry):
                slot = lax.rem(j, 2)

                @pl.when(j + 1 < total)
                def _():
                    for copy in chunk_loads(j + 1, 1 - slot):
                        copy.start()

                for copy in chunk_loads(j, slot):
                    copy.wait()
                rows = pl.ds(pl.multiple_of(j * chunk, chunk), chunk)
                values = chunks[slot, 0]
                centre = values - jnp.mean(values, axis=-1, keepdims=True)
                spread = lax.rsqrt(jnp.mean(centre * centre, axis=-1, keepdims=True) + EPSILON)
                normed = centre * spread
                grad = back_ref[rows, :]
                grown = grad * gain_ref[...][None]
                mean_one = jnp.mean(grown, axis=-1, keepdims=True)
                mean_two = jnp.mean(grown * normed, axis=-1, keepdims=True)
                made = chunks[slot, 1] + (grown - mean_one - normed * mean_two) * spread
                sums_ref[0:1] += jnp.sum(grad * normed, axis=0, keepdims=True)
                sums_ref[1:2] += jnp.sum(grad, axis=0, keepdims=True)
                back_ref[rows, :] = made
                acts_ref[rows, :] = made.astype(low)
                return carry

            lax.fori_loop(0, total, norm_back, 0)
            first_out.start()
            low_out.start()

        again = exchange(1, pairs, back_pairs)
        home = pltpu.make_async_copy(pairs.at[seq], back_pairs.at[seq], local.at[0])

        @pl.when(tick == self.norm + 1)
        def _():
            for copy in outs:
                copy.wait()
            per = width // (heads * HEAD_DIM)
            step = heads * HEAD_DIM
            for g in range(per):
                made = sum(
                    dot(acts_ref[:, n * third : (n + 1) * third],
                        turned_ref[n * width + g * step : n * width + (g + 1) * step, :], NT)
                    for n in range(thirds)
                ).astype(low)
                for s in range(count // per):
                    for p in range(heads):
                        pairs[s * per + g, p] = made[s * columns : (s + 1) * columns, p * HEAD_DIM : (p + 1) * HEAD_DIM]
            for copy in again + [home]:
                copy.start()

        @pl.when(tick == self.ticks - 1)
        def _():
            for copy in again + [home, done, first_out, low_out]:
                copy.wait()


def settle_kernel(piece, *refs):
    (out_any, dx_any, heads_any, down_any, rest_any, norms_ref), refs = refs[:6], refs[6:]
    (output, dx, d_query, d_key, d_value, d_out, d_up, d_down), refs = refs[:8], refs[8:]
    sums, (out_ref, dx_ref, heads_ref, down_ref, rest_ref, load_sem, store_sem) = refs[:4], refs[4:]
    rows = heads_ref.shape[1]
    parts = out_ref.shape[0]
    across = heads_ref.shape[2] // piece
    loads, stores = [], []

    def move(src, held, targets):
        load = pltpu.make_async_copy(src, held, load_sem.at[len(loads)])
        load.start()
        loads.append((load, [
            pltpu.make_async_copy(part, target, store_sem.at[len(stores) + n]) for n, (part, target) in enumerate(targets)
        ]))
        stores.extend(loads[-1][1])

    for i in range(parts):
        move(out_any.at[i], out_ref.at[i], [(out_ref.at[i], output.at[i])])
        move(dx_any.at[i], dx_ref.at[i], [(dx_ref.at[i], dx.at[i])])
    wide_count = rest_any.shape[0] - across
    move(rest_any, rest_ref, [
        (rest_ref.at[n], d_up.at[:, pl.ds(n * piece, piece)] if n < wide_count
         else d_out.at[:, pl.ds((n - wide_count) * piece, piece)])
        for n in range(rest_any.shape[0])
    ])
    move(down_any, down_ref, [
        (down_ref.at[n], d_down.at[pl.ds(n // across * rows, rows), pl.ds(n % across * piece, piece)])
        for n in range(down_any.shape[0])
    ])
    for i, target in enumerate((d_query, d_key, d_value)):
        move(heads_any.at[i], heads_ref.at[i], [(heads_ref.at[i], target)])
    turned = norms_ref[...].T
    for i, target in enumerate(sums):
        target[...] = turned[i : i + 1, :].reshape(target.shape)
    for load, after in loads:
        load.wait()
        for store in after:
            store.start()
    for store in stores:
        store.wait()


def settle(output, dx, heads, down, rest, norms, piece):
    rows, width = heads.shape[1:]
    across = width // piece
    up_width = (rest.shape[0] - across) * piece
    blocks = down.shape[0] // across
    hbm = pl.BlockSpec(memory_space=pl.ANY)
    vmem = pl.BlockSpec(memory_space=pltpu.VMEM)
    f32 = jnp.float32
    arrays = (output, dx, heads, down, rest)
    return pl.pallas_call(
        functools.partial(settle_kernel, piece),
        in_specs=[hbm] * 5 + [vmem],
        out_specs=[hbm] * 8 + [vmem] * 4,
        out_shape=[jax.ShapeDtypeStruct(output.shape, f32), jax.ShapeDtypeStruct(dx.shape, f32)]
        + [jax.ShapeDtypeStruct((rows, width), f32)] * 4
        + [jax.ShapeDtypeStruct((rows, up_width), f32), jax.ShapeDtypeStruct((blocks * rows, width), f32)]
        + [jax.ShapeDtypeStruct((rows,), f32)] * 4,
        scratch_shapes=[pltpu.VMEM(a.shape, f32) for a in arrays] + [
            pltpu.SemaphoreType.DMA((2 * output.shape[0] + 5,)),
            pltpu.SemaphoreType.DMA((2 * output.shape[0] + 3 + down.shape[0] + rest.shape[0],)),
        ],
        compiler_params=pltpu.CompilerParams(vmem_limit_bytes=63 << 20),
    )(output, dx, heads, down, rest, norms)


def layer_norm(values, gain, offset):
    centre = values - jnp.mean(values, axis=-1, keepdims=True)
    spread = jnp.mean(centre * centre, axis=-1, keepdims=True)
    return centre * lax.rsqrt(spread + EPSILON) * gain + offset


def gelu(values):
    return 0.5 * values * (1.0 + lax.erf(values * (1.0 / math.sqrt(2.0))))


def angles(positions):
    half = HEAD_DIM // 2
    rates = jnp.exp(jnp.arange(half, dtype=jnp.float32) * (-math.log(10000.0) / half))
    turned = positions.astype(jnp.float32)[:, None] * rates[None, :]
    return (jnp.cos(turned)[:, None, :], jnp.sin(turned)[:, None, :])


def rotary(values, cosine, sine):
    half = values.shape[-1] // 2
    first = values[..., :half]
    second = values[..., half:]
    return jnp.concatenate(
        [first * cosine - second * sine, second * cosine + first * sine], axis=-1
    )


def lower(values):
    return values.astype(jnp.bfloat16)


def project(acts, weight):
    return jnp.einsum("gcd,de->gce", acts, weight, preferred_element_type=jnp.float32)


def project_back(grads, weight):
    return jnp.einsum("gce,de->gcd", grads, weight, preferred_element_type=jnp.float32)


def outer_sum(left, right):
    return jnp.einsum("gci,gcj->ij", left, right, preferred_element_type=jnp.float32)


def plain_shards(
    inputs,
    segments,
    norm1_gain,
    norm1_bias,
    w_query,
    w_key,
    w_value,
    w_out,
    norm2_gain,
    norm2_bias,
    w_up,
    w_down,
    cotangent,
):
    groups, columns, width = inputs.shape
    heads_count = width // HEAD_DIM
    scale = 1.0 / math.sqrt(HEAD_DIM)
    full_query, full_key, full_value, full_out, full_up, full_down = (
        lax.all_gather(w_query, ("dp", "seq"), axis=0, tiled=True),
        lax.all_gather(w_key, ("dp", "seq"), axis=0, tiled=True),
        lax.all_gather(w_value, ("dp", "seq"), axis=0, tiled=True),
        lax.all_gather(w_out, ("dp", "seq"), axis=0, tiled=True),
        lax.all_gather(w_up, ("dp", "seq"), axis=0, tiled=True),
        lax.all_gather(w_down, ("dp", "seq"), axis=0, tiled=True),
    )
    key_ids = lax.all_gather(segments, "seq", axis=1, tiled=True)
    length = key_ids.shape[1]
    rank = lax.axis_index("seq")
    places = rank * columns + jnp.arange(columns, dtype=jnp.int32)
    key_places = jnp.arange(length, dtype=jnp.int32)
    cosine, sine = angles(places)

    def turn(values):
        shaped = values.reshape(groups, columns, heads_count, HEAD_DIM)
        return rotary(shaped, cosine, sine).reshape(groups, columns, width)

    def permitted(segment_row, key_row):
        same = segment_row[:, None] == key_row[None, :]
        causal = key_places[None, :] <= places[:, None]
        live = (key_row[None, :] >= 0) | (key_places[None, :] == places[:, None])
        return same & causal & live

    def scores_of(query_row, key_block, segment_row, key_row):
        heads_query = query_row.reshape(columns, heads_count, HEAD_DIM)
        heads_key = key_block.reshape(length, heads_count, HEAD_DIM)
        raw = (
            jnp.einsum("chd,lhd->hcl", heads_query, heads_key, preferred_element_type=jnp.float32)
            * scale
        )
        return jnp.where(permitted(segment_row, key_row)[None], raw, MASKED)

    normed_one = layer_norm(inputs, norm1_gain, norm1_bias)
    act_one = lower(normed_one)
    query_zero = project(act_one, full_query)
    key_zero = project(act_one, full_key)
    value_low = lower(project(act_one, full_value))
    query_low = lower(turn(query_zero))
    key_low = lower(turn(key_zero))
    keys_all, values_all = (
        lax.all_gather(key_low, "seq", axis=1, tiled=True),
        lax.all_gather(value_low, "seq", axis=1, tiled=True),
    )

    def attend(items):
        query_row, key_block, value_block, segment_row, key_row = items
        scores = scores_of(query_row, key_block, segment_row, key_row)
        top = jnp.max(scores, axis=-1, keepdims=True)
        expo = jnp.exp(scores - top)
        total = jnp.sum(expo, axis=-1, keepdims=True)
        probs = lower(expo / total)
        heads_value = value_block.reshape(length, heads_count, HEAD_DIM)
        mixed = jnp.einsum("hcl,lhd->chd", probs, heads_value, preferred_element_type=jnp.float32)
        return (mixed.reshape(columns, width), top[..., 0] + jnp.log(total[..., 0]))

    mixed_all, log_totals = lax.map(attend, (query_low, keys_all, values_all, segments, key_ids))
    mixed_low = lower(mixed_all)
    first_sum = inputs + project(mixed_low, full_out)
    act_two = lower(layer_norm(first_sum, norm2_gain, norm2_bias))
    upper = project(act_two, full_up)
    hidden_low = lower(gelu(upper))
    output = first_sum + project(hidden_low, full_down)
    half_width = width // 2
    half_hidden = full_up.shape[1] // 2
    grad_out_low = lower(cotangent)
    down_left = outer_sum(hidden_low, grad_out_low[..., :half_width])
    down_right = outer_sum(hidden_low, grad_out_low[..., half_width:])
    grad_hidden = project_back(grad_out_low, full_down)
    gelu_values, gelu_back = jax.vjp(gelu, upper)
    grad_upper = lower(gelu_back(grad_hidden)[0])
    up_left = outer_sum(act_two, grad_upper[..., :half_hidden])
    up_right = outer_sum(act_two, grad_upper[..., half_hidden:])
    grad_act_two = project_back(grad_upper, full_up)
    normed_two, norm_two_back = jax.vjp(layer_norm, first_sum, norm2_gain, norm2_bias)
    grad_first_norm, gain_two_grad, offset_two_grad = norm_two_back(grad_act_two)
    grad_first = cotangent + grad_first_norm
    grad_attn_low = lower(grad_first)
    out_grad = outer_sum(mixed_low, grad_attn_low)
    grad_mixed = lower(project_back(grad_attn_low, full_out))
    heads_mixed = mixed_all.reshape(groups, columns, heads_count, HEAD_DIM)
    heads_gm = grad_mixed.astype(jnp.float32).reshape(groups, columns, heads_count, HEAD_DIM)
    deltas = jnp.transpose(jnp.sum(heads_mixed * heads_gm, axis=-1), (0, 2, 1))
    key_source, value_source = (key_low, value_low)

    def attend_back(carry, items):
        query_row, grad_row, log_row, delta_row, segment_row, key_row, key_part, value_part = items
        queries_all, grads_all = (
            lax.all_gather(query_row, "seq", axis=0, tiled=True),
            lax.all_gather(grad_row, "seq", axis=0, tiled=True),
        )
        logs_all, deltas_all = (
            lax.all_gather(log_row, "seq", axis=1, tiled=True),
            lax.all_gather(delta_row, "seq", axis=1, tiled=True),
        )
        own_mask = (segment_row[None, :] == key_row[:, None]) & (
            places[None, :] <= key_places[:, None]
        )
        own_mask = own_mask & (
            (segment_row[None, :] >= 0) | (places[None, :] == key_places[:, None])
        )
        heads_query = queries_all.reshape(length, heads_count, HEAD_DIM)
        heads_grad = grads_all.reshape(length, heads_count, HEAD_DIM)
        heads_key = key_part.reshape(columns, heads_count, HEAD_DIM)
        heads_value = value_part.reshape(columns, heads_count, HEAD_DIM)
        raw = (
            jnp.einsum("lhd,chd->hlc", heads_query, heads_key, preferred_element_type=jnp.float32)
            * scale
        )
        scores = jnp.where(own_mask[None], raw, MASKED)
        probs = jnp.exp(scores - logs_all[..., None])
        grad_probs = jnp.einsum(
            "lhd,chd->hlc", heads_grad, heads_value, preferred_element_type=jnp.float32
        )
        grad_scores = lower(probs * (grad_probs - deltas_all[..., None]))
        grad_values = jnp.einsum(
            "hlc,lhd->chd", lower(probs), heads_grad, preferred_element_type=jnp.float32
        )
        grad_keys = (
            jnp.einsum("hlc,lhd->chd", grad_scores, heads_query, preferred_element_type=jnp.float32)
            * scale
        )
        partial_query = (
            jnp.einsum("hlc,chd->lhd", grad_scores, heads_key, preferred_element_type=jnp.float32)
            * scale
        )
        grad_query = lax.psum_scatter(
            partial_query.reshape(length, width).astype(jnp.bfloat16),
            "seq",
            scatter_dimension=0,
            tiled=True,
        ).astype(jnp.float32)
        return (
            carry,
            (grad_query, grad_keys.reshape(columns, width), grad_values.reshape(columns, width)),
        )

    start_carry = jnp.zeros((), jnp.float32)
    end_carry, grads_seq = lax.scan(
        attend_back,
        start_carry,
        (query_low, grad_mixed, log_totals, deltas, segments, key_ids, key_source, value_source),
    )
    grad_query_all, grad_key_all, grad_value_all = grads_seq
    turned_query, turn_back = jax.vjp(turn, query_zero)
    grad_query_low = lower(turn_back(grad_query_all)[0])
    grad_key_low = lower(turn_back(grad_key_all)[0])
    grad_value_low = lower(grad_value_all)
    query_grad = outer_sum(act_one, grad_query_low)
    key_grad = outer_sum(act_one, grad_key_low)
    value_grad = outer_sum(act_one, grad_value_low)
    grad_act_one = project_back(grad_query_low, full_query) + project_back(grad_key_low, full_key)
    grad_act_one = grad_act_one + project_back(grad_value_low, full_value)
    normed_again, norm_one_back = jax.vjp(layer_norm, inputs, norm1_gain, norm1_bias)
    grad_input_norm, gain_one_grad, offset_one_grad = norm_one_back(grad_act_one)
    grad_input = grad_first + grad_input_norm
    summed = (
        lax.psum_scatter(query_grad, ("dp", "seq"), scatter_dimension=0, tiled=True),
        lax.psum_scatter(key_grad, ("dp", "seq"), scatter_dimension=0, tiled=True),
        lax.psum_scatter(value_grad, ("dp", "seq"), scatter_dimension=0, tiled=True),
        lax.psum_scatter(out_grad, ("dp", "seq"), scatter_dimension=0, tiled=True),
        lax.psum_scatter(up_left, ("dp", "seq"), scatter_dimension=0, tiled=True),
        lax.psum_scatter(up_right, ("dp", "seq"), scatter_dimension=0, tiled=True),
        lax.psum_scatter(down_left, ("dp", "seq"), scatter_dimension=0, tiled=True),
        lax.psum_scatter(down_right, ("dp", "seq"), scatter_dimension=0, tiled=True),
        lax.psum_scatter(gain_one_grad, ("dp", "seq"), scatter_dimension=0, tiled=True),
        lax.psum_scatter(offset_one_grad, ("dp", "seq"), scatter_dimension=0, tiled=True),
        lax.psum_scatter(gain_two_grad, ("dp", "seq"), scatter_dimension=0, tiled=True),
        lax.psum_scatter(offset_two_grad, ("dp", "seq"), scatter_dimension=0, tiled=True),
    )
    query_grad, key_grad, value_grad, out_grad = (summed[0], summed[1], summed[2], summed[3])
    up_left, up_right, down_left, down_right = (summed[4], summed[5], summed[6], summed[7])
    gain_one_grad, offset_one_grad, gain_two_grad, offset_two_grad = (
        summed[8],
        summed[9],
        summed[10],
        summed[11],
    )
    up_grad = jnp.concatenate([up_left, up_right], axis=1)
    down_grad = jnp.concatenate([down_left, down_right], axis=1)
    return (
        output,
        grad_input,
        gain_one_grad,
        offset_one_grad,
        query_grad,
        key_grad,
        value_grad,
        out_grad,
        gain_two_grad,
        offset_two_grad,
        up_grad,
        down_grad,
    )


def shards(
    inputs,
    segments,
    norm1_gain,
    norm1_bias,
    w_query,
    w_key,
    w_value,
    w_out,
    norm2_gain,
    norm2_bias,
    w_up,
    w_down,
    cotangent,
    *,
    plan,
):
    groups, columns, width = inputs.shape
    length = columns * plan.n_seq
    lag, piece = 2, 512
    every = plan.n_dp * plan.n_seq

    half = HEAD_DIM // 2
    rates = np.exp(np.arange(half, dtype=np.float32) * np.float32(-math.log(10000.0) / half))
    angle = (np.arange(length, dtype=np.float32)[:, None] * rates[None, :]).astype(np.float32)
    cosine = jnp.asarray(np.concatenate([np.cos(angle), np.cos(angle)], axis=1), jnp.float32)
    sine = jnp.asarray(np.concatenate([-np.sin(angle), np.sin(angle)], axis=1), jnp.float32)

    def flat(values):
        return values.reshape(groups * columns, width)

    act_one = lower(layer_norm(inputs, norm1_gain, norm1_bias))
    packed, turned_one, mixed, mixed_t, lse, seg_col, seg_row, _, _, heads_weight, full_out, full_up = attention(
        plan, act_one, segments, (w_query, w_key, w_value), cosine, sine, w_out, w_up, lag, 1
    )
    grad_low = lower(flat(cotangent))
    mlp = Mlp(
        plan, lag, mixed, full_out.reshape(width, width), flat(inputs), norm2_gain, norm2_bias,
        full_up.reshape(width, -1), grad_low, flat(cotangent), w_down,
    )
    rows = width // every

    (
        down_grad, output, _, grad_first, grad_first_low, mixed_turned, acts_turned, grad_upper, grad_pairs,
        sums_two, _,
    ) = reduce_products(
        plan, [(w_down.shape[0] // rows, grad_low)], rows, piece, lag, "late", 3, mlp, 14
    )
    work = Finish(
        plan, 0, packed, grad_pairs, mixed_t, lse, seg_col, seg_row, cosine, sine, turned_one,
        heads_weight.reshape(3, width, -1), inputs, grad_first.reshape(inputs.shape), norm1_gain, sums_two,
    )
    rest_grads, grad_input, heads_grad, norm_rows = reduce_products(
        plan, [(acts_turned[None], grad_upper), (mixed_turned[None], grad_first_low)], rows, piece, lag, "x late", 4, work
    )
    (
        output, grad_input, query_grad, key_grad, value_grad, out_grad, up_grad, down_grad, *norm_sums
    ) = settle(output.reshape(inputs.shape), grad_input, heads_grad, down_grad, rest_grads, norm_rows, piece)
    return (
        output,
        grad_input,
        norm_sums[0],
        norm_sums[1],
        query_grad,
        key_grad,
        value_grad,
        out_grad,
        norm_sums[2],
        norm_sums[3],
        up_grad,
        down_grad,
    )


def fits(mesh, groups, columns, width, rows):
    return (
        mesh.shape["seq"] == 8
        and groups == 2
        and width % (4 * HEAD_DIM) == 0
        and columns == 256
        and rows % 16 == 0
    )


def solution(mesh):
    placed = (
        P("dp", "seq", None),
        P("dp", "seq"),
        P(),
        P(),
        P(("dp", "seq"), None),
        P(("dp", "seq"), None),
        P(("dp", "seq"), None),
        P(("dp", "seq"), None),
        P(),
        P(),
        P(("dp", "seq"), None),
        P(("dp", "seq"), None),
        P("dp", "seq", None),
    )
    plan = Plan(mesh)

    def layer(inputs, segments, *rest):
        groups, columns, width = inputs.shape
        if fits(mesh, groups, columns, width, rest[2].shape[0]):
            return shards(inputs, segments, *rest, plan=plan)
        return plain_shards(inputs, segments, *rest)

    return jax.shard_map(
        layer,
        mesh=mesh,
        in_specs=placed,
        out_specs=(
            P("dp", "seq", None),
            P("dp", "seq", None),
            P(("dp", "seq")),
            P(("dp", "seq")),
            P(("dp", "seq"), None),
            P(("dp", "seq"), None),
            P(("dp", "seq"), None),
            P(("dp", "seq"), None),
            P(("dp", "seq")),
            P(("dp", "seq")),
            P(("dp", "seq"), None),
            P(("dp", "seq"), None),
        ),
        check_vma=False,
    )
```

```python
import functools
import math

import jax
import jax.numpy as jnp
import numpy as np
from jax import lax
from jax.experimental import pallas as pl
from jax.experimental.pallas import tpu as pltpu
from jax.sharding import PartitionSpec as P

HEAD_DIM = 128


EPSILON = 1e-05
MASKED = -1e30
LOG2E = math.log2(math.e)
NT = (((1,), (1,)), ((), ()))
NN = (((1,), (0,)), ((), ()))


def dot(left, right, dims=NN):
    return lax.dot_general(left, right, dims, preferred_element_type=jnp.float32)


def allowed_pairs(key_col, query_row, diagonal):
    same = key_col == query_row
    if not diagonal:
        return same
    shape = (key_col.shape[0], query_row.shape[1])
    key_at = lax.broadcasted_iota(jnp.int32, shape, 0)
    query_at = lax.broadcasted_iota(jnp.int32, shape, 1)
    return (same & (key_at <= query_at)) | (key_at == query_at)


def attend_back_step(
    block, parts, pair, step, last, q_ref, k_ref, v_ref, g_ref, ot_ref, lse_ref, col_ref, row_ref, cos_ref, sin_ref,
    out_ref, kt_ref, dk_ref, dv_ref,
):
    scale = 1.0 / math.sqrt(HEAD_DIM)

    @pl.when(step == 0)
    def _():
        kt_ref[...] = k_ref[...].reshape(-1, HEAD_DIM).T
        dk_ref[...] = jnp.zeros_like(dk_ref)
        dv_ref[...] = jnp.zeros_like(dv_ref)

    query = q_ref[pl.ds(step * parts, parts)].reshape(block, HEAD_DIM)
    grad = g_ref[pl.ds(step * parts, parts)].reshape(block, HEAD_DIM)
    query_row = row_ref[pl.ds(step, 1), :]
    lse = lse_ref[0, pl.ds(step, 1), :]
    delta = jnp.sum(ot_ref[0, 0] * grad.astype(jnp.float32).T, axis=0, keepdims=True)
    unit = LOG2E * scale

    def visit(j, dqt, diagonal):
        at = pl.multiple_of(j * block, block)
        key = k_ref[pl.ds(j * parts, parts)].reshape(block, HEAD_DIM)
        value = v_ref[pl.ds(j * parts, parts)].reshape(block, HEAD_DIM)
        key_col = col_ref[pl.ds(at, block), :]
        scores = dot(key, query, NT) * unit - lse
        probs = jnp.where(allowed_pairs(key_col, query_row, diagonal), jnp.exp2(scores), 0.0)
        grad_probs = dot(value, grad, NT)
        grad_scores = (probs * (grad_probs - delta)).astype(jnp.bfloat16)
        dv_ref[pl.ds(at, block), :] += dot(probs.astype(jnp.bfloat16), grad)
        dk_ref[pl.ds(at, block), :] += dot(grad_scores, query)
        return dqt + dot(kt_ref[:, pl.ds(at, block)], grad_scores)

    dqt = lax.fori_loop(
        0, step, lambda j, c: visit(j, c, False), jnp.zeros((HEAD_DIM, block), jnp.float32)
    )
    dqt = visit(step, dqt, True)

    def turn_back(values, cosine, sine):
        return values * cosine - pltpu.roll(values, HEAD_DIM // 2, 1) * sine

    at = pl.multiple_of(step * block, block)
    dq = turn_back(dqt.T * scale, cos_ref[pl.ds(at, block), :], sin_ref[pl.ds(at, block), :])
    out_ref[pair, pl.ds(at, block), :HEAD_DIM] = dq.astype(jnp.bfloat16)

    @pl.when(step == last)
    def _():
        dk = turn_back(dk_ref[...] * scale, cos_ref[...], sin_ref[...])
        out_ref[pair, :, HEAD_DIM : 2 * HEAD_DIM] = dk.astype(jnp.bfloat16)
        out_ref[pair, :, 2 * HEAD_DIM :] = dv_ref[...].astype(jnp.bfloat16)


MESH = pl.DeviceIdType.MESH


class Plan:
    def __init__(self, mesh):
        self.n_dp, self.n_seq = mesh.shape["dp"], mesh.shape["seq"]
        bits = [1 << i for i in range(self.n_seq.bit_length() - 1)]
        self.bits = bits[::-1]
        if len(bits) == 3:
            self.orders = ((2, 4, 1), (4, 2, 1))
        else:
            turn = len(bits) // 2
            self.orders = (tuple(bits), tuple(bits[turn:] + bits[:turn]))
        self.hops = len(bits)
        self.masks = range(1, self.n_dp)
        straight = [("dp",) + order for order in self.orders]
        self.routes = {
            "even": [straight, straight],
            "some late": [straight] * 3 + [[order[:1] + ("dp",) + order[1:] for order in self.orders]],
            "late": [straight, [order[:1] + ("dp",) + order[1:] for order in self.orders]],
            "x late": [
                [("dp",) + self.orders[1]] * 2,
                [order[:1] + ("dp",) + order[1:] for order in self.orders],
            ],
        }

    def sems(self, route, stage):
        return sum(len(self.masks) if entry == "dp" else 1 for entry in route[:stage])

    def lead(self):
        return (self.n_dp,) + (2,) * self.hops


def place():
    return lax.axis_index("dp"), lax.axis_index("seq")


def partner_dp(plan, mask):
    dp, seq = place()
    return (lax.bitwise_xor(dp, mask), seq)


def partner_seq(bit):
    dp, seq = place()
    return (dp, lax.bitwise_xor(seq, bit))


def own_bit(bit):
    return lax.bitwise_and(lax.div(place()[1], bit), 1)


def greet(plan, everyone=False):
    barrier = pltpu.get_barrier_semaphore()
    others = [partner_dp(plan, m) for m in plan.masks]
    others += [partner_seq(m) for m in (range(1, plan.n_seq) if everyone else plan.bits)]
    for other in others:
        pl.semaphore_signal(barrier, inc=1, device_id=other, device_id_type=MESH)
    pl.semaphore_wait(barrier, len(others))


def reduce_kernel(plan, jobs, first, count, lag, routes, beside, *refs):
    k, given = len(jobs), sum(job[3] for job in jobs)
    lefts, rights, refs = iter(refs[:given]), refs[given : given + k], refs[given + k :]
    more = [0, 0, 0] if beside is None else [len(beside.in_specs), len(beside.out_specs), len(beside.scratch)]
    extra, refs = refs[: more[0]], refs[more[0] :]
    out_ref, extra = refs[0], extra + refs[1 : 1 + more[1]]
    scratch = refs[1 + more[1] :]
    extra, scratch = extra + scratch[: more[2]], scratch[more[2] :]
    hops, slots = plan.hops, 2 * lag
    stages = hops + 1
    kinds = 1 if routes[0] == routes[1] else 2
    sums, got = [], []
    for h in range(2):
        more = (kinds - 1, 2 * (kinds - 1))
        sums.append(scratch[: stages + more[0]])
        got.append(scratch[stages + more[0] : 2 * stages + sum(more)])
        scratch = scratch[2 * stages + sum(more) :]
    send, recv = scratch
    tick = pl.program_id(0)
    half = out_ref.shape[-1] // 2
    rows = out_ref.shape[-2]
    dp, _ = place()

    @pl.when(tick == 0)
    def _():
        greet(plan, getattr(beside, "everyone", False))

    def sums_at(h, kind, stage, u):
        if stage < stages - 1 or kinds == 1:
            return sums[h][stage], lax.rem(u, lag)
        return sums[h][stage + kind], 0

    def got_at(h, kind, stage, u):
        if stage < stages - 2 or kinds == 1:
            return got[h][stage], lax.rem(u, slots)
        return got[h][stage + 2 * kind], lax.rem(lax.div(u, 2), lag)

    def at_entry(h, kind, stage, value):
        route = routes[kind][h]
        left = [d for d in ("dp",) + tuple(plan.bits) if d not in route[:stage]]
        return tuple(value if d == route[stage] else slice(None) for d in left)

    def own(entry):
        return dp if entry == "dp" else own_bit(entry)

    def copies(h, kind, stage, u):
        route = routes[kind][h]
        entry = route[stage]
        src, kept = sums_at(h, kind, stage, u)
        dst, slot = got_at(h, kind, stage, u)
        at = h * (hops + len(plan.masks)) + plan.sems(route, stage)
        sem = lax.rem(u, slots)
        if entry != "dp":
            return [pltpu.make_async_remote_copy(
                src.at[(kept,) + at_entry(h, kind, stage, 1 - own(entry))], dst.at[slot],
                send.at[sem, at], recv.at[sem, at], device_id=partner_seq(entry), device_id_type=MESH)]
        return [
            pltpu.make_async_remote_copy(
                src.at[(kept,) + at_entry(h, kind, stage, lax.bitwise_xor(dp, mask))], dst.at[slot, n],
                send.at[sem, at + n], recv.at[sem, at + n], device_id=partner_dp(plan, mask), device_id_type=MESH)
            for n, mask in enumerate(plan.masks)
        ]

    def wide(values):
        return values.astype(jnp.float32)

    for stage in reversed(range(1, stages + 1)):
        u = tick - first - lag * stage
        for kind in range(kinds):
            due = (u >= 0) & (u < count)
            if kinds > 1:
                due = due & (lax.rem(u, 2) == kind)

            @pl.when(due)
            def _(stage=stage, kind=kind, u=u):
                for h in range(2):
                    for copy in copies(h, kind, stage - 1, u):
                        copy.wait()
                    entry = routes[kind][h][stage - 1]
                    src, kept = sums_at(h, kind, stage - 1, u)
                    dst, slot = got_at(h, kind, stage - 1, u)
                    total = wide(src[(kept,) + at_entry(h, kind, stage - 1, own(entry))])
                    if entry == "dp":
                        for n in range(len(plan.masks)):
                            total = total + wide(dst[slot, n])
                    else:
                        total = total + wide(dst[slot])
                    if stage == stages:
                        out_ref[0, :, h * half : (h + 1) * half] = total
                        continue
                    to, at = sums_at(h, kind, stage, u)
                    to[at] = total.astype(jnp.bfloat16)
                    for copy in copies(h, kind, stage, u):
                        copy.start()

    for (start, stop, cols, has_left), right in zip(jobs, rights):
        if has_left:
            left = next(lefts)

            def left_rows(which, z, left=left):
                step = rows * plan.n_seq
                return left[which, z * step : (z + 1) * step, :]

        else:
            left_rows = functools.partial(beside.left, extra)

        @pl.when((tick >= first + start) & (tick < first + stop))
        def _(start=start, cols=cols, left_rows=left_rows, right=right):
            u = tick - first
            kept = lax.rem(u, lag)
            which = lax.div(u - start, cols)
            for z in range(plan.n_dp):
                part = dot(left_rows(which, z), right[...]).astype(jnp.bfloat16)
                for h in range(2):
                    piece = part[:, h * half : (h + 1) * half]
                    sums[h][0][kept, z] = piece.reshape(plan.lead()[1:] + (rows, half))
            for h in range(2):
                for copy in copies(h, 0, 0, u):
                    copy.start()

    if beside is not None:
        beside.run(tick, extra)


def reduce_products(plan, pairs, rows, width, lag, routes, collective_id, beside=None, first=0):
    jobs, start = [], 0
    left_specs, right_specs = [], []
    for left, right in pairs:
        cols = right.shape[1] // width
        blocks = left if isinstance(left, int) else left.shape[0]
        stop = start + blocks * cols
        jobs.append((start, stop, cols, left is not blocks))
        if left is not blocks:
            left_specs.append(pl.BlockSpec(left.shape, lambda t: (0, 0, 0), pipeline_mode=pl.Buffered(1)))
        right_specs.append(pl.BlockSpec(
            (right.shape[0], width),
            functools.partial(lambda t, start, stop, cols: (0, lax.rem(jnp.clip(t - first, start, stop - 1) - start, cols)),
                start=start, stop=stop, cols=cols)))
        start = stop
    count = start
    half = width // 2
    slots, hops = 2 * lag, plan.hops
    tail = lag * (hops + 1)
    n_dp, masks = plan.n_dp, len(plan.masks)
    low = jnp.bfloat16

    def room(*shape):
        return pltpu.VMEM(shape + (rows, half), low)

    routes = [[route[::-1] for route in kind] for kind in plan.routes[routes]]

    def left(kind, stage):
        return [n_dp if d == "dp" else 2 for d in ("dp",) + tuple(plan.bits) if d not in routes[kind][0][:stage]]

    def arriving(kind, stage):
        return [masks] * (routes[kind][0][stage] == "dp") + left(kind, stage + 1)

    buffers = []
    for _ in range(2):
        if routes[0] == routes[1]:
            buffers += [room(lag, *left(0, s)) for s in range(hops + 1)]
            buffers += [room(slots, *arriving(0, s)) for s in range(hops + 1)]
            continue
        buffers += [room(lag, *left(0, s)) for s in range(hops)] + [room(1, *left(k, hops)) for k in range(2)]
        buffers += [room(slots, *arriving(0, s)) for s in range(hops - 1)]
        buffers += [room(lag, *arriving(k, s)) for k in range(2) for s in (hops - 1, hops)]
    each = 2 * (hops + len(plan.masks))
    out_specs = [pl.BlockSpec((1, rows, width), lambda t: (jnp.clip(t - first - tail, 0, count - 1), 0, 0))]
    out_shapes = [jax.ShapeDtypeStruct((count, rows, width), jnp.float32)]
    more_in, more_scratch, more_operands = [], [], []
    if beside is not None:
        more_in, more_scratch, more_operands = beside.in_specs, beside.scratch, beside.operands
        out_specs, out_shapes = out_specs + beside.out_specs, out_shapes + beside.out_shapes
    return pl.pallas_call(
        functools.partial(reduce_kernel, plan, jobs, first, count, lag, routes, beside),
        grid=(max(first + count + tail, 0 if beside is None else beside.ticks),),
        in_specs=left_specs + right_specs + more_in,
        out_specs=out_specs,
        out_shape=out_shapes,
        scratch_shapes=more_scratch + buffers + [
            pltpu.SemaphoreType.DMA((slots, each)),
            pltpu.SemaphoreType.DMA((slots, each)),
        ],
        compiler_params=pltpu.CompilerParams(
            collective_id=collective_id, has_side_effects=True, vmem_limit_bytes=63 << 20),
    )(*[p[0] for p in pairs if not isinstance(p[0], int)], *[p[1] for p in pairs], *more_operands)


class Copies:
    def __init__(self, send, recv):
        self.send, self.recv, self.count, self.sent = send, recv, 0, []

    def remote(self, src, dst, device):
        at = self.count
        self.count += 1
        return pltpu.make_async_remote_copy(
            src, dst, self.send.at[at], self.recv.at[at], device_id=device, device_id_type=MESH)

    def run(self, pieces, lag, tick=None):
        last = max(start + lag * len(stages) for start, stages in pieces)
        for now in range(min(start for start, _ in pieces), last + 1):
            due = [
                (start, stages, stage)
                for stage in reversed(range(max(len(stages) for _, stages in pieces) + 1))
                for start, stages in pieces
                if start + lag * stage == now and stage <= len(stages)
            ]

            def step(due=due, now=now):
                for start, stages, stage in due:
                    if stage > 0:
                        for copy in stages[stage - 1][1]:
                            copy.wait()
                    if stage < len(stages):
                        ahead, copies = stages[stage]
                        if ahead is not None:
                            ahead()
                        for copy in copies:
                            copy.start()

            if tick is None:
                step()
            elif due:
                pl.when(tick == now)(step)
        return last


def arrive(plan, lag, tick, h_ref, s_ref, weights, hs_ref, ss_ref, w_ref, hv, both_ref, rows_ref, wv, halves, send, recv, local):
    dp, seq = place()
    y, x, c = own_bit(4), own_bit(2), own_bit(1)
    loads = [pltpu.make_async_copy(h_ref.at[y], hv, local.at[0])]
    loads += [pltpu.make_async_copy(r, wv.at[i], local.at[1 + i]) for i, r in enumerate(weights)]
    own = pltpu.make_async_copy(hv, hs_ref.at[y, x, c], local.at[0])
    named = pltpu.make_async_copy(rows_ref.at[y], ss_ref.at[y, x, c], local.at[4])
    given = pltpu.make_async_copy(s_ref, both_ref, local.at[5])

    @pl.when(tick == 0)
    def _():
        for load in loads + [given]:
            load.start()
        given.wait()
        for i in range(2):
            rows_ref[i] = both_ref[i : i + 1, :]
        named.start()
        for load in loads:
            load.wait()
        own.start()

    run = Copies(send, recv)
    pieces = []
    pieces.append((0, [
        (None, [run.remote(rows_ref.at[1 - y], ss_ref.at[y, x, c], partner_seq(4))]),
        (named.wait, [run.remote(ss_ref.at[:, x, c], ss_ref.at[:, x, c], partner_seq(2))]),
        (None, [run.remote(ss_ref.at[:, :, c], ss_ref.at[:, :, c], partner_seq(1))]),
    ]))
    tokens = hv.shape[0]
    parts = 4
    for i in range(parts):
        rows = pl.ds(i * (tokens // parts), tokens // parts)
        first = run.remote(h_ref.at[1 - y, rows], hs_ref.at[y, x, c, rows], partner_seq(4))
        second = [run.remote(hs_ref.at[:, x, c, rows], hs_ref.at[:, x, c, rows], partner_seq(2))]
        third = [run.remote(hs_ref.at[:, :, c, rows], hs_ref.at[:, :, c, rows], partner_seq(1))]
        pieces.append((ACTS_AT + i, [(None, [first]), (own.wait if i == 0 else None, second), (None, third)]))

    half, quarter = halves.shape[-1], w_ref.shape[-1]
    for i in range(3):
        mine = pltpu.make_async_copy(
            halves.at[i, :, :, pl.ds(c * quarter, quarter)], w_ref.at[i, dp, y, :, c], local.at[1 + i])

        def cut(i=i, mine=mine):
            halves[i, x] = wv[i, :, pl.ds(pl.multiple_of(x * half, 128), half)]
            mine.start()

        to_x = [run.remote(wv.at[i, :, pl.ds((1 - x) * half, half)], halves.at[i, x], partner_seq(2))]
        to_core = [run.remote(
            halves.at[i, :, :, pl.ds((1 - c) * quarter, quarter)], w_ref.at[i, dp, y, :, c], partner_seq(1))]
        to_z = [run.remote(w_ref.at[i, dp, y], w_ref.at[i, dp, y], partner_dp(plan, m)) for m in plan.masks]
        to_y = [run.remote(w_ref.at[i, :, y], w_ref.at[i, :, y], partner_seq(4))]
        pieces.append((WEIGHTS_AT[i], [(None, to_x), (cut, to_core), (mine.wait, to_z), (None, to_y)]))
    run.run(pieces, ARRIVE_LAG, tick)


ARRIVE_LAG = 2
ACTS_AT, WEIGHTS_AT = 2, (0, 2, 4)
ARRIVED = max(ACTS_AT + 3 + 3 * ARRIVE_LAG, WEIGHTS_AT[-1] + 4 * ARRIVE_LAG)


class Finish:
    everyone = True

    def __init__(
        self, plan, first, packed, grads, mixed_t, lse, seg_col, seg_row, cosine, sine, turned, weights, inputs, grad_first, gain, more
    ):
        count, per, _, columns, _ = packed.shape
        length = count * columns
        self.plan, self.first = plan, first
        self.block = seg_row.shape[1]
        self.steps, self.parts = length // self.block, self.block // columns
        self.count = per * self.steps
        self.begin = first + self.count
        self.split = 4
        self.operands = (
            packed, packed, packed, grads, mixed_t, lse, seg_col, seg_row, cosine, sine, turned, weights, inputs, grad_first, gain, more
        )
        width, quarter = turned.shape[0], weights.shape[2]
        n_dp, masks = plan.n_dp, len(plan.masks)
        rows = width // (8 * n_dp)
        size = columns // self.split
        low = jnp.bfloat16

        def pair(t):
            return lax.div(jnp.clip(t - first, 0, self.count - 1), self.steps)

        def step(t):
            return lax.rem(jnp.clip(t - first, 0, self.count - 1), self.steps)

        def whole(which):
            return pl.BlockSpec(
                (count, None, None, columns, HEAD_DIM), lambda t: (0, pair(t), which, 0, 0), pipeline_mode=pl.Buffered(1))

        def fixed(shape):
            return pl.BlockSpec(shape, lambda t: (0,) * len(shape), pipeline_mode=pl.Buffered(1))

        hbm = pl.BlockSpec(memory_space=pl.ANY)
        self.in_specs = [
            whole(0),
            whole(1),
            whole(2),
            pl.BlockSpec((count, None, columns, HEAD_DIM), lambda t: (0, pair(t), 0, 0), pipeline_mode=pl.Buffered(1)),
            pl.BlockSpec((1, 1, HEAD_DIM, self.block), lambda t: (pair(t), step(t), 0, 0)),
            pl.BlockSpec((1, self.steps, self.block), lambda t: (pair(t), 0, 0)),
            fixed((length, 1)),
            fixed((self.steps, self.block)),
            fixed((length, HEAD_DIM)),
            fixed((length, HEAD_DIM)),
            hbm,
            hbm,
            hbm,
            hbm,
            pl.BlockSpec((width,), lambda t: (0,), pipeline_mode=pl.Buffered(1)),
            fixed((8, width)),
        ]
        self.out_specs = [
            hbm,
            pl.BlockSpec((3, rows, width), lambda t: (0, 0, 0)),
            pl.BlockSpec((rows, 128), lambda t: (0, 0)),
        ]
        self.out_shapes = [
            jax.ShapeDtypeStruct(inputs.shape, jnp.float32),
            jax.ShapeDtypeStruct((3, rows, width), jnp.float32),
            jax.ShapeDtypeStruct((rows, 128), jnp.float32),
        ]
        self.copies = 3 * (3 + masks) + 3 * self.split + 7 + masks
        self.scratch = [
            pltpu.VMEM((HEAD_DIM, length), low),
            pltpu.VMEM((length, HEAD_DIM), jnp.float32),
            pltpu.VMEM((length, HEAD_DIM), jnp.float32),
            pltpu.VMEM((3, length, quarter), low),
            pltpu.VMEM(turned.shape, low),
            pltpu.VMEM(weights.shape, low),
            pltpu.VMEM((2, 2, size, width), jnp.float32),
            pltpu.VMEM((2, 2, size, width), jnp.float32),
            pltpu.VMEM((2, n_dp, 2, 2, 2, rows, quarter), low),
            pltpu.VMEM((3, n_dp, 2, 2, rows, quarter), low),
            pltpu.VMEM((3, masks, 2, 2, rows, quarter), low),
            pltpu.VMEM((3, 2, 2, rows, quarter), low),
            pltpu.VMEM((3, 2, rows, 2 * quarter), low),
            pltpu.VMEM((3, rows, 2 * quarter), low),
            pltpu.VMEM((2, 2, 2, 2, size, width), low),
            pltpu.VMEM((2, 2, 2, size, width), low),
            pltpu.VMEM((2, 2, 2, size, width), low),
            pltpu.VMEM((2, 2, size, width), low),
            pltpu.VMEM((2, 2, size, width), low),
            pltpu.VMEM((2, size, width), low),
            pltpu.VMEM((128, width), jnp.float32),
            pltpu.VMEM((n_dp, 2, 2, 2, rows, 128), low),
            pltpu.VMEM((7, n_dp, rows, 128), low),
            pltpu.VMEM((n_dp, rows, 128), low),
            pltpu.VMEM((masks, rows, 128), low),
            pltpu.SemaphoreType.DMA((self.copies,)),
            pltpu.SemaphoreType.DMA((self.copies,)),
            pltpu.SemaphoreType.DMA((2,)),
            pltpu.SemaphoreType.DMA((2, 3)),
        ]
        backs, products = [2 * i for i in range(self.split)], [(i - per + 1) * self.steps + 4 for i in range(per)]
        self.starts = backs, products
        self.last_norm = backs[-1] + 2 * 3 + 1
        self.ticks = self.begin + max(self.last_norm + 2 * 2, products[-1] + 4 * 4) + 1

    def run(self, tick, refs):
        ins, (dx_ref, dw_ref, dn_ref), scratch = refs[:16], refs[16:19], refs[19:]
        turned_any, weights_any, inputs_any, first_any, gain_ref, more_ref = ins[10:16]
        kt_ref, dk_ref, dv_ref, g_ref, t_ref, w_ref, x_ref, gx_ref = scratch[:8]
        made, made_y, made_z, sum_z, sides, made_x = scratch[8:14]
        acts, acts_c, sum_c, acts_x, sum_x, acts_y = scratch[14:20]
        totals, norms, norms_c, norms_sy, norms_z = scratch[20:25]
        send, recv, local, chunked = scratch[25:]
        plan, parts = self.plan, self.split
        dp, _ = place()
        y, x, c = own_bit(4), own_bit(2), own_bit(1)
        width, length = t_ref.shape
        quarter = w_ref.shape[2]
        columns = length // 8
        half = 2 * quarter
        rows = dw_ref.shape[1]
        size = columns // parts
        low = jnp.bfloat16
        loads = [
            pltpu.make_async_copy(weights_any, w_ref, local.at[0]),
            pltpu.make_async_copy(turned_any, t_ref, local.at[1]),
        ]

        @pl.when(tick == 1)
        def _():
            for load in loads:
                load.start()

        @pl.when((tick >= self.first) & (tick < self.begin))
        def _():
            pair, step = lax.div(tick - self.first, self.steps), lax.rem(tick - self.first, self.steps)
            attend_back_step(self.block, self.parts, pair, step, self.steps - 1, *ins[:10], g_ref, kt_ref, dk_ref, dv_ref)

        masks = len(plan.masks)
        now = tick - self.begin

        def wide(values):
            return values.astype(jnp.float32)

        def stream(starts, stages, lag, base, most):
            gap = starts[1] - starts[0]
            for stage in reversed(range(len(stages))):
                since = now - starts[0] - lag * stage
                i = lax.div(since, gap)

                @pl.when((since >= 0) & (since <= starts[-1] - starts[0]) & (lax.rem(since, gap) == 0))
                def _(stage=stage, i=i):
                    def made_copies(n):
                        at = base + i * most + sum(len(c(0)) for _, c in stages[:n])
                        return [
                            pltpu.make_async_remote_copy(
                                src, dst, send.at[at + k], recv.at[at + k], device_id=other, device_id_type=MESH)
                            for k, (src, dst, other) in enumerate(stages[n][1](i))
                        ]

                    if stage > 0:
                        for copy in made_copies(stage - 1):
                            copy.wait()
                    stages[stage][0](i)
                    for copy in made_copies(stage):
                        copy.start()

        def product(i):
            @pl.when(i == 0)
            def _():
                loads[1].wait()

            step = 8 * rows
            for z in range(plan.n_dp):
                part = dot(t_ref[z * step : (z + 1) * step, :], g_ref[i])
                made[lax.rem(i, 2), z] = part.astype(low).reshape(2, 2, 2, rows, quarter)

        def product_y(i):
            made_y[i] = (wide(made[lax.rem(i, 2), :, y]) + wide(made_y[i])).astype(low)

        def product_z(i):
            total = wide(made_y[i, dp])
            for n in range(masks):
                total = total + wide(made_z[i, n])
            sum_z[i] = total.astype(low)

        def product_c(i):
            sides[i, :, :, pl.ds(pl.multiple_of(c * quarter, 128), quarter)] = sum_z[i, :, c]

        def product_x(i):
            for side, values in ((x, sides.at[i, x]), (1 - x, made_x.at[i])):
                for core in range(2):
                    for kind in range(3):
                        start = core * quarter + kind * HEAD_DIM
                        lanes = pl.ds(pl.multiple_of(side * half + core * quarter + i * HEAD_DIM, HEAD_DIM), HEAD_DIM)
                        dw_ref[kind, :, lanes] = wide(values[:, start : start + HEAD_DIM])

        def back(i):
            @pl.when(i == 0)
            def _():
                loads[0].wait()

            slot = lax.rem(i, 2)
            pieces = []
            for k in range(3):
                blocks = []
                for n in range(8):
                    at = pl.ds(pl.multiple_of(n * columns + i * size, size), size)
                    blocks.append(jnp.concatenate(
                        [g_ref[p, at, k * HEAD_DIM : (k + 1) * HEAD_DIM] for p in range(3)], axis=1))
                pieces.append(jnp.concatenate(blocks, axis=0))
            step = 512
            for n in range(width // step):
                total = sum(dot(pieces[k], w_ref[k, n * step : (n + 1) * step, :], NT) for k in range(3))
                acts[slot, :, :, :, :, n * step : (n + 1) * step] = total.astype(low).reshape(2, 2, 2, size, step)

        def back_c(i):
            slot = lax.rem(i, 2)
            sum_c[slot] = (wide(acts[slot, :, :, c]) + wide(acts_c[slot])).astype(low)

        def chunk(i):
            slot, at = lax.rem(i, 2), pl.ds(pl.multiple_of(i * size, size), size)
            return [
                pltpu.make_async_copy(inputs_any.at[:, at], x_ref.at[slot], chunked.at[slot, 0]),
                pltpu.make_async_copy(first_any.at[:, at], gx_ref.at[slot], chunked.at[slot, 1]),
            ]

        def chunk_out(i):
            slot, at = lax.rem(i, 2), pl.ds(pl.multiple_of(i * size, size), size)
            return pltpu.make_async_copy(gx_ref.at[slot], dx_ref.at[:, at], chunked.at[slot, 2])

        def back_x(i):
            slot = lax.rem(i, 2)

            @pl.when(i >= 2)
            def _():
                chunk_out(i - 2).wait()

            for load in chunk(i):
                load.start()
            sum_x[slot] = (wide(sum_c[slot, :, x]) + wide(acts_x[slot])).astype(low)

        def norm_back(i):
            slot = lax.rem(i, 2)
            for load in chunk(i):
                load.wait()

            @pl.when(i == 0)
            def _():
                totals[...] = jnp.zeros_like(totals)

            gain = gain_ref[...][None]

            def one(s, carry):
                grad = jnp.where(y == s, wide(sum_x[slot, s]), wide(acts_y[slot]))
                values = x_ref[slot, s]
                centre = values - jnp.mean(values, axis=-1, keepdims=True)
                spread = lax.rsqrt(jnp.mean(centre * centre, axis=-1, keepdims=True) + EPSILON)
                normed = centre * spread
                grown = grad * gain
                mean_one = jnp.mean(grown, axis=-1, keepdims=True)
                mean_two = jnp.mean(grown * normed, axis=-1, keepdims=True)
                gx_ref[slot, s] = gx_ref[slot, s] + (grown - mean_one - normed * mean_two) * spread
                totals[0:1] += jnp.sum(grad * normed, axis=0, keepdims=True)
                totals[1:2] += jnp.sum(grad, axis=0, keepdims=True)
                return carry

            lax.fori_loop(0, 2, one, 0)
            chunk_out(i).start()

        stream(self.starts[0], [
            (back, lambda i: [(acts.at[lax.rem(i, 2), :, :, 1 - c], acts_c.at[lax.rem(i, 2)], partner_seq(1))]),
            (back_c, lambda i: [(sum_c.at[lax.rem(i, 2), :, 1 - x], acts_x.at[lax.rem(i, 2)], partner_seq(2))]),
            (back_x, lambda i: [(sum_x.at[lax.rem(i, 2), 1 - y], acts_y.at[lax.rem(i, 2)], partner_seq(4))]),
            (norm_back, lambda i: []),
        ], 2, 0, 3)
        stream(self.starts[1], [
            (product, lambda i: [(made.at[lax.rem(i, 2), :, 1 - y], made_y.at[i], partner_seq(4))]),
            (product_y, lambda i: [
                (made_y.at[i, lax.bitwise_xor(dp, m)], made_z.at[i, n], partner_dp(plan, m))
                for n, m in enumerate(plan.masks)]),
            (product_z, lambda i: [
                (sum_z.at[i, :, 1 - c], sides.at[i, :, :, pl.ds(c * quarter, quarter)], partner_seq(1))]),
            (product_c, lambda i: [(sides.at[i, 1 - x], made_x.at[i], partner_seq(2))]),
            (product_x, lambda i: []),
        ], 4, 3 * parts, 3 + masks)
        run = Copies(send, recv)
        run.count = 3 * parts + 3 * (3 + masks)
        pieces = []

        def norms_start():
            totals[2:4] = more_ref[0:2]
            norms[...] = totals[...].T.astype(low).reshape(norms.shape)

        def norms_end():
            total = wide(norms_sy[dp])
            for n in range(len(plan.masks)):
                total = total + wide(norms_z[n])
            dn_ref[...] = total
            for i in range(parts - 2, parts):
                chunk_out(i).wait()

        _, seq = place()

        def norms_to(m):
            return norms.at[(slice(None),) + tuple(lax.bitwise_xor(own_bit(b), int(m & b > 0)) for b in plan.bits)]

        def norms_seq():
            total = wide(norms[:, y, x, c])
            for m in range(1, 8):
                total = total + wide(norms_c[m - 1])
            norms_sy[...] = total.astype(low)

        pieces.append((self.last_norm, [
            (norms_start, [run.remote(norms_to(m), norms_c.at[m - 1], partner_seq(m)) for m in range(1, 8)]),
            (norms_seq, [
                run.remote(norms_sy.at[lax.bitwise_xor(dp, m)], norms_z.at[n], partner_dp(plan, m))
                for n, m in enumerate(plan.masks)]),
            (norms_end, []),
        ]))
        run.run(pieces, 2, now)


class Gather:
    def __init__(self, plan, lag, shard, rows, cols, routes):
        self.plan, self.lag, self.rows, self.cols = plan, lag, rows, cols
        self.routes = plan.routes[routes]
        self.across = shard.shape[1] // cols
        self.pieces = shard.shape[0] // rows * self.across
        self.ticks = self.pieces + lag * (plan.hops + 1)
        self.out_shape = jax.ShapeDtypeStruct(plan.lead() + shard.shape, shard.dtype)
        each = 2 * (len(plan.masks) + plan.hops)
        self.scratch = [
            pltpu.VMEM(shard.shape, shard.dtype),
            pltpu.SemaphoreType.DMA((self.pieces, each)),
            pltpu.SemaphoreType.DMA((self.pieces, each)),
            pltpu.SemaphoreType.DMA((2,)),
        ]

    def copies(self, kind, stage, u, full, held, send, recv):
        plan = self.plan
        dp, _ = place()
        rows = pl.ds(pl.multiple_of(lax.div(u, self.across) * self.rows, 16), self.rows)
        out = []
        routes = self.routes[kind]
        one = routes[0][stage] == routes[1][stage] and set(routes[0][:stage]) == set(routes[1][:stage])
        for h in range(1 if one else 2):
            start = lax.rem(u, self.across) * self.cols + h * (self.cols // 2)
            cols = pl.ds(pl.multiple_of(start, 128), self.cols if one else self.cols // 2)
            route = self.routes[kind][h]
            entry, done = route[stage], route[:stage]
            where = (slice(None) if "dp" in done else dp,)
            where += tuple(slice(None) if b in done else own_bit(b) for b in plan.bits)
            part = full.at[where + (rows, cols)]
            src = part if stage else held.at[rows, cols]
            at = h * (len(plan.masks) + plan.hops) + plan.sems(route, stage)
            others = [partner_dp(plan, m) for m in plan.masks] if entry == "dp" else [partner_seq(entry)]
            for n, other in enumerate(others):
                out.append(pltpu.make_async_remote_copy(
                    src, part, send.at[u, at + n], recv.at[u, at + n], device_id=other, device_id_type=MESH))
        return out

    def run(self, tick, shard, full, held, send, recv, local):
        plan, lag = self.plan, self.lag
        dp, _ = place()
        me = tuple(own_bit(b) for b in plan.bits)
        own = pltpu.make_async_copy(held, full.at[(dp,) + me], local.at[0])

        @pl.when(tick == 0)
        def _():
            load = pltpu.make_async_copy(shard, held, local.at[1])
            load.start()
            load.wait()
            own.start()

        @pl.when(tick == lag)
        def _():
            own.wait()

        stages = plan.hops + 1
        for stage in reversed(range(stages + 1)):
            u = tick - lag * stage
            count = len(self.routes)
            for kind in range(count):
                if self.routes[kind] in self.routes[:kind]:
                    continue
                mine = False
                for other in range(count):
                    if self.routes[other] == self.routes[kind]:
                        mine = mine | (lax.rem(u, count) == other)

                @pl.when((u >= 0) & (u < self.pieces) & mine)
                def _(stage=stage, u=u, kind=kind):
                    if stage > 0:
                        for copy in self.copies(kind, stage - 1, u, full, held, send, recv):
                            copy.wait()
                    if stage < stages:
                        for copy in self.copies(kind, stage, u, full, held, send, recv):
                            copy.start()


def attend_step(block, parts, pair, step, packed, col_ref, row_ref, o_ref, ot_ref, lse_ref, vt_ref):
    @pl.when(step == 0)
    def _():
        vt_ref[...] = packed[:, pair, 2].reshape(-1, HEAD_DIM).T

    query = packed[pl.ds(step * parts, parts), pair, 0].reshape(block, HEAD_DIM)
    query_row = row_ref[pl.ds(step, 1), :]
    unit = LOG2E / math.sqrt(HEAD_DIM)

    def visit(j, carry, diagonal):
        top, total, mixed = carry
        key = packed[pl.ds(j * parts, parts), pair, 1].reshape(block, HEAD_DIM)
        at = pl.multiple_of(j * block, block)
        scores = dot(key, query, NT) * unit
        scores = jnp.where(allowed_pairs(col_ref[pl.ds(at, block), :], query_row, diagonal), scores, MASKED)
        above = jnp.maximum(top, jnp.max(scores, axis=0, keepdims=True))
        expo = jnp.exp2(scores - above)
        fade = jnp.exp2(top - above)
        total = total * fade + jnp.sum(expo, axis=0, keepdims=True)
        mixed = mixed * fade + dot(vt_ref[:, pl.ds(at, block)], expo.astype(jnp.bfloat16))
        return above, total, mixed

    start = (
        jnp.full((1, block), MASKED, jnp.float32),
        jnp.zeros((1, block), jnp.float32),
        jnp.zeros((HEAD_DIM, block), jnp.float32),
    )
    carry = lax.fori_loop(0, step, lambda j, c: visit(j, c, False), start)
    top, total, mixed = visit(step, carry, True)
    mixed = mixed / total
    ot_ref[0, 0] = mixed
    lse_ref[0, pl.ds(step, 1), :] = top + jnp.log2(total)
    o_ref[...] = mixed.T.astype(jnp.bfloat16).reshape(o_ref.shape)


def attention_kernel(
    plan, lag, gathers, block, steps, h_ref, s_ref, q_ref, k_ref, v_ref, cos_ref, sin_ref, out_shard, up_shard,
    packed, turned_ref, o_ref, ot_ref, lse_ref, col_ref, row_ref, hs_ref, ss_ref, w_ref, full_out, full_up,
    vt_ref, x_ref, weights_ref, ids_ref, hv, both_ref, rows_ref, wv, halves, send, recv, local, fetch, *more,
):
    tick = pl.program_id(0)

    @pl.when(tick == 0)
    def _():
        greet(plan)

    arrive(plan, lag, tick, h_ref, s_ref, (q_ref, k_ref, v_ref), hs_ref, ss_ref, w_ref, hv, both_ref, rows_ref, wv, halves, send, recv, local)
    for (first, gather), shard, full, held in zip(
        gathers, (out_shard, up_shard), (full_out, full_up), (more[:4], more[4:])
    ):
        gather.run(tick - first, shard, full, *held)
    _, parts, columns, width = x_ref.shape
    heads = packed.shape[1]
    first = ARRIVED + 1

    def acts_load(i):
        return pltpu.make_async_copy(hs_ref.at[lax.div(i, 2), lax.rem(i, 2)], x_ref.at[lax.rem(i, 2)], fetch.at[lax.rem(i, 2)])

    def weights_load(kind):
        return pltpu.make_async_copy(w_ref.at[kind], weights_ref.at[kind], fetch.at[2 + kind])

    ids_load = pltpu.make_async_copy(ss_ref, ids_ref, fetch.at[5])
    named = 3 * ARRIVE_LAG

    @pl.when(tick == named)
    def _():
        ids_load.start()

    @pl.when(tick == named + 1)
    def _():
        ids_load.wait()
        ids = ids_ref[...].reshape(2 * steps, columns)
        for i in range(2 * steps):
            row_ref[i // parts : i // parts + 1, (i % parts) * columns : (i % parts + 1) * columns] = ids[i : i + 1]
        turned = ids.astype(jnp.float32).T.astype(jnp.int32)
        for i in range(2 * steps):
            mine = turned[:, i : i + 1]
            col_ref[i * columns : (i + 1) * columns, :] = jnp.where(mine < 0, -2, mine)

    for kind in range(3):

        @pl.when(tick == WEIGHTS_AT[kind] + 4 * ARRIVE_LAG)
        def _(kind=kind):
            weights_load(kind).start()

    @pl.when(tick == ARRIVED)
    def _():
        acts_load(0).start()
        for kind in range(3):
            weights_load(kind).wait()

    at = tick - first

    @pl.when((at >= 0) & (at < steps))
    def _():
        @pl.when(at + 1 < steps)
        def _():
            acts_load(at + 1).start()

        acts_load(at).wait()
        acts = x_ref[lax.rem(at, 2)].reshape(block, width)
        for kind in range(3):
            made = dot(acts, weights_ref[kind].reshape(width, heads * HEAD_DIM))
            for p in range(heads):
                head = made[:, p * HEAD_DIM : (p + 1) * HEAD_DIM]
                if kind < 2:
                    head = head * cos_ref[...] + pltpu.roll(head, HEAD_DIM // 2, 1) * sin_ref[...]
                packed[pl.ds(at * parts, parts), p, kind] = head.astype(jnp.bfloat16).reshape(parts, columns, HEAD_DIM)
        turned_ref[...] = acts.T

    @pl.when((at >= steps) & (at < steps * (1 + heads)))
    def _():
        pair, step = lax.div(at - steps, steps), lax.rem(at - steps, steps)
        attend_step(block, parts, pair, step, packed, col_ref, row_ref, o_ref, ot_ref, lse_ref, vt_ref)


def attention(plan, acts, segments, weights, cosine, sine, out_shard, up_shard, lag, collective_id):
    _, columns, width = acts.shape
    rows = weights[0].shape[0]
    quarter = width // 4
    heads = quarter // HEAD_DIM
    owners = 8
    length, block = owners * columns, 2 * columns
    steps, parts = length // block, 2
    gathers = (
        (0, Gather(plan, 3, out_shard, out_shard.shape[0], 512, "late")),
        (7, Gather(plan, 3, up_shard, up_shard.shape[0], 512, "late")),
    )
    low = jnp.bfloat16
    begin = ARRIVED + 1

    def at(t):
        return jnp.clip(t - begin, 0, steps - 1)

    def pair(t):
        return lax.div(jnp.clip(t - begin - steps, 0, steps * heads - 1), steps)

    def step(t):
        return lax.rem(jnp.clip(t - begin - steps, 0, steps * heads - 1), steps)

    def fixed(shape):
        return pl.BlockSpec(shape, lambda t: (0,) * len(shape))

    hbm = pl.BlockSpec(memory_space=pl.ANY)
    table = pl.BlockSpec((block, HEAD_DIM), lambda t: (at(t), 0))
    packed_shape = (owners, heads, 3, columns, HEAD_DIM)
    acts_shape = (2, 2, 2, columns, width)
    ids_shape = (2, 2, 2, 1, columns)
    weights_shape = (3,) + plan.lead() + (rows, quarter)
    copies = 3 + 4 * 3 + 3 * (3 + len(plan.masks))
    ticks = max([begin + steps * (1 + heads)] + [first + gather.ticks for first, gather in gathers])
    return pl.pallas_call(
        functools.partial(attention_kernel, plan, lag, gathers, block, steps),
        grid=(ticks,),
        in_specs=[hbm] * 5 + [table, table, hbm, hbm],
        out_specs=[
            fixed(packed_shape),
            pl.BlockSpec((width, block), lambda t: (0, at(t))),
            pl.BlockSpec((parts, None, columns, HEAD_DIM), lambda t: (step(t), pair(t), 0, 0)),
            pl.BlockSpec((1, 1, HEAD_DIM, block), lambda t: (pair(t), step(t), 0, 0)),
            pl.BlockSpec((1, steps, block), lambda t: (pair(t), 0, 0)),
            fixed((length, 1)),
            fixed((steps, block)),
            hbm,
            hbm,
            hbm,
            hbm,
            hbm,
        ],
        out_shape=[
            jax.ShapeDtypeStruct(packed_shape, low),
            jax.ShapeDtypeStruct((width, length), low),
            jax.ShapeDtypeStruct((owners, heads, columns, HEAD_DIM), low),
            jax.ShapeDtypeStruct((heads, steps, HEAD_DIM, block), jnp.float32),
            jax.ShapeDtypeStruct((heads, steps, block), jnp.float32),
            jax.ShapeDtypeStruct((length, 1), jnp.int32),
            jax.ShapeDtypeStruct((steps, block), jnp.int32),
            jax.ShapeDtypeStruct(acts_shape, low),
            jax.ShapeDtypeStruct(ids_shape, jnp.int32),
            jax.ShapeDtypeStruct(weights_shape, low),
            gathers[0][1].out_shape,
            gathers[1][1].out_shape,
        ],
        scratch_shapes=[
            pltpu.VMEM((HEAD_DIM, length), low),
            pltpu.VMEM((2, parts, columns, width), low),
            pltpu.VMEM(weights_shape, low),
            pltpu.VMEM(ids_shape, jnp.int32),
            pltpu.VMEM((columns, width), low),
            pltpu.VMEM((2, columns), jnp.int32),
            pltpu.VMEM((2, 1, columns), jnp.int32),
            pltpu.VMEM((3, rows, width), low),
            pltpu.VMEM((3, 2, rows, width // 2), low),
            pltpu.SemaphoreType.DMA((copies,)),
            pltpu.SemaphoreType.DMA((copies,)),
            pltpu.SemaphoreType.DMA((6,)),
            pltpu.SemaphoreType.DMA((6,)),
        ] + gathers[0][1].scratch + gathers[1][1].scratch,
        compiler_params=pltpu.CompilerParams(
            collective_id=collective_id, has_side_effects=True, vmem_limit_bytes=56 << 20),
    )(acts, segments, *weights, cosine, sine, out_shard, up_shard)


class Mlp:
    def __init__(self, plan, lag, mixed, w_out, inputs, gain, offset, w_up, grad, cotangent, shard):
        tokens, width = inputs.shape
        hidden = w_up.shape[1]
        self.plan, self.lag = plan, lag
        self.blocks = 2 * plan.n_dp
        self.block = hidden // self.blocks
        self.rows = width // (plan.n_dp * plan.n_seq)
        self.gather = Gather(plan, lag, shard, self.rows, 512, "some late")
        self.meet = 5
        self.up = self.meet + 1
        self.back = max(self.gather.ticks, self.up + self.blocks)
        self.norm = self.back + self.blocks
        self.ticks = self.norm + 5
        self.operands = (mixed, w_out, inputs, gain, offset, w_up, grad, cotangent, shard)
        blocks, back, up = self.blocks, self.back, self.up

        def up_block(t):
            later = jnp.clip(t - (up + blocks) + 1, 0, 1)
            return (0, jnp.clip(t - up, 0, blocks - 1) * (1 - later) + jnp.clip(t - back, 0, blocks - 1) * later)

        once = pl.BlockSpec((tokens, width), lambda t: (0, 0), pipeline_mode=pl.Buffered(1))
        row = pl.BlockSpec((width,), lambda t: (0,))
        hbm = pl.BlockSpec(memory_space=pl.ANY)
        self.in_specs = [hbm, hbm, hbm, row, row, pl.BlockSpec((width, self.block), up_block), once, hbm, hbm]
        self.out_specs = [
            hbm,
            hbm,
            hbm,
            hbm,
            hbm,
            hbm,
            pl.BlockSpec((tokens, self.block), lambda t: (0, jnp.clip(t - back, 0, blocks - 1))),
            hbm,
            pl.BlockSpec((8, width), lambda t: (0, 0)),
            hbm,
        ]
        low = jnp.bfloat16
        flat = jax.ShapeDtypeStruct((tokens, width), jnp.float32)
        self.out_shapes = [
            flat,
            flat,
            flat,
            jax.ShapeDtypeStruct((tokens, width), low),
            jax.ShapeDtypeStruct((width, tokens), low),
            jax.ShapeDtypeStruct((width, tokens), low),
            jax.ShapeDtypeStruct((tokens, hidden), low),
            jax.ShapeDtypeStruct(mixed.shape, low),
            jax.ShapeDtypeStruct((8, width), jnp.float32),
            self.gather.out_shape,
        ]
        self.chunk = 64
        self.scratch = [
            pltpu.VMEM((tokens, hidden), low),
            pltpu.VMEM((hidden, tokens), low),
            pltpu.VMEM((tokens, hidden), low),
            pltpu.VMEM((2, 2, 2) + shard.shape, low),
            pltpu.VMEM((tokens, width), jnp.float32),
            pltpu.VMEM((tokens, width), jnp.float32),
            pltpu.VMEM((tokens, width), low),
            pltpu.VMEM(mixed.shape, low),
            pltpu.VMEM((2, 2, self.chunk, width), jnp.float32),
            pltpu.SemaphoreType.DMA((2, 2, plan.n_seq)),
            pltpu.SemaphoreType.DMA((16,)),
            pltpu.SemaphoreType.DMA((2, 2)),
            pltpu.SemaphoreType.DMA((2,)),
        ] + self.gather.scratch

    everyone = True

    def left(self, refs, which, z):
        turned, n = refs[20], self.plan.n_seq
        every = turned.shape[0] // (n * self.plan.n_dp)
        return jnp.concatenate(
            [
                turned[pl.ds(pl.multiple_of((z * n + d) * every + which * self.rows, 16), self.rows), :]
                for d in range(n)
            ],
            axis=0,
        )

    def run(self, tick, refs):
        mixed_hbm, w_out, inputs, gain_ref, offset_ref, up_ref, grad_ref, cotangent, shard = refs[:9]
        output, first_sum, grad_first, grad_low, mixed_turned, acts_turned, gu_ref, back_pairs, sums_ref, full = refs[9:19]
        hidden_ref, turned_ref, slope_ref, down_ref, out_ref, back_ref, acts_ref, pairs, chunks = refs[19:28]
        swaps, local, loads, fetch = refs[28:32]
        plan, block = self.plan, self.block
        dp, seq = place()
        count, heads, columns, _ = pairs.shape
        tokens, width = acts_ref.shape
        low = jnp.bfloat16
        third = 512
        thirds = width // third
        self.gather.run(tick, shard, full, *refs[32:])

        def exchange(which, src, dst):
            return [
                pltpu.make_async_remote_copy(
                    src.at[lax.bitwise_xor(seq, m)], dst.at[seq], swaps.at[which, 0, m], swaps.at[which, 1, m],
                    device_id=partner_seq(m), device_id_type=MESH)
                for m in range(1, count)
            ]

        there = exchange(0, mixed_hbm, pairs)
        here = pltpu.make_async_copy(mixed_hbm.at[seq], pairs.at[seq], local.at[0])
        based = pltpu.make_async_copy(inputs, out_ref, local.at[1])
        outs = [
            pltpu.make_async_copy(
                w_out.at[:, pl.ds(n * third, third)], turned_ref.at[pl.ds(n * width, width), :], local.at[2 + n])
            for n in range(thirds)
        ]
        kept = pltpu.make_async_copy(out_ref, first_sum, local.at[5])
        turns = []
        for n in range(thirds):
            rows = pl.ds(n * third, third)
            base = slope_ref.shape[1] - 2 * width + n * third
            turns.append(pltpu.make_async_copy(slope_ref.at[:, pl.ds(base, third)], mixed_turned.at[rows, :], local.at[6 + n]))
            turns.append(pltpu.make_async_copy(
                slope_ref.at[:, pl.ds(base + width, third)], acts_turned.at[rows, :], local.at[9 + n]))

        @pl.when(tick == 0)
        def _():
            for copy in there + [here, based] + outs:
                copy.start()

        @pl.when(tick == self.meet)
        def _():
            for copy in there + [here, based] + outs:
                copy.wait()
            per = width // (heads * HEAD_DIM)
            for s in range(count // per):
                for g in range(per):
                    for p in range(heads):
                        at = (g * heads + p) * HEAD_DIM
                        acts_ref[s * columns : (s + 1) * columns, at : at + HEAD_DIM] = pairs[s * per + g, p]
            for n in range(thirds):
                part = slice(n * third, (n + 1) * third)
                out_ref[:, part] += dot(acts_ref[...], turned_ref[n * width : (n + 1) * width, :])
                base = slope_ref.shape[1] - 2 * width + n * third
                slope_ref[:, base : base + third] = acts_ref[:, part].T
            kept.start()

            def norm(i, carry):
                rows = pl.ds(pl.multiple_of(i * self.chunk, self.chunk), self.chunk)
                values = out_ref[rows, :]
                centre = values - jnp.mean(values, axis=-1, keepdims=True)
                spread = lax.rsqrt(jnp.mean(centre * centre, axis=-1, keepdims=True) + EPSILON)
                acts_ref[rows, :] = (centre * spread * gain_ref[...][None] + offset_ref[...][None]).astype(low)
                return carry

            lax.fori_loop(0, tokens // self.chunk, norm, 0)
            for n in range(thirds):
                base = slope_ref.shape[1] - width + n * third
                slope_ref[:, base : base + third] = acts_ref[:, n * third : (n + 1) * third].T
            for copy in turns:
                copy.start()

        @pl.when(tick == self.up + 2)
        def _():
            for copy in turns + [kept]:
                copy.wait()

        def block_at(i):
            return pl.ds(pl.multiple_of(i * block, 128), block)

        @pl.when((tick >= self.up) & (tick < self.up + self.blocks))
        def _():
            step = 256
            for n in range(block // step):
                upper = dot(acts_ref[...], up_ref[:, n * step : (n + 1) * step])
                share = 0.5 + 0.5 * lax.erf(upper * (1.0 / math.sqrt(2.0)))
                density = jnp.exp(upper * upper * -0.5) * (1.0 / math.sqrt(2.0 * math.pi))
                made = (upper * share).astype(low)
                at = pl.multiple_of((tick - self.up) * block + n * step, 128)
                hidden_ref[:, pl.ds(at, step)] = made
                turned_ref[pl.ds(at, step), :] = made.T
                slope_ref[:, pl.ds(at, step)] = (share + upper * density).astype(low)

        def fetched(i):
            z, y = lax.div(i, 2), lax.rem(i, 2)
            return pltpu.make_async_copy(full.at[z, y], down_ref.at[y], fetch.at[y])

        i = tick - self.back

        @pl.when((i >= -1) & (i < self.blocks - 1))
        def _():
            fetched(i + 1).start()

        @pl.when((i >= 0) & (i < self.blocks))
        def _():
            fetched(i).wait()
            down = down_ref[lax.rem(i, 2)].reshape(block, -1)

            @pl.when(i == 0)
            def _():
                back_ref[...] = jnp.zeros_like(back_ref)

            grad = dot(grad_ref[...], down, NT) * slope_ref[:, block_at(i)].astype(jnp.float32)
            gu_ref[...] = grad.astype(low)
            for n in range(thirds):
                part = slice(n * third, (n + 1) * third)
                out_ref[:, part] += dot(hidden_ref[:, block_at(i)], down[:, part])
                back_ref[:, part] += dot(gu_ref[...], up_ref[part, :], NT)

        done = pltpu.make_async_copy(out_ref, output, local.at[12])
        first_out = pltpu.make_async_copy(back_ref, grad_first, local.at[13])
        low_out = pltpu.make_async_copy(acts_ref, grad_low, local.at[14])
        chunk = self.chunk

        def chunk_loads(j, slot):
            rows = pl.ds(pl.multiple_of(j * chunk, chunk), chunk)
            return [
                pltpu.make_async_copy(src.at[rows, :], chunks.at[slot, n], loads.at[slot, n])
                for n, src in enumerate((first_sum, cotangent))
            ]

        @pl.when(tick == self.norm - 1)
        def _():
            for copy in outs:
                copy.start()

        @pl.when(tick == self.norm)
        def _():
            done.start()
            sums_ref[...] = jnp.zeros_like(sums_ref)
            for copy in chunk_loads(0, 0):
                copy.start()
            total = tokens // chunk

            def norm_back(j, carry):
                slot = lax.rem(j, 2)

                @pl.when(j + 1 < total)
                def _():
                    for copy in chunk_loads(j + 1, 1 - slot):
                        copy.start()

                for copy in chunk_loads(j, slot):
                    copy.wait()
                rows = pl.ds(pl.multiple_of(j * chunk, chunk), chunk)
                values = chunks[slot, 0]
                centre = values - jnp.mean(values, axis=-1, keepdims=True)
                spread = lax.rsqrt(jnp.mean(centre * centre, axis=-1, keepdims=True) + EPSILON)
                normed = centre * spread
                grad = back_ref[rows, :]
                grown = grad * gain_ref[...][None]
                mean_one = jnp.mean(grown, axis=-1, keepdims=True)
                mean_two = jnp.mean(grown * normed, axis=-1, keepdims=True)
                made = chunks[slot, 1] + (grown - mean_one - normed * mean_two) * spread
                sums_ref[0:1] += jnp.sum(grad * normed, axis=0, keepdims=True)
                sums_ref[1:2] += jnp.sum(grad, axis=0, keepdims=True)
                back_ref[rows, :] = made
                acts_ref[rows, :] = made.astype(low)
                return carry

            lax.fori_loop(0, total, norm_back, 0)
            first_out.start()
            low_out.start()

        again = exchange(1, pairs, back_pairs)
        home = pltpu.make_async_copy(pairs.at[seq], back_pairs.at[seq], local.at[0])

        @pl.when(tick == self.norm + 1)
        def _():
            for copy in outs:
                copy.wait()
            per = width // (heads * HEAD_DIM)
            step = heads * HEAD_DIM
            for g in range(per):
                made = sum(
                    dot(acts_ref[:, n * third : (n + 1) * third],
                        turned_ref[n * width + g * step : n * width + (g + 1) * step, :], NT)
                    for n in range(thirds)
                ).astype(low)
                for s in range(count // per):
                    for p in range(heads):
                        pairs[s * per + g, p] = made[s * columns : (s + 1) * columns, p * HEAD_DIM : (p + 1) * HEAD_DIM]
            for copy in again + [home]:
                copy.start()

        @pl.when(tick == self.ticks - 1)
        def _():
            for copy in again + [home, done, first_out, low_out]:
                copy.wait()


def settle_kernel(piece, *refs):
    (out_any, dx_any, heads_any, down_any, rest_any, norms_ref), refs = refs[:6], refs[6:]
    (output, dx, d_query, d_key, d_value, d_out, d_up, d_down), refs = refs[:8], refs[8:]
    sums, (out_ref, dx_ref, heads_ref, down_ref, rest_ref, load_sem, store_sem) = refs[:4], refs[4:]
    rows = heads_ref.shape[1]
    parts = out_ref.shape[0]
    across = heads_ref.shape[2] // piece
    loads, stores = [], []

    def move(src, held, targets):
        load = pltpu.make_async_copy(src, held, load_sem.at[len(loads)])
        load.start()
        loads.append((load, [
            pltpu.make_async_copy(part, target, store_sem.at[len(stores) + n]) for n, (part, target) in enumerate(targets)
        ]))
        stores.extend(loads[-1][1])

    for i in range(parts):
        move(out_any.at[i], out_ref.at[i], [(out_ref.at[i], output.at[i])])
        move(dx_any.at[i], dx_ref.at[i], [(dx_ref.at[i], dx.at[i])])
    wide_count = rest_any.shape[0] - across
    move(rest_any, rest_ref, [
        (rest_ref.at[n], d_up.at[:, pl.ds(n * piece, piece)] if n < wide_count
         else d_out.at[:, pl.ds((n - wide_count) * piece, piece)])
        for n in range(rest_any.shape[0])
    ])
    move(down_any, down_ref, [
        (down_ref.at[n], d_down.at[pl.ds(n // across * rows, rows), pl.ds(n % across * piece, piece)])
        for n in range(down_any.shape[0])
    ])
    for i, target in enumerate((d_query, d_key, d_value)):
        move(heads_any.at[i], heads_ref.at[i], [(heads_ref.at[i], target)])
    turned = norms_ref[...].T
    for i, target in enumerate(sums):
        target[...] = turned[i : i + 1, :].reshape(target.shape)
    for load, after in loads:
        load.wait()
        for store in after:
            store.start()
    for store in stores:
        store.wait()


def settle(output, dx, heads, down, rest, norms, piece):
    rows, width = heads.shape[1:]
    across = width // piece
    up_width = (rest.shape[0] - across) * piece
    blocks = down.shape[0] // across
    hbm = pl.BlockSpec(memory_space=pl.ANY)
    vmem = pl.BlockSpec(memory_space=pltpu.VMEM)
    f32 = jnp.float32
    arrays = (output, dx, heads, down, rest)
    return pl.pallas_call(
        functools.partial(settle_kernel, piece),
        in_specs=[hbm] * 5 + [vmem],
        out_specs=[hbm] * 8 + [vmem] * 4,
        out_shape=[jax.ShapeDtypeStruct(output.shape, f32), jax.ShapeDtypeStruct(dx.shape, f32)]
        + [jax.ShapeDtypeStruct((rows, width), f32)] * 4
        + [jax.ShapeDtypeStruct((rows, up_width), f32), jax.ShapeDtypeStruct((blocks * rows, width), f32)]
        + [jax.ShapeDtypeStruct((rows,), f32)] * 4,
        scratch_shapes=[pltpu.VMEM(a.shape, f32) for a in arrays] + [
            pltpu.SemaphoreType.DMA((2 * output.shape[0] + 5,)),
            pltpu.SemaphoreType.DMA((2 * output.shape[0] + 3 + down.shape[0] + rest.shape[0],)),
        ],
        compiler_params=pltpu.CompilerParams(vmem_limit_bytes=63 << 20),
    )(output, dx, heads, down, rest, norms)


def layer_norm(values, gain, offset):
    centre = values - jnp.mean(values, axis=-1, keepdims=True)
    spread = jnp.mean(centre * centre, axis=-1, keepdims=True)
    return centre * lax.rsqrt(spread + EPSILON) * gain + offset


def gelu(values):
    return 0.5 * values * (1.0 + lax.erf(values * (1.0 / math.sqrt(2.0))))


def angles(positions):
    half = HEAD_DIM // 2
    rates = jnp.exp(jnp.arange(half, dtype=jnp.float32) * (-math.log(10000.0) / half))
    turned = positions.astype(jnp.float32)[:, None] * rates[None, :]
    return (jnp.cos(turned)[:, None, :], jnp.sin(turned)[:, None, :])


def rotary(values, cosine, sine):
    half = values.shape[-1] // 2
    first = values[..., :half]
    second = values[..., half:]
    return jnp.concatenate(
        [first * cosine - second * sine, second * cosine + first * sine], axis=-1
    )


def lower(values):
    return values.astype(jnp.bfloat16)


def project(acts, weight):
    return jnp.einsum("gcd,de->gce", acts, weight, preferred_element_type=jnp.float32)


def project_back(grads, weight):
    return jnp.einsum("gce,de->gcd", grads, weight, preferred_element_type=jnp.float32)


def outer_sum(left, right):
    return jnp.einsum("gci,gcj->ij", left, right, preferred_element_type=jnp.float32)


def plain_shards(
    inputs,
    segments,
    norm1_gain,
    norm1_bias,
    w_query,
    w_key,
    w_value,
    w_out,
    norm2_gain,
    norm2_bias,
    w_up,
    w_down,
    cotangent,
):
    groups, columns, width = inputs.shape
    heads_count = width // HEAD_DIM
    scale = 1.0 / math.sqrt(HEAD_DIM)
    full_query, full_key, full_value, full_out, full_up, full_down = (
        lax.all_gather(w_query, ("dp", "seq"), axis=0, tiled=True),
        lax.all_gather(w_key, ("dp", "seq"), axis=0, tiled=True),
        lax.all_gather(w_value, ("dp", "seq"), axis=0, tiled=True),
        lax.all_gather(w_out, ("dp", "seq"), axis=0, tiled=True),
        lax.all_gather(w_up, ("dp", "seq"), axis=0, tiled=True),
        lax.all_gather(w_down, ("dp", "seq"), axis=0, tiled=True),
    )
    key_ids = lax.all_gather(segments, "seq", axis=1, tiled=True)
    length = key_ids.shape[1]
    rank = lax.axis_index("seq")
    places = rank * columns + jnp.arange(columns, dtype=jnp.int32)
    key_places = jnp.arange(length, dtype=jnp.int32)
    cosine, sine = angles(places)

    def turn(values):
        shaped = values.reshape(groups, columns, heads_count, HEAD_DIM)
        return rotary(shaped, cosine, sine).reshape(groups, columns, width)

    def permitted(segment_row, key_row):
        same = segment_row[:, None] == key_row[None, :]
        causal = key_places[None, :] <= places[:, None]
        live = (key_row[None, :] >= 0) | (key_places[None, :] == places[:, None])
        return same & causal & live

    def scores_of(query_row, key_block, segment_row, key_row):
        heads_query = query_row.reshape(columns, heads_count, HEAD_DIM)
        heads_key = key_block.reshape(length, heads_count, HEAD_DIM)
        raw = (
            jnp.einsum("chd,lhd->hcl", heads_query, heads_key, preferred_element_type=jnp.float32)
            * scale
        )
        return jnp.where(permitted(segment_row, key_row)[None], raw, MASKED)

    normed_one = layer_norm(inputs, norm1_gain, norm1_bias)
    act_one = lower(normed_one)
    query_zero = project(act_one, full_query)
    key_zero = project(act_one, full_key)
    value_low = lower(project(act_one, full_value))
    query_low = lower(turn(query_zero))
    key_low = lower(turn(key_zero))
    keys_all, values_all = (
        lax.all_gather(key_low, "seq", axis=1, tiled=True),
        lax.all_gather(value_low, "seq", axis=1, tiled=True),
    )

    def attend(items):
        query_row, key_block, value_block, segment_row, key_row = items
        scores = scores_of(query_row, key_block, segment_row, key_row)
        top = jnp.max(scores, axis=-1, keepdims=True)
        expo = jnp.exp(scores - top)
        total = jnp.sum(expo, axis=-1, keepdims=True)
        probs = lower(expo / total)
        heads_value = value_block.reshape(length, heads_count, HEAD_DIM)
        mixed = jnp.einsum("hcl,lhd->chd", probs, heads_value, preferred_element_type=jnp.float32)
        return (mixed.reshape(columns, width), top[..., 0] + jnp.log(total[..., 0]))

    mixed_all, log_totals = lax.map(attend, (query_low, keys_all, values_all, segments, key_ids))
    mixed_low = lower(mixed_all)
    first_sum = inputs + project(mixed_low, full_out)
    act_two = lower(layer_norm(first_sum, norm2_gain, norm2_bias))
    upper = project(act_two, full_up)
    hidden_low = lower(gelu(upper))
    output = first_sum + project(hidden_low, full_down)
    half_width = width // 2
    half_hidden = full_up.shape[1] // 2
    grad_out_low = lower(cotangent)
    down_left = outer_sum(hidden_low, grad_out_low[..., :half_width])
    down_right = outer_sum(hidden_low, grad_out_low[..., half_width:])
    grad_hidden = project_back(grad_out_low, full_down)
    gelu_values, gelu_back = jax.vjp(gelu, upper)
    grad_upper = lower(gelu_back(grad_hidden)[0])
    up_left = outer_sum(act_two, grad_upper[..., :half_hidden])
    up_right = outer_sum(act_two, grad_upper[..., half_hidden:])
    grad_act_two = project_back(grad_upper, full_up)
    normed_two, norm_two_back = jax.vjp(layer_norm, first_sum, norm2_gain, norm2_bias)
    grad_first_norm, gain_two_grad, offset_two_grad = norm_two_back(grad_act_two)
    grad_first = cotangent + grad_first_norm
    grad_attn_low = lower(grad_first)
    out_grad = outer_sum(mixed_low, grad_attn_low)
    grad_mixed = lower(project_back(grad_attn_low, full_out))
    heads_mixed = mixed_all.reshape(groups, columns, heads_count, HEAD_DIM)
    heads_gm = grad_mixed.astype(jnp.float32).reshape(groups, columns, heads_count, HEAD_DIM)
    deltas = jnp.transpose(jnp.sum(heads_mixed * heads_gm, axis=-1), (0, 2, 1))
    key_source, value_source = (key_low, value_low)

    def attend_back(carry, items):
        query_row, grad_row, log_row, delta_row, segment_row, key_row, key_part, value_part = items
        queries_all, grads_all = (
            lax.all_gather(query_row, "seq", axis=0, tiled=True),
            lax.all_gather(grad_row, "seq", axis=0, tiled=True),
        )
        logs_all, deltas_all = (
            lax.all_gather(log_row, "seq", axis=1, tiled=True),
            lax.all_gather(delta_row, "seq", axis=1, tiled=True),
        )
        own_mask = (segment_row[None, :] == key_row[:, None]) & (
            places[None, :] <= key_places[:, None]
        )
        own_mask = own_mask & (
            (segment_row[None, :] >= 0) | (places[None, :] == key_places[:, None])
        )
        heads_query = queries_all.reshape(length, heads_count, HEAD_DIM)
        heads_grad = grads_all.reshape(length, heads_count, HEAD_DIM)
        heads_key = key_part.reshape(columns, heads_count, HEAD_DIM)
        heads_value = value_part.reshape(columns, heads_count, HEAD_DIM)
        raw = (
            jnp.einsum("lhd,chd->hlc", heads_query, heads_key, preferred_element_type=jnp.float32)
            * scale
        )
        scores = jnp.where(own_mask[None], raw, MASKED)
        probs = jnp.exp(scores - logs_all[..., None])
        grad_probs = jnp.einsum(
            "lhd,chd->hlc", heads_grad, heads_value, preferred_element_type=jnp.float32
        )
        grad_scores = lower(probs * (grad_probs - deltas_all[..., None]))
        grad_values = jnp.einsum(
            "hlc,lhd->chd", lower(probs), heads_grad, preferred_element_type=jnp.float32
        )
        grad_keys = (
            jnp.einsum("hlc,lhd->chd", grad_scores, heads_query, preferred_element_type=jnp.float32)
            * scale
        )
        partial_query = (
            jnp.einsum("hlc,chd->lhd", grad_scores, heads_key, preferred_element_type=jnp.float32)
            * scale
        )
        grad_query = lax.psum_scatter(
            partial_query.reshape(length, width).astype(jnp.bfloat16),
            "seq",
            scatter_dimension=0,
            tiled=True,
        ).astype(jnp.float32)
        return (
            carry,
            (grad_query, grad_keys.reshape(columns, width), grad_values.reshape(columns, width)),
        )

    start_carry = jnp.zeros((), jnp.float32)
    end_carry, grads_seq = lax.scan(
        attend_back,
        start_carry,
        (query_low, grad_mixed, log_totals, deltas, segments, key_ids, key_source, value_source),
    )
    grad_query_all, grad_key_all, grad_value_all = grads_seq
    turned_query, turn_back = jax.vjp(turn, query_zero)
    grad_query_low = lower(turn_back(grad_query_all)[0])
    grad_key_low = lower(turn_back(grad_key_all)[0])
    grad_value_low = lower(grad_value_all)
    query_grad = outer_sum(act_one, grad_query_low)
    key_grad = outer_sum(act_one, grad_key_low)
    value_grad = outer_sum(act_one, grad_value_low)
    grad_act_one = project_back(grad_query_low, full_query) + project_back(grad_key_low, full_key)
    grad_act_one = grad_act_one + project_back(grad_value_low, full_value)
    normed_again, norm_one_back = jax.vjp(layer_norm, inputs, norm1_gain, norm1_bias)
    grad_input_norm, gain_one_grad, offset_one_grad = norm_one_back(grad_act_one)
    grad_input = grad_first + grad_input_norm
    summed = (
        lax.psum_scatter(query_grad, ("dp", "seq"), scatter_dimension=0, tiled=True),
        lax.psum_scatter(key_grad, ("dp", "seq"), scatter_dimension=0, tiled=True),
        lax.psum_scatter(value_grad, ("dp", "seq"), scatter_dimension=0, tiled=True),
        lax.psum_scatter(out_grad, ("dp", "seq"), scatter_dimension=0, tiled=True),
        lax.psum_scatter(up_left, ("dp", "seq"), scatter_dimension=0, tiled=True),
        lax.psum_scatter(up_right, ("dp", "seq"), scatter_dimension=0, tiled=True),
        lax.psum_scatter(down_left, ("dp", "seq"), scatter_dimension=0, tiled=True),
        lax.psum_scatter(down_right, ("dp", "seq"), scatter_dimension=0, tiled=True),
        lax.psum_scatter(gain_one_grad, ("dp", "seq"), scatter_dimension=0, tiled=True),
        lax.psum_scatter(offset_one_grad, ("dp", "seq"), scatter_dimension=0, tiled=True),
        lax.psum_scatter(gain_two_grad, ("dp", "seq"), scatter_dimension=0, tiled=True),
        lax.psum_scatter(offset_two_grad, ("dp", "seq"), scatter_dimension=0, tiled=True),
    )
    query_grad, key_grad, value_grad, out_grad = (summed[0], summed[1], summed[2], summed[3])
    up_left, up_right, down_left, down_right = (summed[4], summed[5], summed[6], summed[7])
    gain_one_grad, offset_one_grad, gain_two_grad, offset_two_grad = (
        summed[8],
        summed[9],
        summed[10],
        summed[11],
    )
    up_grad = jnp.concatenate([up_left, up_right], axis=1)
    down_grad = jnp.concatenate([down_left, down_right], axis=1)
    return (
        output,
        grad_input,
        gain_one_grad,
        offset_one_grad,
        query_grad,
        key_grad,
        value_grad,
        out_grad,
        gain_two_grad,
        offset_two_grad,
        up_grad,
        down_grad,
    )


def shards(
    inputs,
    segments,
    norm1_gain,
    norm1_bias,
    w_query,
    w_key,
    w_value,
    w_out,
    norm2_gain,
    norm2_bias,
    w_up,
    w_down,
    cotangent,
    *,
    plan,
):
    groups, columns, width = inputs.shape
    length = columns * plan.n_seq
    lag, piece = 2, 512
    every = plan.n_dp * plan.n_seq

    half = HEAD_DIM // 2
    rates = np.exp(np.arange(half, dtype=np.float32) * np.float32(-math.log(10000.0) / half))
    angle = (np.arange(length, dtype=np.float32)[:, None] * rates[None, :]).astype(np.float32)
    cosine = jnp.asarray(np.concatenate([np.cos(angle), np.cos(angle)], axis=1), jnp.float32)
    sine = jnp.asarray(np.concatenate([-np.sin(angle), np.sin(angle)], axis=1), jnp.float32)

    def flat(values):
        return values.reshape(groups * columns, width)

    act_one = lower(layer_norm(inputs, norm1_gain, norm1_bias))
    packed, turned_one, mixed, mixed_t, lse, seg_col, seg_row, _, _, heads_weight, full_out, full_up = attention(
        plan, act_one, segments, (w_query, w_key, w_value), cosine, sine, w_out, w_up, lag, 1
    )
    grad_low = lower(flat(cotangent))
    mlp = Mlp(
        plan, lag, mixed, full_out.reshape(width, width), flat(inputs), norm2_gain, norm2_bias,
        full_up.reshape(width, -1), grad_low, flat(cotangent), w_down,
    )
    rows = width // every

    (
        down_grad, output, _, grad_first, grad_first_low, mixed_turned, acts_turned, grad_upper, grad_pairs,
        sums_two, _,
    ) = reduce_products(
        plan, [(w_down.shape[0] // rows, grad_low)], rows, piece, lag, "late", 3, mlp, 14
    )
    work = Finish(
        plan, 0, packed, grad_pairs, mixed_t, lse, seg_col, seg_row, cosine, sine, turned_one,
        heads_weight.reshape(3, width, -1), inputs, grad_first.reshape(inputs.shape), norm1_gain, sums_two,
    )
    rest_grads, grad_input, heads_grad, norm_rows = reduce_products(
        plan, [(acts_turned[None], grad_upper), (mixed_turned[None], grad_first_low)], rows, piece, lag, "x late", 4, work
    )
    (
        output, grad_input, query_grad, key_grad, value_grad, out_grad, up_grad, down_grad, *norm_sums
    ) = settle(output.reshape(inputs.shape), grad_input, heads_grad, down_grad, rest_grads, norm_rows, piece)
    return (
        output,
        grad_input,
        norm_sums[0],
        norm_sums[1],
        query_grad,
        key_grad,
        value_grad,
        out_grad,
        norm_sums[2],
        norm_sums[3],
        up_grad,
        down_grad,
    )


def fits(mesh, groups, columns, width, rows):
    return (
        mesh.shape["seq"] == 8
        and groups == 2
        and width % (4 * HEAD_DIM) == 0
        and columns == 256
        and rows % 16 == 0
    )


def solution(mesh):
    placed = (
        P("dp", "seq", None),
        P("dp", "seq"),
        P(),
        P(),
        P(("dp", "seq"), None),
        P(("dp", "seq"), None),
        P(("dp", "seq"), None),
        P(("dp", "seq"), None),
        P(),
        P(),
        P(("dp", "seq"), None),
        P(("dp", "seq"), None),
        P("dp", "seq", None),
    )
    plan = Plan(mesh)

    def layer(inputs, segments, *rest):
        groups, columns, width = inputs.shape
        if fits(mesh, groups, columns, width, rest[2].shape[0]):
            return shards(inputs, segments, *rest, plan=plan)
        return plain_shards(inputs, segments, *rest)

    return jax.shard_map(
        layer,
        mesh=mesh,
        in_specs=placed,
        out_specs=(
            P("dp", "seq", None),
            P("dp", "seq", None),
            P(("dp", "seq")),
            P(("dp", "seq")),
            P(("dp", "seq"), None),
            P(("dp", "seq"), None),
            P(("dp", "seq"), None),
            P(("dp", "seq"), None),
            P(("dp", "seq")),
            P(("dp", "seq")),
            P(("dp", "seq"), None),
            P(("dp", "seq"), None),
        ),
        check_vma=False,
    )
```

```python
import functools
import math

import jax
import jax.numpy as jnp
import numpy as np
from jax import lax
from jax.experimental import pallas as pl
from jax.experimental.pallas import tpu as pltpu
from jax.sharding import PartitionSpec as P

HEAD_DIM = 128


EPSILON = 1e-05
MASKED = -1e30
LOG2E = math.log2(math.e)
NT = (((1,), (1,)), ((), ()))
NN = (((1,), (0,)), ((), ()))


def dot(left, right, dims=NN):
    return lax.dot_general(left, right, dims, preferred_element_type=jnp.float32)


def allowed_pairs(key_col, query_row, diagonal):
    same = key_col == query_row
    if not diagonal:
        return same
    shape = (key_col.shape[0], query_row.shape[1])
    key_at = lax.broadcasted_iota(jnp.int32, shape, 0)
    query_at = lax.broadcasted_iota(jnp.int32, shape, 1)
    return (same & (key_at <= query_at)) | (key_at == query_at)


def attend_back_step(
    block, parts, pair, step, last, q_ref, k_ref, v_ref, g_ref, ot_ref, lse_ref, col_ref, row_ref, cos_ref, sin_ref,
    out_ref, kt_ref, dk_ref, dv_ref,
):
    scale = 1.0 / math.sqrt(HEAD_DIM)

    @pl.when(step == 0)
    def _():
        kt_ref[...] = k_ref[...].reshape(-1, HEAD_DIM).T
        dk_ref[...] = jnp.zeros_like(dk_ref)
        dv_ref[...] = jnp.zeros_like(dv_ref)

    query = q_ref[pl.ds(step * parts, parts)].reshape(block, HEAD_DIM)
    grad = g_ref[pl.ds(step * parts, parts)].reshape(block, HEAD_DIM)
    query_row = row_ref[pl.ds(step, 1), :]
    lse = lse_ref[0, pl.ds(step, 1), :]
    delta = jnp.sum(ot_ref[0, 0] * grad.astype(jnp.float32).T, axis=0, keepdims=True)
    unit = LOG2E * scale

    def visit(j, dqt, diagonal):
        at = pl.multiple_of(j * block, block)
        key = k_ref[pl.ds(j * parts, parts)].reshape(block, HEAD_DIM)
        value = v_ref[pl.ds(j * parts, parts)].reshape(block, HEAD_DIM)
        key_col = col_ref[pl.ds(at, block), :]
        scores = dot(key, query, NT) * unit - lse
        probs = jnp.where(allowed_pairs(key_col, query_row, diagonal), jnp.exp2(scores), 0.0)
        grad_probs = dot(value, grad, NT)
        grad_scores = (probs * (grad_probs - delta)).astype(jnp.bfloat16)
        dv_ref[pl.ds(at, block), :] += dot(probs.astype(jnp.bfloat16), grad)
        dk_ref[pl.ds(at, block), :] += dot(grad_scores, query)
        return dqt + dot(kt_ref[:, pl.ds(at, block)], grad_scores)

    dqt = lax.fori_loop(
        0, step, lambda j, c: visit(j, c, False), jnp.zeros((HEAD_DIM, block), jnp.float32)
    )
    dqt = visit(step, dqt, True)

    def turn_back(values, cosine, sine):
        return values * cosine - pltpu.roll(values, HEAD_DIM // 2, 1) * sine

    at = pl.multiple_of(step * block, block)
    dq = turn_back(dqt.T * scale, cos_ref[pl.ds(at, block), :], sin_ref[pl.ds(at, block), :])
    out_ref[pair, pl.ds(at, block), :HEAD_DIM] = dq.astype(jnp.bfloat16)

    @pl.when(step == last)
    def _():
        dk = turn_back(dk_ref[...] * scale, cos_ref[...], sin_ref[...])
        out_ref[pair, :, HEAD_DIM : 2 * HEAD_DIM] = dk.astype(jnp.bfloat16)
        out_ref[pair, :, 2 * HEAD_DIM :] = dv_ref[...].astype(jnp.bfloat16)


MESH = pl.DeviceIdType.MESH


class Plan:
    def __init__(self, mesh):
        self.n_dp, self.n_seq = mesh.shape["dp"], mesh.shape["seq"]
        bits = [1 << i for i in range(self.n_seq.bit_length() - 1)]
        self.bits = bits[::-1]
        if len(bits) == 3:
            self.orders = ((2, 4, 1), (4, 2, 1))
        else:
            turn = len(bits) // 2
            self.orders = (tuple(bits), tuple(bits[turn:] + bits[:turn]))
        self.hops = len(bits)
        self.masks = range(1, self.n_dp)
        straight = [("dp",) + order for order in self.orders]
        self.routes = {
            "even": [straight, straight],
            "some late": [straight] * 3 + [[order[:1] + ("dp",) + order[1:] for order in self.orders]],
            "late": [straight, [order[:1] + ("dp",) + order[1:] for order in self.orders]],
            "x late": [
                [("dp",) + self.orders[1]] * 2,
                [order[:1] + ("dp",) + order[1:] for order in self.orders],
            ],
        }

    def sems(self, route, stage):
        return sum(len(self.masks) if entry == "dp" else 1 for entry in route[:stage])

    def lead(self):
        return (self.n_dp,) + (2,) * self.hops


def place():
    return lax.axis_index("dp"), lax.axis_index("seq")


def partner_dp(plan, mask):
    dp, seq = place()
    return (lax.bitwise_xor(dp, mask), seq)


def partner_seq(bit):
    dp, seq = place()
    return (dp, lax.bitwise_xor(seq, bit))


def own_bit(bit):
    return lax.bitwise_and(lax.div(place()[1], bit), 1)


def greet(plan, everyone=False):
    barrier = pltpu.get_barrier_semaphore()
    others = [partner_dp(plan, m) for m in plan.masks]
    others += [partner_seq(m) for m in (range(1, plan.n_seq) if everyone else plan.bits)]
    for other in others:
        pl.semaphore_signal(barrier, inc=1, device_id=other, device_id_type=MESH)
    pl.semaphore_wait(barrier, len(others))


def reduce_kernel(plan, jobs, first, count, lag, routes, beside, *refs):
    k, given = len(jobs), sum(job[3] for job in jobs)
    lefts, rights, refs = iter(refs[:given]), refs[given : given + k], refs[given + k :]
    more = [0, 0, 0] if beside is None else [len(beside.in_specs), len(beside.out_specs), len(beside.scratch)]
    extra, refs = refs[: more[0]], refs[more[0] :]
    out_ref, extra = refs[0], extra + refs[1 : 1 + more[1]]
    scratch = refs[1 + more[1] :]
    extra, scratch = extra + scratch[: more[2]], scratch[more[2] :]
    hops, slots = plan.hops, 2 * lag
    stages = hops + 1
    kinds = 1 if routes[0] == routes[1] else 2
    sums, got = [], []
    for h in range(2):
        more = (kinds - 1, 2 * (kinds - 1))
        sums.append(scratch[: stages + more[0]])
        got.append(scratch[stages + more[0] : 2 * stages + sum(more)])
        scratch = scratch[2 * stages + sum(more) :]
    send, recv = scratch
    tick = pl.program_id(0)
    half = out_ref.shape[-1] // 2
    rows = out_ref.shape[-2]
    dp, _ = place()

    @pl.when(tick == 0)
    def _():
        greet(plan, getattr(beside, "everyone", False))

    def sums_at(h, kind, stage, u):
        if stage < stages - 1 or kinds == 1:
            return sums[h][stage], lax.rem(u, lag)
        return sums[h][stage + kind], 0

    def got_at(h, kind, stage, u):
        if stage < stages - 2 or kinds == 1:
            return got[h][stage], lax.rem(u, slots)
        return got[h][stage + 2 * kind], lax.rem(lax.div(u, 2), lag)

    def at_entry(h, kind, stage, value):
        route = routes[kind][h]
        left = [d for d in ("dp",) + tuple(plan.bits) if d not in route[:stage]]
        return tuple(value if d == route[stage] else slice(None) for d in left)

    def own(entry):
        return dp if entry == "dp" else own_bit(entry)

    def copies(h, kind, stage, u):
        route = routes[kind][h]
        entry = route[stage]
        src, kept = sums_at(h, kind, stage, u)
        dst, slot = got_at(h, kind, stage, u)
        at = h * (hops + len(plan.masks)) + plan.sems(route, stage)
        sem = lax.rem(u, slots)
        if entry != "dp":
            return [pltpu.make_async_remote_copy(
                src.at[(kept,) + at_entry(h, kind, stage, 1 - own(entry))], dst.at[slot],
                send.at[sem, at], recv.at[sem, at], device_id=partner_seq(entry), device_id_type=MESH)]
        return [
            pltpu.make_async_remote_copy(
                src.at[(kept,) + at_entry(h, kind, stage, lax.bitwise_xor(dp, mask))], dst.at[slot, n],
                send.at[sem, at + n], recv.at[sem, at + n], device_id=partner_dp(plan, mask), device_id_type=MESH)
            for n, mask in enumerate(plan.masks)
        ]

    def wide(values):
        return values.astype(jnp.float32)

    for stage in reversed(range(1, stages + 1)):
        u = tick - first - lag * stage
        for kind in range(kinds):
            due = (u >= 0) & (u < count)
            if kinds > 1:
                due = due & (lax.rem(u, 2) == kind)

            @pl.when(due)
            def _(stage=stage, kind=kind, u=u):
                for h in range(2):
                    for copy in copies(h, kind, stage - 1, u):
                        copy.wait()
                    entry = routes[kind][h][stage - 1]
                    src, kept = sums_at(h, kind, stage - 1, u)
                    dst, slot = got_at(h, kind, stage - 1, u)
                    total = wide(src[(kept,) + at_entry(h, kind, stage - 1, own(entry))])
                    if entry == "dp":
                        for n in range(len(plan.masks)):
                            total = total + wide(dst[slot, n])
                    else:
                        total = total + wide(dst[slot])
                    if stage == stages:
                        out_ref[0, :, h * half : (h + 1) * half] = total
                        continue
                    to, at = sums_at(h, kind, stage, u)
                    to[at] = total.astype(jnp.bfloat16)
                    for copy in copies(h, kind, stage, u):
                        copy.start()

    for (start, stop, cols, has_left), right in zip(jobs, rights):
        if has_left:
            left = next(lefts)

            def left_rows(which, z, left=left):
                step = rows * plan.n_seq
                return left[which, z * step : (z + 1) * step, :]

        else:
            left_rows = functools.partial(beside.left, extra)

        @pl.when((tick >= first + start) & (tick < first + stop))
        def _(start=start, cols=cols, left_rows=left_rows, right=right):
            u = tick - first
            kept = lax.rem(u, lag)
            which = lax.div(u - start, cols)
            given = right[...].astype(jnp.bfloat16)
            for z in range(plan.n_dp):
                part = dot(left_rows(which, z), given).astype(jnp.bfloat16)
                for h in range(2):
                    piece = part[:, h * half : (h + 1) * half]
                    sums[h][0][kept, z] = piece.reshape(plan.lead()[1:] + (rows, half))
            for h in range(2):
                for copy in copies(h, 0, 0, u):
                    copy.start()

    if beside is not None:
        beside.run(tick, extra)


def reduce_products(plan, pairs, rows, width, lag, routes, collective_id, beside=None, first=0):
    jobs, start = [], 0
    left_specs, right_specs = [], []
    for left, right in pairs:
        cols = right.shape[1] // width
        blocks = left if isinstance(left, int) else left.shape[0]
        stop = start + blocks * cols
        jobs.append((start, stop, cols, left is not blocks))
        if left is not blocks:
            left_specs.append(pl.BlockSpec(left.shape, lambda t: (0, 0, 0), pipeline_mode=pl.Buffered(1)))
        right_specs.append(pl.BlockSpec(
            (right.shape[0], width),
            functools.partial(lambda t, start, stop, cols: (0, lax.rem(jnp.clip(t - first, start, stop - 1) - start, cols)),
                start=start, stop=stop, cols=cols)))
        start = stop
    count = start
    half = width // 2
    slots, hops = 2 * lag, plan.hops
    tail = lag * (hops + 1)
    n_dp, masks = plan.n_dp, len(plan.masks)
    low = jnp.bfloat16

    def room(*shape):
        return pltpu.VMEM(shape + (rows, half), low)

    routes = [[route[::-1] for route in kind] for kind in plan.routes[routes]]

    def left(kind, stage):
        return [n_dp if d == "dp" else 2 for d in ("dp",) + tuple(plan.bits) if d not in routes[kind][0][:stage]]

    def arriving(kind, stage):
        return [masks] * (routes[kind][0][stage] == "dp") + left(kind, stage + 1)

    buffers = []
    for _ in range(2):
        if routes[0] == routes[1]:
            buffers += [room(lag, *left(0, s)) for s in range(hops + 1)]
            buffers += [room(slots, *arriving(0, s)) for s in range(hops + 1)]
            continue
        buffers += [room(lag, *left(0, s)) for s in range(hops)] + [room(1, *left(k, hops)) for k in range(2)]
        buffers += [room(slots, *arriving(0, s)) for s in range(hops - 1)]
        buffers += [room(lag, *arriving(k, s)) for k in range(2) for s in (hops - 1, hops)]
    each = 2 * (hops + len(plan.masks))
    out_specs = [pl.BlockSpec((1, rows, width), lambda t: (jnp.clip(t - first - tail, 0, count - 1), 0, 0))]
    out_shapes = [jax.ShapeDtypeStruct((count, rows, width), jnp.float32)]
    more_in, more_scratch, more_operands = [], [], []
    if beside is not None:
        more_in, more_scratch, more_operands = beside.in_specs, beside.scratch, beside.operands
        out_specs, out_shapes = out_specs + beside.out_specs, out_shapes + beside.out_shapes
    return pl.pallas_call(
        functools.partial(reduce_kernel, plan, jobs, first, count, lag, routes, beside),
        grid=(max(first + count + tail, 0 if beside is None else beside.ticks),),
        in_specs=left_specs + right_specs + more_in,
        out_specs=out_specs,
        out_shape=out_shapes,
        scratch_shapes=more_scratch + buffers + [
            pltpu.SemaphoreType.DMA((slots, each)),
            pltpu.SemaphoreType.DMA((slots, each)),
        ],
        compiler_params=pltpu.CompilerParams(
            collective_id=collective_id, has_side_effects=True, vmem_limit_bytes=63 << 20),
    )(*[p[0] for p in pairs if not isinstance(p[0], int)], *[p[1] for p in pairs], *more_operands)


class Copies:
    def __init__(self, send, recv):
        self.send, self.recv, self.count, self.sent = send, recv, 0, []

    def remote(self, src, dst, device):
        at = self.count
        self.count += 1
        return pltpu.make_async_remote_copy(
            src, dst, self.send.at[at], self.recv.at[at], device_id=device, device_id_type=MESH)

    def run(self, pieces, lag, tick=None):
        last = max(start + lag * len(stages) for start, stages in pieces)
        for now in range(min(start for start, _ in pieces), last + 1):
            due = [
                (start, stages, stage)
                for stage in reversed(range(max(len(stages) for _, stages in pieces) + 1))
                for start, stages in pieces
                if start + lag * stage == now and stage <= len(stages)
            ]

            def step(due=due, now=now):
                for start, stages, stage in due:
                    if stage > 0:
                        for copy in stages[stage - 1][1]:
                            copy.wait()
                    if stage < len(stages):
                        ahead, copies = stages[stage]
                        if ahead is not None:
                            ahead()
                        for copy in copies:
                            copy.start()

            if tick is None:
                step()
            elif due:
                pl.when(tick == now)(step)
        return last


def arrive(plan, lag, tick, h_ref, s_ref, weights, hs_ref, ss_ref, w_ref, hv, both_ref, rows_ref, wv, halves, send, recv, local):
    dp, seq = place()
    y, x, c = own_bit(4), own_bit(2), own_bit(1)
    loads = [pltpu.make_async_copy(h_ref.at[y], hv, local.at[0])]
    loads += [pltpu.make_async_copy(r, wv.at[i], local.at[1 + i]) for i, r in enumerate(weights)]
    own = pltpu.make_async_copy(hv, hs_ref.at[y, x, c], local.at[0])
    named = pltpu.make_async_copy(rows_ref.at[y], ss_ref.at[y, x, c], local.at[4])
    given = pltpu.make_async_copy(s_ref, both_ref, local.at[5])

    @pl.when(tick == 0)
    def _():
        for load in loads + [given]:
            load.start()
        given.wait()
        for i in range(2):
            rows_ref[i] = both_ref[i : i + 1, :]
        named.start()
        for load in loads:
            load.wait()
        own.start()

    run = Copies(send, recv)
    pieces = []
    pieces.append((0, [
        (None, [run.remote(rows_ref.at[1 - y], ss_ref.at[y, x, c], partner_seq(4))]),
        (named.wait, [run.remote(ss_ref.at[:, x, c], ss_ref.at[:, x, c], partner_seq(2))]),
        (None, [run.remote(ss_ref.at[:, :, c], ss_ref.at[:, :, c], partner_seq(1))]),
    ]))
    tokens = hv.shape[0]
    parts = 4
    for i in range(parts):
        rows = pl.ds(i * (tokens // parts), tokens // parts)
        first = run.remote(h_ref.at[1 - y, rows], hs_ref.at[y, x, c, rows], partner_seq(4))
        second = [run.remote(hs_ref.at[:, x, c, rows], hs_ref.at[:, x, c, rows], partner_seq(2))]
        third = [run.remote(hs_ref.at[:, :, c, rows], hs_ref.at[:, :, c, rows], partner_seq(1))]
        pieces.append((ACTS_AT + i, [(None, [first]), (own.wait if i == 0 else None, second), (None, third)]))

    half, quarter = halves.shape[-1], w_ref.shape[-1]
    for i in range(3):
        mine = pltpu.make_async_copy(
            halves.at[i, :, :, pl.ds(c * quarter, quarter)], w_ref.at[i, dp, y, :, c], local.at[1 + i])

        def cut(i=i, mine=mine):
            halves[i, x] = wv[i, :, pl.ds(pl.multiple_of(x * half, 128), half)]
            mine.start()

        to_x = [run.remote(wv.at[i, :, pl.ds((1 - x) * half, half)], halves.at[i, x], partner_seq(2))]
        to_core = [run.remote(
            halves.at[i, :, :, pl.ds((1 - c) * quarter, quarter)], w_ref.at[i, dp, y, :, c], partner_seq(1))]
        to_z = [run.remote(w_ref.at[i, dp, y], w_ref.at[i, dp, y], partner_dp(plan, m)) for m in plan.masks]
        to_y = [run.remote(w_ref.at[i, :, y], w_ref.at[i, :, y], partner_seq(4))]
        pieces.append((WEIGHTS_AT[i], [(None, to_x), (cut, to_core), (mine.wait, to_z), (None, to_y)]))
    run.run(pieces, ARRIVE_LAG, tick)


ARRIVE_LAG = 2
ACTS_AT, WEIGHTS_AT = 2, (0, 2, 4)
ARRIVED = max(ACTS_AT + 3 + 3 * ARRIVE_LAG, WEIGHTS_AT[-1] + 4 * ARRIVE_LAG)


class Finish:
    everyone = True

    def __init__(
        self, plan, first, packed, grads, mixed_t, lse, seg_col, seg_row, cosine, sine, turned, weights, inputs, grad_first, gain, more
    ):
        count, per, _, columns, _ = packed.shape
        length = count * columns
        self.plan, self.first = plan, first
        self.block = seg_row.shape[1]
        self.steps, self.parts = length // self.block, self.block // columns
        self.count = per * self.steps
        self.begin = first + self.count
        self.split = 4
        self.operands = (
            packed, packed, packed, grads, mixed_t, lse, seg_col, seg_row, cosine, sine, turned, weights, inputs, grad_first, gain, more
        )
        width, quarter = turned.shape[0], weights.shape[2]
        n_dp, masks = plan.n_dp, len(plan.masks)
        rows = width // (8 * n_dp)
        size = columns // self.split
        low = jnp.bfloat16

        def pair(t):
            return lax.div(jnp.clip(t - first, 0, self.count - 1), self.steps)

        def step(t):
            return lax.rem(jnp.clip(t - first, 0, self.count - 1), self.steps)

        def whole(which):
            return pl.BlockSpec(
                (count, None, None, columns, HEAD_DIM), lambda t: (0, pair(t), which, 0, 0), pipeline_mode=pl.Buffered(1))

        def fixed(shape):
            return pl.BlockSpec(shape, lambda t: (0,) * len(shape), pipeline_mode=pl.Buffered(1))

        hbm = pl.BlockSpec(memory_space=pl.ANY)
        self.in_specs = [
            whole(0),
            whole(1),
            whole(2),
            pl.BlockSpec((count, None, columns, HEAD_DIM), lambda t: (0, pair(t), 0, 0), pipeline_mode=pl.Buffered(1)),
            pl.BlockSpec((1, 1, HEAD_DIM, self.block), lambda t: (pair(t), step(t), 0, 0)),
            pl.BlockSpec((1, self.steps, self.block), lambda t: (pair(t), 0, 0)),
            fixed((length, 1)),
            fixed((self.steps, self.block)),
            fixed((length, HEAD_DIM)),
            fixed((length, HEAD_DIM)),
            hbm,
            hbm,
            hbm,
            hbm,
            pl.BlockSpec((width,), lambda t: (0,), pipeline_mode=pl.Buffered(1)),
            fixed((8, width)),
        ]
        self.out_specs = [
            hbm,
            pl.BlockSpec((3, rows, width), lambda t: (0, 0, 0)),
            pl.BlockSpec((rows, 128), lambda t: (0, 0)),
        ]
        self.out_shapes = [
            jax.ShapeDtypeStruct(inputs.shape, jnp.float32),
            jax.ShapeDtypeStruct((3, rows, width), jnp.float32),
            jax.ShapeDtypeStruct((rows, 128), jnp.float32),
        ]
        self.copies = 3 * (3 + masks) + 3 * self.split + 7 + masks
        self.scratch = [
            pltpu.VMEM((HEAD_DIM, length), low),
            pltpu.VMEM((length, HEAD_DIM), jnp.float32),
            pltpu.VMEM((length, HEAD_DIM), jnp.float32),
            pltpu.VMEM((3, length, quarter), low),
            pltpu.VMEM(turned.shape, low),
            pltpu.VMEM(weights.shape, low),
            pltpu.VMEM((2, 2, size, width), jnp.float32),
            pltpu.VMEM((2, 2, size, width), jnp.float32),
            pltpu.VMEM((2, n_dp, 2, 2, 2, rows, quarter), low),
            pltpu.VMEM((3, n_dp, 2, 2, rows, quarter), low),
            pltpu.VMEM((3, masks, 2, 2, rows, quarter), low),
            pltpu.VMEM((3, 2, 2, rows, quarter), low),
            pltpu.VMEM((3, 2, rows, 2 * quarter), low),
            pltpu.VMEM((3, rows, 2 * quarter), low),
            pltpu.VMEM((2, 2, 2, 2, size, width), low),
            pltpu.VMEM((2, 2, 2, size, width), low),
            pltpu.VMEM((2, 2, 2, size, width), low),
            pltpu.VMEM((2, 2, size, width), low),
            pltpu.VMEM((2, 2, size, width), low),
            pltpu.VMEM((2, size, width), low),
            pltpu.VMEM((128, width), jnp.float32),
            pltpu.VMEM((n_dp, 2, 2, 2, rows, 128), low),
            pltpu.VMEM((7, n_dp, rows, 128), low),
            pltpu.VMEM((n_dp, rows, 128), low),
            pltpu.VMEM((masks, rows, 128), low),
            pltpu.SemaphoreType.DMA((self.copies,)),
            pltpu.SemaphoreType.DMA((self.copies,)),
            pltpu.SemaphoreType.DMA((2,)),
            pltpu.SemaphoreType.DMA((2, 3)),
        ]
        backs, products = [2 * i for i in range(self.split)], [(i - per + 1) * self.steps + 4 for i in range(per)]
        self.starts = backs, products
        self.last_norm = backs[-1] + 2 * 3 + 1
        self.ticks = self.begin + max(self.last_norm + 2 * 2, products[-1] + 4 * 4) + 1

    def run(self, tick, refs):
        ins, (dx_ref, dw_ref, dn_ref), scratch = refs[:16], refs[16:19], refs[19:]
        turned_any, weights_any, inputs_any, first_any, gain_ref, more_ref = ins[10:16]
        kt_ref, dk_ref, dv_ref, g_ref, t_ref, w_ref, x_ref, gx_ref = scratch[:8]
        made, made_y, made_z, sum_z, sides, made_x = scratch[8:14]
        acts, acts_c, sum_c, acts_x, sum_x, acts_y = scratch[14:20]
        totals, norms, norms_c, norms_sy, norms_z = scratch[20:25]
        send, recv, local, chunked = scratch[25:]
        plan, parts = self.plan, self.split
        dp, _ = place()
        y, x, c = own_bit(4), own_bit(2), own_bit(1)
        width, length = t_ref.shape
        quarter = w_ref.shape[2]
        columns = length // 8
        half = 2 * quarter
        rows = dw_ref.shape[1]
        size = columns // parts
        low = jnp.bfloat16
        loads = [
            pltpu.make_async_copy(weights_any, w_ref, local.at[0]),
            pltpu.make_async_copy(turned_any, t_ref, local.at[1]),
        ]

        @pl.when(tick == 1)
        def _():
            for load in loads:
                load.start()

        @pl.when((tick >= self.first) & (tick < self.begin))
        def _():
            pair, step = lax.div(tick - self.first, self.steps), lax.rem(tick - self.first, self.steps)
            attend_back_step(self.block, self.parts, pair, step, self.steps - 1, *ins[:10], g_ref, kt_ref, dk_ref, dv_ref)

        masks = len(plan.masks)
        now = tick - self.begin

        def wide(values):
            return values.astype(jnp.float32)

        def stream(starts, stages, lag, base, most):
            gap = starts[1] - starts[0]
            for stage in reversed(range(len(stages))):
                since = now - starts[0] - lag * stage
                i = lax.div(since, gap)

                @pl.when((since >= 0) & (since <= starts[-1] - starts[0]) & (lax.rem(since, gap) == 0))
                def _(stage=stage, i=i):
                    def made_copies(n):
                        at = base + i * most + sum(len(c(0)) for _, c in stages[:n])
                        return [
                            pltpu.make_async_remote_copy(
                                src, dst, send.at[at + k], recv.at[at + k], device_id=other, device_id_type=MESH)
                            for k, (src, dst, other) in enumerate(stages[n][1](i))
                        ]

                    if stage > 0:
                        for copy in made_copies(stage - 1):
                            copy.wait()
                    stages[stage][0](i)
                    for copy in made_copies(stage):
                        copy.start()

        def product(i):
            @pl.when(i == 0)
            def _():
                loads[1].wait()

            step = 8 * rows
            for z in range(plan.n_dp):
                part = dot(t_ref[z * step : (z + 1) * step, :], g_ref[i])
                made[lax.rem(i, 2), z] = part.astype(low).reshape(2, 2, 2, rows, quarter)

        def product_y(i):
            made_y[i] = (wide(made[lax.rem(i, 2), :, y]) + wide(made_y[i])).astype(low)

        def product_z(i):
            total = wide(made_y[i, dp])
            for n in range(masks):
                total = total + wide(made_z[i, n])
            sum_z[i] = total.astype(low)

        def product_c(i):
            sides[i, :, :, pl.ds(pl.multiple_of(c * quarter, 128), quarter)] = sum_z[i, :, c]

        def product_x(i):
            for side, values in ((x, sides.at[i, x]), (1 - x, made_x.at[i])):
                for core in range(2):
                    for kind in range(3):
                        start = core * quarter + kind * HEAD_DIM
                        lanes = pl.ds(pl.multiple_of(side * half + core * quarter + i * HEAD_DIM, HEAD_DIM), HEAD_DIM)
                        dw_ref[kind, :, lanes] = wide(values[:, start : start + HEAD_DIM])

        def back(i):
            @pl.when(i == 0)
            def _():
                loads[0].wait()

            slot = lax.rem(i, 2)
            pieces = []
            for k in range(3):
                blocks = []
                for n in range(8):
                    at = pl.ds(pl.multiple_of(n * columns + i * size, size), size)
                    blocks.append(jnp.concatenate(
                        [g_ref[p, at, k * HEAD_DIM : (k + 1) * HEAD_DIM] for p in range(3)], axis=1))
                pieces.append(jnp.concatenate(blocks, axis=0))
            step = 512
            for n in range(width // step):
                total = sum(dot(pieces[k], w_ref[k, n * step : (n + 1) * step, :], NT) for k in range(3))
                acts[slot, :, :, :, :, n * step : (n + 1) * step] = total.astype(low).reshape(2, 2, 2, size, step)

        def back_c(i):
            slot = lax.rem(i, 2)
            sum_c[slot] = (wide(acts[slot, :, :, c]) + wide(acts_c[slot])).astype(low)

        def chunk(i):
            slot, at = lax.rem(i, 2), pl.ds(pl.multiple_of(i * size, size), size)
            return [
                pltpu.make_async_copy(inputs_any.at[:, at], x_ref.at[slot], chunked.at[slot, 0]),
                pltpu.make_async_copy(first_any.at[:, at], gx_ref.at[slot], chunked.at[slot, 1]),
            ]

        def chunk_out(i):
            slot, at = lax.rem(i, 2), pl.ds(pl.multiple_of(i * size, size), size)
            return pltpu.make_async_copy(gx_ref.at[slot], dx_ref.at[:, at], chunked.at[slot, 2])

        def back_x(i):
            slot = lax.rem(i, 2)

            @pl.when(i >= 2)
            def _():
                chunk_out(i - 2).wait()

            for load in chunk(i):
                load.start()
            sum_x[slot] = (wide(sum_c[slot, :, x]) + wide(acts_x[slot])).astype(low)

        def norm_back(i):
            slot = lax.rem(i, 2)
            for load in chunk(i):
                load.wait()

            @pl.when(i == 0)
            def _():
                totals[...] = jnp.zeros_like(totals)

            gain = gain_ref[...][None]

            def one(s, carry):
                grad = jnp.where(y == s, wide(sum_x[slot, s]), wide(acts_y[slot]))
                values = x_ref[slot, s]
                centre = values - jnp.mean(values, axis=-1, keepdims=True)
                spread = lax.rsqrt(jnp.mean(centre * centre, axis=-1, keepdims=True) + EPSILON)
                normed = centre * spread
                grown = grad * gain
                mean_one = jnp.mean(grown, axis=-1, keepdims=True)
                mean_two = jnp.mean(grown * normed, axis=-1, keepdims=True)
                gx_ref[slot, s] = gx_ref[slot, s] + (grown - mean_one - normed * mean_two) * spread
                totals[0:1] += jnp.sum(grad * normed, axis=0, keepdims=True)
                totals[1:2] += jnp.sum(grad, axis=0, keepdims=True)
                return carry

            lax.fori_loop(0, 2, one, 0)
            chunk_out(i).start()

        stream(self.starts[0], [
            (back, lambda i: [(acts.at[lax.rem(i, 2), :, :, 1 - c], acts_c.at[lax.rem(i, 2)], partner_seq(1))]),
            (back_c, lambda i: [(sum_c.at[lax.rem(i, 2), :, 1 - x], acts_x.at[lax.rem(i, 2)], partner_seq(2))]),
            (back_x, lambda i: [(sum_x.at[lax.rem(i, 2), 1 - y], acts_y.at[lax.rem(i, 2)], partner_seq(4))]),
            (norm_back, lambda i: []),
        ], 2, 0, 3)
        stream(self.starts[1], [
            (product, lambda i: [(made.at[lax.rem(i, 2), :, 1 - y], made_y.at[i], partner_seq(4))]),
            (product_y, lambda i: [
                (made_y.at[i, lax.bitwise_xor(dp, m)], made_z.at[i, n], partner_dp(plan, m))
                for n, m in enumerate(plan.masks)]),
            (product_z, lambda i: [
                (sum_z.at[i, :, 1 - c], sides.at[i, :, :, pl.ds(c * quarter, quarter)], partner_seq(1))]),
            (product_c, lambda i: [(sides.at[i, 1 - x], made_x.at[i], partner_seq(2))]),
            (product_x, lambda i: []),
        ], 4, 3 * parts, 3 + masks)
        run = Copies(send, recv)
        run.count = 3 * parts + 3 * (3 + masks)
        pieces = []

        def norms_start():
            totals[2:4] = more_ref[0:2]
            norms[...] = totals[...].T.astype(low).reshape(norms.shape)

        def norms_end():
            total = wide(norms_sy[dp])
            for n in range(len(plan.masks)):
                total = total + wide(norms_z[n])
            dn_ref[...] = total
            for i in range(parts - 2, parts):
                chunk_out(i).wait()

        _, seq = place()

        def norms_to(m):
            return norms.at[(slice(None),) + tuple(lax.bitwise_xor(own_bit(b), int(m & b > 0)) for b in plan.bits)]

        def norms_seq():
            total = wide(norms[:, y, x, c])
            for m in range(1, 8):
                total = total + wide(norms_c[m - 1])
            norms_sy[...] = total.astype(low)

        pieces.append((self.last_norm, [
            (norms_start, [run.remote(norms_to(m), norms_c.at[m - 1], partner_seq(m)) for m in range(1, 8)]),
            (norms_seq, [
                run.remote(norms_sy.at[lax.bitwise_xor(dp, m)], norms_z.at[n], partner_dp(plan, m))
                for n, m in enumerate(plan.masks)]),
            (norms_end, []),
        ]))
        run.run(pieces, 2, now)


class Gather:
    def __init__(self, plan, lag, shard, rows, cols, routes):
        self.plan, self.lag, self.rows, self.cols = plan, lag, rows, cols
        self.routes = plan.routes[routes]
        self.across = shard.shape[1] // cols
        self.pieces = shard.shape[0] // rows * self.across
        self.ticks = self.pieces + lag * (plan.hops + 1)
        self.out_shape = jax.ShapeDtypeStruct(plan.lead() + shard.shape, shard.dtype)
        each = 2 * (len(plan.masks) + plan.hops)
        self.scratch = [
            pltpu.VMEM(shard.shape, shard.dtype),
            pltpu.SemaphoreType.DMA((self.pieces, each)),
            pltpu.SemaphoreType.DMA((self.pieces, each)),
            pltpu.SemaphoreType.DMA((2,)),
        ]

    def copies(self, kind, stage, u, full, held, send, recv):
        plan = self.plan
        dp, _ = place()
        rows = pl.ds(pl.multiple_of(lax.div(u, self.across) * self.rows, 16), self.rows)
        out = []
        routes = self.routes[kind]
        one = routes[0][stage] == routes[1][stage] and set(routes[0][:stage]) == set(routes[1][:stage])
        for h in range(1 if one else 2):
            start = lax.rem(u, self.across) * self.cols + h * (self.cols // 2)
            cols = pl.ds(pl.multiple_of(start, 128), self.cols if one else self.cols // 2)
            route = self.routes[kind][h]
            entry, done = route[stage], route[:stage]
            where = (slice(None) if "dp" in done else dp,)
            where += tuple(slice(None) if b in done else own_bit(b) for b in plan.bits)
            part = full.at[where + (rows, cols)]
            src = part if stage else held.at[rows, cols]
            at = h * (len(plan.masks) + plan.hops) + plan.sems(route, stage)
            others = [partner_dp(plan, m) for m in plan.masks] if entry == "dp" else [partner_seq(entry)]
            for n, other in enumerate(others):
                out.append(pltpu.make_async_remote_copy(
                    src, part, send.at[u, at + n], recv.at[u, at + n], device_id=other, device_id_type=MESH))
        return out

    def run(self, tick, shard, full, held, send, recv, local):
        plan, lag = self.plan, self.lag
        dp, _ = place()
        me = tuple(own_bit(b) for b in plan.bits)
        own = pltpu.make_async_copy(held, full.at[(dp,) + me], local.at[0])

        @pl.when(tick == 0)
        def _():
            load = pltpu.make_async_copy(shard, held, local.at[1])
            load.start()
            load.wait()
            own.start()

        @pl.when(tick == lag)
        def _():
            own.wait()

        stages = plan.hops + 1
        for stage in reversed(range(stages + 1)):
            u = tick - lag * stage
            count = len(self.routes)
            for kind in range(count):
                if self.routes[kind] in self.routes[:kind]:
                    continue
                mine = False
                for other in range(count):
                    if self.routes[other] == self.routes[kind]:
                        mine = mine | (lax.rem(u, count) == other)

                @pl.when((u >= 0) & (u < self.pieces) & mine)
                def _(stage=stage, u=u, kind=kind):
                    if stage > 0:
                        for copy in self.copies(kind, stage - 1, u, full, held, send, recv):
                            copy.wait()
                    if stage < stages:
                        for copy in self.copies(kind, stage, u, full, held, send, recv):
                            copy.start()


def attend_step(block, parts, pair, step, packed, col_ref, row_ref, o_ref, ot_ref, lse_ref, vt_ref):
    @pl.when(step == 0)
    def _():
        vt_ref[...] = packed[:, pair, 2].reshape(-1, HEAD_DIM).T

    query = packed[pl.ds(step * parts, parts), pair, 0].reshape(block, HEAD_DIM)
    query_row = row_ref[pl.ds(step, 1), :]
    unit = LOG2E / math.sqrt(HEAD_DIM)

    def visit(j, carry, diagonal):
        top, total, mixed = carry
        key = packed[pl.ds(j * parts, parts), pair, 1].reshape(block, HEAD_DIM)
        at = pl.multiple_of(j * block, block)
        scores = dot(key, query, NT) * unit
        scores = jnp.where(allowed_pairs(col_ref[pl.ds(at, block), :], query_row, diagonal), scores, MASKED)
        above = jnp.maximum(top, jnp.max(scores, axis=0, keepdims=True))
        expo = jnp.exp2(scores - above)
        fade = jnp.exp2(top - above)
        total = total * fade + jnp.sum(expo, axis=0, keepdims=True)
        mixed = mixed * fade + dot(vt_ref[:, pl.ds(at, block)], expo.astype(jnp.bfloat16))
        return above, total, mixed

    start = (
        jnp.full((1, block), MASKED, jnp.float32),
        jnp.zeros((1, block), jnp.float32),
        jnp.zeros((HEAD_DIM, block), jnp.float32),
    )
    carry = lax.fori_loop(0, step, lambda j, c: visit(j, c, False), start)
    top, total, mixed = visit(step, carry, True)
    mixed = mixed / total
    ot_ref[0, 0] = mixed
    lse_ref[0, pl.ds(step, 1), :] = top + jnp.log2(total)
    o_ref[...] = mixed.T.astype(jnp.bfloat16).reshape(o_ref.shape)


def attention_kernel(
    plan, lag, gathers, block, steps, h_ref, s_ref, q_ref, k_ref, v_ref, cos_ref, sin_ref, out_shard, up_shard,
    packed, turned_ref, o_ref, ot_ref, lse_ref, col_ref, row_ref, hs_ref, ss_ref, w_ref, full_out, full_up,
    vt_ref, x_ref, weights_ref, ids_ref, hv, both_ref, rows_ref, wv, halves, send, recv, local, fetch, *more,
):
    tick = pl.program_id(0)

    @pl.when(tick == 0)
    def _():
        greet(plan)

    arrive(plan, lag, tick, h_ref, s_ref, (q_ref, k_ref, v_ref), hs_ref, ss_ref, w_ref, hv, both_ref, rows_ref, wv, halves, send, recv, local)
    for (first, gather), shard, full, held in zip(
        gathers, (out_shard, up_shard), (full_out, full_up), (more[:4], more[4:])
    ):
        gather.run(tick - first, shard, full, *held)
    _, parts, columns, width = x_ref.shape
    heads = packed.shape[1]
    first = ARRIVED + 1

    def acts_load(i):
        return pltpu.make_async_copy(hs_ref.at[lax.div(i, 2), lax.rem(i, 2)], x_ref.at[lax.rem(i, 2)], fetch.at[lax.rem(i, 2)])

    def weights_load(kind):
        return pltpu.make_async_copy(w_ref.at[kind], weights_ref.at[kind], fetch.at[2 + kind])

    ids_load = pltpu.make_async_copy(ss_ref, ids_ref, fetch.at[5])
    named = 3 * ARRIVE_LAG

    @pl.when(tick == named)
    def _():
        ids_load.start()

    @pl.when(tick == named + 1)
    def _():
        ids_load.wait()
        ids = ids_ref[...].reshape(2 * steps, columns)
        for i in range(2 * steps):
            row_ref[i // parts : i // parts + 1, (i % parts) * columns : (i % parts + 1) * columns] = ids[i : i + 1]
        turned = ids.astype(jnp.float32).T.astype(jnp.int32)
        for i in range(2 * steps):
            mine = turned[:, i : i + 1]
            col_ref[i * columns : (i + 1) * columns, :] = jnp.where(mine < 0, -2, mine)

    for kind in range(3):

        @pl.when(tick == WEIGHTS_AT[kind] + 4 * ARRIVE_LAG)
        def _(kind=kind):
            weights_load(kind).start()

    @pl.when(tick == ARRIVED)
    def _():
        acts_load(0).start()
        for kind in range(3):
            weights_load(kind).wait()

    at = tick - first

    @pl.when((at >= 0) & (at < steps))
    def _():
        @pl.when(at + 1 < steps)
        def _():
            acts_load(at + 1).start()

        acts_load(at).wait()
        acts = x_ref[lax.rem(at, 2)].reshape(block, width)
        for kind in range(3):
            made = dot(acts, weights_ref[kind].reshape(width, heads * HEAD_DIM))
            for p in range(heads):
                head = made[:, p * HEAD_DIM : (p + 1) * HEAD_DIM]
                if kind < 2:
                    head = head * cos_ref[...] + pltpu.roll(head, HEAD_DIM // 2, 1) * sin_ref[...]
                packed[pl.ds(at * parts, parts), p, kind] = head.astype(jnp.bfloat16).reshape(parts, columns, HEAD_DIM)
        turned_ref[...] = acts.T

    @pl.when((at >= steps) & (at < steps * (1 + heads)))
    def _():
        pair, step = lax.div(at - steps, steps), lax.rem(at - steps, steps)
        attend_step(block, parts, pair, step, packed, col_ref, row_ref, o_ref, ot_ref, lse_ref, vt_ref)


def attention(plan, acts, segments, weights, cosine, sine, out_shard, up_shard, lag, collective_id):
    _, columns, width = acts.shape
    rows = weights[0].shape[0]
    quarter = width // 4
    heads = quarter // HEAD_DIM
    owners = 8
    length, block = owners * columns, 2 * columns
    steps, parts = length // block, 2
    gathers = (
        (0, Gather(plan, 3, out_shard, out_shard.shape[0], 512, "late")),
        (7, Gather(plan, 3, up_shard, up_shard.shape[0], 512, "late")),
    )
    low = jnp.bfloat16
    begin = ARRIVED + 1

    def at(t):
        return jnp.clip(t - begin, 0, steps - 1)

    def pair(t):
        return lax.div(jnp.clip(t - begin - steps, 0, steps * heads - 1), steps)

    def step(t):
        return lax.rem(jnp.clip(t - begin - steps, 0, steps * heads - 1), steps)

    def fixed(shape):
        return pl.BlockSpec(shape, lambda t: (0,) * len(shape))

    hbm = pl.BlockSpec(memory_space=pl.ANY)
    table = pl.BlockSpec((block, HEAD_DIM), lambda t: (at(t), 0))
    packed_shape = (owners, heads, 3, columns, HEAD_DIM)
    acts_shape = (2, 2, 2, columns, width)
    ids_shape = (2, 2, 2, 1, columns)
    weights_shape = (3,) + plan.lead() + (rows, quarter)
    copies = 3 + 4 * 3 + 3 * (3 + len(plan.masks))
    ticks = max([begin + steps * (1 + heads)] + [first + gather.ticks for first, gather in gathers])
    return pl.pallas_call(
        functools.partial(attention_kernel, plan, lag, gathers, block, steps),
        grid=(ticks,),
        in_specs=[hbm] * 5 + [table, table, hbm, hbm],
        out_specs=[
            fixed(packed_shape),
            pl.BlockSpec((width, block), lambda t: (0, at(t))),
            pl.BlockSpec((parts, None, columns, HEAD_DIM), lambda t: (step(t), pair(t), 0, 0)),
            pl.BlockSpec((1, 1, HEAD_DIM, block), lambda t: (pair(t), step(t), 0, 0)),
            pl.BlockSpec((1, steps, block), lambda t: (pair(t), 0, 0)),
            fixed((length, 1)),
            fixed((steps, block)),
            hbm,
            hbm,
            hbm,
            hbm,
            hbm,
        ],
        out_shape=[
            jax.ShapeDtypeStruct(packed_shape, low),
            jax.ShapeDtypeStruct((width, length), low),
            jax.ShapeDtypeStruct((owners, heads, columns, HEAD_DIM), low),
            jax.ShapeDtypeStruct((heads, steps, HEAD_DIM, block), jnp.float32),
            jax.ShapeDtypeStruct((heads, steps, block), jnp.float32),
            jax.ShapeDtypeStruct((length, 1), jnp.int32),
            jax.ShapeDtypeStruct((steps, block), jnp.int32),
            jax.ShapeDtypeStruct(acts_shape, low),
            jax.ShapeDtypeStruct(ids_shape, jnp.int32),
            jax.ShapeDtypeStruct(weights_shape, low),
            gathers[0][1].out_shape,
            gathers[1][1].out_shape,
        ],
        scratch_shapes=[
            pltpu.VMEM((HEAD_DIM, length), low),
            pltpu.VMEM((2, parts, columns, width), low),
            pltpu.VMEM(weights_shape, low),
            pltpu.VMEM(ids_shape, jnp.int32),
            pltpu.VMEM((columns, width), low),
            pltpu.VMEM((2, columns), jnp.int32),
            pltpu.VMEM((2, 1, columns), jnp.int32),
            pltpu.VMEM((3, rows, width), low),
            pltpu.VMEM((3, 2, rows, width // 2), low),
            pltpu.SemaphoreType.DMA((copies,)),
            pltpu.SemaphoreType.DMA((copies,)),
            pltpu.SemaphoreType.DMA((6,)),
            pltpu.SemaphoreType.DMA((6,)),
        ] + gathers[0][1].scratch + gathers[1][1].scratch,
        compiler_params=pltpu.CompilerParams(
            collective_id=collective_id, has_side_effects=True, vmem_limit_bytes=56 << 20),
    )(acts, segments, *weights, cosine, sine, out_shard, up_shard)


class Mlp:
    def __init__(self, plan, lag, mixed, w_out, inputs, gain, offset, w_up, grad, cotangent, shard):
        tokens, width = inputs.shape
        hidden = w_up.shape[1]
        self.plan, self.lag = plan, lag
        self.blocks = 2 * plan.n_dp
        self.block = hidden // self.blocks
        self.rows = width // (plan.n_dp * plan.n_seq)
        self.gather = Gather(plan, lag, shard, self.rows, 512, "some late")
        self.meet = 5
        self.up = self.meet + 1
        self.back = max(self.gather.ticks, self.up + self.blocks)
        self.norm = self.back + self.blocks
        self.ticks = self.norm + 5
        self.operands = (mixed, w_out, inputs, gain, offset, w_up, grad, cotangent, shard)
        blocks, back, up = self.blocks, self.back, self.up

        def up_block(t):
            later = jnp.clip(t - (up + blocks) + 1, 0, 1)
            return (0, jnp.clip(t - up, 0, blocks - 1) * (1 - later) + jnp.clip(t - back, 0, blocks - 1) * later)

        once = pl.BlockSpec((tokens, width), lambda t: (0, 0), pipeline_mode=pl.Buffered(1))
        row = pl.BlockSpec((width,), lambda t: (0,))
        hbm = pl.BlockSpec(memory_space=pl.ANY)
        self.in_specs = [hbm, hbm, hbm, row, row, pl.BlockSpec((width, self.block), up_block), hbm, hbm, hbm]
        self.out_specs = [
            hbm,
            hbm,
            hbm,
            hbm,
            hbm,
            hbm,
            pl.BlockSpec((tokens, self.block), lambda t: (0, jnp.clip(t - back, 0, blocks - 1))),
            hbm,
            pl.BlockSpec((8, width), lambda t: (0, 0)),
            hbm,
        ]
        low = jnp.bfloat16
        flat = jax.ShapeDtypeStruct((tokens, width), jnp.float32)
        self.out_shapes = [
            flat,
            flat,
            flat,
            jax.ShapeDtypeStruct((tokens, width), low),
            jax.ShapeDtypeStruct((width, tokens), low),
            jax.ShapeDtypeStruct((width, tokens), low),
            jax.ShapeDtypeStruct((tokens, hidden), low),
            jax.ShapeDtypeStruct(mixed.shape, low),
            jax.ShapeDtypeStruct((8, width), jnp.float32),
            self.gather.out_shape,
        ]
        self.chunk = 64
        self.scratch = [
            pltpu.VMEM((tokens, hidden), low),
            pltpu.VMEM((hidden, tokens), low),
            pltpu.VMEM((tokens, hidden), low),
            pltpu.VMEM((2, 2, 2) + shard.shape, low),
            pltpu.VMEM((tokens, width), jnp.float32),
            pltpu.VMEM((tokens, width), jnp.float32),
            pltpu.VMEM((tokens, width), low),
            pltpu.VMEM(mixed.shape, low),
            pltpu.VMEM((2, 2, self.chunk, width), jnp.float32),
            pltpu.SemaphoreType.DMA((2, 2, plan.n_seq)),
            pltpu.SemaphoreType.DMA((16,)),
            pltpu.SemaphoreType.DMA((2, 2)),
            pltpu.SemaphoreType.DMA((2,)),
        ] + self.gather.scratch + [pltpu.VMEM((tokens, width), low)]

    everyone = True

    def left(self, refs, which, z):
        turned, n = refs[20], self.plan.n_seq
        every = turned.shape[0] // (n * self.plan.n_dp)
        return jnp.concatenate(
            [
                turned[pl.ds(pl.multiple_of((z * n + d) * every + which * self.rows, 16), self.rows), :]
                for d in range(n)
            ],
            axis=0,
        )

    def run(self, tick, refs):
        mixed_hbm, w_out, inputs, gain_ref, offset_ref, up_ref, _, cotangent, shard = refs[:9]
        grad_ref = refs[36]
        output, first_sum, grad_first, grad_low, mixed_turned, acts_turned, gu_ref, back_pairs, sums_ref, full = refs[9:19]
        hidden_ref, turned_ref, slope_ref, down_ref, out_ref, back_ref, acts_ref, pairs, chunks = refs[19:28]
        swaps, local, loads, fetch = refs[28:32]
        plan, block = self.plan, self.block
        dp, seq = place()
        count, heads, columns, _ = pairs.shape
        tokens, width = acts_ref.shape
        low = jnp.bfloat16
        third = 512
        thirds = width // third
        self.gather.run(tick, shard, full, *refs[32:36])

        def exchange(which, src, dst):
            return [
                pltpu.make_async_remote_copy(
                    src.at[lax.bitwise_xor(seq, m)], dst.at[seq], swaps.at[which, 0, m], swaps.at[which, 1, m],
                    device_id=partner_seq(m), device_id_type=MESH)
                for m in range(1, count)
            ]

        there = exchange(0, mixed_hbm, pairs)
        here = pltpu.make_async_copy(mixed_hbm.at[seq], pairs.at[seq], local.at[0])
        based = pltpu.make_async_copy(inputs, out_ref, local.at[1])
        outs = [
            pltpu.make_async_copy(
                w_out.at[:, pl.ds(n * third, third)], turned_ref.at[pl.ds(n * width, width), :], local.at[2 + n])
            for n in range(thirds)
        ]
        kept = pltpu.make_async_copy(out_ref, first_sum, local.at[5])
        turns = []
        for n in range(thirds):
            rows = pl.ds(n * third, third)
            base = slope_ref.shape[1] - 2 * width + n * third
            turns.append(pltpu.make_async_copy(slope_ref.at[:, pl.ds(base, third)], mixed_turned.at[rows, :], local.at[6 + n]))
            turns.append(pltpu.make_async_copy(
                slope_ref.at[:, pl.ds(base + width, third)], acts_turned.at[rows, :], local.at[9 + n]))

        @pl.when(tick == 0)
        def _():
            for copy in there + [here, based] + outs:
                copy.start()

        @pl.when(tick == 1)
        def _():
            size = self.chunk
            total = tokens // size

            def load(j):
                slot = lax.rem(j, 2)
                rows = pl.ds(pl.multiple_of(j * size, size), size)
                return pltpu.make_async_copy(cotangent.at[rows, :], chunks.at[slot, 0], loads.at[slot, 0])

            load(0).start()

            def rounded(j, carry):
                @pl.when(j + 1 < total)
                def _():
                    load(j + 1).start()

                load(j).wait()
                rows = pl.ds(pl.multiple_of(j * size, size), size)
                grad_ref[rows, :] = chunks[lax.rem(j, 2), 0].astype(low)
                return carry

            lax.fori_loop(0, total, rounded, 0)

        @pl.when(tick == self.meet)
        def _():
            for copy in there + [here, based] + outs:
                copy.wait()
            per = width // (heads * HEAD_DIM)
            for s in range(count // per):
                for g in range(per):
                    for p in range(heads):
                        at = (g * heads + p) * HEAD_DIM
                        acts_ref[s * columns : (s + 1) * columns, at : at + HEAD_DIM] = pairs[s * per + g, p]
            for n in range(thirds):
                part = slice(n * third, (n + 1) * third)
                out_ref[:, part] += dot(acts_ref[...], turned_ref[n * width : (n + 1) * width, :])
                base = slope_ref.shape[1] - 2 * width + n * third
                slope_ref[:, base : base + third] = acts_ref[:, part].T
            kept.start()

            def norm(i, carry):
                rows = pl.ds(pl.multiple_of(i * self.chunk, self.chunk), self.chunk)
                values = out_ref[rows, :]
                centre = values - jnp.mean(values, axis=-1, keepdims=True)
                spread = lax.rsqrt(jnp.mean(centre * centre, axis=-1, keepdims=True) + EPSILON)
                acts_ref[rows, :] = (centre * spread * gain_ref[...][None] + offset_ref[...][None]).astype(low)
                return carry

            lax.fori_loop(0, tokens // self.chunk, norm, 0)
            for n in range(thirds):
                base = slope_ref.shape[1] - width + n * third
                slope_ref[:, base : base + third] = acts_ref[:, n * third : (n + 1) * third].T
            for copy in turns:
                copy.start()

        @pl.when(tick == self.up + 2)
        def _():
            for copy in turns + [kept]:
                copy.wait()

        def block_at(i):
            return pl.ds(pl.multiple_of(i * block, 128), block)

        @pl.when((tick >= self.up) & (tick < self.up + self.blocks))
        def _():
            step = 256
            for n in range(block // step):
                upper = dot(acts_ref[...], up_ref[:, n * step : (n + 1) * step])
                share = 0.5 + 0.5 * lax.erf(upper * (1.0 / math.sqrt(2.0)))
                density = jnp.exp(upper * upper * -0.5) * (1.0 / math.sqrt(2.0 * math.pi))
                made = (upper * share).astype(low)
                at = pl.multiple_of((tick - self.up) * block + n * step, 128)
                hidden_ref[:, pl.ds(at, step)] = made
                turned_ref[pl.ds(at, step), :] = made.T
                slope_ref[:, pl.ds(at, step)] = (share + upper * density).astype(low)

        def fetched(i):
            z, y = lax.div(i, 2), lax.rem(i, 2)
            return pltpu.make_async_copy(full.at[z, y], down_ref.at[y], fetch.at[y])

        i = tick - self.back

        @pl.when((i >= -1) & (i < self.blocks - 1))
        def _():
            fetched(i + 1).start()

        @pl.when((i >= 0) & (i < self.blocks))
        def _():
            fetched(i).wait()
            down = down_ref[lax.rem(i, 2)].reshape(block, -1)

            @pl.when(i == 0)
            def _():
                back_ref[...] = jnp.zeros_like(back_ref)

            grad = dot(grad_ref[...], down, NT) * slope_ref[:, block_at(i)].astype(jnp.float32)
            gu_ref[...] = grad.astype(low)
            for n in range(thirds):
                part = slice(n * third, (n + 1) * third)
                out_ref[:, part] += dot(hidden_ref[:, block_at(i)], down[:, part])
                back_ref[:, part] += dot(gu_ref[...], up_ref[part, :], NT)

        done = pltpu.make_async_copy(out_ref, output, local.at[12])
        first_out = pltpu.make_async_copy(back_ref, grad_first, local.at[13])
        low_out = pltpu.make_async_copy(acts_ref, grad_low, local.at[14])
        chunk = self.chunk

        def chunk_loads(j, slot):
            rows = pl.ds(pl.multiple_of(j * chunk, chunk), chunk)
            return [
                pltpu.make_async_copy(src.at[rows, :], chunks.at[slot, n], loads.at[slot, n])
                for n, src in enumerate((first_sum, cotangent))
            ]

        @pl.when(tick == self.norm - 1)
        def _():
            for copy in outs:
                copy.start()

        @pl.when(tick == self.norm)
        def _():
            done.start()
            sums_ref[...] = jnp.zeros_like(sums_ref)
            for copy in chunk_loads(0, 0):
                copy.start()
            total = tokens // chunk

            def norm_back(j, carry):
                slot = lax.rem(j, 2)

                @pl.when(j + 1 < total)
                def _():
                    for copy in chunk_loads(j + 1, 1 - slot):
                        copy.start()

                for copy in chunk_loads(j, slot):
                    copy.wait()
                rows = pl.ds(pl.multiple_of(j * chunk, chunk), chunk)
                values = chunks[slot, 0]
                centre = values - jnp.mean(values, axis=-1, keepdims=True)
                spread = lax.rsqrt(jnp.mean(centre * centre, axis=-1, keepdims=True) + EPSILON)
                normed = centre * spread
                grad = back_ref[rows, :]
                grown = grad * gain_ref[...][None]
                mean_one = jnp.mean(grown, axis=-1, keepdims=True)
                mean_two = jnp.mean(grown * normed, axis=-1, keepdims=True)
                made = chunks[slot, 1] + (grown - mean_one - normed * mean_two) * spread
                sums_ref[0:1] += jnp.sum(grad * normed, axis=0, keepdims=True)
                sums_ref[1:2] += jnp.sum(grad, axis=0, keepdims=True)
                back_ref[rows, :] = made
                acts_ref[rows, :] = made.astype(low)
                return carry

            lax.fori_loop(0, total, norm_back, 0)
            first_out.start()
            low_out.start()

        again = exchange(1, pairs, back_pairs)
        home = pltpu.make_async_copy(pairs.at[seq], back_pairs.at[seq], local.at[0])

        @pl.when(tick == self.norm + 1)
        def _():
            for copy in outs:
                copy.wait()
            per = width // (heads * HEAD_DIM)
            step = heads * HEAD_DIM
            for g in range(per):
                made = sum(
                    dot(acts_ref[:, n * third : (n + 1) * third],
                        turned_ref[n * width + g * step : n * width + (g + 1) * step, :], NT)
                    for n in range(thirds)
                ).astype(low)
                for s in range(count // per):
                    for p in range(heads):
                        pairs[s * per + g, p] = made[s * columns : (s + 1) * columns, p * HEAD_DIM : (p + 1) * HEAD_DIM]
            for copy in again + [home]:
                copy.start()

        @pl.when(tick == self.ticks - 1)
        def _():
            for copy in again + [home, done, first_out, low_out]:
                copy.wait()


def settle_kernel(piece, *refs):
    (out_any, dx_any, heads_any, down_any, rest_any, norms_ref), refs = refs[:6], refs[6:]
    (output, dx, d_query, d_key, d_value, d_out, d_up, d_down), refs = refs[:8], refs[8:]
    sums, (out_ref, dx_ref, heads_ref, down_ref, rest_ref, load_sem, store_sem) = refs[:4], refs[4:]
    rows = heads_ref.shape[1]
    parts = out_ref.shape[0]
    across = heads_ref.shape[2] // piece
    loads, stores = [], []

    def move(src, held, targets):
        load = pltpu.make_async_copy(src, held, load_sem.at[len(loads)])
        load.start()
        loads.append((load, [
            pltpu.make_async_copy(part, target, store_sem.at[len(stores) + n]) for n, (part, target) in enumerate(targets)
        ]))
        stores.extend(loads[-1][1])

    for i in range(parts):
        move(out_any.at[i], out_ref.at[i], [(out_ref.at[i], output.at[i])])
        move(dx_any.at[i], dx_ref.at[i], [(dx_ref.at[i], dx.at[i])])
    wide_count = rest_any.shape[0] - across
    move(rest_any, rest_ref, [
        (rest_ref.at[n], d_up.at[:, pl.ds(n * piece, piece)] if n < wide_count
         else d_out.at[:, pl.ds((n - wide_count) * piece, piece)])
        for n in range(rest_any.shape[0])
    ])
    move(down_any, down_ref, [
        (down_ref.at[n], d_down.at[pl.ds(n // across * rows, rows), pl.ds(n % across * piece, piece)])
        for n in range(down_any.shape[0])
    ])
    for i, target in enumerate((d_query, d_key, d_value)):
        move(heads_any.at[i], heads_ref.at[i], [(heads_ref.at[i], target)])
    turned = norms_ref[...].T
    for i, target in enumerate(sums):
        target[...] = turned[i : i + 1, :].reshape(target.shape)
    for load, after in loads:
        load.wait()
        for store in after:
            store.start()
    for store in stores:
        store.wait()


def settle(output, dx, heads, down, rest, norms, piece):
    rows, width = heads.shape[1:]
    across = width // piece
    up_width = (rest.shape[0] - across) * piece
    blocks = down.shape[0] // across
    hbm = pl.BlockSpec(memory_space=pl.ANY)
    vmem = pl.BlockSpec(memory_space=pltpu.VMEM)
    f32 = jnp.float32
    arrays = (output, dx, heads, down, rest)
    return pl.pallas_call(
        functools.partial(settle_kernel, piece),
        in_specs=[hbm] * 5 + [vmem],
        out_specs=[hbm] * 8 + [vmem] * 4,
        out_shape=[jax.ShapeDtypeStruct(output.shape, f32), jax.ShapeDtypeStruct(dx.shape, f32)]
        + [jax.ShapeDtypeStruct((rows, width), f32)] * 4
        + [jax.ShapeDtypeStruct((rows, up_width), f32), jax.ShapeDtypeStruct((blocks * rows, width), f32)]
        + [jax.ShapeDtypeStruct((rows,), f32)] * 4,
        scratch_shapes=[pltpu.VMEM(a.shape, f32) for a in arrays] + [
            pltpu.SemaphoreType.DMA((2 * output.shape[0] + 5,)),
            pltpu.SemaphoreType.DMA((2 * output.shape[0] + 3 + down.shape[0] + rest.shape[0],)),
        ],
        compiler_params=pltpu.CompilerParams(vmem_limit_bytes=63 << 20),
    )(output, dx, heads, down, rest, norms)


def layer_norm(values, gain, offset):
    centre = values - jnp.mean(values, axis=-1, keepdims=True)
    spread = jnp.mean(centre * centre, axis=-1, keepdims=True)
    return centre * lax.rsqrt(spread + EPSILON) * gain + offset


def gelu(values):
    return 0.5 * values * (1.0 + lax.erf(values * (1.0 / math.sqrt(2.0))))


def angles(positions):
    half = HEAD_DIM // 2
    rates = jnp.exp(jnp.arange(half, dtype=jnp.float32) * (-math.log(10000.0) / half))
    turned = positions.astype(jnp.float32)[:, None] * rates[None, :]
    return (jnp.cos(turned)[:, None, :], jnp.sin(turned)[:, None, :])


def rotary(values, cosine, sine):
    half = values.shape[-1] // 2
    first = values[..., :half]
    second = values[..., half:]
    return jnp.concatenate(
        [first * cosine - second * sine, second * cosine + first * sine], axis=-1
    )


def lower(values):
    return values.astype(jnp.bfloat16)


def project(acts, weight):
    return jnp.einsum("gcd,de->gce", acts, weight, preferred_element_type=jnp.float32)


def project_back(grads, weight):
    return jnp.einsum("gce,de->gcd", grads, weight, preferred_element_type=jnp.float32)


def outer_sum(left, right):
    return jnp.einsum("gci,gcj->ij", left, right, preferred_element_type=jnp.float32)


def plain_shards(
    inputs,
    segments,
    norm1_gain,
    norm1_bias,
    w_query,
    w_key,
    w_value,
    w_out,
    norm2_gain,
    norm2_bias,
    w_up,
    w_down,
    cotangent,
):
    groups, columns, width = inputs.shape
    heads_count = width // HEAD_DIM
    scale = 1.0 / math.sqrt(HEAD_DIM)
    full_query, full_key, full_value, full_out, full_up, full_down = (
        lax.all_gather(w_query, ("dp", "seq"), axis=0, tiled=True),
        lax.all_gather(w_key, ("dp", "seq"), axis=0, tiled=True),
        lax.all_gather(w_value, ("dp", "seq"), axis=0, tiled=True),
        lax.all_gather(w_out, ("dp", "seq"), axis=0, tiled=True),
        lax.all_gather(w_up, ("dp", "seq"), axis=0, tiled=True),
        lax.all_gather(w_down, ("dp", "seq"), axis=0, tiled=True),
    )
    key_ids = lax.all_gather(segments, "seq", axis=1, tiled=True)
    length = key_ids.shape[1]
    rank = lax.axis_index("seq")
    places = rank * columns + jnp.arange(columns, dtype=jnp.int32)
    key_places = jnp.arange(length, dtype=jnp.int32)
    cosine, sine = angles(places)

    def turn(values):
        shaped = values.reshape(groups, columns, heads_count, HEAD_DIM)
        return rotary(shaped, cosine, sine).reshape(groups, columns, width)

    def permitted(segment_row, key_row):
        same = segment_row[:, None] == key_row[None, :]
        causal = key_places[None, :] <= places[:, None]
        live = (key_row[None, :] >= 0) | (key_places[None, :] == places[:, None])
        return same & causal & live

    def scores_of(query_row, key_block, segment_row, key_row):
        heads_query = query_row.reshape(columns, heads_count, HEAD_DIM)
        heads_key = key_block.reshape(length, heads_count, HEAD_DIM)
        raw = (
            jnp.einsum("chd,lhd->hcl", heads_query, heads_key, preferred_element_type=jnp.float32)
            * scale
        )
        return jnp.where(permitted(segment_row, key_row)[None], raw, MASKED)

    normed_one = layer_norm(inputs, norm1_gain, norm1_bias)
    act_one = lower(normed_one)
    query_zero = project(act_one, full_query)
    key_zero = project(act_one, full_key)
    value_low = lower(project(act_one, full_value))
    query_low = lower(turn(query_zero))
    key_low = lower(turn(key_zero))
    keys_all, values_all = (
        lax.all_gather(key_low, "seq", axis=1, tiled=True),
        lax.all_gather(value_low, "seq", axis=1, tiled=True),
    )

    def attend(items):
        query_row, key_block, value_block, segment_row, key_row = items
        scores = scores_of(query_row, key_block, segment_row, key_row)
        top = jnp.max(scores, axis=-1, keepdims=True)
        expo = jnp.exp(scores - top)
        total = jnp.sum(expo, axis=-1, keepdims=True)
        probs = lower(expo / total)
        heads_value = value_block.reshape(length, heads_count, HEAD_DIM)
        mixed = jnp.einsum("hcl,lhd->chd", probs, heads_value, preferred_element_type=jnp.float32)
        return (mixed.reshape(columns, width), top[..., 0] + jnp.log(total[..., 0]))

    mixed_all, log_totals = lax.map(attend, (query_low, keys_all, values_all, segments, key_ids))
    mixed_low = lower(mixed_all)
    first_sum = inputs + project(mixed_low, full_out)
    act_two = lower(layer_norm(first_sum, norm2_gain, norm2_bias))
    upper = project(act_two, full_up)
    hidden_low = lower(gelu(upper))
    output = first_sum + project(hidden_low, full_down)
    half_width = width // 2
    half_hidden = full_up.shape[1] // 2
    grad_out_low = lower(cotangent)
    down_left = outer_sum(hidden_low, grad_out_low[..., :half_width])
    down_right = outer_sum(hidden_low, grad_out_low[..., half_width:])
    grad_hidden = project_back(grad_out_low, full_down)
    gelu_values, gelu_back = jax.vjp(gelu, upper)
    grad_upper = lower(gelu_back(grad_hidden)[0])
    up_left = outer_sum(act_two, grad_upper[..., :half_hidden])
    up_right = outer_sum(act_two, grad_upper[..., half_hidden:])
    grad_act_two = project_back(grad_upper, full_up)
    normed_two, norm_two_back = jax.vjp(layer_norm, first_sum, norm2_gain, norm2_bias)
    grad_first_norm, gain_two_grad, offset_two_grad = norm_two_back(grad_act_two)
    grad_first = cotangent + grad_first_norm
    grad_attn_low = lower(grad_first)
    out_grad = outer_sum(mixed_low, grad_attn_low)
    grad_mixed = lower(project_back(grad_attn_low, full_out))
    heads_mixed = mixed_all.reshape(groups, columns, heads_count, HEAD_DIM)
    heads_gm = grad_mixed.astype(jnp.float32).reshape(groups, columns, heads_count, HEAD_DIM)
    deltas = jnp.transpose(jnp.sum(heads_mixed * heads_gm, axis=-1), (0, 2, 1))
    key_source, value_source = (key_low, value_low)

    def attend_back(carry, items):
        query_row, grad_row, log_row, delta_row, segment_row, key_row, key_part, value_part = items
        queries_all, grads_all = (
            lax.all_gather(query_row, "seq", axis=0, tiled=True),
            lax.all_gather(grad_row, "seq", axis=0, tiled=True),
        )
        logs_all, deltas_all = (
            lax.all_gather(log_row, "seq", axis=1, tiled=True),
            lax.all_gather(delta_row, "seq", axis=1, tiled=True),
        )
        own_mask = (segment_row[None, :] == key_row[:, None]) & (
            places[None, :] <= key_places[:, None]
        )
        own_mask = own_mask & (
            (segment_row[None, :] >= 0) | (places[None, :] == key_places[:, None])
        )
        heads_query = queries_all.reshape(length, heads_count, HEAD_DIM)
        heads_grad = grads_all.reshape(length, heads_count, HEAD_DIM)
        heads_key = key_part.reshape(columns, heads_count, HEAD_DIM)
        heads_value = value_part.reshape(columns, heads_count, HEAD_DIM)
        raw = (
            jnp.einsum("lhd,chd->hlc", heads_query, heads_key, preferred_element_type=jnp.float32)
            * scale
        )
        scores = jnp.where(own_mask[None], raw, MASKED)
        probs = jnp.exp(scores - logs_all[..., None])
        grad_probs = jnp.einsum(
            "lhd,chd->hlc", heads_grad, heads_value, preferred_element_type=jnp.float32
        )
        grad_scores = lower(probs * (grad_probs - deltas_all[..., None]))
        grad_values = jnp.einsum(
            "hlc,lhd->chd", lower(probs), heads_grad, preferred_element_type=jnp.float32
        )
        grad_keys = (
            jnp.einsum("hlc,lhd->chd", grad_scores, heads_query, preferred_element_type=jnp.float32)
            * scale
        )
        partial_query = (
            jnp.einsum("hlc,chd->lhd", grad_scores, heads_key, preferred_element_type=jnp.float32)
            * scale
        )
        grad_query = lax.psum_scatter(
            partial_query.reshape(length, width).astype(jnp.bfloat16),
            "seq",
            scatter_dimension=0,
            tiled=True,
        ).astype(jnp.float32)
        return (
            carry,
            (grad_query, grad_keys.reshape(columns, width), grad_values.reshape(columns, width)),
        )

    start_carry = jnp.zeros((), jnp.float32)
    end_carry, grads_seq = lax.scan(
        attend_back,
        start_carry,
        (query_low, grad_mixed, log_totals, deltas, segments, key_ids, key_source, value_source),
    )
    grad_query_all, grad_key_all, grad_value_all = grads_seq
    turned_query, turn_back = jax.vjp(turn, query_zero)
    grad_query_low = lower(turn_back(grad_query_all)[0])
    grad_key_low = lower(turn_back(grad_key_all)[0])
    grad_value_low = lower(grad_value_all)
    query_grad = outer_sum(act_one, grad_query_low)
    key_grad = outer_sum(act_one, grad_key_low)
    value_grad = outer_sum(act_one, grad_value_low)
    grad_act_one = project_back(grad_query_low, full_query) + project_back(grad_key_low, full_key)
    grad_act_one = grad_act_one + project_back(grad_value_low, full_value)
    normed_again, norm_one_back = jax.vjp(layer_norm, inputs, norm1_gain, norm1_bias)
    grad_input_norm, gain_one_grad, offset_one_grad = norm_one_back(grad_act_one)
    grad_input = grad_first + grad_input_norm
    summed = (
        lax.psum_scatter(query_grad, ("dp", "seq"), scatter_dimension=0, tiled=True),
        lax.psum_scatter(key_grad, ("dp", "seq"), scatter_dimension=0, tiled=True),
        lax.psum_scatter(value_grad, ("dp", "seq"), scatter_dimension=0, tiled=True),
        lax.psum_scatter(out_grad, ("dp", "seq"), scatter_dimension=0, tiled=True),
        lax.psum_scatter(up_left, ("dp", "seq"), scatter_dimension=0, tiled=True),
        lax.psum_scatter(up_right, ("dp", "seq"), scatter_dimension=0, tiled=True),
        lax.psum_scatter(down_left, ("dp", "seq"), scatter_dimension=0, tiled=True),
        lax.psum_scatter(down_right, ("dp", "seq"), scatter_dimension=0, tiled=True),
        lax.psum_scatter(gain_one_grad, ("dp", "seq"), scatter_dimension=0, tiled=True),
        lax.psum_scatter(offset_one_grad, ("dp", "seq"), scatter_dimension=0, tiled=True),
        lax.psum_scatter(gain_two_grad, ("dp", "seq"), scatter_dimension=0, tiled=True),
        lax.psum_scatter(offset_two_grad, ("dp", "seq"), scatter_dimension=0, tiled=True),
    )
    query_grad, key_grad, value_grad, out_grad = (summed[0], summed[1], summed[2], summed[3])
    up_left, up_right, down_left, down_right = (summed[4], summed[5], summed[6], summed[7])
    gain_one_grad, offset_one_grad, gain_two_grad, offset_two_grad = (
        summed[8],
        summed[9],
        summed[10],
        summed[11],
    )
    up_grad = jnp.concatenate([up_left, up_right], axis=1)
    down_grad = jnp.concatenate([down_left, down_right], axis=1)
    return (
        output,
        grad_input,
        gain_one_grad,
        offset_one_grad,
        query_grad,
        key_grad,
        value_grad,
        out_grad,
        gain_two_grad,
        offset_two_grad,
        up_grad,
        down_grad,
    )


def shards(
    inputs,
    segments,
    norm1_gain,
    norm1_bias,
    w_query,
    w_key,
    w_value,
    w_out,
    norm2_gain,
    norm2_bias,
    w_up,
    w_down,
    cotangent,
    *,
    plan,
):
    groups, columns, width = inputs.shape
    length = columns * plan.n_seq
    lag, piece = 2, 512
    every = plan.n_dp * plan.n_seq

    half = HEAD_DIM // 2
    rates = np.exp(np.arange(half, dtype=np.float32) * np.float32(-math.log(10000.0) / half))
    angle = (np.arange(length, dtype=np.float32)[:, None] * rates[None, :]).astype(np.float32)
    cosine = jnp.asarray(np.concatenate([np.cos(angle), np.cos(angle)], axis=1), jnp.float32)
    sine = jnp.asarray(np.concatenate([-np.sin(angle), np.sin(angle)], axis=1), jnp.float32)

    def flat(values):
        return values.reshape(groups * columns, width)

    act_one = lower(layer_norm(inputs, norm1_gain, norm1_bias))
    packed, turned_one, mixed, mixed_t, lse, seg_col, seg_row, _, _, heads_weight, full_out, full_up = attention(
        plan, act_one, segments, (w_query, w_key, w_value), cosine, sine, w_out, w_up, lag, 1
    )
    grad_out = flat(cotangent)
    mlp = Mlp(
        plan, lag, mixed, full_out.reshape(width, width), flat(inputs), norm2_gain, norm2_bias,
        full_up.reshape(width, -1), grad_out, grad_out, w_down,
    )
    rows = width // every

    (
        down_grad, output, _, grad_first, grad_first_low, mixed_turned, acts_turned, grad_upper, grad_pairs,
        sums_two, _,
    ) = reduce_products(
        plan, [(w_down.shape[0] // rows, grad_out)], rows, piece, lag, "late", 3, mlp, 14
    )
    work = Finish(
        plan, 0, packed, grad_pairs, mixed_t, lse, seg_col, seg_row, cosine, sine, turned_one,
        heads_weight.reshape(3, width, -1), inputs, grad_first.reshape(inputs.shape), norm1_gain, sums_two,
    )
    rest_grads, grad_input, heads_grad, norm_rows = reduce_products(
        plan, [(acts_turned[None], grad_upper), (mixed_turned[None], grad_first_low)], rows, piece, lag, "x late", 4, work
    )
    (
        output, grad_input, query_grad, key_grad, value_grad, out_grad, up_grad, down_grad, *norm_sums
    ) = settle(output.reshape(inputs.shape), grad_input, heads_grad, down_grad, rest_grads, norm_rows, piece)
    return (
        output,
        grad_input,
        norm_sums[0],
        norm_sums[1],
        query_grad,
        key_grad,
        value_grad,
        out_grad,
        norm_sums[2],
        norm_sums[3],
        up_grad,
        down_grad,
    )


def fits(mesh, groups, columns, width, rows):
    return (
        mesh.shape["seq"] == 8
        and groups == 2
        and width % (4 * HEAD_DIM) == 0
        and columns == 256
        and rows % 16 == 0
    )


def solution(mesh):
    placed = (
        P("dp", "seq", None),
        P("dp", "seq"),
        P(),
        P(),
        P(("dp", "seq"), None),
        P(("dp", "seq"), None),
        P(("dp", "seq"), None),
        P(("dp", "seq"), None),
        P(),
        P(),
        P(("dp", "seq"), None),
        P(("dp", "seq"), None),
        P("dp", "seq", None),
    )
    plan = Plan(mesh)

    def layer(inputs, segments, *rest):
        groups, columns, width = inputs.shape
        if fits(mesh, groups, columns, width, rest[2].shape[0]):
            return shards(inputs, segments, *rest, plan=plan)
        return plain_shards(inputs, segments, *rest)

    return jax.shard_map(
        layer,
        mesh=mesh,
        in_specs=placed,
        out_specs=(
            P("dp", "seq", None),
            P("dp", "seq", None),
            P(("dp", "seq")),
            P(("dp", "seq")),
            P(("dp", "seq"), None),
            P(("dp", "seq"), None),
            P(("dp", "seq"), None),
            P(("dp", "seq"), None),
            P(("dp", "seq")),
            P(("dp", "seq")),
            P(("dp", "seq"), None),
            P(("dp", "seq"), None),
        ),
        check_vma=False,
    )
```
